32 devices in a mesh: batch: 2 (over y), hidden: 8 (over z, core), width: 2 (over x).
Axes of the slice: x: 2, y: 2, z: 4, core: 2. Of those that a mesh axis runs over, the one named last changes fastest.
Arguments:
- tokens: bfloat16 [8192, 512], P(('batch', 'hidden'), 'width'), may hold values from -6 to 6
- ln1_gain: float32 [512], P('width'), may hold values from 0.5 to 1.5
- ln1_bias: float32 [512], P('width'), may hold values from -1.5 to 1.5
- w_query: bfloat16 [512, 512], P(None, 'width'), may hold values from -0.25 to 0.25
- w_key: bfloat16 [512, 512], P(None, 'width'), may hold values from -0.25 to 0.25
- w_value: bfloat16 [512, 512], P(None, 'width'), may hold values from -0.25 to 0.25
- w_out: bfloat16 [512, 512], P('width'), may hold values from -2 to 2
- gate1_weight: bfloat16 [512, 512], P(None, 'width'), may hold values from -0.25 to 0.25
- gate1_bias: float32 [512], P('width'), may hold values from -2 to 2
- ln2_gain: float32 [512], P('width'), may hold values from 0.5 to 1.5
- ln2_bias: float32 [512], P('width'), may hold values from -1.5 to 1.5
- gate2_weight: bfloat16 [512, 512], P(None, 'width'), may hold values from -0.25 to 0.25
- gate2_bias: float32 [512], P('width'), may hold values from -2 to 2
- w_up: bfloat16 [512, 2048], P('width', 'hidden'), may hold values from -0.25 to 0.25
- w_down: bfloat16 [2048, 512], P('hidden', 'width'), may hold values from -0.25 to 0.25
- lengths: int32 [2, 3], P('batch'), may hold values from 1 to 4094, as said below
- cotangent: bfloat16 [8192, 512], P(('batch', 'hidden'), 'width'), may hold values from -6 to 6
Outputs:
- output: bfloat16 [8192, 512], P(('batch', 'hidden'), 'width')
- grad_tokens: float32 [8192, 512], P(('batch', 'hidden'), 'width')
- grad_ln1_gain: float32 [512], P('width')
- grad_ln1_bias: float32 [512], P('width')
- grad_w_query: float32 [512, 512], P(None, 'width')
- grad_w_key: float32 [512, 512], P(None, 'width')
- grad_w_value: float32 [512, 512], P(None, 'width')
- grad_w_out: float32 [512, 512], P('width')
- grad_gate1_weight: float32 [512, 512], P(None, 'width')
- grad_gate1_bias: float32 [512], P('width')
- grad_ln2_gain: float32 [512], P('width')
- grad_ln2_bias: float32 [512], P('width')
- grad_gate2_weight: float32 [512, 512], P(None, 'width')
- grad_gate2_bias: float32 [512], P('width')
- grad_w_up: float32 [512, 2048], P('width', 'hidden')
- grad_w_down: float32 [2048, 512], P('hidden', 'width')
The draws below stay inside these ranges and needn't reach their ends.
Inputs may be any that keep to these rules, and one draw needn't show every extreme that they name: `lengths`: in every group, slot 1 starts at or before position 256 and ends within the last 256 positions; slot 0 holds 1 to 256 tokens, slot 2 holds 1 to 128, and at most 128 padding positions follow. In one group, drawn from the seed, slots 0 and 2 hold one token each and no padding follows.
All inputs are finite; a program needn't handle non-finite values.
Results may differ from the reference program's by a relative error of at most 0.014.
Values may be sent and summed in bfloat16 or wider, within the bound.
A program may use at most 192 MiB of HBM per device.

```python
import jax
import jax.numpy as jnp
from jax import lax

D = 512
FF = 2048
HEAD_DIM = 64
HEADS = 8
ROWS = 512
GROUP = 4096
GROUPS = 2
TOKENS = 8192


def draw_lengths(key, part):
    key = jax.random.fold_in(key, 11)
    first_key, second_key, third_key, fourth_key = jax.random.split(key, 4)
    head_len = jax.random.randint(first_key, (GROUPS,), 1, ROWS // 2 + 1)
    tail_len = jax.random.randint(second_key, (GROUPS,), 1, ROWS // 4 + 1)
    padding = jax.random.randint(third_key, (GROUPS,), 0, ROWS // 4 + 1)
    chosen = jax.random.randint(fourth_key, (), 0, GROUPS)
    picked = jnp.arange(GROUPS, dtype=jnp.int32) == chosen
    head_len = jnp.where(picked, 1, head_len)
    tail_len = jnp.where(picked, 1, tail_len)
    padding = jnp.where(picked, 0, padding)
    middle_len = GROUP - head_len - tail_len - padding
    return jnp.stack([head_len, middle_len, tail_len], 1).astype(jnp.int32)


def levels(key, extent, cuts, smallest, high):
    def one(axis_at, parts):
        draws = jax.random.uniform(jax.random.fold_in(jax.random.fold_in(key, 6), axis_at), (parts,), jnp.float32, smallest / len(cuts), high / len(cuts))
        return jnp.repeat(jnp.exp(draws), extent[axis_at] // parts).reshape((-1,) + (1,) * (len(extent) - axis_at - 1))

    level = one(*cuts[0])
    for cut in cuts[1:]:
        level = level * one(*cut)
    return level


def noise(rng, extent, scale, bound, cuts=(), kind=jnp.bfloat16):
    factor_of = levels(rng, extent, cuts, -0.22, 0.18) if cuts else 1.0
    entries = jax.random.normal(rng, extent, jnp.float32) * scale * factor_of
    return jnp.minimum(jnp.maximum(entries, -bound), bound).astype(kind)


def setup_inputs(seed: int = 0) -> dict:
    seeds = jax.random.split(jax.random.key(seed), 18)
    tokens = noise(seeds[0], (TOKENS, D), 1.0, 6.0, ((0, 16), (1, 2)))
    ln1_gain = jnp.clip(1.0 + 0.1 * jax.random.normal(seeds[1], (D,), jnp.float32), 0.5, 1.5)
    ln1_bias = noise(seeds[2], (D,), 0.3, 1.5, ((0, 2),), jnp.float32)
    w_query = noise(seeds[3], (D, D), D ** -0.5, 0.25, ((1, 2),))
    w_key = noise(seeds[4], (D, D), D ** -0.5, 0.25, ((1, 2),))
    w_value = noise(seeds[5], (D, D), D ** -0.5, 0.25, ((1, 2),))
    w_out = noise(seeds[6], (D, D), (D // 64) ** -0.5, 2.0, ((0, 2),))
    gate1_weight = noise(seeds[7], (D, D), D ** -0.5, 0.25, ((1, 2),))
    gate1_bias = noise(seeds[8], (D,), 0.5, 2.0, ((0, 2),), jnp.float32)
    ln2_gain = jnp.clip(1.0 + 0.1 * jax.random.normal(seeds[9], (D,), jnp.float32), 0.5, 1.5)
    ln2_bias = noise(seeds[10], (D,), 0.3, 1.5, ((0, 2),), jnp.float32)
    gate2_weight = noise(seeds[11], (D, D), D ** -0.5, 0.25, ((1, 2),))
    gate2_bias = noise(seeds[12], (D,), 0.5, 2.0, ((0, 2),), jnp.float32)
    w_up = noise(seeds[13], (D, FF), D ** -0.5, 0.25, ((0, 2), (1, 8)))
    w_down = noise(seeds[14], (FF, D), (FF // 4) ** -0.5, 0.25, ((0, 8), (1, 2)))
    lengths = draw_lengths(jax.random.fold_in(seeds[17], 71), 0)
    cotangent = noise(seeds[16], (TOKENS, D), 1.0, 6.0, ((0, 16), (1, 2)))
    return {"tokens": tokens, "ln1_gain": ln1_gain, "ln1_bias": ln1_bias, "w_query": w_query, "w_key": w_key, "w_value": w_value, "w_out": w_out, "gate1_weight": gate1_weight, "gate1_bias": gate1_bias, "ln2_gain": ln2_gain, "ln2_bias": ln2_bias, "gate2_weight": gate2_weight, "gate2_bias": gate2_bias, "w_up": w_up, "w_down": w_down, "lengths": lengths, "cotangent": cotangent}


EPSILON = 1e-05

@jax.custom_vjp
def low(v):
    return lax.optimization_barrier(v.astype(jnp.bfloat16)).astype(jnp.float32)

@jax.custom_vjp
def low_back(v):
    return v

def low_keep(v):
    return (low(v), None)

def low_pass(kept, grad):
    return (grad,)

def back_keep(v):
    return (v, None)

def back_low(kept, grad):
    return (low(grad),)
low.defvjp(low_keep, low_pass)
low_back.defvjp(back_keep, back_low)

def layer_norm(values, gain, shift):
    centre = values - lax.optimization_barrier(jnp.mean(values, -1, keepdims=True))
    spread = lax.optimization_barrier(jnp.mean(centre * centre, -1, keepdims=True))
    return centre * lax.rsqrt(spread + EPSILON) * gain + shift

def matmul(left, right):
    return jnp.dot(left, right, precision=lax.Precision.HIGHEST)

def attend_group(queries, keys, values, segment):
    block = min(512, GROUP)
    count = GROUP // block
    query_heads = queries.reshape(GROUP, HEADS, HEAD_DIM)
    key_heads = keys.reshape(GROUP, HEADS, HEAD_DIM)
    value_heads = values.reshape(GROUP, HEADS, HEAD_DIM)
    positions = jnp.arange(GROUP, dtype=jnp.int32)

    def one_block(start):
        query_block = lax.dynamic_slice_in_dim(query_heads, start, block, 0)
        query_pos = start + jnp.arange(block, dtype=jnp.int32)
        query_seg = lax.dynamic_slice_in_dim(segment, start, block, 0)
        scores = jnp.einsum('qhd,khd->hqk', query_block, key_heads, precision=lax.Precision.HIGHEST) * HEAD_DIM ** (-0.5)
        scores = low_back(scores)
        allowed = (query_seg[:, None] == segment[None, :]) & (positions[None, :] <= query_pos[:, None])
        scores = jnp.where(allowed[None], scores, -1e+30)
        top = lax.optimization_barrier(jnp.max(scores, -1, keepdims=True))
        weights = jnp.exp(scores - top)
        probs = weights / lax.optimization_barrier(jnp.sum(weights, -1, keepdims=True))
        return jnp.einsum('hqk,khd->qhd', low(probs), value_heads, precision=lax.Precision.HIGHEST)
    starts = jnp.arange(count, dtype=jnp.int32) * block
    mixed = lax.map(jax.checkpoint(one_block), starts)
    return mixed.reshape(GROUP, HEADS * HEAD_DIM)

def forward(tokens, params, segments):
    ln1_gain, ln1_bias, w_query, w_key, w_value, w_out, gate1_weight, gate1_bias, ln2_gain, ln2_bias, gate2_weight, gate2_bias, w_up, w_down = params
    normed_one = low(layer_norm(tokens, ln1_gain, ln1_bias))
    queries = low_back(low(matmul(normed_one, w_query)))
    keys = low_back(low(matmul(normed_one, w_key)))
    values = low_back(low(matmul(normed_one, w_value)))
    pieces = []
    for group_index in range(GROUPS):
        lower = group_index * GROUP
        pieces.append(attend_group(queries[lower:lower + GROUP], keys[lower:lower + GROUP], values[lower:lower + GROUP], segments[group_index]))
    attended = low_back(low(jnp.concatenate(pieces, 0)))
    branch_one = low_back(matmul(attended, w_out))
    gate_one = jax.nn.sigmoid(low_back(matmul(normed_one, gate1_weight) + gate1_bias))
    middle = tokens + gate_one * (branch_one - tokens)
    normed_two = low(layer_norm(middle, ln2_gain, ln2_bias))
    gate_two = jax.nn.sigmoid(low_back(matmul(normed_two, gate2_weight) + gate2_bias))
    pre_act = low_back(matmul(normed_two, w_up))
    hidden_act = low(jax.nn.gelu(pre_act))
    branch_two = low_back(matmul(hidden_act, w_down))
    return middle + gate_two * (branch_two - middle)

def reference(tokens, ln1_gain, ln1_bias, w_query, w_key, w_value, w_out, gate1_weight, gate1_bias, ln2_gain, ln2_bias, gate2_weight, gate2_bias, w_up, w_down, lengths, cotangent):
    seq_ends = jnp.cumsum(lengths, 1)
    positions = jnp.arange(GROUP, dtype=jnp.int32)
    segments = lax.optimization_barrier(jnp.sum((positions[None, :, None] >= seq_ends[:, None, :]).astype(jnp.int32), -1))
    params = tuple((item.astype(jnp.float32) for item in (ln1_gain, ln1_bias, w_query, w_key, w_value, w_out, gate1_weight, gate1_bias, ln2_gain, ln2_bias, gate2_weight, gate2_bias, w_up, w_down)))

    def apply_layer(values_in, *weights):
        return forward(values_in, weights, segments)
    result, back = jax.vjp(apply_layer, tokens.astype(jnp.float32), *params)
    grads = back(cotangent.astype(jnp.float32))
    return (result.astype(jnp.bfloat16), grads[0], grads[1], grads[2], grads[3], grads[4], grads[5], grads[6], grads[7], grads[8], grads[9], grads[10], grads[11], grads[12], grads[13], grads[14])
```

```python
import functools

import jax
import jax.numpy as jnp
from jax import lax
from jax.experimental import pallas as pl
from jax.experimental.pallas import tpu as pltpu
from jax.sharding import PartitionSpec as P

HD = 64
EPSILON = 1e-05
MESH = pl.DeviceIdType.MESH
F32 = jnp.float32
BF16 = jnp.bfloat16
NEG = -1e30
VMEM_LIMIT = 60 * 1024 * 1024


def nn(a, b):
    return lax.dot_general(a, b, (((1,), (0,)), ((), ())), preferred_element_type=F32)


def nt(a, b):
    return lax.dot_general(a, b, (((1,), (1,)), ((), ())), preferred_element_type=F32)


def place():
    return lax.axis_index("batch"), lax.axis_index("hidden"), lax.axis_index("width")


def remote(src, dst, send, recv, dev):
    return pltpu.make_async_remote_copy(
        src_ref=src, dst_ref=dst, send_sem=send, recv_sem=recv, device_id=dev, device_id_type=MESH
    )


def at(index, size):
    return pl.ds(pl.multiple_of(index * size, size), size)


def greet_group(nh, b, h, w):
    barrier = pltpu.get_barrier_semaphore()
    for dw in range(2):
        for dh in range(nh):
            if dh or dw:
                dev = (b, lax.rem(h + dh, nh), lax.rem(w + dw, 2))
                pl.semaphore_signal(barrier, inc=1, device_id=dev, device_id_type=MESH)
    pl.semaphore_wait(barrier, 2 * nh - 1)


def sub_row(index, sub, dph):
    return jnp.where(lax.rem(index, 2) == 0, sub, dph - 1 - sub)


def segments(pos, ends):
    total = jnp.zeros(pos.shape, jnp.int32)
    for end in ends:
        total = total + (pos >= end).astype(jnp.int32)
    return total


def allowed_mask(key_base, query_base, keys, queries, ends):
    key_pos = key_base + lax.broadcasted_iota(jnp.int32, (keys, 1), 0)
    query_pos = query_base + lax.broadcasted_iota(jnp.int32, (1, queries), 1)
    same = segments(key_pos, ends) == segments(query_pos, ends)
    return same & (key_pos <= query_pos)


def for_key_blocks(h, nh, block, carry):
    plain_end = jnp.where(h == nh - 1, 1, jnp.maximum(h, 1))
    carry = lax.fori_loop(1, plain_end, lambda j, c: block(j, c, False), carry)
    masked = 1 + jnp.where(h > 0, h + 1 - plain_end, 0)

    def some(t, c):
        return block(jnp.where(t == 0, 0, plain_end + t - 1), c, True)

    return lax.fori_loop(0, masked, some, carry)


def front_kernel(nh, rows, dims, *refs):
    (
        lens, tok, cot, vecs, wq, wk, wv,
        tok_rows, cot_rows, vecf, normed, att_t, kvt, kvn, qt, ot, lse, wqt_out, wkvt_out,
        tokf, wqt, wkvt, qsrc, kvsrc, osend,
        xs, xr, qs, qr, ks, kr, fs, fr, osnd, orcv, lsem,
    ) = refs
    heads, dph, tq, half = dims
    b, h, w = place()
    group, sub = lax.div(h, dph), lax.rem(h, dph)
    partner = (b, h, 1 - w)
    cw = 256
    chunks = rows // half
    own = at(w, cw)
    other = at(1 - w, cw)
    ends = [lens[0, 0], lens[0, 0] + lens[0, 1], lens[0, 0] + lens[0, 1] + lens[0, 2]]

    greet_group(nh, b, h, w)

    vecf[:, own] = vecs[...]
    copies = [remote(vecs, vecf.at[:, own], xs.at[0], xr.at[0], partner)]
    for c in range(chunks):
        part = pl.ds(c * half, half)
        copies.append(
            remote(tok.at[part], tokf.at[part, own], xs.at[1 + c], xr.at[1 + c], partner)
        )
    copies.append(
        remote(cot.at[at(1 - w, half)], cot_rows.at[:, own], xs.at[1 + chunks], xr.at[1 + chunks], partner)
    )
    for copy in copies:
        copy.start()
    tokf[:, own] = tok[...]
    cot_rows[:, own] = cot[at(w, half), :]

    wqt[...] = wq[...].astype(F32).T.astype(BF16)
    wkt = wk[...].astype(F32).T.astype(BF16)
    wvt = wv[...].astype(F32).T.astype(BF16)
    for t in range(heads):
        wkvt[t, :HD, :] = wkt[t * HD : (t + 1) * HD]
        wkvt[t, HD:, :] = wvt[t * HD : (t + 1) * HD]
    wqt_out[...] = wqt[...]
    wkvt_out[...] = wkvt[...]

    copies[0].wait()
    gain = vecf[0:1, :]
    shift = vecf[1:2, :]
    sends = []
    per_chunk = half // tq
    for c in range(chunks):
        part = slice(c * half, (c + 1) * half)
        copies[1 + c].wait()
        x = tokf[part, :].astype(F32)
        centre = x - jnp.mean(x, -1, keepdims=True)
        spread = jnp.mean(centre * centre, -1, keepdims=True)
        n = (centre * lax.rsqrt(spread + EPSILON) * gain + shift).astype(BF16)
        normed[part, :] = n
        q = (nt(wqt[...], n)).astype(BF16)
        for t in range(heads):
            qsrc[t, :, part] = q[t * HD : (t + 1) * HD]
            kvsrc[t, :, part] = nt(wkvt[t], n).astype(BF16)
        for k in range(heads - 1, -1, -1):
            t = lax.rem(group + k, heads)
            dev = (b, t * dph + sub, w)
            src, dst = kvsrc.at[t, :, pl.ds(c * half, half)], kvt.at[h, :, pl.ds(c * half, half)]
            if k:
                copy = remote(src, dst, ks.at[k, c], kr.at[h, c], dev)
                copy.start()
                sends.append((None, copy))
            else:
                pltpu.make_async_copy(src, dst, kr.at[h, c]).start()
            for i in range(per_chunk):
                r = c * per_chunk + i
                target = sub_row(h, r, dph)
                src, dst = qsrc.at[t, :, pl.ds(r * tq, tq)], qt.at[h]
                copy = remote(src, dst, qs.at[k, r], qr.at[h], (b, t * dph + target, w))
                if k:
                    copy.start()
                    sends.append((None, copy))
                else:
                    away = target != sub

                    @pl.when(away)
                    def _(copy=copy):
                        copy.start()

                    @pl.when(jnp.logical_not(away))
                    def _(src=src, dst=dst):
                        pltpu.make_async_copy(src, dst, qr.at[h]).start()

                    sends.append((away, copy))

    tok_rows[...] = tokf[at(w, half), :]

    def pass_on(s, _):
        direct = lax.rem(s, dph) == sub

        @pl.when(direct)
        def _():
            for c in range(chunks):
                part = kvt.at[s, :, pl.ds(c * half, half)]
                pltpu.make_async_copy(part, part, kr.at[s, c]).wait()
            for k in range(1, dph):
                dev = (b, group * dph + lax.rem(sub + k, dph), w)
                remote(kvt.at[s], kvt.at[s], fs.at[s, k], fr.at[s], dev).start()

        return 0

    lax.fori_loop(0, nh, pass_on, 0)

    def arrive(s):
        @pl.when(lax.rem(s, dph) != sub)
        def _():
            pltpu.make_async_copy(kvt.at[s], kvt.at[s], fr.at[s]).wait()

        kvn[s] = kvt[s].astype(F32).T.astype(BF16)
        pltpu.make_async_copy(qt.at[s], qt.at[s], qr.at[s]).wait()

    def one_query_block(s, _):
        arrive(s)
        r = sub_row(s, sub, dph)
        query_base = s * rows + r * tq
        q = qt[s].astype(F32) * (HD**-0.5)
        q = jnp.concatenate([q, jnp.zeros_like(q)], 0).astype(BF16)

        def block(j, carry, masked):
            top, total, mixed = carry
            scores = nn(kvn[j], q)
            if masked:
                keep = allowed_mask(j * rows, query_base, rows, tq, ends)
                scores = jnp.where(keep, scores, NEG)
            new_top = jnp.maximum(top, jnp.max(scores, 0, keepdims=True))
            fade = jnp.exp(top - new_top)
            weights = jnp.exp(scores - new_top)
            total = total * fade + jnp.sum(weights, 0, keepdims=True)
            mixed = mixed * fade + nn(kvt[j, HD:, :], weights.astype(BF16))
            return new_top, total, mixed

        init = (jnp.full((1, tq), NEG, F32), jnp.zeros((1, tq), F32), jnp.zeros((HD, tq), F32))
        top, total, mixed = for_key_blocks(s, nh, block, init)
        mixed = mixed / total
        ot[s] = mixed
        lse[s] = top + jnp.log(total)
        osend[s] = mixed.astype(BF16)
        row_w = lax.div(r * tq, half)
        lane = lax.rem(r * tq, half)
        place_in = lax.div(lane, tq)
        dst = att_t.at[at(w * heads + group, HD), pl.ds(pl.multiple_of(lane, tq), tq)]
        slot = orcv.at[w * heads + group, place_in]
        here = (s == h) & (row_w == w)

        @pl.when(here)
        def _():
            pltpu.make_async_copy(osend.at[s], dst, slot).start()

        @pl.when(jnp.logical_not(here))
        def _():
            remote(osend.at[s], dst, osnd.at[s], slot, (b, s, row_w)).start()

        return 0

    lax.fori_loop(0, nh, one_query_block, 0)

    for g in range(2 * heads):
        for i in range(half // tq):
            dst = att_t.at[pl.ds(g * HD, HD), pl.ds(i * tq, tq)]
            pltpu.make_async_copy(dst, dst, orcv.at[g, i]).wait()

    def sent(s, _):
        r = sub_row(s, sub, dph)
        here = (s == h) & (lax.div(r * tq, half) == w)

        @pl.when(jnp.logical_not(here))
        def _():
            pltpu.make_async_copy(osend.at[s], osend.at[s], osnd.at[s]).wait()

        @pl.when(lax.rem(s, dph) == sub)
        def _():
            for k in range(1, dph):
                pltpu.make_async_copy(kvt.at[s], kvt.at[s], fs.at[s, k]).wait()

        return 0

    lax.fori_loop(0, nh, sent, 0)
    copies[-1].wait()
    for away, copy in sends:
        if away is None:
            copy.wait_send()
        else:

            @pl.when(away)
            def _(copy=copy):
                copy.wait_send()


def sigmoid(x):
    return 1.0 / (1.0 + jnp.exp(-x))


def middle_kernel(nh, *refs):
    (
        tok_rows, cot_rows, vecf, normed, att_t, wg1, wg2, wout, wup, wdn,
        out_rows, gatt_t, gup, gdn_t, gwo, gg1, gg2, vecp, ginp, gterm,
        pre_s, act_s,
    ) = refs
    half = tok_rows.shape[0]
    w = lax.axis_index("width")
    cw = 256
    tok = tok_rows[...].astype(F32)
    n1 = normed[at(w, half), :]

    def two(a, wt):
        return jnp.concatenate([nn(a, wt[0]), nn(a, wt[1])], 1)

    def two_back(g, wt):
        return nt(g[:, :cw], wt[0]) + nt(g[:, cw:], wt[1])

    attended = att_t[...].astype(F32).T.astype(BF16)
    branch_one = nn(attended, wout[...])
    gate_one = sigmoid(two(n1, wg1) + vecf[2:3, :])
    middle = tok + gate_one * (branch_one - tok)
    centre = middle - jnp.mean(middle, -1, keepdims=True)
    rstd = lax.rsqrt(jnp.mean(centre * centre, -1, keepdims=True) + EPSILON)
    n2 = centre * rstd
    gain_two = vecf[3:4, :]
    normed_two = (n2 * gain_two + vecf[4:5, :]).astype(BF16)
    gate_two = sigmoid(two(normed_two, wg2) + vecf[5:6, :])

    def up(i, branch):
        pre = nn(normed_two, wup[i])
        pre_s[i] = pre
        act = jax.nn.gelu(pre).astype(BF16)
        act_s[i] = act
        return branch + jnp.concatenate([nn(act, wdn[i, 0]), nn(act, wdn[i, 1])], 1)

    branch_two = lax.fori_loop(0, nh, up, jnp.zeros(middle.shape, F32))
    delta = branch_two - middle
    out_rows[...] = (middle + gate_two * delta).astype(BF16)
    grad = cot_rows[...].astype(F32)
    gb2 = (grad * gate_two).astype(BF16)
    gl2 = (grad * delta * gate_two * (1.0 - gate_two)).astype(BF16)
    gmid = grad * (1.0 - gate_two)
    normed_two_t = normed_two.astype(F32).T.astype(BF16)
    gb2_t = gb2.astype(F32).T.astype(BF16)

    def down(i, total):
        ghid = nt(gb2[:, :cw], wdn[i, 0]) + nt(gb2[:, cw:], wdn[i, 1])
        pre = pre_s[i]
        c = 0.7978845608028654
        t = jnp.tanh(c * (pre + 0.044715 * pre * pre * pre))
        slope = 0.5 * (1.0 + t) + 0.5 * pre * (1.0 - t * t) * (c * (1.0 + 3 * 0.044715 * pre * pre))
        gpre = (ghid * slope).astype(BF16)
        gdn_t[i] = nn(gb2_t, act_s[i]).astype(BF16)
        gup[i] = nn(normed_two_t, gpre).astype(BF16)
        return total + nt(gpre, wup[i])

    gnorm = lax.fori_loop(0, nh, down, two_back(gl2, wg2))
    gg2[...] = nn(normed_two_t, gl2).astype(BF16)
    e = gnorm * gain_two
    gmid = gmid + rstd * (
        e - jnp.mean(e, -1, keepdims=True) - n2 * jnp.mean(e * n2, -1, keepdims=True)
    )
    gb1 = (gmid * gate_one).astype(BF16)
    gl1 = (gmid * (branch_one - tok) * gate_one * (1.0 - gate_one)).astype(BF16)
    ginp[...] = gmid * (1.0 - gate_one)
    gatt_t[...] = nt(wout[...], gb1).astype(BF16)
    gwo[...] = nn(att_t[...], gb1).astype(BF16)
    gg1[...] = nn(n1.astype(F32).T.astype(BF16), gl1).astype(BF16)
    gterm[...] = two_back(gl1, wg1)
    vecp[...] = jnp.zeros_like(vecp)
    vecp[2:3, :] = jnp.sum(gl1.astype(F32), 0, keepdims=True)
    vecp[3:4, :] = jnp.sum(gnorm * n2, 0, keepdims=True)
    vecp[4:5, :] = jnp.sum(gnorm, 0, keepdims=True)
    vecp[5:6, :] = jnp.sum(gl2.astype(F32), 0, keepdims=True)


def back_kernel(nh, rows, dims, *refs):
    (
        lens, gatt_t, kvt, kvn, qt, ot, lse, normed, wqt, wkvt, tok_rows, ginp, gterm, out_rows, vecf,
        out_c, gtok, gq_t, gkv_t, vecp,
        dot_all, acc, part_in, dqsend, dkvsend, dq_t, dkv_t, psend, precv, tsend, trecv,
        ds, dr, xs, xr, qs, qr, ps, pr, ks, kr,
    ) = refs
    heads, dph, tq, half = dims
    b, h, w = place()
    group, sub = lax.div(h, dph), lax.rem(h, dph)
    partner = (b, h, 1 - w)
    cw = 256
    own, other = at(w, cw), at(1 - w, cw)
    per = half // tq
    ends = [lens[0, 0], lens[0, 0] + lens[0, 1], lens[0, 0] + lens[0, 1] + lens[0, 2]]

    greet_group(nh, b, h, w)

    sends = []
    for dw in (1, 0):
        wt = lax.rem(w + dw, 2)
        for k in range(heads - 1, -1, -1):
            t = lax.rem(group + k, heads)
            for i in range(per):
                r = w * per + i
                target = sub_row(h, r, dph)
                src = gatt_t.at[at(wt * heads + t, HD), pl.ds(i * tq, tq)]
                dst = dot_all.at[h]
                copy = remote(src, dst, ds.at[dw, k, i], dr.at[h], (b, t * dph + target, wt))
                if k or dw:
                    copy.start()
                    sends.append((None, copy))
                else:
                    away = target != sub

                    @pl.when(away)
                    def _(copy=copy):
                        copy.start()

                    @pl.when(jnp.logical_not(away))
                    def _(src=src, dst=dst):
                        pltpu.make_async_copy(src, dst, dr.at[h]).start()

                    sends.append((away, copy))
    mine = at(w, half)
    out_copy = remote(out_rows.at[:, other], out_c.at[mine, :], xs.at[0], xr.at[0], partner)
    out_copy.start()
    out_c[mine, :] = out_rows[:, own]
    acc[...] = jnp.zeros_like(acc)

    def send_kv(s, total):
        dkvsend[s] = total.astype(BF16)
        dst = dkv_t.at[group]

        @pl.when(s == h)
        def _():
            pltpu.make_async_copy(dkvsend.at[s], dst, kr.at[group]).start()

        @pl.when(s != h)
        def _():
            remote(dkvsend.at[s], dst, ks.at[s], kr.at[group], (b, s, w)).start()

    def finish(s):
        @pl.when(lax.rem(s, dph) == sub)
        def _():
            total = acc[s]
            for k in range(1, dph):
                slot = part_in.at[lax.div(s, dph), k - 1]
                pltpu.make_async_copy(slot, slot, pr.at[lax.div(s, dph), k - 1]).wait()
                total = total + part_in[lax.div(s, dph), k - 1]
            send_kv(s, total)

    def one_query_block(step, _):
        s = nh - 1 - step
        r = sub_row(s, sub, dph)
        query_base = s * rows + r * tq
        pltpu.make_async_copy(dot_all.at[s], dot_all.at[s], dr.at[s]).wait()
        q = qt[s]
        dout = dot_all[s]
        q_low = jnp.concatenate([q.astype(F32) * (HD**-0.5), jnp.zeros((HD, tq), F32)], 0).astype(BF16)
        d_high = jnp.concatenate([jnp.zeros((HD, tq), BF16), dout], 0)
        log_sum = lse[s]
        centre = jnp.sum(ot[s] * dout.astype(F32), 0, keepdims=True)

        def block(j, dq, masked):
            scores = nn(kvn[j], q_low)
            if masked:
                keep = allowed_mask(j * rows, query_base, rows, tq, ends)
                scores = jnp.where(keep, scores, NEG)
            probs = jnp.exp(scores - log_sum)
            gprobs = nn(kvn[j], d_high)
            gscores = (probs * (gprobs - centre)).astype(BF16)
            acc[j, HD:, :] += nt(dout, probs.astype(BF16))
            acc[j, :HD, :] += nt(q, gscores) * (HD**-0.5)
            return dq + nn(kvt[j, :HD, :], gscores)

        dq = for_key_blocks(s, nh, block, jnp.zeros((HD, tq), F32))
        dqsend[s] = (dq * (HD**-0.5)).astype(BF16)
        dst = dq_t.at[pl.ds(pl.multiple_of(group * HD, HD), HD), pl.ds(pl.multiple_of(r * tq, tq), tq)]

        @pl.when(s == h)
        def _():
            pltpu.make_async_copy(dqsend.at[s], dst, qr.at[group, r]).start()

        @pl.when(s != h)
        def _():
            remote(dqsend.at[s], dst, qs.at[s], qr.at[group, r], (b, s, w)).start()

        owner = lax.rem(s, dph)

        @pl.when(owner != sub)
        def _():
            k = lax.rem(sub - owner + dph, dph)
            dev = (b, group * dph + owner, w)
            remote(acc.at[s], part_in.at[lax.div(s, dph), k - 1], ps.at[s], pr.at[lax.div(s, dph), k - 1], dev).start()

        @pl.when(step > 0)
        def _():
            finish(s + 1)

        return 0

    lax.fori_loop(0, nh, one_query_block, 0)
    finish(0)

    for g in range(heads):
        pltpu.make_async_copy(dkv_t.at[g], dkv_t.at[g], kr.at[g]).wait()
        for r in range(dph):
            dst = dq_t.at[pl.ds(g * HD, HD), pl.ds(r * tq, tq)]
            pltpu.make_async_copy(dst, dst, qr.at[g, r]).wait()

    kv = dkv_t[...].reshape(heads * 2 * HD, rows)
    wkv = wkvt[...].reshape(heads * 2 * HD, wkvt.shape[2])

    def wide(lanes):
        a = dq_t[:, lanes].astype(F32).T.astype(BF16)
        c = dkv_t[:, :, lanes].reshape(heads * 2 * HD, half).astype(F32).T.astype(BF16)
        return nn(a, wqt[...]) + nn(c, wkv)

    psend[...] = wide(at(1 - w, half)).astype(BF16)
    pcopy = remote(psend, precv, xs.at[1], xr.at[1], partner)
    pcopy.start()
    gnorm = wide(at(w, half)) + gterm[...]
    gq_t[...] = nn(dq_t[...], normed[...])
    gkv_t[...] = nn(kv, normed[...])
    x = tok_rows[...].astype(F32)
    centre = x - jnp.mean(x, -1, keepdims=True)
    rstd = lax.rsqrt(jnp.mean(centre * centre, -1, keepdims=True) + EPSILON)
    n = centre * rstd
    pcopy.wait()
    gnorm = gnorm + precv[...].astype(F32)
    e = gnorm * vecf[0:1, :]
    result = ginp[...] + rstd * (
        e - jnp.mean(e, -1, keepdims=True) - n * jnp.mean(e * n, -1, keepdims=True)
    )
    tsend[...] = result.astype(BF16)
    tcopy = remote(tsend.at[:, other], trecv, xs.at[2], xr.at[2], partner)
    tcopy.start()
    vecp[...] = jnp.zeros_like(vecp)
    vecp[0:1, :] = jnp.sum(gnorm * n, 0, keepdims=True)
    vecp[1:2, :] = jnp.sum(gnorm, 0, keepdims=True)
    gtok[mine, :] = jnp.where(w == 0, result[:, :cw], result[:, cw:])
    tcopy.wait()
    gtok[at(1 - w, half), :] = trecv[...].astype(F32)
    out_copy.wait()

    def sent(s, _):
        @pl.when(s != h)
        def _():
            pltpu.make_async_copy(dqsend.at[s], dqsend.at[s], qs.at[s]).wait()

        @pl.when((s != h) & (lax.rem(s, dph) == sub))
        def _():
            pltpu.make_async_copy(dkvsend.at[s], dkvsend.at[s], ks.at[s]).wait()

        @pl.when(lax.rem(s, dph) != sub)
        def _():
            pltpu.make_async_copy(acc.at[s], acc.at[s], ps.at[s]).wait()

        return 0

    lax.fori_loop(0, nh, sent, 0)
    for away, copy in sends:
        if away is None:
            copy.wait_send()
        else:

            @pl.when(away)
            def _(copy=copy):
                copy.wait_send()


def call(kernel, ins, smem, outs, scratch, collective_id=None, flops=0, nbytes=0):
    specs = [pl.BlockSpec(memory_space=pltpu.SMEM if i < smem else pltpu.VMEM) for i in range(len(ins))]
    params = dict(vmem_limit_bytes=VMEM_LIMIT)
    if collective_id is not None:
        params.update(collective_id=collective_id, has_side_effects=True)
    return pl.pallas_call(
        kernel,
        out_shape=[jax.ShapeDtypeStruct(shape, kind) for shape, kind in outs],
        in_specs=specs,
        out_specs=[pl.BlockSpec(memory_space=pltpu.VMEM)] * len(outs),
        scratch_shapes=scratch,
        compiler_params=pltpu.CompilerParams(**params),
        cost_estimate=pl.CostEstimate(flops=flops, bytes_accessed=nbytes, transcendentals=0),
    )(*ins)


def local(
    tokens, ln1_gain, ln1_bias, w_query, w_key, w_value, w_out, gate1_weight, gate1_bias,
    ln2_gain, ln2_bias, gate2_weight, gate2_bias, w_up, w_down, lengths, cotangent,
):
    nh = lax.axis_size("hidden")
    rows, cw = tokens.shape
    wide = 2 * cw
    heads = cw // HD
    dph = nh // heads
    tq = rows // dph
    half = rows // 2
    units = w_up.shape[1]
    dims = (heads, dph, tq, half)
    dma, vmem = pltpu.SemaphoreType.DMA, pltpu.VMEM

    vecs = jnp.stack([ln1_gain, ln1_bias, gate1_bias, ln2_gain, ln2_bias, gate2_bias, ln1_gain, ln1_gain])
    wup = lax.all_gather(w_up, ("hidden", "width"), axis=0, tiled=True).reshape(nh, wide, units)
    wdn = lax.all_gather(w_down, ("hidden", "width"), axis=0).reshape(nh, 2, units, cw)
    wg1 = lax.all_gather(gate1_weight, "width", axis=0)
    wg2 = lax.all_gather(gate2_weight, "width", axis=0)
    wout = lax.all_gather(w_out, "width", axis=0, tiled=True)

    front = call(
        functools.partial(front_kernel, nh, rows, dims),
        [lengths, tokens, cotangent, vecs, w_query, w_key, w_value],
        1,
        [
            ((half, wide), BF16), ((half, wide), BF16), ((8, wide), F32), ((rows, wide), BF16),
            ((2 * heads * HD, half), BF16), ((nh, 2 * HD, rows), BF16), ((nh, rows, 2 * HD), BF16),
            ((nh, HD, tq), BF16), ((nh, HD, tq), F32), ((nh, 1, tq), F32),
            ((cw, wide), BF16), ((heads, 2 * HD, wide), BF16),
        ],
        [
            vmem((rows, wide), BF16), vmem((cw, wide), BF16), vmem((heads, 2 * HD, wide), BF16),
            vmem((heads, HD, rows), BF16), vmem((heads, 2 * HD, rows), BF16), vmem((nh, HD, tq), BF16),
            dma((4,)), dma((4,)), dma((heads, dph)), dma((nh,)), dma((heads, 2)), dma((nh, 2)),
            dma((nh, dph)), dma((nh,)), dma((nh,)), dma((2 * heads, half // tq)), dma((1,)),
        ],
        collective_id=1,
        flops=30 * 10**9,
        nbytes=20 * 10**6,
    )
    tok_rows, cot_rows, vecf, normed, att_t, kvt, kvn, qt, ot, lse, wqt, wkvt = front

    mid = call(
        functools.partial(middle_kernel, nh),
        [tok_rows, cot_rows, vecf, normed, att_t, wg1, wg2, wout, wup, wdn],
        0,
        [
            ((half, wide), BF16), ((wide, half), BF16), ((nh, wide, units), BF16), ((nh, wide, units), BF16),
            ((wide, wide), BF16), ((wide, wide), BF16), ((wide, wide), BF16), ((8, wide), F32),
            ((half, wide), F32), ((half, wide), F32),
        ],
        [vmem((nh, half, units), F32), vmem((nh, half, units), BF16)],
        flops=10 * 10**9,
        nbytes=20 * 10**6,
    )
    out_rows, gatt_t, gup, gdn_t, gwo, gg1, gg2, vecp_two, ginp, gterm = mid

    back = call(
        functools.partial(back_kernel, nh, rows, dims),
        [lengths, gatt_t, kvt, kvn, qt, ot, lse, normed, wqt, wkvt, tok_rows, ginp, gterm, out_rows, vecf],
        1,
        [
            ((rows, cw), BF16), ((rows, cw), F32), ((cw, wide), F32), ((2 * cw, wide), F32), ((8, wide), F32),
        ],
        [
            vmem((nh, HD, tq), BF16), vmem((nh, 2 * HD, rows), F32),
            vmem((nh // dph, max(dph - 1, 1), 2 * HD, rows), F32), vmem((nh, HD, tq), BF16),
            vmem((nh, 2 * HD, rows), BF16), vmem((cw, rows), BF16), vmem((heads, 2 * HD, rows), BF16),
            vmem((half, wide), BF16), vmem((half, wide), BF16), vmem((half, wide), BF16), vmem((half, cw), BF16),
            dma((2, heads, half // tq)), dma((nh,)), dma((3,)), dma((3,)), dma((nh,)), dma((heads, dph)),
            dma((nh,)), dma((nh // dph, max(dph - 1, 1))), dma((nh,)), dma((heads,)),
        ],
        collective_id=2,
        flops=40 * 10**9,
        nbytes=20 * 10**6,
    )
    out_c, gtok, gq_t, gkv_t, vecp_one = back

    ffn = jnp.concatenate([gup.reshape(2 * nh, cw, units), gdn_t.reshape(2 * nh, cw, units)], 2)
    ffn = lax.psum(lax.psum_scatter(ffn, ("hidden", "width"), scatter_dimension=0, tiled=True), "batch")[0]
    grad_up = ffn[:, :units].astype(F32)
    grad_down = ffn[:, units:].astype(F32).T
    width_pos = lax.axis_index("width")
    every = ("batch", "hidden")
    gwo, gg1, gg2 = lax.psum(
        (
            lax.psum_scatter(gwo, "width", scatter_dimension=0, tiled=True),
            lax.psum_scatter(gg1, "width", scatter_dimension=1, tiled=True),
            lax.psum_scatter(gg2, "width", scatter_dimension=1, tiled=True),
        ),
        every,
    )
    gq_t, gkv_t = lax.psum((gq_t, gkv_t), every)
    vec = lax.psum(vecp_one + vecp_two, ("batch", "hidden", "width"))
    vec = lax.dynamic_slice_in_dim(vec, width_pos * cw, cw, 1)
    gkv_t = gkv_t.reshape(heads, 2, HD, wide)
    return (
        out_c,
        gtok,
        vec[0],
        vec[1],
        gq_t.T,
        gkv_t[:, 0].reshape(cw, wide).T,
        gkv_t[:, 1].reshape(cw, wide).T,
        gwo.astype(F32),
        gg1.astype(F32),
        vec[2],
        vec[3],
        vec[4],
        gg2.astype(F32),
        vec[5],
        grad_up,
        grad_down,
    )


def solution(mesh):
    cols = P(None, "width")
    vec = P("width")
    in_specs = (
        P(("batch", "hidden"), "width"), vec, vec, cols, cols, cols, P("width", None), cols, vec, vec, vec,
        cols, vec, P("width", "hidden"), P("hidden", "width"), P("batch", None),
        P(("batch", "hidden"), "width"),
    )
    out_specs = (
        P(("batch", "hidden"), "width"), P(("batch", "hidden"), "width"), vec, vec, cols, cols, cols,
        P("width", None), cols, vec, vec, vec, cols, vec, P("width", "hidden"), P("hidden", "width"),
    )
    return jax.shard_map(local, mesh=mesh, in_specs=in_specs, out_specs=out_specs, check_vma=False)
```

```python
import functools
import types

import jax
import jax.numpy as jnp
from jax import lax
from jax.experimental import pallas as pl
from jax.experimental.pallas import tpu as pltpu
from jax.sharding import PartitionSpec as P

HD = 64
EPSILON = 1e-05
MESH = pl.DeviceIdType.MESH
F32 = jnp.float32
BF16 = jnp.bfloat16
NEG = -1e30
VMEM_LIMIT = 62 * 1024 * 1024
SCALE = HD**-0.5


def nn(a, b):
    return lax.dot_general(a, b, (((1,), (0,)), ((), ())), preferred_element_type=F32)


def nt(a, b):
    return lax.dot_general(a, b, (((1,), (1,)), ((), ())), preferred_element_type=F32)


def flip(a):
    return a.astype(F32).T.astype(BF16)


def remote(src, dst, send, recv, dev):
    return pltpu.make_async_remote_copy(
        src_ref=src, dst_ref=dst, send_sem=send, recv_sem=recv, device_id=dev, device_id_type=MESH
    )


def await_copy(ref, sem):
    pltpu.make_async_copy(ref, ref, sem).wait()


def at(index, size):
    return pl.ds(pl.multiple_of(index * size, size), size)


def sub_row(index, sub, dph):
    return jnp.where(lax.rem(index, 2) == 0, sub, dph - 1 - sub)


def segments(pos, ends):
    total = jnp.zeros(pos.shape, jnp.int32)
    for end in ends:
        total = total + (pos >= end).astype(jnp.int32)
    return total


def allowed_mask(key_base, query_base, keys, queries, ends):
    key_pos = key_base + lax.broadcasted_iota(jnp.int32, (keys, 1), 0)
    query_pos = query_base + lax.broadcasted_iota(jnp.int32, (1, queries), 1)
    same = segments(key_pos, ends) == segments(query_pos, ends)
    return same & (key_pos <= query_pos)


def sigmoid(x):
    return 1.0 / (1.0 + jnp.exp(-x))


class Sends:
    def __init__(self):
        self.items = []

    def start(self, copy):
        copy.start()
        self.items.append((None, copy))

    def start_if(self, cond, copy):
        @pl.when(cond)
        def _():
            copy.start()

        self.items.append((cond, copy))

    def finish(self):
        for cond, copy in self.items:
            if cond is None:
                copy.wait_send()
            else:

                @pl.when(cond)
                def _(copy=copy):
                    copy.wait_send()


def layer_kernel(names, sizes, *refs):
    r = types.SimpleNamespace(**dict(zip(names, refs)))
    nb, nh, rows, cw, units, heads, dph, tq = sizes
    half, wide, nz = rows // 2, 2 * cw, nh // 2
    per = half // tq
    pairs = nb // 2
    b, h, w = lax.axis_index("batch"), lax.axis_index("hidden"), lax.axis_index("width")
    group, sub = lax.div(h, dph), lax.rem(h, dph)
    z, c, bp = lax.div(h, 2), lax.rem(h, 2), lax.rem(b, 2)
    x_dev = (b, h, 1 - w)
    c_dev = (b, h + 1 - 2 * c, w)
    y_dev = (b + 1 - 2 * bp, h, w)

    def z_dev(k):
        zz = lax.rem(z + k, nz)
        return zz, (b, 2 * zz + c, w)

    own, other = at(w, cw), at(1 - w, cw)
    mine, theirs = at(w, half), at(1 - w, half)
    lanes = at(c, half)
    ends = [
        r.lens[0, 0],
        r.lens[0, 0] + r.lens[0, 1],
        r.lens[0, 0] + r.lens[0, 1] + r.lens[0, 2],
    ]
    sends = Sends()

    barrier = pltpu.get_barrier_semaphore()
    count = 0
    for dw in range(2):
        for dh in range(nh):
            if dh or dw:
                dev = (b, lax.rem(h + dh, nh), lax.rem(w + dw, 2))
                pl.semaphore_signal(barrier, inc=1, device_id=dev, device_id_type=MESH)
                count += 1
    for db in range(1, nb):
        dev = (lax.rem(b + db, nb), h, w)
        pl.semaphore_signal(barrier, inc=1, device_id=dev, device_id_type=MESH)
        count += 1
    pl.semaphore_wait(barrier, count)

    for i, vec in enumerate((r.v0, r.v1, r.v2, r.v3, r.v4, r.v5)):
        r.vsrc[i : i + 1, :] = vec[...]
    vcopy = remote(r.vsrc, r.vecf.at[:, own], r.xs.at[0], r.xr.at[0], x_dev)
    sends.start(vcopy)
    tcopies = []
    for k in range(2):
        part = pl.ds(k * half, half)
        copy = remote(r.tok.at[part], r.tokf.at[part, own], r.xs.at[1 + k], r.xr.at[1 + k], x_dev)
        sends.start(copy)
        tcopies.append(copy)
    for kind, (src, dst) in enumerate(((r.wu, r.wup), (r.wd, r.wdn))):
        for k in range(nz - 1, 0, -1):
            _, dev = z_dev(k)
            copy = remote(src, dst.at[z, c, w], r.wzs.at[k], r.wzr.at[z], dev)
            sends.start_if(bp == kind, copy)
    ccopy = remote(r.cot.at[theirs], r.cotr.at[:, own], r.xs.at[3], r.xr.at[3], x_dev)
    sends.start(ccopy)
    gates = ((r.wg1, r.g1f), (r.wg2, r.g2f), (r.wo, r.wof))
    for i, (src, dst) in enumerate(gates):
        piece = at(c, src.shape[0] // 2)
        sends.start(remote(src.at[piece], dst.at[w, piece], r.gxs.at[i], r.gxr.at[i], x_dev))
        dst[w] = src[...]
    r.wup[z, c, w] = r.wu[...]
    r.wdn[z, c, w] = r.wd[...]
    r.vecf[:, own] = r.vsrc[...]
    r.tokf[:, own] = r.tok[...]
    r.cotr[:, own] = r.cot[mine, :]

    for i, weight in enumerate((r.wq, r.wk, r.wv)):
        turned = flip(weight[...])
        for t in range(heads):
            r.wt[t, i * HD : (i + 1) * HD, :] = turned[t * HD : (t + 1) * HD]

    vcopy.wait_recv()
    gain, shift = r.vecf[0:1, :], r.vecf[1:2, :]
    for k in range(2):
        part = slice(k * half, (k + 1) * half)
        tcopies[k].wait_recv()
        x = r.tokf[part, :].astype(F32)
        centre = x - jnp.mean(x, -1, keepdims=True)
        spread = jnp.mean(centre * centre, -1, keepdims=True)
        n = (centre * lax.rsqrt(spread + EPSILON) * gain + shift).astype(BF16)
        r.npair[c, part, :] = n
        for t in range(heads):
            qkv = nt(r.wt[t], n).astype(BF16)
            r.qsrc[t, :, part] = qkv[:HD]
            r.kvsrc[t, :, part] = qkv[HD:]
        for step in range(heads - 1, -1, -1):
            t = lax.rem(group + step, heads)
            span = pl.ds(k * half, half)
            src, dst = r.kvsrc.at[t, :, span], r.kvt.at[h, :, span]
            if step:
                dev = (b, t * dph + sub, w)
                sends.start(remote(src, dst, r.ks.at[step, k], r.kr.at[h, k], dev))
            else:
                pltpu.make_async_copy(src, dst, r.kr.at[h, k]).start()
            for i in range(per):
                row = k * per + i
                target = sub_row(h, row, dph)
                src, dst = r.qsrc.at[t, :, pl.ds(row * tq, tq)], r.qt.at[h]
                copy = remote(src, dst, r.qs.at[step, row], r.qr.at[h], (b, t * dph + target, w))
                if step:
                    sends.start(copy)
                else:
                    sends.start_if(target != sub, copy)

                    @pl.when(target == sub)
                    def _(src=src, dst=dst):
                        pltpu.make_async_copy(src, dst, r.qr.at[h]).start()

    sends.start(remote(r.npair.at[c], r.npair.at[c], r.cs.at[0], r.cr.at[0], c_dev))

    def weights_over_x():
        for kind, buf in enumerate((r.wup, r.wdn)):

            @pl.when(bp == kind)
            def _(buf=buf):
                for k in range(nz):
                    zz, _ = z_dev(k)
                    if k:
                        await_copy(buf.at[zz, c, w], r.wzr.at[zz])
                    block = buf.at[zz, c, w]
                    remote(block, block, r.wxs.at[zz], r.wxr.at[zz], x_dev).start()

    def weights_over_y():
        for kind, buf in enumerate((r.wup, r.wdn)):

            @pl.when(bp == kind)
            def _(buf=buf):
                for k in range(nz):
                    zz, _ = z_dev(k)
                    if k:
                        block = buf.at[zz, c, w]
                        remote(block, block, r.wys.at[zz, w], r.wyr.at[zz, w], y_dev).start()
                for k in range(nz):
                    zz, _ = z_dev(k)
                    block = buf.at[zz, c, 1 - w]
                    await_copy(block, r.wxr.at[zz])
                    remote(block, block, r.wys.at[zz, 1 - w], r.wyr.at[zz, 1 - w], y_dev).start()

    def weights_over_core():
        for kind, buf in enumerate((r.wup, r.wdn)):

            @pl.when(bp != kind)
            def _(buf=buf):
                for k in range(nz):
                    zz, _ = z_dev(k)
                    if k:
                        await_copy(buf.at[zz, c, w], r.wyr.at[zz, w])
                    await_copy(buf.at[zz, c, 1 - w], r.wyr.at[zz, 1 - w])

            block = buf.at[:, c]
            sends.start(remote(block, block, r.wcs.at[kind], r.wcr.at[kind], c_dev))
        for i, (src, dst) in enumerate(gates):
            piece = dst.at[1 - w, at(c, src.shape[0] // 2)]
            await_copy(piece, r.gxr.at[i])
            sends.start(remote(piece, piece, r.gcs.at[i], r.gcr.at[i], c_dev))

    def weights_sent():
        for kind, buf in enumerate((r.wup, r.wdn)):

            @pl.when(bp == kind)
            def _(buf=buf):
                for k in range(nz):
                    zz, _ = z_dev(k)
                    if k:
                        await_copy(buf.at[zz, c, w], r.wys.at[zz, w])
                    await_copy(buf.at[zz, c, w], r.wxs.at[zz])
                    await_copy(buf.at[zz, c, w], r.wys.at[zz, 1 - w])

    def pass_on(s):
        @pl.when(lax.rem(s, dph) == sub)
        def _():
            for k in range(2):
                await_copy(r.kvt.at[s, :, pl.ds(k * half, half)], r.kr.at[s, k])
            for k in range(1, dph):
                dev = (b, group * dph + lax.rem(sub + k, dph), w)
                remote(r.kvt.at[s], r.kvt.at[s], r.fs.at[s, k], r.fr.at[s], dev).start()

    def query_forward(s, _):
        @pl.when(s + 1 < nh)
        def _():
            pass_on(s + 1)

        @pl.when(lax.rem(s, dph) != sub)
        def _():
            await_copy(r.kvt.at[s], r.fr.at[s])

        r.kvn[s] = flip(r.kvt[s])
        await_copy(r.qt.at[s], r.qr.at[s])
        row = sub_row(s, sub, dph)
        query_base = s * rows + row * tq
        q = r.qt[s].astype(F32) * SCALE
        q = jnp.concatenate([q, jnp.zeros_like(q)], 0).astype(BF16)

        def masked(j, scores):
            return jnp.where(allowed_mask(j * rows, query_base, rows, tq, ends), scores, NEG)

        def absorb(j, scores, carry):
            top, total, mixed = carry
            new_top = jnp.maximum(top, jnp.max(scores, 0, keepdims=True))
            fade = jnp.exp(top - new_top)
            weights = jnp.exp(scores - new_top)
            total = total * fade + jnp.sum(weights, 0, keepdims=True)
            mixed = mixed * fade + nn(r.kvt[j, HD:, :], weights.astype(BF16))
            return new_top, total, mixed

        def plain_step(j, carry):
            scores = r.sbuf[lax.rem(j, 2)]
            r.sbuf[lax.rem(j + 1, 2)] = nn(r.kvn[j + 1], q)
            return absorb(j, scores, carry)

        def masked_step(j, carry):
            scores = masked(j, r.sbuf[lax.rem(j, 2)])
            r.sbuf[lax.rem(j + 1, 2)] = nn(r.kvn[j + 1], q)
            return absorb(j, scores, carry)

        r.sbuf[0] = masked(0, nn(r.kvn[0], q))
        plain = jnp.where(s == nh - 1, 0, s)
        carry = (jnp.full((1, tq), NEG, F32), jnp.zeros((1, tq), F32), jnp.zeros((HD, tq), F32))
        carry = lax.fori_loop(0, plain, plain_step, carry)
        carry = lax.fori_loop(plain, s, masked_step, carry)
        top, total, mixed = absorb(s, masked(s, r.sbuf[lax.rem(s, 2)]), carry)
        mixed = mixed / total
        r.ot[s] = mixed
        r.lse[s] = top + jnp.log(total)
        r.osend[s] = mixed.astype(BF16)
        row_w = lax.div(row * tq, half)
        lane = lax.rem(row * tq, half)
        dst = r.att.at[at(w * heads + group, HD), pl.ds(pl.multiple_of(lane, tq), tq)]
        slot = r.orc.at[w * heads + group, lax.div(lane, tq)]
        here = (s == h) & (row_w == w)

        @pl.when(here)
        def _():
            pltpu.make_async_copy(r.osend.at[s], dst, slot).start()

        @pl.when(jnp.logical_not(here))
        def _():
            remote(r.osend.at[s], dst, r.osd.at[s], slot, (b, s, row_w)).start()

        @pl.when(s == nh // 4)
        def _():
            weights_over_x()

        @pl.when(s == nh // 2)
        def _():
            weights_over_y()

        return 0

    pass_on(0)
    lax.fori_loop(0, nh, query_forward, 0)
    weights_over_core()

    for i, (src, dst) in enumerate(gates):
        await_copy(dst.at[1 - w, at(1 - c, src.shape[0] // 2)], r.gcr.at[i])

    def two(a, weight):
        return jnp.concatenate([nn(a, weight[0]), nn(a, weight[1])], 1)

    def two_back(g, weight):
        return nt(g[:, :cw], weight[0]) + nt(g[:, cw:], weight[1])

    tok = r.tokf[mine, :].astype(F32)
    n1 = r.npair[c, mine, :]
    gate_one = sigmoid(two(n1, r.g1f) + r.vecf[2:3, :])
    for g in range(2 * heads):
        for i in range(per):
            await_copy(r.att.at[pl.ds(g * HD, HD), pl.ds(i * tq, tq)], r.orc.at[g, i])
    wof = r.wof[...].reshape(wide, wide)
    branch_one = nn(flip(r.att[...]), wof)
    middle = tok + gate_one * (branch_one - tok)
    centre = middle - jnp.mean(middle, -1, keepdims=True)
    rstd = lax.rsqrt(jnp.mean(centre * centre, -1, keepdims=True) + EPSILON)
    n2 = centre * rstd
    gain_two = r.vecf[3:4, :]
    normed_two = (n2 * gain_two + r.vecf[4:5, :]).astype(BF16)
    gate_two = sigmoid(two(normed_two, r.g2f) + r.vecf[5:6, :])
    for kind, buf in enumerate((r.wup, r.wdn)):
        await_copy(buf.at[:, 1 - c], r.wcr.at[kind])

    def units_of(i2, p):
        return i2, lax.rem(c + p, 2)

    def up(i2, branch):
        for p in range(2):
            i, q = units_of(i2, p)
            pre = nn(normed_two, r.wup[i, q].reshape(wide, units))
            r.pre[i2, p] = pre
            act = jax.nn.gelu(pre).astype(BF16)
            branch = branch + jnp.concatenate([nn(act, r.wdn[i, q, 0]), nn(act, r.wdn[i, q, 1])], 1)
            if p:
                r.acts[i2] = act
                dst = r.actp.at[i2, lanes, :]
                remote(r.acts.at[i2], dst, r.as_.at[i2], r.ar.at[i2], c_dev).start()
            else:
                r.actp[i2, lanes, :] = act
        return branch

    branch_two = lax.fori_loop(0, nz, up, jnp.zeros(middle.shape, F32))
    delta = branch_two - middle
    r.outr[...] = (middle + gate_two * delta).astype(BF16)
    ocopy = remote(r.outr.at[:, other], r.out_c.at[mine, :], r.xs.at[4], r.xr.at[4], x_dev)
    sends.start(ocopy)
    ccopy.wait_recv()
    grad = r.cotr[...].astype(F32)
    gb2 = (grad * gate_two).astype(BF16)
    gl2 = (grad * delta * gate_two * (1.0 - gate_two)).astype(BF16)
    gmid = grad * (1.0 - gate_two)

    def down(i2, total):
        for p in range(2):
            i, q = units_of(i2, p)
            ghid = nt(gb2[:, :cw], r.wdn[i, q, 0]) + nt(gb2[:, cw:], r.wdn[i, q, 1])
            pre = r.pre[i2, p]
            k = 0.7978845608028654
            t = jnp.tanh(k * (pre + 0.044715 * pre * pre * pre))
            slope = 0.5 * (1.0 + t) + 0.5 * pre * (1.0 - t * t) * (k * (1.0 + 3 * 0.044715 * pre * pre))
            gpre = (ghid * slope).astype(BF16)
            total = total + nt(gpre, r.wup[i, q].reshape(wide, units))
            if p:
                r.gpres[i2] = gpre
                dst = r.gprep.at[i2, lanes, :]
                remote(r.gpres.at[i2], dst, r.ps_.at[i2], r.pr.at[i2], c_dev).start()
            else:
                r.gprep[i2, lanes, :] = gpre
        return total

    gnorm = lax.fori_loop(0, nz, down, two_back(gl2, r.g2f))
    e = gnorm * gain_two
    gmid = gmid + rstd * (
        e - jnp.mean(e, -1, keepdims=True) - n2 * jnp.mean(e * n2, -1, keepdims=True)
    )
    gb1 = (gmid * gate_one).astype(BF16)
    r.gatt[...] = nt(wof, gb1).astype(BF16)
    for dw in (1, 0):
        wt = lax.rem(w + dw, 2)
        for step in range(heads - 1, -1, -1):
            t = lax.rem(group + step, heads)
            for i in range(per):
                target = sub_row(h, w * per + i, dph)
                src = r.gatt.at[at(wt * heads + t, HD), pl.ds(i * tq, tq)]
                dst = r.dot.at[h]
                dev = (b, t * dph + target, wt)
                copy = remote(src, dst, r.ds.at[dw, step, i], r.dr.at[h], dev)
                if step or dw:
                    sends.start(copy)
                else:
                    sends.start_if(target != sub, copy)

                    @pl.when(target == sub)
                    def _(src=src, dst=dst):
                        pltpu.make_async_copy(src, dst, r.dr.at[h]).start()

    gl1 = (gmid * (branch_one - tok) * gate_one * (1.0 - gate_one)).astype(BF16)
    r.ginp[...] = gmid * (1.0 - gate_one)
    r.npt[:, lanes] = flip(normed_two)
    sends.start(remote(r.npt.at[:, lanes], r.npt.at[:, lanes], r.cs.at[1], r.cr.at[1], c_dev))
    r.gbt[:, lanes] = flip(gb2)
    sends.start(remote(r.gbt.at[:, lanes], r.gbt.at[:, lanes], r.cs.at[2], r.cr.at[2], c_dev))
    quarter = half // 2
    r.lsrc[0] = r.att[...]
    r.lsrc[1] = flip(gl1)
    r.lsrc[2] = flip(gl2)
    for m, right in enumerate((gb1, n1, normed_two)):
        r.bpair[m, lanes, :] = right
        block = r.bpair.at[m, lanes, :]
        sends.start(remote(block, block, r.cs.at[3 + m], r.cr.at[3 + m], c_dev))
        for v in range(2):
            src = r.lsrc.at[m, at(2 * v + 1 - c, quarter), :]
            dst = r.apair.at[m, v, :, lanes]
            sends.start(remote(src, dst, r.cs.at[6 + 2 * m + v], r.cr.at[6 + 2 * m + v], c_dev))
            r.apair[m, v, :, lanes] = r.lsrc[m, at(2 * v + c, quarter), :]
    r.gterm[...] = two_back(gl1, r.g1f)
    r.vsum[...] = jnp.zeros_like(r.vsum)
    r.vsum[2:3, :] = jnp.sum(gl1.astype(F32), 0, keepdims=True)
    r.vsum[3:4, :] = jnp.sum(gnorm * n2, 0, keepdims=True)
    r.vsum[4:5, :] = jnp.sum(gnorm, 0, keepdims=True)
    r.vsum[5:6, :] = jnp.sum(gl2.astype(F32), 0, keepdims=True)
    r.out_c[mine, :] = r.outr[:, own]

    eighth = quarter // 2
    for m in range(3):
        await_copy(r.bpair.at[m, lanes, :], r.cr.at[3 + m])
        for v in range(2):
            await_copy(r.apair.at[m, v, :, lanes], r.cr.at[6 + 2 * m + v])
            block = nn(r.apair[m, v], r.bpair[m]).astype(BF16)
            for y in range(2):
                r.gb[v, y, m * eighth : (m + 1) * eighth, :] = block[y * eighth : (y + 1) * eighth]
    sends.start(remote(r.gb.at[:, 1 - bp], r.ybin, r.ys.at[0], r.yr.at[0], y_dev))
    await_copy(r.npt.at[:, lanes], r.cr.at[1])
    await_copy(r.gbt.at[:, lanes], r.cr.at[2])

    def weight_grads(i2, _):
        await_copy(r.gprep.at[i2, lanes, :], r.pr.at[i2])
        await_copy(r.actp.at[i2, lanes, :], r.ar.at[i2])
        r.ga[0, i2] = nn(r.npt[...], r.gprep[i2]).astype(BF16).reshape(2, 2, quarter, units)
        r.ga[1, i2] = nn(r.gbt[...], r.actp[i2]).astype(BF16).reshape(2, 2, quarter, units)
        return 0

    lax.fori_loop(0, nz, weight_grads, 0)
    sends.start(remote(r.ga.at[0, :, 1 - w], r.xin0, r.xs.at[5], r.xr.at[5], x_dev))
    sends.start(remote(r.ga.at[1, :, :, 1 - bp], r.yin1, r.ys.at[1], r.yr.at[1], y_dev))

    def ffn_second():
        await_copy(r.xin0, r.xr.at[5])
        r.ga[0, :, w] = (r.ga[0, :, w].astype(F32) + r.xin0[...].astype(F32)).astype(BF16)
        remote(r.ga.at[0, :, w, 1 - bp], r.yin0, r.ys.at[2], r.yr.at[2], y_dev).start()
        await_copy(r.yin1, r.yr.at[1])
        r.ga[1, :, :, bp] = (r.ga[1, :, :, bp].astype(F32) + r.yin1[...].astype(F32)).astype(BF16)
        remote(r.ga.at[1, :, 1 - w, bp], r.xin1, r.xs.at[6], r.xr.at[6], x_dev).start()

    def ffn_third():
        await_copy(r.yin0, r.yr.at[2])
        await_copy(r.xin1, r.xr.at[6])
        r.zs[:, 0] = (r.ga[0, :, w, bp].astype(F32) + r.yin0[...].astype(F32)).astype(BF16)
        r.zs[:, 1] = (r.ga[1, :, w, bp].astype(F32) + r.xin1[...].astype(F32)).astype(BF16)
        for k in range(nz - 1, 0, -1):
            zz, dev = z_dev(k)
            remote(r.zs.at[zz], r.zin.at[z], r.zss.at[k], r.zsr.at[z], dev).start()
        r.zin[z] = r.zs[z]

    def ffn_fourth():
        for k in range(1, nz):
            zz, _ = z_dev(k)
            await_copy(r.zin.at[zz], r.zsr.at[zz])
        total = r.zin[0].astype(F32)
        for k in range(1, nz):
            total = total + r.zin[k].astype(F32)
        if pairs > 1:
            mypair = lax.div(b, 2)
            r.pin[mypair] = total.astype(BF16)
            for k in range(1, pairs):
                dev = (lax.rem(b + 2 * k, nb), h, w)
                block = r.pin.at[mypair]
                sends.start(remote(block, block, r.pas.at[k], r.par.at[mypair], dev))
            for k in range(1, pairs):
                pp = lax.rem(mypair + k, pairs)
                await_copy(r.pin.at[pp], r.par.at[pp])
            total = r.pin[0].astype(F32)
            for k in range(1, pairs):
                total = total + r.pin[k].astype(F32)
        r.red_a[bp] = total.astype(BF16)
        block = r.red_a.at[bp]
        sends.start(remote(block, block, r.ys.at[3], r.yr.at[3], y_dev))

    def ffn_sent():
        await_copy(r.yin0, r.ys.at[2])
        await_copy(r.xin1, r.xs.at[6])
        for k in range(1, nz):
            await_copy(r.zin.at[z], r.zss.at[k])

    deep = (heads // 2) * 3 * HD // 2
    zr = deep * 4 // nz

    def z_part(zz):
        return pl.ds(pl.multiple_of(lax.div(zz, 4) * zr, zr), zr), at(lax.rem(zz, 4), 128)

    def square_x():
        await_copy(r.ybin, r.yr.at[0])
        r.gb[:, bp] = (r.gb[:, bp].astype(F32) + r.ybin[...].astype(F32)).astype(BF16)
        remote(r.gb.at[1 - w, bp], r.xbin, r.xs.at[7], r.xr.at[7], x_dev).start()

    def square_z(which):
        if which == 0:
            await_copy(r.xbin, r.xr.at[7])
            total = r.gb[w, bp].astype(F32) + r.xbin[...].astype(F32)
        else:
            await_copy(r.ycin, r.yr.at[4])
            total = r.gc[bp].astype(F32) + r.ycin[...].astype(F32)
        r.sq[which] = total.astype(BF16)
        for k in range(nz - 1, 0, -1):
            zz, dev = z_dev(k)
            src = r.sq.at[(which,) + z_part(zz)]
            remote(src, r.sqin.at[which, z], r.sqs.at[which, k], r.sqr.at[which, z], dev).start()

    def square_spread(which):
        total = r.sq[(which,) + z_part(z)].astype(F32)
        r.sqin[which, z] = total.astype(BF16)
        for k in range(1, nz):
            zz, _ = z_dev(k)
            await_copy(r.sqin.at[which, zz], r.sqr.at[which, zz])
        total = r.sqin[which, 0].astype(F32)
        for k in range(1, nz):
            total = total + r.sqin[which, k].astype(F32)
        if pairs > 1:
            mypair = lax.div(b, 2)
            r.sqpair[which, mypair] = total.astype(BF16)
            for k in range(1, pairs):
                dev = (lax.rem(b + 2 * k, nb), h, w)
                block = r.sqpair.at[which, mypair]
                remote(block, block, r.sqps.at[which, k], r.sqpr.at[which, mypair], dev).start()
            for k in range(1, pairs):
                pp = lax.rem(mypair + k, pairs)
                await_copy(r.sqpair.at[which, pp], r.sqpr.at[which, pp])
            total = r.sqpair[which, 0].astype(F32)
            for k in range(1, pairs):
                total = total + r.sqpair[which, k].astype(F32)
        r.red_s[(which, c, bp) + z_part(z)] = total.astype(BF16)
        for k in range(nz - 1, 0, -1):
            _, dev = z_dev(k)
            block = r.red_s.at[(which, c, bp) + z_part(z)]
            remote(block, block, r.sgs.at[which, k], r.sgr.at[which, z], dev).start()

    def square_y(which):
        for k in range(1, nz):
            zz, _ = z_dev(k)
            await_copy(r.red_s.at[(which, c, bp) + z_part(zz)], r.sgr.at[which, zz])
        block = r.red_s.at[which, c, bp]
        remote(block, block, r.sys.at[which], r.syr.at[which], y_dev).start()

    def square_core(which):
        await_copy(r.red_s.at[which, c, 1 - bp], r.syr.at[which])
        block = r.red_s.at[which, c]
        remote(block, block, r.scs.at[which], r.scr.at[which], c_dev).start()

    def square_end(which):
        await_copy(r.red_s.at[which, 1 - c], r.scr.at[which])
        await_copy(r.red_s.at[which, c], r.scs.at[which])
        await_copy(r.red_s.at[which, c, bp], r.sys.at[which])
        for k in range(1, nz):
            await_copy(r.sqin.at[which, z], r.sqs.at[which, k])
            await_copy(r.sqin.at[which, z], r.sgs.at[which, k])
            if k < pairs:
                await_copy(r.sqpair.at[which, 0], r.sqps.at[which, k])

    r.acc[...] = jnp.zeros_like(r.acc)

    def finish(s):
        @pl.when(lax.rem(s, dph) == sub)
        def _():
            total = r.acc[s]
            for k in range(1, dph):
                slot = r.pin_kv.at[lax.div(s, dph), k - 1]
                await_copy(slot, r.pkr.at[lax.div(s, dph), k - 1])
                total = total + r.pin_kv[lax.div(s, dph), k - 1]
            r.dkvsend[s] = total.astype(BF16)
            dst = r.dqkv.at[group, pl.ds(HD, 2 * HD), :]

            @pl.when(s == h)
            def _():
                pltpu.make_async_copy(r.dkvsend.at[s], dst, r.dkr.at[group]).start()

            @pl.when(s != h)
            def _():
                remote(r.dkvsend.at[s], dst, r.dks.at[s], r.dkr.at[group], (b, s, w)).start()

    def query_backward(step, _):
        s = nh - 1 - step
        row = sub_row(s, sub, dph)
        query_base = s * rows + row * tq
        await_copy(r.dot.at[s], r.dr.at[s])
        q = r.qt[s]
        dout = r.dot[s]
        q_low = jnp.concatenate([q.astype(F32) * SCALE, jnp.zeros((HD, tq), F32)], 0).astype(BF16)
        d_high = jnp.concatenate([jnp.zeros((HD, tq), BF16), dout], 0)
        log_sum = r.lse[s]
        centre = jnp.sum(r.ot[s] * dout.astype(F32), 0, keepdims=True)

        def block(j, dq, masked):
            scores = nn(r.kvn[j], q_low)
            if masked:
                scores = jnp.where(allowed_mask(j * rows, query_base, rows, tq, ends), scores, NEG)
            probs = jnp.exp(scores - log_sum)
            gprobs = nn(r.kvn[j], d_high)
            gscores = (probs * (gprobs - centre)).astype(BF16)
            r.acc[j, HD:, :] += nt(dout, probs.astype(BF16))
            r.acc[j, :HD, :] += nt(q, gscores) * SCALE
            return dq + nn(r.kvt[j, :HD, :], gscores)

        plain_end = jnp.where(s == nh - 1, 1, jnp.maximum(s, 1))
        dq = jnp.zeros((HD, tq), F32)
        dq = lax.fori_loop(1, plain_end, lambda j, d: block(j, d, False), dq)
        count = 1 + jnp.where(s > 0, s + 1 - plain_end, 0)

        def with_mask(t, d):
            return block(jnp.where(t == 0, 0, plain_end + t - 1), d, True)

        dq = lax.fori_loop(0, count, with_mask, dq)
        r.dqsend[s] = (dq * SCALE).astype(BF16)
        dst = r.dqkv.at[group, pl.ds(0, HD), pl.ds(pl.multiple_of(row * tq, tq), tq)]

        @pl.when(s == h)
        def _():
            pltpu.make_async_copy(r.dqsend.at[s], dst, r.dqr.at[group, row]).start()

        @pl.when(s != h)
        def _():
            remote(r.dqsend.at[s], dst, r.dqs.at[s], r.dqr.at[group, row], (b, s, w)).start()

        owner = lax.rem(s, dph)

        @pl.when(owner != sub)
        def _():
            k = lax.rem(sub - owner + dph, dph)
            dev = (b, group * dph + owner, w)
            slot = lax.div(s, dph)
            remote(r.acc.at[s], r.pin_kv.at[slot, k - 1], r.pks.at[s], r.pkr.at[slot, k - 1], dev).start()

        @pl.when(step > 0)
        def _():
            finish(s + 1)

        unit = nh // 8

        @pl.when(step == 2 * unit)
        def _():
            square_x()
            ffn_second()

        @pl.when(step == 4 * unit)
        def _():
            square_z(0)
            ffn_third()

        @pl.when(step == 6 * unit)
        def _():
            square_spread(0)

        return 0

    lax.fori_loop(0, nh, query_backward, 0)
    finish(0)

    for t in range(heads):
        await_copy(r.dqkv.at[t, pl.ds(HD, 2 * HD), :], r.dkr.at[t])
        for i in range(dph):
            await_copy(r.dqkv.at[t, pl.ds(0, HD), pl.ds(i * tq, tq)], r.dqr.at[t, i])
        sends.start_if(
            t % 2 != c, remote(r.dqkv.at[t], r.dsib.at[t // 2], r.ts.at[t], r.tr.at[t // 2], c_dev)
        )
    wts = r.wt[...].reshape(heads * 3 * HD, wide)

    def grad_normed(span):
        return nn(flip(r.dqkv[:, :, span].reshape(heads * 3 * HD, half)), wts)

    r.psend[...] = grad_normed(theirs).astype(BF16)
    pcopy = remote(r.psend, r.precv, r.xs.at[8], r.xr.at[8], x_dev)
    sends.start(pcopy)
    await_copy(r.npair.at[1 - c], r.cr.at[0])
    for j in range(heads // 2):
        await_copy(r.dsib.at[j], r.tr.at[j])
        part = nn(r.dqkv[2 * j + c], r.npair[c]) + nn(r.dsib[j], r.npair[1 - c])
        span = slice((j % (heads // 4)) * 3 * HD, (j % (heads // 4) + 1) * 3 * HD)
        r.gc[j // (heads // 4), span, :] = part.astype(BF16)
    sends.start(remote(r.gc.at[1 - bp], r.ycin, r.ys.at[4], r.yr.at[4], y_dev))
    gnorm = grad_normed(mine) + r.gterm[...]
    x = r.tokf[mine, :].astype(F32)
    centre = x - jnp.mean(x, -1, keepdims=True)
    rstd = lax.rsqrt(jnp.mean(centre * centre, -1, keepdims=True) + EPSILON)
    n = centre * rstd
    square_y(0)
    ffn_fourth()
    square_z(1)
    pcopy.wait_recv()
    gnorm = gnorm + r.precv[...].astype(F32)
    e = gnorm * r.vecf[0:1, :]
    result = r.ginp[...] + rstd * (
        e - jnp.mean(e, -1, keepdims=True) - n * jnp.mean(e * n, -1, keepdims=True)
    )
    r.tsend[...] = result.astype(BF16)
    tcopy = remote(r.tsend.at[:, other], r.trecv, r.xs.at[9], r.xr.at[9], x_dev)
    sends.start(tcopy)
    r.vsum[0:1, :] = jnp.sum(gnorm * n, 0, keepdims=True)
    r.vsum[1:2, :] = jnp.sum(gnorm, 0, keepdims=True)
    me4 = 2 * c + w
    r.vin4[me4] = r.vsum[...]
    k = 0
    for dc in range(2):
        for dw in range(2):
            if dc or dw:
                cc, ww = lax.rem(c + dc, 2), lax.rem(w + dw, 2)
                dev = (b, 2 * z + cc, ww)
                sends.start(remote(r.vin4.at[me4], r.vin4.at[me4], r.v4s.at[k], r.v4r.at[me4], dev))
                k += 1
    r.gtok[mine, :] = jnp.where(w == 0, result[:, :cw], result[:, cw:])
    square_core(0)
    square_spread(1)
    for dc in range(2):
        for dw in range(2):
            if dc or dw:
                peer = 2 * lax.rem(c + dc, 2) + lax.rem(w + dw, 2)
                await_copy(r.vin4.at[peer], r.v4r.at[peer])
    r.vinz[z] = r.vin4[0] + r.vin4[1] + r.vin4[2] + r.vin4[3]
    for k in range(1, nz):
        _, dev = z_dev(k)
        sends.start(remote(r.vinz.at[z], r.vinz.at[z], r.vzs.at[k], r.vzr.at[z], dev))
    tcopy.wait_recv()
    r.gtok[theirs, :] = r.trecv[...].astype(F32)
    ocopy.wait_recv()
    for k in range(1, nz):
        zz, _ = z_dev(k)
        await_copy(r.vinz.at[zz], r.vzr.at[zz])
    total = r.vinz[0]
    for k in range(1, nz):
        total = total + r.vinz[k]
    r.vinb[b] = total
    for k in range(1, nb):
        dev = (lax.rem(b + k, nb), h, w)
        sends.start(remote(r.vinb.at[b], r.vinb.at[b], r.vbs.at[k], r.vbr.at[b], dev))
    square_y(1)
    for k in range(1, nb):
        bb = lax.rem(b + k, nb)
        await_copy(r.vinb.at[bb], r.vbr.at[bb])
    total = r.vinb[0]
    for k in range(1, nb):
        total = total + r.vinb[k]
    r.red_v[...] = jnp.where(w == 0, total[:, :cw], total[:, cw:])
    await_copy(r.red_a.at[1 - bp], r.yr.at[3])
    square_core(1)

    def sent(s, _):
        row = sub_row(s, sub, dph)
        here = (s == h) & (lax.div(row * tq, half) == w)

        @pl.when(jnp.logical_not(here))
        def _():
            await_copy(r.osend.at[s], r.osd.at[s])

        @pl.when(lax.rem(s, dph) == sub)
        def _():
            for k in range(1, dph):
                await_copy(r.kvt.at[s], r.fs.at[s, k])

        @pl.when(s != h)
        def _():
            await_copy(r.dqsend.at[s], r.dqs.at[s])

        @pl.when((s != h) & (lax.rem(s, dph) == sub))
        def _():
            await_copy(r.dkvsend.at[s], r.dks.at[s])

        @pl.when(lax.rem(s, dph) != sub)
        def _():
            await_copy(r.acc.at[s], r.pks.at[s])

        return 0

    lax.fori_loop(0, nh, sent, 0)
    weights_sent()
    for i2 in range(nz):
        await_copy(r.acts.at[i2], r.as_.at[i2])
        await_copy(r.gpres.at[i2], r.ps_.at[i2])
    ffn_sent()
    await_copy(r.xbin, r.xs.at[7])
    sends.finish()
    square_end(0)
    square_end(1)


def final_kernel(heads, *refs):
    (
        out_c, gtok, red_a, red_s, red_v,
        o_out, o_tok, o_g1, o_b1, o_wq, o_wk, o_wv, o_wo, o_gw1, o_gb1, o_g2, o_b2, o_gw2, o_gb2, o_up, o_dn,
    ) = refs
    o_out[...] = out_c[...]
    o_tok[...] = gtok[...]
    for i, ref in enumerate((o_g1, o_b1, o_gb1, o_g2, o_b2, o_gb2)):
        ref[...] = red_v[i : i + 1, :]
    _, quarter, units = red_a.shape[1:]
    o_up[:quarter, :] = red_a[0, 0].astype(F32)
    o_up[quarter:, :] = red_a[1, 0].astype(F32)
    o_dn[:, :quarter] = red_a[0, 1].astype(F32).T
    o_dn[:, quarter:] = red_a[1, 1].astype(F32).T
    eighth = quarter // 2
    for core in range(2):
        for y in range(2):
            base = (2 * core + y) * eighth
            o_wo[base : base + eighth, :] = red_s[0, core, y, :eighth, :].astype(F32)
    for m, ref in ((1, o_gw1), (2, o_gw2)):
        full = [red_s[0, core, y, m * eighth : (m + 1) * eighth, :] for core in range(2) for y in range(2)]
        ref[...] = jnp.concatenate(full, 0).astype(F32).T
    for i, ref in enumerate((o_wq, o_wk, o_wv)):
        full = []
        for t in range(heads):
            j, core = t // 2, t % 2
            base = (j % (heads // 4)) * 3 * HD + i * HD
            full.append(red_s[1, core, j // (heads // 4), base : base + HD, :])
        ref[...] = jnp.concatenate(full, 0).astype(F32).T


def local(
    tokens, ln1_gain, ln1_bias, w_query, w_key, w_value, w_out, gate1_weight, gate1_bias,
    ln2_gain, ln2_bias, gate2_weight, gate2_bias, w_up, w_down, lengths, cotangent,
):
    nb, nh = lax.axis_size("batch"), lax.axis_size("hidden")
    rows, cw = tokens.shape
    units = w_up.shape[1]
    heads = cw // HD
    dph = nh // heads
    tq, half, wide, nz, pairs = rows // dph, rows // 2, 2 * cw, nh // 2, nb // 2
    quarter = half // 2
    deep = (heads // 2) * 3 * HD // 2
    zr = deep * 4 // nz
    per = half // tq
    sizes = (nb, nh, rows, cw, units, heads, dph, tq)

    ins = dict(
        lens=lengths, tok=tokens, cot=cotangent, v0=ln1_gain[None], v1=ln1_bias[None], v2=gate1_bias[None],
        v3=ln2_gain[None], v4=ln2_bias[None], v5=gate2_bias[None], wq=w_query, wk=w_key, wv=w_value,
        wo=w_out, wg1=gate1_weight, wg2=gate2_weight, wu=w_up, wd=w_down,
    )
    outs = dict(
        out_c=((rows, cw), BF16),
        gtok=((rows, cw), F32),
        red_a=((2, 2, quarter, units), BF16),
        red_s=((2, 2, 2, deep, wide), BF16),
        red_v=((8, cw), F32),
    )
    bufs = dict(
        vsrc=((8, cw), F32), vecf=((8, wide), F32), tokf=((rows, wide), BF16), cotr=((half, wide), BF16),
        g1f=((2, wide, cw), BF16), g2f=((2, wide, cw), BF16), wof=((2, cw, wide), BF16),
        wup=((nz, 2, 2, cw, units), BF16), wdn=((nz, 2, 2, units, cw), BF16),
        wt=((heads, 3 * HD, wide), BF16), npair=((2, rows, wide), BF16),
        qsrc=((heads, HD, rows), BF16), kvsrc=((heads, 2 * HD, rows), BF16),
        kvt=((nh, 2 * HD, rows), BF16), kvn=((nh, rows, 2 * HD), BF16), qt=((nh, HD, tq), BF16),
        sbuf=((2, rows, tq), F32), ot=((nh, HD, tq), F32), lse=((nh, 1, tq), F32), osend=((nh, HD, tq), BF16),
        att=((2 * heads * HD, half), BF16),
        pre=((nz, 2, half, units), F32), acts=((nz, half, units), BF16), actp=((nz, rows, units), BF16),
        gpres=((nz, half, units), BF16), gprep=((nz, rows, units), BF16),
        outr=((half, wide), BF16), gatt=((wide, half), BF16), dot=((nh, HD, tq), BF16),
        ginp=((half, wide), F32), gterm=((half, wide), F32), npt=((wide, rows), BF16), gbt=((wide, rows), BF16),
        lsrc=((3, wide, half), BF16), bpair=((3, rows, wide), BF16), apair=((3, 2, quarter, rows), BF16),
        vsum=((8, wide), F32),
        gb=((2, 2, deep, wide), BF16), ybin=((2, deep, wide), BF16), xbin=((deep, wide), BF16),
        ga=((2, nz, 2, 2, quarter, units), BF16), xin0=((nz, 2, quarter, units), BF16),
        yin1=((nz, 2, quarter, units), BF16), yin0=((nz, quarter, units), BF16), xin1=((nz, quarter, units), BF16),
        zs=((nz, 2, quarter, units), BF16), zin=((nz, 2, quarter, units), BF16),
        pin=((pairs, 2, quarter, units), BF16),
        gc=((2, deep, wide), BF16), ycin=((deep, wide), BF16), sq=((2, deep, wide), BF16),
        sqin=((2, nz, zr, 128), BF16), sqpair=((2, pairs, zr, 128), BF16),
        acc=((nh, 2 * HD, rows), F32), pin_kv=((nh // dph, max(dph - 1, 1), 2 * HD, rows), F32),
        dkvsend=((nh, 2 * HD, rows), BF16), dqsend=((nh, HD, tq), BF16),
        dqkv=((heads, 3 * HD, rows), BF16), dsib=((heads // 2, 3 * HD, rows), BF16),
        psend=((half, wide), BF16), precv=((half, wide), BF16),
        tsend=((half, wide), BF16), trecv=((half, cw), BF16),
        vin4=((4, 8, wide), F32), vinz=((nz, 8, wide), F32), vinb=((nb, 8, wide), F32),
    )
    sems = dict(
        xs=(10,), xr=(10,), wzs=(nz,), wzr=(nz,), gxs=(3,), gxr=(3,), gcs=(3,), gcr=(3,),
        ks=(heads, 2), kr=(nh, 2), qs=(heads, dph), qr=(nh,), cs=(12,), cr=(12,),
        wxs=(nz,), wxr=(nz,), wys=(nz, 2), wyr=(nz, 2), wcs=(2,), wcr=(2,),
        fs=(nh, dph), fr=(nh,), osd=(nh,), orc=(2 * heads, per),
        as_=(nz,), ar=(nz,), ps_=(nz,), pr=(nz,), ds=(2, heads, per), dr=(nh,),
        ys=(5,), yr=(5,), zss=(nz,), zsr=(nz,), pas=(pairs,), par=(pairs,),
        sqs=(2, nz), sqr=(2, nz), sqps=(2, pairs), sqpr=(2, pairs), sgs=(2, nz), sgr=(2, nz),
        sys=(2,), syr=(2,), scs=(2,), scr=(2,),
        pks=(nh,), pkr=(nh // dph, max(dph - 1, 1)), dqs=(nh,), dqr=(heads, dph), dks=(nh,), dkr=(heads,),
        ts=(heads,), tr=(heads // 2,), v4s=(3,), v4r=(4,), vzs=(nz,), vzr=(nz,), vbs=(nb,), vbr=(nb,),
    )
    names = list(ins) + list(outs) + list(bufs) + list(sems)
    vmem = pl.BlockSpec(memory_space=pltpu.VMEM)
    results = pl.pallas_call(
        functools.partial(layer_kernel, names, sizes),
        out_shape=[jax.ShapeDtypeStruct(shape, kind) for shape, kind in outs.values()],
        in_specs=[pl.BlockSpec(memory_space=pltpu.SMEM)] + [vmem] * (len(ins) - 1),
        out_specs=[vmem] * len(outs),
        scratch_shapes=[pltpu.VMEM(shape, kind) for shape, kind in bufs.values()]
        + [pltpu.SemaphoreType.DMA(shape) for shape in sems.values()],
        compiler_params=pltpu.CompilerParams(
            collective_id=1, has_side_effects=True, vmem_limit_bytes=VMEM_LIMIT
        ),
        cost_estimate=pl.CostEstimate(flops=10**10, bytes_accessed=10**7, transcendentals=10**7),
    )(*ins.values())
    grads = [
        ((rows, cw), BF16), ((rows, cw), F32), ((1, cw), F32), ((1, cw), F32),
        ((wide, cw), F32), ((wide, cw), F32), ((wide, cw), F32), ((cw, wide), F32),
        ((wide, cw), F32), ((1, cw), F32), ((1, cw), F32), ((1, cw), F32), ((wide, cw), F32), ((1, cw), F32),
        ((cw, units), F32), ((units, cw), F32),
    ]
    done = pl.pallas_call(
        functools.partial(final_kernel, heads),
        out_shape=[jax.ShapeDtypeStruct(shape, kind) for shape, kind in grads],
        in_specs=[vmem] * len(outs),
        out_specs=[vmem] * len(grads),
        compiler_params=pltpu.CompilerParams(vmem_limit_bytes=32 * 1024 * 1024),
    )(*results)
    return tuple(a[0] if a.shape[0] == 1 else a for a in done)


def solution(mesh):
    cols = P(None, "width")
    vec = P("width")
    in_specs = (
        P(("batch", "hidden"), "width"), vec, vec, cols, cols, cols, P("width", None), cols, vec, vec, vec,
        cols, vec, P("width", "hidden"), P("hidden", "width"), P("batch", None),
        P(("batch", "hidden"), "width"),
    )
    out_specs = (
        P(("batch", "hidden"), "width"), P(("batch", "hidden"), "width"), vec, vec, cols, cols, cols,
        P("width", None), cols, vec, vec, vec, cols, vec, P("width", "hidden"), P("hidden", "width"),
    )
    return jax.shard_map(local, mesh=mesh, in_specs=in_specs, out_specs=out_specs, check_vma=False)
```

```python
import functools
import types

import jax
import jax.numpy as jnp
from jax import lax
from jax.experimental import pallas as pl
from jax.experimental.pallas import tpu as pltpu
from jax.sharding import PartitionSpec as P

HD = 64
EPSILON = 1e-05
MESH = pl.DeviceIdType.MESH
F32 = jnp.float32
BF16 = jnp.bfloat16
NEG = -1e30
VMEM_LIMIT = 62 * 1024 * 1024
SCALE = HD**-0.5


def nn(a, b):
    return lax.dot_general(a, b, (((1,), (0,)), ((), ())), preferred_element_type=F32)


def nt(a, b):
    return lax.dot_general(a, b, (((1,), (1,)), ((), ())), preferred_element_type=F32)


def flip(a):
    return a.astype(F32).T.astype(BF16)


def remote(src, dst, send, recv, dev):
    return pltpu.make_async_remote_copy(
        src_ref=src, dst_ref=dst, send_sem=send, recv_sem=recv, device_id=dev, device_id_type=MESH
    )


def await_copy(ref, sem):
    pltpu.make_async_copy(ref, ref, sem).wait()


def at(index, size):
    return pl.ds(pl.multiple_of(index * size, size), size)


def sub_row(index, sub, dph):
    return jnp.where(lax.rem(index, 2) == 0, sub, dph - 1 - sub)


def segments(pos, ends):
    total = jnp.zeros(pos.shape, jnp.int32)
    for end in ends:
        total = total + (pos >= end).astype(jnp.int32)
    return total


def allowed_mask(key_base, query_base, keys, queries, ends):
    key_pos = key_base + lax.broadcasted_iota(jnp.int32, (keys, 1), 0)
    query_pos = query_base + lax.broadcasted_iota(jnp.int32, (1, queries), 1)
    same = segments(key_pos, ends) == segments(query_pos, ends)
    return same & (key_pos <= query_pos)


def sigmoid(x):
    return 1.0 / (1.0 + jnp.exp(-x))


class Sends:
    def __init__(self):
        self.items = []

    def start(self, copy):
        copy.start()
        self.items.append((None, copy))

    def start_if(self, cond, copy):
        @pl.when(cond)
        def _():
            copy.start()

        self.items.append((cond, copy))

    def finish(self):
        for cond, copy in self.items:
            if cond is None:
                copy.wait_send()
            else:

                @pl.when(cond)
                def _(copy=copy):
                    copy.wait_send()


def layer_kernel(names, sizes, *refs):
    r = types.SimpleNamespace(**dict(zip(names, refs)))
    nb, nh, rows, cw, units, heads, dph, tq = sizes
    half, wide, nz = rows // 2, 2 * cw, nh // 2
    per = half // tq
    pairs = nb // 2
    b, h, w = lax.axis_index("batch"), lax.axis_index("hidden"), lax.axis_index("width")
    group, sub = lax.div(h, dph), lax.rem(h, dph)
    z, c, bp = lax.div(h, 2), lax.rem(h, 2), lax.rem(b, 2)
    x_dev = (b, h, 1 - w)
    c_dev = (b, h + 1 - 2 * c, w)
    y_dev = (b + 1 - 2 * bp, h, w)

    def z_dev(k):
        zz = lax.rem(z + k, nz)
        return zz, (b, 2 * zz + c, w)

    own, other = at(w, cw), at(1 - w, cw)
    mine, theirs = at(w, half), at(1 - w, half)
    lanes = at(c, half)
    ends = [
        r.lens[0, 0],
        r.lens[0, 0] + r.lens[0, 1],
        r.lens[0, 0] + r.lens[0, 1] + r.lens[0, 2],
    ]
    sends = Sends()

    barrier = pltpu.get_barrier_semaphore()
    count = 0
    for dw in range(2):
        for dh in range(nh):
            if dh or dw:
                dev = (b, lax.rem(h + dh, nh), lax.rem(w + dw, 2))
                pl.semaphore_signal(barrier, inc=1, device_id=dev, device_id_type=MESH)
                count += 1
    for db in range(1, nb):
        dev = (lax.rem(b + db, nb), h, w)
        pl.semaphore_signal(barrier, inc=1, device_id=dev, device_id_type=MESH)
        count += 1
    pl.semaphore_wait(barrier, count)

    for i, vec in enumerate((r.v0, r.v1, r.v2, r.v3, r.v4, r.v5)):
        r.vsrc[i : i + 1, :] = vec[...]
    vcopy = remote(r.vsrc, r.vecf.at[:, own], r.xs.at[0], r.xr.at[0], x_dev)
    sends.start(vcopy)
    tcopies = []
    for k in range(2):
        part = pl.ds(k * half, half)
        copy = remote(r.tok.at[part], r.tokf.at[part, own], r.xs.at[1 + k], r.xr.at[1 + k], x_dev)
        sends.start(copy)
        tcopies.append(copy)
    r.wup[z, c, w] = r.wu[...]
    r.wdn[z, c, w] = r.wd[...]

    def weight_hop(k):
        for kind, buf in enumerate((r.wup, r.wdn)):
            for way, step in enumerate((1, -1)):
                zz = z - step * (k - 1)
                have = (zz >= 0) & (zz < nz) & (bp == kind)
                onward = (z + step >= 0) & (z + step < nz)
                index = jnp.clip(zz, 0, nz - 1)
                block = buf.at[index, c, w]
                if k > 1:

                    @pl.when(have)
                    def _(block=block, index=index):
                        await_copy(block, r.wzr.at[index])

                if k < nz:
                    dev = (b, 2 * jnp.clip(z + step, 0, nz - 1) + c, w)
                    copy = remote(block, block, r.wzs.at[way, k], r.wzr.at[index], dev)
                    sends.start_if(have & onward, copy)
                if k > 1 or way == 0:
                    copy = remote(block, block, r.wxs.at[way, k - 1], r.wxr.at[index], x_dev)
                    sends.start_if(have, copy)
                if k > 1:
                    copy = remote(block, block, r.wys.at[way, k - 1], r.wyr.at[index, w], y_dev)
                    sends.start_if(have, copy)

    weight_hop(1)
    gates = ((r.wg1, r.g1f), (r.wg2, r.g2f), (r.wo, r.wof))
    for i, (src, dst) in enumerate(gates):
        piece = at(c, src.shape[0] // 2)
        sends.start(remote(src.at[piece], dst.at[w, piece], r.gxs.at[i], r.gxr.at[i], x_dev))
        dst[w] = src[...]
    ccopy = remote(r.cot.at[theirs], r.cotr.at[:, own], r.xs.at[3], r.xr.at[3], x_dev)
    r.vecf[:, own] = r.vsrc[...]
    r.tokf[:, own] = r.tok[...]
    r.cotr[:, own] = r.cot[mine, :]

    for i, weight in enumerate((r.wq, r.wk, r.wv)):
        turned = flip(weight[...])
        for t in range(heads):
            r.wt[t, i * HD : (i + 1) * HD, :] = turned[t * HD : (t + 1) * HD]

    vcopy.wait_recv()
    gain, shift = r.vecf[0:1, :], r.vecf[1:2, :]
    for k in range(2):
        part = slice(k * half, (k + 1) * half)
        tcopies[k].wait_recv()
        x = r.tokf[part, :].astype(F32)
        centre = x - jnp.mean(x, -1, keepdims=True)
        spread = jnp.mean(centre * centre, -1, keepdims=True)
        n = (centre * lax.rsqrt(spread + EPSILON) * gain + shift).astype(BF16)
        r.npair[c, part, :] = n
        for t in range(heads):
            qkv = nt(r.wt[t], n).astype(BF16)
            r.qsrc[t, :, part] = qkv[:HD]
            r.kvsrc[t, :, part] = qkv[HD:]
        weight_hop(2 + k)
        for step in range(heads - 1, -1, -1):
            t = lax.rem(group + step, heads)
            span = pl.ds(k * half, half)
            src, dst = r.kvsrc.at[t, :, span], r.kvt.at[h, :, span]
            if step:
                dev = (b, t * dph + sub, w)
                sends.start(remote(src, dst, r.ks.at[step, k], r.kr.at[h, k], dev))
            else:
                pltpu.make_async_copy(src, dst, r.kr.at[h, k]).start()
            for i in range(per):
                row = k * per + i
                target = sub_row(h, row, dph)
                src, dst = r.qsrc.at[t, :, pl.ds(row * tq, tq)], r.qt.at[h]
                copy = remote(src, dst, r.qs.at[step, row], r.qr.at[h], (b, t * dph + target, w))
                if step:
                    sends.start(copy)
                else:
                    sends.start_if(target != sub, copy)

                    @pl.when(target == sub)
                    def _(src=src, dst=dst):
                        pltpu.make_async_copy(src, dst, r.qr.at[h]).start()

    for k in range(4, nz + 1):
        weight_hop(k)

    def weights_over_y():
        for kind, buf in enumerate((r.wup, r.wdn)):

            @pl.when(bp == kind)
            def _(buf=buf):
                for k in range(nz):
                    zz, _ = z_dev(k)
                    block = buf.at[zz, c, 1 - w]
                    await_copy(block, r.wxr.at[zz])
                    remote(block, block, r.wyd.at[zz], r.wyr.at[zz, 1 - w], y_dev).start()

    def weights_over_core():
        for kind, buf in enumerate((r.wup, r.wdn)):

            @pl.when(bp != kind)
            def _(buf=buf):
                for k in range(nz):
                    zz, _ = z_dev(k)
                    if k:
                        await_copy(buf.at[zz, c, w], r.wyr.at[zz, w])
                    await_copy(buf.at[zz, c, 1 - w], r.wyr.at[zz, 1 - w])

            block = buf.at[:, c]
            sends.start(remote(block, block, r.wcs.at[kind], r.wcr.at[kind], c_dev))

    def gates_over_core():
        for i, (src, dst) in enumerate(gates):
            piece = dst.at[1 - w, at(c, src.shape[0] // 2)]
            await_copy(piece, r.gxr.at[i])
            sends.start(remote(piece, piece, r.gcs.at[i], r.gcr.at[i], c_dev))

    def weights_sent():
        for kind, buf in enumerate((r.wup, r.wdn)):

            @pl.when(bp == kind)
            def _(buf=buf):
                for k in range(nz):
                    await_copy(buf.at[z, c, w], r.wyd.at[k])

    def pass_on(s):
        @pl.when(lax.rem(s, dph) == sub)
        def _():
            for k in range(2):
                await_copy(r.kvt.at[s, :, pl.ds(k * half, half)], r.kr.at[s, k])
            for k in range(1, dph):
                dev = (b, group * dph + lax.rem(sub + k, dph), w)
                remote(r.kvt.at[s], r.kvt.at[s], r.fs.at[s, k], r.fr.at[s], dev).start()

    def query_forward(s, _):
        @pl.when(s + 1 < nh)
        def _():
            pass_on(s + 1)

        @pl.when(lax.rem(s, dph) != sub)
        def _():
            await_copy(r.kvt.at[s], r.fr.at[s])

        r.kvn[s] = flip(r.kvt[s])
        await_copy(r.qt.at[s], r.qr.at[s])
        row = sub_row(s, sub, dph)
        query_base = s * rows + row * tq
        q = r.qt[s].astype(F32) * SCALE
        q = jnp.concatenate([q, jnp.zeros_like(q)], 0).astype(BF16)

        def masked(j, scores):
            return jnp.where(allowed_mask(j * rows, query_base, rows, tq, ends), scores, NEG)

        def absorb(j, scores, carry):
            top, total, mixed = carry
            new_top = jnp.maximum(top, jnp.max(scores, 0, keepdims=True))
            fade = jnp.exp(top - new_top)
            weights = jnp.exp(scores - new_top)
            total = total * fade + jnp.sum(weights, 0, keepdims=True)
            mixed = mixed * fade + nn(r.kvt[j, HD:, :], weights.astype(BF16))
            return new_top, total, mixed

        def plain_step(j, carry):
            scores = r.sbuf[lax.rem(j, 2)]
            r.sbuf[lax.rem(j + 1, 2)] = nn(r.kvn[j + 1], q)
            return absorb(j, scores, carry)

        def masked_step(j, carry):
            scores = masked(j, r.sbuf[lax.rem(j, 2)])
            r.sbuf[lax.rem(j + 1, 2)] = nn(r.kvn[j + 1], q)
            return absorb(j, scores, carry)

        r.sbuf[0] = masked(0, nn(r.kvn[0], q))
        plain = jnp.where(s == nh - 1, 0, s)
        carry = (jnp.full((1, tq), NEG, F32), jnp.zeros((1, tq), F32), jnp.zeros((HD, tq), F32))
        carry = lax.fori_loop(0, plain, plain_step, carry)
        carry = lax.fori_loop(plain, s, masked_step, carry)
        top, total, mixed = absorb(s, masked(s, r.sbuf[lax.rem(s, 2)]), carry)
        mixed = mixed / total
        r.ot[s] = mixed
        r.lse[s] = top + jnp.log(total)
        r.osend[s] = mixed.astype(BF16)
        row_w = lax.div(row * tq, half)
        lane = lax.rem(row * tq, half)
        dst = r.att.at[at(w * heads + group, HD), pl.ds(pl.multiple_of(lane, tq), tq)]
        slot = r.orc.at[w * heads + group, lax.div(lane, tq)]
        here = (s == h) & (row_w == w)

        @pl.when(here)
        def _():
            pltpu.make_async_copy(r.osend.at[s], dst, slot).start()

        @pl.when(jnp.logical_not(here))
        def _():
            remote(r.osend.at[s], dst, r.osd.at[s], slot, (b, s, row_w)).start()

        @pl.when(s == nh // 4)
        def _():
            weights_over_y()

        return 0

    sends.start(remote(r.npair.at[c], r.npair.at[c], r.cs.at[0], r.cr.at[0], c_dev))
    gates_over_core()
    sends.start(ccopy)
    pass_on(0)
    lax.fori_loop(0, nh, query_forward, 0)
    weights_over_core()

    for i, (src, dst) in enumerate(gates):
        await_copy(dst.at[1 - w, at(1 - c, src.shape[0] // 2)], r.gcr.at[i])

    def two(a, weight):
        return jnp.concatenate([nn(a, weight[0]), nn(a, weight[1])], 1)

    def two_back(g, weight):
        return nt(g[:, :cw], weight[0]) + nt(g[:, cw:], weight[1])

    tok = r.tokf[mine, :].astype(F32)
    n1 = r.npair[c, mine, :]
    gate_one = sigmoid(two(n1, r.g1f) + r.vecf[2:3, :])
    for g in range(2 * heads):
        for i in range(per):
            await_copy(r.att.at[pl.ds(g * HD, HD), pl.ds(i * tq, tq)], r.orc.at[g, i])
    wof = r.wof[...].reshape(wide, wide)
    branch_one = nn(flip(r.att[...]), wof)
    middle = tok + gate_one * (branch_one - tok)
    centre = middle - jnp.mean(middle, -1, keepdims=True)
    rstd = lax.rsqrt(jnp.mean(centre * centre, -1, keepdims=True) + EPSILON)
    n2 = centre * rstd
    gain_two = r.vecf[3:4, :]
    normed_two = (n2 * gain_two + r.vecf[4:5, :]).astype(BF16)
    gate_two = sigmoid(two(normed_two, r.g2f) + r.vecf[5:6, :])
    for kind, buf in enumerate((r.wup, r.wdn)):
        await_copy(buf.at[:, 1 - c], r.wcr.at[kind])

    def units_of(i2, p):
        return i2, lax.rem(c + p, 2)

    def up(i2, branch):
        for p in range(2):
            i, q = units_of(i2, p)
            pre = nn(normed_two, r.wup[i, q].reshape(wide, units))
            r.pre[i2, p] = pre
            act = jax.nn.gelu(pre).astype(BF16)
            branch = branch + jnp.concatenate([nn(act, r.wdn[i, q, 0]), nn(act, r.wdn[i, q, 1])], 1)
            if p:
                r.acts[i2] = act
                dst = r.actp.at[i2, lanes, :]
                remote(r.acts.at[i2], dst, r.as_.at[i2], r.ar.at[i2], c_dev).start()
            else:
                r.actp[i2, lanes, :] = act
        return branch

    branch_two = lax.fori_loop(0, nz, up, jnp.zeros(middle.shape, F32))
    delta = branch_two - middle
    r.outr[...] = (middle + gate_two * delta).astype(BF16)
    ocopy = remote(r.outr.at[:, other], r.out_c.at[mine, :], r.xs.at[4], r.xr.at[4], x_dev)
    sends.start(ocopy)
    ccopy.wait_recv()
    grad = r.cotr[...].astype(F32)
    gb2 = (grad * gate_two).astype(BF16)
    gl2 = (grad * delta * gate_two * (1.0 - gate_two)).astype(BF16)
    gmid = grad * (1.0 - gate_two)

    def down(i2, total):
        for p in range(2):
            i, q = units_of(i2, p)
            ghid = nt(gb2[:, :cw], r.wdn[i, q, 0]) + nt(gb2[:, cw:], r.wdn[i, q, 1])
            pre = r.pre[i2, p]
            k = 0.7978845608028654
            t = jnp.tanh(k * (pre + 0.044715 * pre * pre * pre))
            slope = 0.5 * (1.0 + t) + 0.5 * pre * (1.0 - t * t) * (k * (1.0 + 3 * 0.044715 * pre * pre))
            gpre = (ghid * slope).astype(BF16)
            total = total + nt(gpre, r.wup[i, q].reshape(wide, units))
            if p:
                r.gpres[i2] = gpre
                dst = r.gprep.at[i2, lanes, :]
                remote(r.gpres.at[i2], dst, r.ps_.at[i2], r.pr.at[i2], c_dev).start()
            else:
                r.gprep[i2, lanes, :] = gpre
        return total

    gnorm = lax.fori_loop(0, nz, down, two_back(gl2, r.g2f))
    e = gnorm * gain_two
    gmid = gmid + rstd * (
        e - jnp.mean(e, -1, keepdims=True) - n2 * jnp.mean(e * n2, -1, keepdims=True)
    )
    gb1 = (gmid * gate_one).astype(BF16)
    r.gatt[...] = nt(wof, gb1).astype(BF16)
    for dw in (1, 0):
        wt = lax.rem(w + dw, 2)
        for step in range(heads - 1, -1, -1):
            t = lax.rem(group + step, heads)
            for i in range(per):
                target = sub_row(h, w * per + i, dph)
                src = r.gatt.at[at(wt * heads + t, HD), pl.ds(i * tq, tq)]
                dst = r.dot.at[h]
                dev = (b, t * dph + target, wt)
                copy = remote(src, dst, r.ds.at[dw, step, i], r.dr.at[h], dev)
                if step or dw:
                    sends.start(copy)
                else:
                    sends.start_if(target != sub, copy)

                    @pl.when(target == sub)
                    def _(src=src, dst=dst):
                        pltpu.make_async_copy(src, dst, r.dr.at[h]).start()

    gl1 = (gmid * (branch_one - tok) * gate_one * (1.0 - gate_one)).astype(BF16)
    r.ginp[...] = gmid * (1.0 - gate_one)
    r.npt[:, lanes] = flip(normed_two)
    sends.start(remote(r.npt.at[:, lanes], r.npt.at[:, lanes], r.cs.at[1], r.cr.at[1], c_dev))
    r.gbt[:, lanes] = flip(gb2)
    sends.start(remote(r.gbt.at[:, lanes], r.gbt.at[:, lanes], r.cs.at[2], r.cr.at[2], c_dev))
    quarter = half // 2
    r.lsrc[0] = r.att[...]
    r.lsrc[1] = flip(gl1)
    r.lsrc[2] = flip(gl2)
    for m, right in enumerate((gb1, n1, normed_two)):
        r.bpair[m, lanes, :] = right
        block = r.bpair.at[m, lanes, :]
        sends.start(remote(block, block, r.cs.at[3 + m], r.cr.at[3 + m], c_dev))
        for v in range(2):
            src = r.lsrc.at[m, at(2 * v + 1 - c, quarter), :]
            dst = r.apair.at[m, v, :, lanes]
            sends.start(remote(src, dst, r.cs.at[6 + 2 * m + v], r.cr.at[6 + 2 * m + v], c_dev))
            r.apair[m, v, :, lanes] = r.lsrc[m, at(2 * v + c, quarter), :]
    r.gterm[...] = two_back(gl1, r.g1f)
    r.vsum[...] = jnp.zeros_like(r.vsum)
    r.vsum[2:3, :] = jnp.sum(gl1.astype(F32), 0, keepdims=True)
    r.vsum[3:4, :] = jnp.sum(gnorm * n2, 0, keepdims=True)
    r.vsum[4:5, :] = jnp.sum(gnorm, 0, keepdims=True)
    r.vsum[5:6, :] = jnp.sum(gl2.astype(F32), 0, keepdims=True)
    r.out_c[mine, :] = r.outr[:, own]

    eighth = quarter // 2
    for m in range(3):
        await_copy(r.bpair.at[m, lanes, :], r.cr.at[3 + m])
        for v in range(2):
            await_copy(r.apair.at[m, v, :, lanes], r.cr.at[6 + 2 * m + v])
            block = nn(r.apair[m, v], r.bpair[m]).astype(BF16)
            for y in range(2):
                r.gb[v, y, m * eighth : (m + 1) * eighth, :] = block[y * eighth : (y + 1) * eighth]
    await_copy(r.npt.at[:, lanes], r.cr.at[1])
    await_copy(r.gbt.at[:, lanes], r.cr.at[2])

    def weight_grads(i2, _):
        await_copy(r.gprep.at[i2, lanes, :], r.pr.at[i2])
        await_copy(r.actp.at[i2, lanes, :], r.ar.at[i2])
        r.ga[0, i2] = nn(r.npt[...], r.gprep[i2]).astype(BF16).reshape(2, 2, quarter, units)
        r.ga[1, i2] = nn(r.gbt[...], r.actp[i2]).astype(BF16).reshape(2, 2, quarter, units)
        return 0

    lax.fori_loop(0, nz, weight_grads, 0)
    sends.start(remote(r.ga.at[0, :, 1 - w], r.xin0, r.xs.at[5], r.xr.at[5], x_dev))
    sends.start(remote(r.ga.at[1, :, :, 1 - bp], r.yin1, r.ys.at[1], r.yr.at[1], y_dev))


    def ffn_second():
        await_copy(r.xin0, r.xr.at[5])
        r.ga[0, :, w] = (r.ga[0, :, w].astype(F32) + r.xin0[...].astype(F32)).astype(BF16)
        remote(r.ga.at[0, :, w, 1 - bp], r.yin0, r.ys.at[2], r.yr.at[2], y_dev).start()
        await_copy(r.yin1, r.yr.at[1])
        r.ga[1, :, :, bp] = (r.ga[1, :, :, bp].astype(F32) + r.yin1[...].astype(F32)).astype(BF16)
        remote(r.ga.at[1, :, 1 - w, bp], r.xin1, r.xs.at[6], r.xr.at[6], x_dev).start()
        remote(r.gb.at[:, 1 - bp], r.ybin, r.ys.at[0], r.yr.at[0], y_dev).start()

    def ffn_third():
        await_copy(r.yin0, r.yr.at[2])
        await_copy(r.xin1, r.xr.at[6])
        r.zs[:, 0] = (r.ga[0, :, w, bp].astype(F32) + r.yin0[...].astype(F32)).astype(BF16)
        r.zs[:, 1] = (r.ga[1, :, w, bp].astype(F32) + r.xin1[...].astype(F32)).astype(BF16)
        for k in range(nz - 1, 0, -1):
            zz, dev = z_dev(k)
            remote(r.zs.at[zz], r.zin.at[z], r.zss.at[k], r.zsr.at[z], dev).start()
        r.zin[z] = r.zs[z]

    def ffn_fourth():
        for k in range(1, nz):
            zz, _ = z_dev(k)
            await_copy(r.zin.at[zz], r.zsr.at[zz])
        total = r.zin[0].astype(F32)
        for k in range(1, nz):
            total = total + r.zin[k].astype(F32)
        if pairs > 1:
            mypair = lax.div(b, 2)
            r.pin[mypair] = total.astype(BF16)
            for k in range(1, pairs):
                dev = (lax.rem(b + 2 * k, nb), h, w)
                block = r.pin.at[mypair]
                sends.start(remote(block, block, r.pas.at[k], r.par.at[mypair], dev))
            for k in range(1, pairs):
                pp = lax.rem(mypair + k, pairs)
                await_copy(r.pin.at[pp], r.par.at[pp])
            total = r.pin[0].astype(F32)
            for k in range(1, pairs):
                total = total + r.pin[k].astype(F32)
        r.red_a[bp] = total.astype(BF16)
        block = r.red_a.at[bp]
        sends.start(remote(block, block, r.ys.at[3], r.yr.at[3], y_dev))

    def ffn_sent():
        await_copy(r.yin0, r.ys.at[2])
        await_copy(r.xin1, r.xs.at[6])
        for k in range(1, nz):
            await_copy(r.zin.at[z], r.zss.at[k])

    deep = (heads // 2) * 3 * HD // 2
    zr = deep * 4 // nz

    def z_part(zz):
        return pl.ds(pl.multiple_of(lax.div(zz, 4) * zr, zr), zr), at(lax.rem(zz, 4), 128)

    def square_x():
        await_copy(r.ybin, r.yr.at[0])
        r.gb[:, bp] = (r.gb[:, bp].astype(F32) + r.ybin[...].astype(F32)).astype(BF16)
        remote(r.gb.at[1 - w, bp], r.xbin, r.xs.at[7], r.xr.at[7], x_dev).start()

    def square_z(which):
        if which == 0:
            await_copy(r.xbin, r.xr.at[7])
            total = r.gb[w, bp].astype(F32) + r.xbin[...].astype(F32)
        else:
            await_copy(r.ycin, r.yr.at[4])
            total = r.gc[bp].astype(F32) + r.ycin[...].astype(F32)
        r.sq[which] = total.astype(BF16)
        for k in range(nz - 1, 0, -1):
            zz, dev = z_dev(k)
            src = r.sq.at[(which,) + z_part(zz)]
            remote(src, r.sqin.at[which, z], r.sqs.at[which, k], r.sqr.at[which, z], dev).start()

    def square_spread(which):
        total = r.sq[(which,) + z_part(z)].astype(F32)
        r.sqin[which, z] = total.astype(BF16)
        for k in range(1, nz):
            zz, _ = z_dev(k)
            await_copy(r.sqin.at[which, zz], r.sqr.at[which, zz])
        total = r.sqin[which, 0].astype(F32)
        for k in range(1, nz):
            total = total + r.sqin[which, k].astype(F32)
        if pairs > 1:
            mypair = lax.div(b, 2)
            r.sqpair[which, mypair] = total.astype(BF16)
            for k in range(1, pairs):
                dev = (lax.rem(b + 2 * k, nb), h, w)
                block = r.sqpair.at[which, mypair]
                remote(block, block, r.sqps.at[which, k], r.sqpr.at[which, mypair], dev).start()
            for k in range(1, pairs):
                pp = lax.rem(mypair + k, pairs)
                await_copy(r.sqpair.at[which, pp], r.sqpr.at[which, pp])
            total = r.sqpair[which, 0].astype(F32)
            for k in range(1, pairs):
                total = total + r.sqpair[which, k].astype(F32)
        r.red_s[(which, c, bp) + z_part(z)] = total.astype(BF16)
        for k in range(nz - 1, 0, -1):
            _, dev = z_dev(k)
            block = r.red_s.at[(which, c, bp) + z_part(z)]
            remote(block, block, r.sgs.at[which, k], r.sgr.at[which, z], dev).start()

    def square_y(which):
        for k in range(1, nz):
            zz, _ = z_dev(k)
            await_copy(r.red_s.at[(which, c, bp) + z_part(zz)], r.sgr.at[which, zz])
        block = r.red_s.at[which, c, bp]
        remote(block, block, r.sys.at[which], r.syr.at[which], y_dev).start()

    def square_core(which):
        await_copy(r.red_s.at[which, c, 1 - bp], r.syr.at[which])
        block = r.red_s.at[which, c]
        remote(block, block, r.scs.at[which], r.scr.at[which], c_dev).start()

    def square_end(which):
        await_copy(r.red_s.at[which, 1 - c], r.scr.at[which])
        await_copy(r.red_s.at[which, c], r.scs.at[which])
        await_copy(r.red_s.at[which, c, bp], r.sys.at[which])
        for k in range(1, nz):
            await_copy(r.sqin.at[which, z], r.sqs.at[which, k])
            await_copy(r.sqin.at[which, z], r.sgs.at[which, k])
            if k < pairs:
                await_copy(r.sqpair.at[which, 0], r.sqps.at[which, k])

    r.acc[...] = jnp.zeros_like(r.acc)

    def finish(s):
        @pl.when(lax.rem(s, dph) == sub)
        def _():
            total = r.acc[s]
            for k in range(1, dph):
                slot = r.pin_kv.at[lax.div(s, dph), k - 1]
                await_copy(slot, r.pkr.at[lax.div(s, dph), k - 1])
                total = total + r.pin_kv[lax.div(s, dph), k - 1]
            r.dkvsend[s] = total.astype(BF16)
            dst = r.dqkv.at[group, pl.ds(HD, 2 * HD), :]

            @pl.when(s == h)
            def _():
                pltpu.make_async_copy(r.dkvsend.at[s], dst, r.dkr.at[group]).start()

            @pl.when(s != h)
            def _():
                remote(r.dkvsend.at[s], dst, r.dks.at[s], r.dkr.at[group], (b, s, w)).start()

    def query_backward(step, _):
        s = nh - 1 - step
        row = sub_row(s, sub, dph)
        query_base = s * rows + row * tq
        await_copy(r.dot.at[s], r.dr.at[s])
        q = r.qt[s]
        dout = r.dot[s]
        q_low = jnp.concatenate([q.astype(F32) * SCALE, jnp.zeros((HD, tq), F32)], 0).astype(BF16)
        d_high = jnp.concatenate([jnp.zeros((HD, tq), BF16), dout], 0)
        log_sum = r.lse[s]
        centre = jnp.sum(r.ot[s] * dout.astype(F32), 0, keepdims=True)

        def block(j, dq, masked):
            scores = nn(r.kvn[j], q_low)
            if masked:
                scores = jnp.where(allowed_mask(j * rows, query_base, rows, tq, ends), scores, NEG)
            probs = jnp.exp(scores - log_sum)
            gprobs = nn(r.kvn[j], d_high)
            gscores = (probs * (gprobs - centre)).astype(BF16)
            r.acc[j, HD:, :] += nt(dout, probs.astype(BF16))
            r.acc[j, :HD, :] += nt(q, gscores) * SCALE
            return dq + nn(r.kvt[j, :HD, :], gscores)

        plain_end = jnp.where(s == nh - 1, 1, jnp.maximum(s, 1))
        dq = jnp.zeros((HD, tq), F32)
        dq = lax.fori_loop(1, plain_end, lambda j, d: block(j, d, False), dq)
        count = 1 + jnp.where(s > 0, s + 1 - plain_end, 0)

        def with_mask(t, d):
            return block(jnp.where(t == 0, 0, plain_end + t - 1), d, True)

        dq = lax.fori_loop(0, count, with_mask, dq)
        r.dqsend[s] = (dq * SCALE).astype(BF16)
        dst = r.dqkv.at[group, pl.ds(0, HD), pl.ds(pl.multiple_of(row * tq, tq), tq)]

        @pl.when(s == h)
        def _():
            pltpu.make_async_copy(r.dqsend.at[s], dst, r.dqr.at[group, row]).start()

        @pl.when(s != h)
        def _():
            remote(r.dqsend.at[s], dst, r.dqs.at[s], r.dqr.at[group, row], (b, s, w)).start()

        owner = lax.rem(s, dph)

        @pl.when(owner != sub)
        def _():
            k = lax.rem(sub - owner + dph, dph)
            dev = (b, group * dph + owner, w)
            slot = lax.div(s, dph)
            remote(r.acc.at[s], r.pin_kv.at[slot, k - 1], r.pks.at[s], r.pkr.at[slot, k - 1], dev).start()

        @pl.when(step > 0)
        def _():
            finish(s + 1)

        unit = nh // 8

        @pl.when(step == 2 * unit)
        def _():
            ffn_second()

        @pl.when(step == 4 * unit)
        def _():
            ffn_third()

        return 0

    lax.fori_loop(0, nh, query_backward, 0)
    finish(0)
    square_x()

    for t in range(heads):
        await_copy(r.dqkv.at[t, pl.ds(HD, 2 * HD), :], r.dkr.at[t])
        for i in range(dph):
            await_copy(r.dqkv.at[t, pl.ds(0, HD), pl.ds(i * tq, tq)], r.dqr.at[t, i])
        sends.start_if(
            t % 2 != c, remote(r.dqkv.at[t], r.dsib.at[t // 2], r.ts.at[t], r.tr.at[t // 2], c_dev)
        )
    wts = r.wt[...].reshape(heads * 3 * HD, wide)

    def grad_normed(span):
        return nn(flip(r.dqkv[:, :, span].reshape(heads * 3 * HD, half)), wts)

    square_z(0)
    r.psend[...] = grad_normed(theirs).astype(BF16)
    pcopy = remote(r.psend, r.precv, r.xs.at[8], r.xr.at[8], x_dev)
    sends.start(pcopy)
    await_copy(r.npair.at[1 - c], r.cr.at[0])
    for j in range(heads // 2):
        await_copy(r.dsib.at[j], r.tr.at[j])
        part = nn(r.dqkv[2 * j + c], r.npair[c]) + nn(r.dsib[j], r.npair[1 - c])
        span = slice((j % (heads // 4)) * 3 * HD, (j % (heads // 4) + 1) * 3 * HD)
        r.gc[j // (heads // 4), span, :] = part.astype(BF16)
    sends.start(remote(r.gc.at[1 - bp], r.ycin, r.ys.at[4], r.yr.at[4], y_dev))
    gnorm = grad_normed(mine) + r.gterm[...]
    x = r.tokf[mine, :].astype(F32)
    centre = x - jnp.mean(x, -1, keepdims=True)
    rstd = lax.rsqrt(jnp.mean(centre * centre, -1, keepdims=True) + EPSILON)
    n = centre * rstd
    square_spread(0)
    square_z(1)
    pcopy.wait_recv()
    gnorm = gnorm + r.precv[...].astype(F32)
    e = gnorm * r.vecf[0:1, :]
    result = r.ginp[...] + rstd * (
        e - jnp.mean(e, -1, keepdims=True) - n * jnp.mean(e * n, -1, keepdims=True)
    )
    r.tsend[...] = result.astype(BF16)
    tcopy = remote(r.tsend.at[:, other], r.trecv, r.xs.at[9], r.xr.at[9], x_dev)
    sends.start(tcopy)
    r.vsum[0:1, :] = jnp.sum(gnorm * n, 0, keepdims=True)
    r.vsum[1:2, :] = jnp.sum(gnorm, 0, keepdims=True)
    me4 = 2 * c + w
    r.vin4[me4] = r.vsum[...]
    k = 0
    for dc in range(2):
        for dw in range(2):
            if dc or dw:
                cc, ww = lax.rem(c + dc, 2), lax.rem(w + dw, 2)
                dev = (b, 2 * z + cc, ww)
                sends.start(remote(r.vin4.at[me4], r.vin4.at[me4], r.v4s.at[k], r.v4r.at[me4], dev))
                k += 1
    r.gtok[mine, :] = jnp.where(w == 0, result[:, :cw], result[:, cw:])
    square_y(0)
    for dc in range(2):
        for dw in range(2):
            if dc or dw:
                peer = 2 * lax.rem(c + dc, 2) + lax.rem(w + dw, 2)
                await_copy(r.vin4.at[peer], r.v4r.at[peer])
    r.vinz[z] = r.vin4[0] + r.vin4[1] + r.vin4[2] + r.vin4[3]
    for k in range(1, nz):
        _, dev = z_dev(k)
        sends.start(remote(r.vinz.at[z], r.vinz.at[z], r.vzs.at[k], r.vzr.at[z], dev))
    square_spread(1)
    ffn_fourth()
    square_core(0)
    tcopy.wait_recv()
    r.gtok[theirs, :] = r.trecv[...].astype(F32)
    ocopy.wait_recv()
    for k in range(1, nz):
        zz, _ = z_dev(k)
        await_copy(r.vinz.at[zz], r.vzr.at[zz])
    total = r.vinz[0]
    for k in range(1, nz):
        total = total + r.vinz[k]
    r.vinb[b] = total
    for k in range(1, nb):
        dev = (lax.rem(b + k, nb), h, w)
        sends.start(remote(r.vinb.at[b], r.vinb.at[b], r.vbs.at[k], r.vbr.at[b], dev))
    square_y(1)
    for k in range(1, nb):
        bb = lax.rem(b + k, nb)
        await_copy(r.vinb.at[bb], r.vbr.at[bb])
    total = r.vinb[0]
    for k in range(1, nb):
        total = total + r.vinb[k]
    r.red_v[...] = jnp.where(w == 0, total[:, :cw], total[:, cw:])
    await_copy(r.red_a.at[1 - bp], r.yr.at[3])
    square_core(1)

    def sent(s, _):
        row = sub_row(s, sub, dph)
        here = (s == h) & (lax.div(row * tq, half) == w)

        @pl.when(jnp.logical_not(here))
        def _():
            await_copy(r.osend.at[s], r.osd.at[s])

        @pl.when(lax.rem(s, dph) == sub)
        def _():
            for k in range(1, dph):
                await_copy(r.kvt.at[s], r.fs.at[s, k])

        @pl.when(s != h)
        def _():
            await_copy(r.dqsend.at[s], r.dqs.at[s])

        @pl.when((s != h) & (lax.rem(s, dph) == sub))
        def _():
            await_copy(r.dkvsend.at[s], r.dks.at[s])

        @pl.when(lax.rem(s, dph) != sub)
        def _():
            await_copy(r.acc.at[s], r.pks.at[s])

        return 0

    lax.fori_loop(0, nh, sent, 0)
    weights_sent()
    for i2 in range(nz):
        await_copy(r.acts.at[i2], r.as_.at[i2])
        await_copy(r.gpres.at[i2], r.ps_.at[i2])
    ffn_sent()
    await_copy(r.ybin, r.ys.at[0])
    await_copy(r.xbin, r.xs.at[7])
    sends.finish()
    square_end(0)
    square_end(1)


def final_kernel(heads, *refs):
    (
        out_c, gtok, red_a, red_s, red_v,
        o_out, o_tok, o_g1, o_b1, o_wq, o_wk, o_wv, o_wo, o_gw1, o_gb1, o_g2, o_b2, o_gw2, o_gb2, o_up, o_dn,
    ) = refs
    o_out[...] = out_c[...]
    o_tok[...] = gtok[...]
    for i, ref in enumerate((o_g1, o_b1, o_gb1, o_g2, o_b2, o_gb2)):
        ref[...] = red_v[i : i + 1, :]
    _, quarter, units = red_a.shape[1:]
    o_up[:quarter, :] = red_a[0, 0].astype(F32)
    o_up[quarter:, :] = red_a[1, 0].astype(F32)
    o_dn[:, :quarter] = red_a[0, 1].astype(F32).T
    o_dn[:, quarter:] = red_a[1, 1].astype(F32).T
    eighth = quarter // 2
    for core in range(2):
        for y in range(2):
            base = (2 * core + y) * eighth
            o_wo[base : base + eighth, :] = red_s[0, core, y, :eighth, :].astype(F32)
    for m, ref in ((1, o_gw1), (2, o_gw2)):
        full = [red_s[0, core, y, m * eighth : (m + 1) * eighth, :] for core in range(2) for y in range(2)]
        ref[...] = jnp.concatenate(full, 0).astype(F32).T
    for i, ref in enumerate((o_wq, o_wk, o_wv)):
        full = []
        for t in range(heads):
            j, core = t // 2, t % 2
            base = (j % (heads // 4)) * 3 * HD + i * HD
            full.append(red_s[1, core, j // (heads // 4), base : base + HD, :])
        ref[...] = jnp.concatenate(full, 0).astype(F32).T


def local(
    tokens, ln1_gain, ln1_bias, w_query, w_key, w_value, w_out, gate1_weight, gate1_bias,
    ln2_gain, ln2_bias, gate2_weight, gate2_bias, w_up, w_down, lengths, cotangent,
):
    nb, nh = lax.axis_size("batch"), lax.axis_size("hidden")
    rows, cw = tokens.shape
    units = w_up.shape[1]
    heads = cw // HD
    dph = nh // heads
    tq, half, wide, nz, pairs = rows // dph, rows // 2, 2 * cw, nh // 2, nb // 2
    quarter = half // 2
    deep = (heads // 2) * 3 * HD // 2
    zr = deep * 4 // nz
    per = half // tq
    sizes = (nb, nh, rows, cw, units, heads, dph, tq)

    ins = dict(
        lens=lengths, tok=tokens, cot=cotangent, v0=ln1_gain[None], v1=ln1_bias[None], v2=gate1_bias[None],
        v3=ln2_gain[None], v4=ln2_bias[None], v5=gate2_bias[None], wq=w_query, wk=w_key, wv=w_value,
        wo=w_out, wg1=gate1_weight, wg2=gate2_weight, wu=w_up, wd=w_down,
    )
    outs = dict(
        out_c=((rows, cw), BF16),
        gtok=((rows, cw), F32),
        red_a=((2, 2, quarter, units), BF16),
        red_s=((2, 2, 2, deep, wide), BF16),
        red_v=((8, cw), F32),
    )
    bufs = dict(
        vsrc=((8, cw), F32), vecf=((8, wide), F32), tokf=((rows, wide), BF16), cotr=((half, wide), BF16),
        g1f=((2, wide, cw), BF16), g2f=((2, wide, cw), BF16), wof=((2, cw, wide), BF16),
        wup=((nz, 2, 2, cw, units), BF16), wdn=((nz, 2, 2, units, cw), BF16),
        wt=((heads, 3 * HD, wide), BF16), npair=((2, rows, wide), BF16),
        qsrc=((heads, HD, rows), BF16), kvsrc=((heads, 2 * HD, rows), BF16),
        kvt=((nh, 2 * HD, rows), BF16), kvn=((nh, rows, 2 * HD), BF16), qt=((nh, HD, tq), BF16),
        sbuf=((2, rows, tq), F32), ot=((nh, HD, tq), F32), lse=((nh, 1, tq), F32), osend=((nh, HD, tq), BF16),
        att=((2 * heads * HD, half), BF16),
        pre=((nz, 2, half, units), F32), acts=((nz, half, units), BF16), actp=((nz, rows, units), BF16),
        gpres=((nz, half, units), BF16), gprep=((nz, rows, units), BF16),
        outr=((half, wide), BF16), gatt=((wide, half), BF16), dot=((nh, HD, tq), BF16),
        ginp=((half, wide), F32), gterm=((half, wide), F32), npt=((wide, rows), BF16), gbt=((wide, rows), BF16),
        lsrc=((3, wide, half), BF16), bpair=((3, rows, wide), BF16), apair=((3, 2, quarter, rows), BF16),
        vsum=((8, wide), F32),
        gb=((2, 2, deep, wide), BF16), ybin=((2, deep, wide), BF16), xbin=((deep, wide), BF16),
        ga=((2, nz, 2, 2, quarter, units), BF16), xin0=((nz, 2, quarter, units), BF16),
        yin1=((nz, 2, quarter, units), BF16), yin0=((nz, quarter, units), BF16), xin1=((nz, quarter, units), BF16),
        zs=((nz, 2, quarter, units), BF16), zin=((nz, 2, quarter, units), BF16),
        pin=((pairs, 2, quarter, units), BF16),
        gc=((2, deep, wide), BF16), ycin=((deep, wide), BF16), sq=((2, deep, wide), BF16),
        sqin=((2, nz, zr, 128), BF16), sqpair=((2, pairs, zr, 128), BF16),
        acc=((nh, 2 * HD, rows), F32), pin_kv=((nh // dph, max(dph - 1, 1), 2 * HD, rows), F32),
        dkvsend=((nh, 2 * HD, rows), BF16), dqsend=((nh, HD, tq), BF16),
        dqkv=((heads, 3 * HD, rows), BF16), dsib=((heads // 2, 3 * HD, rows), BF16),
        psend=((half, wide), BF16), precv=((half, wide), BF16),
        tsend=((half, wide), BF16), trecv=((half, cw), BF16),
        vin4=((4, 8, wide), F32), vinz=((nz, 8, wide), F32), vinb=((nb, 8, wide), F32),
    )
    sems = dict(
        xs=(10,), xr=(10,), wzs=(2, nz), wzr=(nz,), gxs=(3,), gxr=(3,), gcs=(3,), gcr=(3,),
        ks=(heads, 2), kr=(nh, 2), qs=(heads, dph), qr=(nh,), cs=(12,), cr=(12,),
        wxs=(2, nz), wxr=(nz,), wys=(2, nz), wyr=(nz, 2), wyd=(nz,), wcs=(2,), wcr=(2,),
        fs=(nh, dph), fr=(nh,), osd=(nh,), orc=(2 * heads, per),
        as_=(nz,), ar=(nz,), ps_=(nz,), pr=(nz,), ds=(2, heads, per), dr=(nh,),
        ys=(5,), yr=(5,), zss=(nz,), zsr=(nz,), pas=(pairs,), par=(pairs,),
        sqs=(2, nz), sqr=(2, nz), sqps=(2, pairs), sqpr=(2, pairs), sgs=(2, nz), sgr=(2, nz),
        sys=(2,), syr=(2,), scs=(2,), scr=(2,),
        pks=(nh,), pkr=(nh // dph, max(dph - 1, 1)), dqs=(nh,), dqr=(heads, dph), dks=(nh,), dkr=(heads,),
        ts=(heads,), tr=(heads // 2,), v4s=(3,), v4r=(4,), vzs=(nz,), vzr=(nz,), vbs=(nb,), vbr=(nb,),
    )
    names = list(ins) + list(outs) + list(bufs) + list(sems)
    vmem = pl.BlockSpec(memory_space=pltpu.VMEM)
    results = pl.pallas_call(
        functools.partial(layer_kernel, names, sizes),
        out_shape=[jax.ShapeDtypeStruct(shape, kind) for shape, kind in outs.values()],
        in_specs=[pl.BlockSpec(memory_space=pltpu.SMEM)] + [vmem] * (len(ins) - 1),
        out_specs=[vmem] * len(outs),
        scratch_shapes=[pltpu.VMEM(shape, kind) for shape, kind in bufs.values()]
        + [pltpu.SemaphoreType.DMA(shape) for shape in sems.values()],
        compiler_params=pltpu.CompilerParams(
            collective_id=1, has_side_effects=True, vmem_limit_bytes=VMEM_LIMIT
        ),
        cost_estimate=pl.CostEstimate(flops=10**10, bytes_accessed=10**7, transcendentals=10**7),
    )(*ins.values())
    grads = [
        ((rows, cw), BF16), ((rows, cw), F32), ((1, cw), F32), ((1, cw), F32),
        ((wide, cw), F32), ((wide, cw), F32), ((wide, cw), F32), ((cw, wide), F32),
        ((wide, cw), F32), ((1, cw), F32), ((1, cw), F32), ((1, cw), F32), ((wide, cw), F32), ((1, cw), F32),
        ((cw, units), F32), ((units, cw), F32),
    ]
    done = pl.pallas_call(
        functools.partial(final_kernel, heads),
        out_shape=[jax.ShapeDtypeStruct(shape, kind) for shape, kind in grads],
        in_specs=[vmem] * len(outs),
        out_specs=[vmem] * len(grads),
        compiler_params=pltpu.CompilerParams(vmem_limit_bytes=VMEM_LIMIT),
    )(*results)
    return tuple(a[0] if a.shape[0] == 1 else a for a in done)


def solution(mesh):
    cols = P(None, "width")
    vec = P("width")
    in_specs = (
        P(("batch", "hidden"), "width"), vec, vec, cols, cols, cols, P("width", None), cols, vec, vec, vec,
        cols, vec, P("width", "hidden"), P("hidden", "width"), P("batch", None),
        P(("batch", "hidden"), "width"),
    )
    out_specs = (
        P(("batch", "hidden"), "width"), P(("batch", "hidden"), "width"), vec, vec, cols, cols, cols,
        P("width", None), cols, vec, vec, vec, cols, vec, P("width", "hidden"), P("hidden", "width"),
    )
    return jax.shard_map(local, mesh=mesh, in_specs=in_specs, out_specs=out_specs, check_vma=False)
```

```python
import functools
import types

import jax
import jax.numpy as jnp
from jax import lax
from jax.experimental import pallas as pl
from jax.experimental.pallas import tpu as pltpu
from jax.sharding import PartitionSpec as P

HD = 64
EPSILON = 1e-05
MESH = pl.DeviceIdType.MESH
F32 = jnp.float32
BF16 = jnp.bfloat16
NEG = -1e30
VMEM_LIMIT = 62 * 1024 * 1024
SCALE = HD**-0.5


def nn(a, b):
    return lax.dot_general(a, b, (((1,), (0,)), ((), ())), preferred_element_type=F32)


def nt(a, b):
    return lax.dot_general(a, b, (((1,), (1,)), ((), ())), preferred_element_type=F32)


def flip(a):
    return a.astype(F32).T.astype(BF16)


def remote(src, dst, send, recv, dev):
    return pltpu.make_async_remote_copy(
        src_ref=src, dst_ref=dst, send_sem=send, recv_sem=recv, device_id=dev, device_id_type=MESH
    )


def await_copy(ref, sem):
    pltpu.make_async_copy(ref, ref, sem).wait()


def at(index, size):
    return pl.ds(pl.multiple_of(index * size, size), size)


def sub_row(index, sub, dph):
    return jnp.where(lax.rem(index, 2) == 0, sub, dph - 1 - sub)


def segments(pos, ends):
    total = jnp.zeros(pos.shape, jnp.int32)
    for end in ends:
        total = total + (pos >= end).astype(jnp.int32)
    return total


def allowed_mask(key_base, query_base, keys, queries, ends):
    key_pos = key_base + lax.broadcasted_iota(jnp.int32, (keys, 1), 0)
    query_pos = query_base + lax.broadcasted_iota(jnp.int32, (1, queries), 1)
    same = segments(key_pos, ends) == segments(query_pos, ends)
    return same & (key_pos <= query_pos)


def sigmoid(x):
    return 1.0 / (1.0 + jnp.exp(-x))


class Sends:
    def __init__(self):
        self.items = []

    def start(self, copy):
        copy.start()
        self.items.append((None, copy))

    def start_if(self, cond, copy):
        @pl.when(cond)
        def _():
            copy.start()

        self.items.append((cond, copy))

    def finish(self):
        for cond, copy in self.items:
            if cond is None:
                copy.wait_send()
            else:

                @pl.when(cond)
                def _(copy=copy):
                    copy.wait_send()


def layer_kernel(names, sizes, *refs):
    r = types.SimpleNamespace(**dict(zip(names, refs)))
    nb, nh, rows, cw, units, heads, dph, tq = sizes
    half, wide, nz = rows // 2, 2 * cw, nh // 2
    per = half // tq
    pairs = nb // 2
    hops = nz.bit_length() - 1
    b, h, w = lax.axis_index("batch"), lax.axis_index("hidden"), lax.axis_index("width")
    group, sub = lax.div(h, dph), lax.rem(h, dph)
    z, c, bp = lax.div(h, 2), lax.rem(h, 2), lax.rem(b, 2)
    x_dev = (b, h, 1 - w)
    c_dev = (b, h + 1 - 2 * c, w)
    y_dev = (b + 1 - 2 * bp, h, w)

    def z_dev(k):
        zz = lax.rem(z + k, nz)
        return zz, (b, 2 * zz + c, w)

    own, other = at(w, cw), at(1 - w, cw)
    mine, theirs = at(w, half), at(1 - w, half)
    lanes = at(c, half)
    ends = [
        r.lens[0, 0],
        r.lens[0, 0] + r.lens[0, 1],
        r.lens[0, 0] + r.lens[0, 1] + r.lens[0, 2],
    ]
    sends = Sends()

    barrier = pltpu.get_barrier_semaphore()
    count = 0
    for dw in range(2):
        for dh in range(nh):
            if dh or dw:
                dev = (b, lax.rem(h + dh, nh), lax.rem(w + dw, 2))
                pl.semaphore_signal(barrier, inc=1, device_id=dev, device_id_type=MESH)
                count += 1
    for db in range(1, nb):
        dev = (lax.rem(b + db, nb), h, w)
        pl.semaphore_signal(barrier, inc=1, device_id=dev, device_id_type=MESH)
        count += 1
    pl.semaphore_wait(barrier, count)

    for i, vec in enumerate((r.v0, r.v1, r.v2, r.v3, r.v4, r.v5)):
        r.vsrc[i : i + 1, :] = vec[...]
    vcopy = remote(r.vsrc, r.vecf.at[:, own], r.xs.at[0], r.xr.at[0], x_dev)
    sends.start(vcopy)
    tcopies = []
    for k in range(2):
        part = pl.ds(k * half, half)
        copy = remote(r.tok.at[part], r.tokf.at[part, own], r.xs.at[1 + k], r.xr.at[1 + k], x_dev)
        sends.start(copy)
        tcopies.append(copy)
    r.wup[z, c, w] = r.wu[...]
    r.wdn[z, c, w] = r.wd[...]

    def weight_hop(k, ending=False):
        for kind, buf in enumerate((r.wup, r.wdn)):
            for way, step in enumerate((1, -1)):
                zz = z - step * (k - 1)
                onward = (z + step >= 0) & (z + step < nz)
                here = (zz >= 0) & (zz < nz) & (bp == kind)
                here = here & (jnp.logical_not(onward) if ending else onward)
                index = jnp.clip(zz, 0, nz - 1)
                block = buf.at[index, c, w]
                if k > 1:

                    @pl.when(here)
                    def _(block=block, index=index):
                        await_copy(block, r.wzr.at[index])

                if not ending:
                    dev = (b, 2 * jnp.clip(z + step, 0, nz - 1) + c, w)
                    copy = remote(block, block, r.wzs.at[way, k], r.wzr.at[index], dev)
                    sends.start_if(here, copy)
                if k > 1:
                    copy = remote(block, block, r.wxs.at[way, k - 1], r.wxr.at[index], x_dev)
                    sends.start_if(here, copy)
                    copy = remote(block, block, r.wys.at[way, k - 1], r.wyr.at[index, w], y_dev)
                    sends.start_if(here, copy)

    for kind, buf in enumerate((r.wup, r.wdn)):
        block = buf.at[z, c, w]
        sends.start_if(bp == kind, remote(block, block, r.wxs.at[0, 0], r.wxr.at[z], x_dev))
    weight_hop(1)
    gates = ((r.wg1, r.g1f), (r.wg2, r.g2f), (r.wo, r.wof))
    for i, (src, dst) in enumerate(gates):
        piece = at(c, src.shape[0] // 2)
        sends.start(remote(src.at[piece], dst.at[w, piece], r.gxs.at[i], r.gxr.at[i], x_dev))
        dst[w] = src[...]
    ccopy = remote(r.cot.at[theirs], r.cotr.at[:, own], r.xs.at[3], r.xr.at[3], x_dev)
    r.vecf[:, own] = r.vsrc[...]
    r.tokf[:, own] = r.tok[...]
    r.cotr[:, own] = r.cot[mine, :]

    for i, weight in enumerate((r.wq, r.wk, r.wv)):
        turned = flip(weight[...])
        for t in range(heads):
            r.wt[t, i * HD : (i + 1) * HD, :] = turned[t * HD : (t + 1) * HD]

    vcopy.wait_recv()
    gain, shift = r.vecf[0:1, :], r.vecf[1:2, :]

    def project(k):
        part = slice(k * half, (k + 1) * half)
        tcopies[k].wait_recv()
        x = r.tokf[part, :].astype(F32)
        centre = x - jnp.mean(x, -1, keepdims=True)
        spread = jnp.mean(centre * centre, -1, keepdims=True)
        n = (centre * lax.rsqrt(spread + EPSILON) * gain + shift).astype(BF16)
        r.npair[c, part, :] = n
        for t in range(heads):
            qkv = nt(r.wt[t], n).astype(BF16)
            r.qsrc[t, :, part] = qkv[:HD]
            r.kvsrc[t, :, part] = qkv[HD:]

    def send_heads(step, k):
        t = lax.rem(group + step, heads)
        span = pl.ds(k * half, half)
        src, dst = r.kvsrc.at[t, :, span], r.kvt.at[h, :, span]
        if step:
            dev = (b, t * dph + sub, w)
            sends.start(remote(src, dst, r.ks.at[step, k], r.kr.at[h, k], dev))
        else:
            pltpu.make_async_copy(src, dst, r.kr.at[h, k]).start()
        for i in range(per):
            row = k * per + i
            target = sub_row(h, row, dph)
            src, dst = r.qsrc.at[t, :, pl.ds(row * tq, tq)], r.qt.at[h]
            copy = remote(src, dst, r.qs.at[step, row], r.qr.at[h], (b, t * dph + target, w))
            if step:
                sends.start(copy)
            else:
                sends.start_if(target != sub, copy)

                @pl.when(target == sub)
                def _(src=src, dst=dst):
                    pltpu.make_async_copy(src, dst, r.qr.at[h]).start()

    weight_hop(2)
    project(0)
    send_heads(heads - 1, 0)
    weight_hop(3)
    project(1)
    send_heads(heads - 1, 1)
    for step in range(heads - 2, -1, -1):
        for k in range(2):
            send_heads(step, k)


    def weights_over_y():
        for kind, buf in enumerate((r.wup, r.wdn)):

            @pl.when(bp == kind)
            def _(buf=buf):
                for k in range(nz):
                    zz, _ = z_dev(k)
                    block = buf.at[zz, c, 1 - w]
                    await_copy(block, r.wxr.at[zz])
                    remote(block, block, r.wyd.at[zz], r.wyr.at[zz, 1 - w], y_dev).start()

    def weights_over_core():
        for kind, buf in enumerate((r.wup, r.wdn)):

            @pl.when(bp != kind)
            def _(buf=buf):
                for k in range(nz):
                    zz, _ = z_dev(k)
                    if k:
                        await_copy(buf.at[zz, c, w], r.wyr.at[zz, w])
                    await_copy(buf.at[zz, c, 1 - w], r.wyr.at[zz, 1 - w])

            block = buf.at[:, c]
            sends.start(remote(block, block, r.wcs.at[kind], r.wcr.at[kind], c_dev))

    def gates_over_core():
        for i, (src, dst) in enumerate(gates):
            piece = dst.at[1 - w, at(c, src.shape[0] // 2)]
            await_copy(piece, r.gxr.at[i])
            remote(piece, piece, r.gcs.at[i], r.gcr.at[i], c_dev).start()

    def weights_sent():
        for kind, buf in enumerate((r.wup, r.wdn)):

            @pl.when(bp == kind)
            def _(buf=buf):
                for k in range(nz):
                    await_copy(buf.at[z, c, w], r.wyd.at[k])

        for i, (src, dst) in enumerate(gates):
            await_copy(dst.at[1 - w, at(c, src.shape[0] // 2)], r.gcs.at[i])

    def pass_on(s):
        @pl.when(lax.rem(s, dph) == sub)
        def _():
            for k in range(2):
                await_copy(r.kvt.at[s, :, pl.ds(k * half, half)], r.kr.at[s, k])
            for k in range(1, dph):
                dev = (b, group * dph + lax.rem(sub + k, dph), w)
                remote(r.kvt.at[s], r.kvt.at[s], r.fs.at[s, k], r.fr.at[s], dev).start()

    def arrive(s):
        @pl.when(lax.rem(s, dph) != sub)
        def _():
            await_copy(r.kvt.at[s], r.fr.at[s])

        r.kvn[s] = flip(r.kvt[s])
        await_copy(r.qt.at[s], r.qr.at[s])
        q = r.qt[s].astype(F32) * SCALE
        r.qlow[s] = jnp.concatenate([q, jnp.zeros_like(q)], 0).astype(BF16)

    def masked(scores, i, j):
        query_base = i * rows + sub_row(i, sub, dph) * tq
        return jnp.where(allowed_mask(j * rows, query_base, rows, tq, ends), scores, NEG)

    def bias(scores, j):
        key_pos = j * rows + lax.broadcasted_iota(jnp.int32, (rows, 1), 0)
        return scores + jnp.where(key_pos < ends[0], NEG, 0.0)

    def absorb(i, blocks):
        top = r.top[i]
        new_top = top
        for scores, _ in blocks:
            new_top = jnp.maximum(new_top, jnp.max(scores, 0, keepdims=True))
        fade = jnp.exp(top - new_top)
        total, mixed = r.total[i] * fade, r.ot[i] * fade
        for scores, j in blocks:
            weights = jnp.exp(scores - new_top)
            total = total + jnp.sum(weights, 0, keepdims=True)
            mixed = mixed + nn(r.kvt[j, HD:, :], weights.astype(BF16))
        r.top[i], r.total[i], r.ot[i] = new_top, total, mixed

    def send_attended(s):
        row = sub_row(s, sub, dph)
        total = r.total[s]
        mixed = r.ot[s] / total
        r.ot[s] = mixed
        r.lse[s] = r.top[s] + jnp.log(total)
        r.osend[s] = mixed.astype(BF16)
        row_w = lax.div(row * tq, half)
        lane = lax.rem(row * tq, half)
        dst = r.att.at[at(w * heads + group, HD), pl.ds(pl.multiple_of(lane, tq), tq)]
        slot = r.orc.at[w * heads + group, lax.div(lane, tq)]
        here = (s == h) & (row_w == w)

        @pl.when(here)
        def _():
            pltpu.make_async_copy(r.osend.at[s], dst, slot).start()

        @pl.when(jnp.logical_not(here))
        def _():
            remote(r.osend.at[s], dst, r.osd.at[s], slot, (b, s, row_w)).start()

    def own_chip(n):
        i = 2 * n
        first = masked(nn(r.kvn[i], r.qlow[i]), i, i)
        low = masked(nn(r.kvn[i], r.qlow[i + 1]), i + 1, i)
        high = masked(nn(r.kvn[i + 1], r.qlow[i + 1]), i + 1, i + 1)
        absorb(i, [(first, i)])
        absorb(i + 1, [(low, i), (high, i + 1)])

    def two_chips(hi, lo, last):
        queries, keys = (2 * hi, 2 * hi + 1), (2 * lo, 2 * lo + 1)
        scores = [[nn(r.kvn[j], r.qlow[i]) for j in keys] for i in queries]
        for a, i in enumerate(queries):
            if last and a:
                blocks = [(masked(x, i, j), j) for x, j in zip(scores[a], keys)]
            else:
                blocks = [(bias(scores[a][0], keys[0]), keys[0]), (scores[a][1], keys[1])]
            absorb(i, blocks)

    def completes(chip):
        return jnp.where(z == 0, chip, nz - z + jnp.minimum(chip, z - 1))

    def forward_stage(d, _):
        n = lax.rem(z + d, nz)

        @pl.when(d == nz // 2)
        def _():
            weights_over_y()
            gates_over_core()

        pass_on(2 * n)
        pass_on(2 * n + 1)
        arrive(2 * n)
        arrive(2 * n + 1)
        own_chip(n)

        def with_earlier(e, _):
            m = lax.rem(z + e, nz)
            hi, lo = jnp.maximum(n, m), jnp.minimum(n, m)

            @pl.when(hi == nz - 1)
            def _():
                two_chips(hi, lo, True)

            @pl.when(hi != nz - 1)
            def _():
                two_chips(hi, lo, False)

            @pl.when((m > n) & (completes(m) == d))
            def _():
                send_attended(2 * m)
                send_attended(2 * m + 1)

            return 0

        lax.fori_loop(0, d, with_earlier, 0)

        @pl.when(completes(n) == d)
        def _():
            send_attended(2 * n)
            send_attended(2 * n + 1)

        return 0

    r.top[...] = jnp.full_like(r.top, NEG)
    r.total[...] = jnp.zeros_like(r.total)
    r.ot[...] = jnp.zeros_like(r.ot)
    forward_stage(0, 0)
    sends.start(remote(r.npair.at[c], r.npair.at[c], r.cs.at[0], r.cr.at[0], c_dev))
    for k in range(4, nz):
        weight_hop(k)
    for k in range(2, nz + 1):
        weight_hop(k, ending=True)
    sends.start(ccopy)
    lax.fori_loop(1, nz, forward_stage, 0)
    weights_over_core()

    for i, (src, dst) in enumerate(gates):
        await_copy(dst.at[1 - w, at(1 - c, src.shape[0] // 2)], r.gcr.at[i])

    def two(a, weight):
        return jnp.concatenate([nn(a, weight[0]), nn(a, weight[1])], 1)

    def two_back(g, weight):
        return nt(g[:, :cw], weight[0]) + nt(g[:, cw:], weight[1])

    tok = r.tokf[mine, :].astype(F32)
    n1 = r.npair[c, mine, :]
    gate_one = sigmoid(two(n1, r.g1f) + r.vecf[2:3, :])
    for g in range(2 * heads):
        for i in range(per):
            await_copy(r.att.at[pl.ds(g * HD, HD), pl.ds(i * tq, tq)], r.orc.at[g, i])
    wof = r.wof[...].reshape(wide, wide)
    branch_one = nn(flip(r.att[...]), wof)
    middle = tok + gate_one * (branch_one - tok)
    centre = middle - jnp.mean(middle, -1, keepdims=True)
    rstd = lax.rsqrt(jnp.mean(centre * centre, -1, keepdims=True) + EPSILON)
    n2 = centre * rstd
    gain_two = r.vecf[3:4, :]
    normed_two = (n2 * gain_two + r.vecf[4:5, :]).astype(BF16)
    gate_two = sigmoid(two(normed_two, r.g2f) + r.vecf[5:6, :])
    for kind, buf in enumerate((r.wup, r.wdn)):
        await_copy(buf.at[:, 1 - c], r.wcr.at[kind])

    def units_of(i2, p):
        return i2, lax.rem(c + p, 2)

    def up(i2, branch):
        for p in range(2):
            i, q = units_of(i2, p)
            pre = nn(normed_two, r.wup[i, q].reshape(wide, units))
            r.pre[i2, p] = pre
            act = jax.nn.gelu(pre).astype(BF16)
            branch = branch + jnp.concatenate([nn(act, r.wdn[i, q, 0]), nn(act, r.wdn[i, q, 1])], 1)
            if p:
                r.acts[i2] = act
                dst = r.actp.at[i2, lanes, :]
                remote(r.acts.at[i2], dst, r.as_.at[i2], r.ar.at[i2], c_dev).start()
            else:
                r.actp[i2, lanes, :] = act
        return branch

    branch_two = lax.fori_loop(0, nz, up, jnp.zeros(middle.shape, F32))
    delta = branch_two - middle
    r.outr[...] = (middle + gate_two * delta).astype(BF16)
    ocopy = remote(r.outr.at[:, other], r.out_c.at[mine, :], r.xs.at[4], r.xr.at[4], x_dev)
    sends.start(ocopy)
    ccopy.wait_recv()
    grad = r.cotr[...].astype(F32)
    gb2 = (grad * gate_two).astype(BF16)
    gl2 = (grad * delta * gate_two * (1.0 - gate_two)).astype(BF16)
    gmid = grad * (1.0 - gate_two)

    def down(i2, total):
        for p in range(2):
            i, q = units_of(i2, p)
            ghid = nt(gb2[:, :cw], r.wdn[i, q, 0]) + nt(gb2[:, cw:], r.wdn[i, q, 1])
            pre = r.pre[i2, p]
            k = 0.7978845608028654
            t = jnp.tanh(k * (pre + 0.044715 * pre * pre * pre))
            slope = 0.5 * (1.0 + t) + 0.5 * pre * (1.0 - t * t) * (k * (1.0 + 3 * 0.044715 * pre * pre))
            gpre = (ghid * slope).astype(BF16)
            total = total + nt(gpre, r.wup[i, q].reshape(wide, units))
            if p:
                r.gpres[i2] = gpre
                dst = r.gprep.at[i2, lanes, :]
                remote(r.gpres.at[i2], dst, r.ps_.at[i2], r.pr.at[i2], c_dev).start()
            else:
                r.gprep[i2, lanes, :] = gpre
        return total

    gnorm = lax.fori_loop(0, nz, down, two_back(gl2, r.g2f))
    e = gnorm * gain_two
    gmid = gmid + rstd * (
        e - jnp.mean(e, -1, keepdims=True) - n2 * jnp.mean(e * n2, -1, keepdims=True)
    )
    gb1 = (gmid * gate_one).astype(BF16)
    r.gatt[...] = nt(wof, gb1).astype(BF16)
    for dw in (1, 0):
        wt = lax.rem(w + dw, 2)
        for step in range(heads - 1, -1, -1):
            t = lax.rem(group + step, heads)
            for i in range(per):
                target = sub_row(h, w * per + i, dph)
                src = r.gatt.at[at(wt * heads + t, HD), pl.ds(i * tq, tq)]
                dst = r.dot.at[h]
                dev = (b, t * dph + target, wt)
                copy = remote(src, dst, r.ds.at[dw, step, i], r.dr.at[h], dev)
                if step or dw:
                    sends.start(copy)
                else:
                    sends.start_if(target != sub, copy)

                    @pl.when(target == sub)
                    def _(src=src, dst=dst):
                        pltpu.make_async_copy(src, dst, r.dr.at[h]).start()

    gl1 = (gmid * (branch_one - tok) * gate_one * (1.0 - gate_one)).astype(BF16)
    r.ginp[...] = gmid * (1.0 - gate_one)
    r.npt[:, lanes] = flip(normed_two)
    sends.start(remote(r.npt.at[:, lanes], r.npt.at[:, lanes], r.cs.at[1], r.cr.at[1], c_dev))
    r.gbt[:, lanes] = flip(gb2)
    sends.start(remote(r.gbt.at[:, lanes], r.gbt.at[:, lanes], r.cs.at[2], r.cr.at[2], c_dev))
    quarter = half // 2
    r.lsrc[0] = r.att[...]
    r.lsrc[1] = flip(gl1)
    r.lsrc[2] = flip(gl2)
    for m, right in enumerate((gb1, n1, normed_two)):
        r.bpair[m, lanes, :] = right
        block = r.bpair.at[m, lanes, :]
        sends.start(remote(block, block, r.cs.at[3 + m], r.cr.at[3 + m], c_dev))
        for v in range(2):
            src = r.lsrc.at[m, at(2 * v + 1 - c, quarter), :]
            dst = r.apair.at[m, v, :, lanes]
            sends.start(remote(src, dst, r.cs.at[6 + 2 * m + v], r.cr.at[6 + 2 * m + v], c_dev))
            r.apair[m, v, :, lanes] = r.lsrc[m, at(2 * v + c, quarter), :]
    r.gterm[...] = two_back(gl1, r.g1f)
    r.vsum[...] = jnp.zeros_like(r.vsum)
    r.vsum[2:3, :] = jnp.sum(gl1.astype(F32), 0, keepdims=True)
    r.vsum[3:4, :] = jnp.sum(gnorm * n2, 0, keepdims=True)
    r.vsum[4:5, :] = jnp.sum(gnorm, 0, keepdims=True)
    r.vsum[5:6, :] = jnp.sum(gl2.astype(F32), 0, keepdims=True)
    r.out_c[mine, :] = r.outr[:, own]

    eighth = quarter // 2
    for m in range(3):
        await_copy(r.bpair.at[m, lanes, :], r.cr.at[3 + m])
        for v in range(2):
            await_copy(r.apair.at[m, v, :, lanes], r.cr.at[6 + 2 * m + v])
            block = nn(r.apair[m, v], r.bpair[m]).astype(BF16)
            for y in range(2):
                r.gb[v, y, m] = block[y * eighth : (y + 1) * eighth]
    for m in range(3):
        sends.start(remote(r.gb.at[1 - w, :, m], r.xbin.at[:, m], r.sxs.at[m], r.sxr.at[m], x_dev))
    await_copy(r.npt.at[:, lanes], r.cr.at[1])
    await_copy(r.gbt.at[:, lanes], r.cr.at[2])

    def weight_grads(i2, _):
        await_copy(r.gprep.at[i2, lanes, :], r.pr.at[i2])
        await_copy(r.actp.at[i2, lanes, :], r.ar.at[i2])
        r.ga[0, i2] = nn(r.npt[...], r.gprep[i2]).astype(BF16).reshape(2, 2, quarter, units)
        r.ga[1, i2] = nn(r.gbt[...], r.actp[i2]).astype(BF16).reshape(2, 2, quarter, units)
        return 0

    lax.fori_loop(0, nz, weight_grads, 0)
    sends.start(remote(r.ga.at[0, :, 1 - w], r.xin0, r.xs.at[5], r.xr.at[5], x_dev))
    sends.start(remote(r.ga.at[1, :, :, 1 - bp], r.yin1, r.ys.at[1], r.yr.at[1], y_dev))


    def ffn_second():
        await_copy(r.xin0, r.xr.at[5])
        r.ga[0, :, w] = (r.ga[0, :, w].astype(F32) + r.xin0[...].astype(F32)).astype(BF16)
        remote(r.ga.at[0, :, w, 1 - bp], r.yin0, r.ys.at[2], r.yr.at[2], y_dev).start()
        await_copy(r.yin1, r.yr.at[1])
        r.ga[1, :, :, bp] = (r.ga[1, :, :, bp].astype(F32) + r.yin1[...].astype(F32)).astype(BF16)
        remote(r.ga.at[1, :, 1 - w, bp], r.xin1, r.xs.at[6], r.xr.at[6], x_dev).start()

    def ffn_third():
        await_copy(r.yin0, r.yr.at[2])
        await_copy(r.xin1, r.xr.at[6])
        r.zs[:, 0] = (r.ga[0, :, w, bp].astype(F32) + r.yin0[...].astype(F32)).astype(BF16)
        r.zs[:, 1] = (r.ga[1, :, w, bp].astype(F32) + r.xin1[...].astype(F32)).astype(BF16)
        ffn_hop(0)

    def z_block(q, flip_bit, v):
        bit = lax.rem(lax.div(z, 1 << q), 2)
        bit = 1 - bit if flip_bit else bit
        return lax.rem(z, 1 << q) + bit * (1 << q) + v * (2 << q)

    def ffn_hop(q):
        if q:
            ffn_add(q - 1)
        bit = lax.rem(lax.div(z, 1 << q), 2)
        dev = (b, 2 * (z + (1 << q) * (1 - 2 * bit)) + c, w)
        for v in range(nz >> (q + 1)):
            slot = nz - (nz >> q) + v
            remote(r.zs.at[z_block(q, True, v)], r.zin.at[slot], r.zss.at[slot], r.zsr.at[slot], dev).start()

    def ffn_add(q):
        for v in range(nz >> (q + 1)):
            slot = nz - (nz >> q) + v
            await_copy(r.zin.at[slot], r.zsr.at[slot])
            kept = z_block(q, False, v)
            r.zs[kept] = (r.zs[kept].astype(F32) + r.zin[slot].astype(F32)).astype(BF16)

    def ffn_fourth():
        ffn_add(hops - 1)
        total = r.zs[z].astype(F32)
        if pairs > 1:
            mypair = lax.div(b, 2)
            r.pin[mypair] = total.astype(BF16)
            for k in range(1, pairs):
                dev = (lax.rem(b + 2 * k, nb), h, w)
                block = r.pin.at[mypair]
                sends.start(remote(block, block, r.pas.at[k], r.par.at[mypair], dev))
            for k in range(1, pairs):
                pp = lax.rem(mypair + k, pairs)
                await_copy(r.pin.at[pp], r.par.at[pp])
            total = r.pin[0].astype(F32)
            for k in range(1, pairs):
                total = total + r.pin[k].astype(F32)
        r.red_a[bp] = total.astype(BF16)
        block = r.red_a.at[bp]
        sends.start(remote(block, block, r.ys.at[3], r.yr.at[3], y_dev))

    def ffn_sent():
        await_copy(r.yin0, r.ys.at[2])
        await_copy(r.xin1, r.xs.at[6])
        for k in range(nz - 1):
            await_copy(r.zin.at[k], r.zss.at[k])

    zr = HD * 4 // nz

    def z_part(zz):
        return pl.ds(pl.multiple_of(lax.div(zz, 4) * zr, zr), zr), at(lax.rem(zz, 4), 128)

    def square_y(which):
        for p in range(3):
            if which == 0:
                await_copy(r.xbin.at[:, p], r.sxr.at[p])
                r.gb[w, :, p] = (r.gb[w, :, p].astype(F32) + r.xbin[:, p].astype(F32)).astype(BF16)
                src = r.gb.at[w, 1 - bp, p]
            else:
                src = r.gc.at[1 - bp, p]
            remote(src, r.yin.at[which, p], r.sys.at[which, p], r.syr.at[which, p], y_dev).start()

    def square_z(which):
        for p in range(3):
            await_copy(r.yin.at[which, p], r.syr.at[which, p])
            mine_part = r.gb[w, bp, p] if which == 0 else r.gc[bp, p]
            r.sq[which, p] = (mine_part.astype(F32) + r.yin[which, p].astype(F32)).astype(BF16)
            for k in range(nz - 1, 0, -1):
                zz, dev = z_dev(k)
                src = r.sq.at[(which, p) + z_part(zz)]
                slot = r.sqin.at[which, p, z]
                remote(src, slot, r.sqs.at[which, p, k], r.sqr.at[which, p, z], dev).start()

    def square_spread(which):
        for p in range(3):
            r.sqin[which, p, z] = r.sq[(which, p) + z_part(z)]
            for k in range(1, nz):
                zz, _ = z_dev(k)
                await_copy(r.sqin.at[which, p, zz], r.sqr.at[which, p, zz])
            total = r.sqin[which, p, 0].astype(F32)
            for k in range(1, nz):
                total = total + r.sqin[which, p, k].astype(F32)
            if pairs > 1:
                mypair = lax.div(b, 2)
                r.sqpair[which, p, mypair] = total.astype(BF16)
                for k in range(1, pairs):
                    dev = (lax.rem(b + 2 * k, nb), h, w)
                    block = r.sqpair.at[which, p, mypair]
                    remote(block, block, r.sqps.at[which, p, k], r.sqpr.at[which, p, mypair], dev).start()
                for k in range(1, pairs):
                    pp = lax.rem(mypair + k, pairs)
                    await_copy(r.sqpair.at[which, p, pp], r.sqpr.at[which, p, pp])
                total = r.sqpair[which, p, 0].astype(F32)
                for k in range(1, pairs):
                    total = total + r.sqpair[which, p, k].astype(F32)
            r.red_s[(which, c, bp, p) + z_part(z)] = total.astype(BF16)
            for k in range(nz - 1, 0, -1):
                _, dev = z_dev(k)
                block = r.red_s.at[(which, c, bp, p) + z_part(z)]
                remote(block, block, r.sgs.at[which, p, k], r.sgr.at[which, p, z], dev).start()

    def square_back(which):
        for p in range(3):
            for k in range(1, nz):
                zz, _ = z_dev(k)
                await_copy(r.red_s.at[(which, c, bp, p) + z_part(zz)], r.sgr.at[which, p, zz])
            block = r.red_s.at[which, c, bp, p]
            remote(block, block, r.sbs.at[which, p], r.sbr.at[which, p], y_dev).start()

    def square_core(which):
        for p in range(3):
            await_copy(r.red_s.at[which, c, 1 - bp, p], r.sbr.at[which, p])
            block = r.red_s.at[which, c, :, p]
            remote(block, block, r.scs.at[which, p], r.scr.at[which, p], c_dev).start()

    def square_end(which):
        for p in range(3):
            await_copy(r.red_s.at[which, 1 - c, :, p], r.scr.at[which, p])
            await_copy(r.red_s.at[which, c, :, p], r.scs.at[which, p])
            await_copy(r.yin.at[which, p], r.sys.at[which, p])
            await_copy(r.yin.at[which, p], r.sbs.at[which, p])
            for k in range(1, nz):
                await_copy(r.sqin.at[which, p, z], r.sqs.at[which, p, k])
                await_copy(r.sqin.at[which, p, z], r.sgs.at[which, p, k])
                if k < pairs:
                    await_copy(r.sqpair.at[which, p, 0], r.sqps.at[which, p, k])

    r.acc[...] = jnp.zeros_like(r.acc)

    def finish(s):
        @pl.when(lax.rem(s, dph) == sub)
        def _():
            total = r.acc[s]
            for k in range(1, dph):
                slot = r.pin_kv.at[lax.div(s, dph), k - 1]
                await_copy(slot, r.pkr.at[lax.div(s, dph), k - 1])
                total = total + r.pin_kv[lax.div(s, dph), k - 1]
            r.dkvsend[s, :HD] = (total[:HD] * SCALE).astype(BF16)
            r.dkvsend[s, HD:] = total[HD:].astype(BF16)
            dst = r.dqkv.at[group, pl.ds(HD, 2 * HD), :]

            @pl.when(s == h)
            def _():
                pltpu.make_async_copy(r.dkvsend.at[s], dst, r.dkr.at[group]).start()

            @pl.when(s != h)
            def _():
                remote(r.dkvsend.at[s], dst, r.dks.at[s], r.dkr.at[group], (b, s, w)).start()

    def pairs_backward(where, full):
        scores = [nn(r.kvn[j], r.qlow[i]) for i, j in where]
        gprobs = [nn(r.kvn[j], r.dhigh[i]) for i, j in where]
        for x, gp, (i, j), whole in zip(scores, gprobs, where, full):
            x = masked(x, i, j) if whole else bias(x, j)
            probs = jnp.exp(x - r.lse[i])
            gscores = (probs * (gp - r.centre[i])).astype(BF16)
            r.acc[j, HD:, :] += nt(r.dhigh[i, HD:, :], probs.astype(BF16))
            r.acc[j, :HD, :] += nt(r.qt[i], gscores)
            r.dqa[i] += nn(r.kvt[j, :HD, :], gscores)

    def choose(kinds, where):
        taken = False
        for cond, full in kinds:

            @pl.when(jnp.logical_and(cond, jnp.logical_not(taken)))
            def _(full=full):
                pairs_backward(where, full)

            taken = jnp.logical_or(taken, cond)

    def pair_at(t, u):
        lo, hi = t, nh - 1 - t
        n = hi - lo + 1
        return jnp.where(u < n, hi, lo + u - n), jnp.where(u < n, lo + u, lo)

    def out_arrives(s):
        await_copy(r.dot.at[s], r.dr.at[s])
        dout = r.dot[s]
        r.dhigh[s] = jnp.concatenate([jnp.zeros((HD, tq), BF16), dout], 0)
        r.centre[s] = jnp.sum(r.ot[s] * dout.astype(F32), 0, keepdims=True)

    def send_block(s):
        row = sub_row(s, sub, dph)
        r.dqsend[s] = (r.dqa[s] * SCALE).astype(BF16)
        dst = r.dqkv.at[group, pl.ds(0, HD), pl.ds(pl.multiple_of(row * tq, tq), tq)]

        @pl.when(s == h)
        def _():
            pltpu.make_async_copy(r.dqsend.at[s], dst, r.dqr.at[group, row]).start()

        @pl.when(s != h)
        def _():
            remote(r.dqsend.at[s], dst, r.dqs.at[s], r.dqr.at[group, row], (b, s, w)).start()

        owner = lax.rem(s, dph)

        @pl.when(owner != sub)
        def _():
            k = lax.rem(sub - owner + dph, dph)
            dev = (b, group * dph + owner, w)
            slot = lax.div(s, dph)
            remote(r.acc.at[s], r.pin_kv.at[slot, k - 1], r.pks.at[s], r.pkr.at[slot, k - 1], dev).start()

    def round_backward(t, _):
        lo, hi = t, nh - 1 - t
        n = hi - lo + 1

        def row_step(v, _):
            where = [pair_at(t, 2 * v), pair_at(t, 2 * v + 1)]
            diagonal = v == lax.div(n, 2) - 1
            choose([(t == 0, (True, True)), (diagonal, (False, True)), (True, (False, False))], where)
            return 0

        lax.fori_loop(0, lax.div(n, 2), row_step, 0)
        send_block(hi)

        @pl.when(t == 0)
        def _():
            lax.fori_loop(0, nh - 1, lambda s, z: (out_arrives(s), z)[1], 0)

        @pl.when(t > 0)
        def _():
            finish(lo - 1)

        def column_step(v, _):
            where = [pair_at(t, n + 2 * v), pair_at(t, n + 2 * v + 1)]
            choose([(v == 0, (True, False)), (True, (False, False))], where)
            return 0

        lax.fori_loop(0, lax.div(n, 2) - 1, column_step, 0)
        pairs_backward([pair_at(t, 2 * n - 2)], (True,))
        send_block(lo)
        finish(hi)

        @pl.when(t == 0)
        def _():
            square_y(0)

        @pl.when(t == nh // 8)
        def _():
            square_z(0)

        @pl.when(t == nh // 4)
        def _():
            ffn_second()

        return 0

    r.dqa[...] = jnp.zeros_like(r.dqa)
    out_arrives(nh - 1)
    lax.fori_loop(0, nh // 2, round_backward, 0)
    finish(nh // 2 - 1)
    ffn_third()
    square_spread(0)

    for t in range(heads):
        await_copy(r.dqkv.at[t, pl.ds(HD, 2 * HD), :], r.dkr.at[t])
        for i in range(dph):
            await_copy(r.dqkv.at[t, pl.ds(0, HD), pl.ds(i * tq, tq)], r.dqr.at[t, i])
        sends.start_if(
            t % 2 != c, remote(r.dqkv.at[t], r.dsib.at[t // 2], r.ts.at[t], r.tr.at[t // 2], c_dev)
        )
    wts = r.wt[...].reshape(heads * 3 * HD, wide)

    def grad_normed(span):
        return nn(flip(r.dqkv[:, :, span].reshape(heads * 3 * HD, half)), wts)

    r.psend[...] = grad_normed(theirs).astype(BF16)
    pcopy = remote(r.psend, r.precv, r.xs.at[8], r.xr.at[8], x_dev)
    sends.start(pcopy)
    await_copy(r.npair.at[1 - c], r.cr.at[0])
    for j in range(heads // 2):
        await_copy(r.dsib.at[j], r.tr.at[j])
        part = nn(r.dqkv[2 * j + c], r.npair[c]) + nn(r.dsib[j], r.npair[1 - c])
        for p in range(3):
            r.gc[j, p] = part[p * HD : (p + 1) * HD].astype(BF16)
    square_y(1)
    for q in range(1, hops):
        ffn_hop(q)
    gnorm = grad_normed(mine) + r.gterm[...]
    x = r.tokf[mine, :].astype(F32)
    centre = x - jnp.mean(x, -1, keepdims=True)
    rstd = lax.rsqrt(jnp.mean(centre * centre, -1, keepdims=True) + EPSILON)
    n = centre * rstd
    square_z(1)
    pcopy.wait_recv()
    gnorm = gnorm + r.precv[...].astype(F32)
    e = gnorm * r.vecf[0:1, :]
    result = r.ginp[...] + rstd * (
        e - jnp.mean(e, -1, keepdims=True) - n * jnp.mean(e * n, -1, keepdims=True)
    )
    r.tsend[...] = result.astype(BF16)
    tcopy = remote(r.tsend.at[:, other], r.trecv, r.xs.at[9], r.xr.at[9], x_dev)
    sends.start(tcopy)
    r.vsum[0:1, :] = jnp.sum(gnorm * n, 0, keepdims=True)
    r.vsum[1:2, :] = jnp.sum(gnorm, 0, keepdims=True)
    me4 = 2 * c + w
    r.vin4[me4] = r.vsum[...]
    k = 0
    for dc in range(2):
        for dw in range(2):
            if dc or dw:
                cc, ww = lax.rem(c + dc, 2), lax.rem(w + dw, 2)
                dev = (b, 2 * z + cc, ww)
                sends.start(remote(r.vin4.at[me4], r.vin4.at[me4], r.v4s.at[k], r.v4r.at[me4], dev))
                k += 1
    r.gtok[mine, :] = jnp.where(w == 0, result[:, :cw], result[:, cw:])
    square_back(0)
    for dc in range(2):
        for dw in range(2):
            if dc or dw:
                peer = 2 * lax.rem(c + dc, 2) + lax.rem(w + dw, 2)
                await_copy(r.vin4.at[peer], r.v4r.at[peer])
    r.vinz[z] = r.vin4[0] + r.vin4[1] + r.vin4[2] + r.vin4[3]
    for k in range(1, nz):
        _, dev = z_dev(k)
        sends.start(remote(r.vinz.at[z], r.vinz.at[z], r.vzs.at[k], r.vzr.at[z], dev))
    square_spread(1)
    ffn_fourth()
    tcopy.wait_recv()
    r.gtok[theirs, :] = r.trecv[...].astype(F32)
    ocopy.wait_recv()
    for k in range(1, nz):
        zz, _ = z_dev(k)
        await_copy(r.vinz.at[zz], r.vzr.at[zz])
    total = r.vinz[0]
    for k in range(1, nz):
        total = total + r.vinz[k]
    r.vinb[b] = total
    for k in range(1, nb):
        dev = (lax.rem(b + k, nb), h, w)
        sends.start(remote(r.vinb.at[b], r.vinb.at[b], r.vbs.at[k], r.vbr.at[b], dev))
    square_core(0)
    square_back(1)
    for k in range(1, nb):
        bb = lax.rem(b + k, nb)
        await_copy(r.vinb.at[bb], r.vbr.at[bb])
    total = r.vinb[0]
    for k in range(1, nb):
        total = total + r.vinb[k]
    r.red_v[...] = jnp.where(w == 0, total[:, :cw], total[:, cw:])
    await_copy(r.red_a.at[1 - bp], r.yr.at[3])
    square_core(1)

    def sent(s, _):
        row = sub_row(s, sub, dph)
        here = (s == h) & (lax.div(row * tq, half) == w)

        @pl.when(jnp.logical_not(here))
        def _():
            await_copy(r.osend.at[s], r.osd.at[s])

        @pl.when(lax.rem(s, dph) == sub)
        def _():
            for k in range(1, dph):
                await_copy(r.kvt.at[s], r.fs.at[s, k])

        @pl.when(s != h)
        def _():
            await_copy(r.dqsend.at[s], r.dqs.at[s])

        @pl.when((s != h) & (lax.rem(s, dph) == sub))
        def _():
            await_copy(r.dkvsend.at[s], r.dks.at[s])

        @pl.when(lax.rem(s, dph) != sub)
        def _():
            await_copy(r.acc.at[s], r.pks.at[s])

        return 0

    lax.fori_loop(0, nh, sent, 0)
    weights_sent()
    for i2 in range(nz):
        await_copy(r.acts.at[i2], r.as_.at[i2])
        await_copy(r.gpres.at[i2], r.ps_.at[i2])
    ffn_sent()
    sends.finish()
    square_end(0)
    square_end(1)


def final_kernel(heads, *refs):
    (
        out_c, gtok, red_a, red_s, red_v,
        o_out, o_tok, o_g1, o_b1, o_wq, o_wk, o_wv, o_wo, o_gw1, o_gb1, o_g2, o_b2, o_gw2, o_gb2, o_up, o_dn,
    ) = refs
    o_out[...] = out_c[...]
    o_tok[...] = gtok[...]
    for i, ref in enumerate((o_g1, o_b1, o_gb1, o_g2, o_b2, o_gb2)):
        ref[...] = red_v[i : i + 1, :]
    _, quarter, units = red_a.shape[1:]
    o_up[:quarter, :] = red_a[0, 0].astype(F32)
    o_up[quarter:, :] = red_a[1, 0].astype(F32)
    o_dn[:, :quarter] = red_a[0, 1].astype(F32).T
    o_dn[:, quarter:] = red_a[1, 1].astype(F32).T
    eighth = quarter // 2
    for core in range(2):
        for y in range(2):
            base = (2 * core + y) * eighth
            o_wo[base : base + eighth, :] = red_s[0, core, y, 0].astype(F32)
    for m, ref in ((1, o_gw1), (2, o_gw2)):
        full = [red_s[0, core, y, m] for core in range(2) for y in range(2)]
        ref[...] = jnp.concatenate(full, 0).astype(F32).T
    for i, ref in enumerate((o_wq, o_wk, o_wv)):
        full = []
        for t in range(heads):
            full.append(red_s[1, t % 2, t // 2, i])
        ref[...] = jnp.concatenate(full, 0).astype(F32).T


def local(
    tokens, ln1_gain, ln1_bias, w_query, w_key, w_value, w_out, gate1_weight, gate1_bias,
    ln2_gain, ln2_bias, gate2_weight, gate2_bias, w_up, w_down, lengths, cotangent,
):
    nb, nh = lax.axis_size("batch"), lax.axis_size("hidden")
    rows, cw = tokens.shape
    units = w_up.shape[1]
    heads = cw // HD
    dph = nh // heads
    tq, half, wide, nz, pairs = rows // dph, rows // 2, 2 * cw, nh // 2, nb // 2
    quarter = half // 2
    zr = HD * 4 // nz
    per = half // tq
    sizes = (nb, nh, rows, cw, units, heads, dph, tq)

    ins = dict(
        lens=lengths, tok=tokens, cot=cotangent, v0=ln1_gain[None], v1=ln1_bias[None], v2=gate1_bias[None],
        v3=ln2_gain[None], v4=ln2_bias[None], v5=gate2_bias[None], wq=w_query, wk=w_key, wv=w_value,
        wo=w_out, wg1=gate1_weight, wg2=gate2_weight, wu=w_up, wd=w_down,
    )
    outs = dict(
        out_c=((rows, cw), BF16),
        gtok=((rows, cw), F32),
        red_a=((2, 2, quarter, units), BF16),
        red_s=((2, 2, 2, 3, HD, wide), BF16),
        red_v=((8, cw), F32),
    )
    bufs = dict(
        vsrc=((8, cw), F32), vecf=((8, wide), F32), tokf=((rows, wide), BF16), cotr=((half, wide), BF16),
        g1f=((2, wide, cw), BF16), g2f=((2, wide, cw), BF16), wof=((2, cw, wide), BF16),
        wup=((nz, 2, 2, cw, units), BF16), wdn=((nz, 2, 2, units, cw), BF16),
        wt=((heads, 3 * HD, wide), BF16), npair=((2, rows, wide), BF16),
        qsrc=((heads, HD, rows), BF16), kvsrc=((heads, 2 * HD, rows), BF16),
        kvt=((nh, 2 * HD, rows), BF16), kvn=((nh, rows, 2 * HD), BF16), qt=((nh, HD, tq), BF16),
        qlow=((nh, 2 * HD, tq), BF16), dhigh=((nh, 2 * HD, tq), BF16), top=((nh, 1, tq), F32), total=((nh, 1, tq), F32),
        centre=((nh, 1, tq), F32), dqa=((nh, HD, tq), F32), ot=((nh, HD, tq), F32), lse=((nh, 1, tq), F32), osend=((nh, HD, tq), BF16),
        att=((2 * heads * HD, half), BF16),
        pre=((nz, 2, half, units), F32), acts=((nz, half, units), BF16), actp=((nz, rows, units), BF16),
        gpres=((nz, half, units), BF16), gprep=((nz, rows, units), BF16),
        outr=((half, wide), BF16), gatt=((wide, half), BF16), dot=((nh, HD, tq), BF16),
        ginp=((half, wide), F32), gterm=((half, wide), F32), npt=((wide, rows), BF16), gbt=((wide, rows), BF16),
        lsrc=((3, wide, half), BF16), bpair=((3, rows, wide), BF16), apair=((3, 2, quarter, rows), BF16),
        vsum=((8, wide), F32),
        gb=((2, 2, 3, HD, wide), BF16), xbin=((2, 3, HD, wide), BF16), yin=((2, 3, HD, wide), BF16),
        ga=((2, nz, 2, 2, quarter, units), BF16), xin0=((nz, 2, quarter, units), BF16),
        yin1=((nz, 2, quarter, units), BF16), yin0=((nz, quarter, units), BF16), xin1=((nz, quarter, units), BF16),
        zs=((nz, 2, quarter, units), BF16), zin=((nz, 2, quarter, units), BF16),
        pin=((pairs, 2, quarter, units), BF16),
        gc=((2, 3, HD, wide), BF16), sq=((2, 3, HD, wide), BF16),
        sqin=((2, 3, nz, zr, 128), BF16), sqpair=((2, 3, pairs, zr, 128), BF16),
        acc=((nh, 2 * HD, rows), F32), pin_kv=((nh // dph, max(dph - 1, 1), 2 * HD, rows), F32),
        dkvsend=((nh, 2 * HD, rows), BF16), dqsend=((nh, HD, tq), BF16),
        dqkv=((heads, 3 * HD, rows), BF16), dsib=((heads // 2, 3 * HD, rows), BF16),
        psend=((half, wide), BF16), precv=((half, wide), BF16),
        tsend=((half, wide), BF16), trecv=((half, cw), BF16),
        vin4=((4, 8, wide), F32), vinz=((nz, 8, wide), F32), vinb=((nb, 8, wide), F32),
    )
    sems = dict(
        xs=(10,), xr=(10,), wzs=(2, nz), wzr=(nz,), gxs=(3,), gxr=(3,), gcs=(3,), gcr=(3,),
        ks=(heads, 2), kr=(nh, 2), qs=(heads, dph), qr=(nh,), cs=(12,), cr=(12,),
        wxs=(2, nz), wxr=(nz,), wys=(2, nz), wyr=(nz, 2), wyd=(nz,), wcs=(2,), wcr=(2,),
        fs=(nh, dph), fr=(nh,), osd=(nh,), orc=(2 * heads, per),
        as_=(nz,), ar=(nz,), ps_=(nz,), pr=(nz,), ds=(2, heads, per), dr=(nh,),
        ys=(5,), yr=(5,), zss=(nz,), zsr=(nz,), pas=(pairs,), par=(pairs,),
        sqs=(2, 3, nz), sqr=(2, 3, nz), sqps=(2, 3, pairs), sqpr=(2, 3, pairs), sgs=(2, 3, nz), sgr=(2, 3, nz),
        sxs=(3,), sxr=(3,), sys=(2, 3), syr=(2, 3), sbs=(2, 3), sbr=(2, 3), scs=(2, 3), scr=(2, 3),
        pks=(nh,), pkr=(nh // dph, max(dph - 1, 1)), dqs=(nh,), dqr=(heads, dph), dks=(nh,), dkr=(heads,),
        ts=(heads,), tr=(heads // 2,), v4s=(3,), v4r=(4,), vzs=(nz,), vzr=(nz,), vbs=(nb,), vbr=(nb,),
    )
    names = list(ins) + list(outs) + list(bufs) + list(sems)
    vmem = pl.BlockSpec(memory_space=pltpu.VMEM)
    results = pl.pallas_call(
        functools.partial(layer_kernel, names, sizes),
        out_shape=[jax.ShapeDtypeStruct(shape, kind) for shape, kind in outs.values()],
        in_specs=[pl.BlockSpec(memory_space=pltpu.SMEM)] + [vmem] * (len(ins) - 1),
        out_specs=[vmem] * len(outs),
        scratch_shapes=[pltpu.VMEM(shape, kind) for shape, kind in bufs.values()]
        + [pltpu.SemaphoreType.DMA(shape) for shape in sems.values()],
        compiler_params=pltpu.CompilerParams(
            collective_id=1, has_side_effects=True, vmem_limit_bytes=VMEM_LIMIT
        ),
        cost_estimate=pl.CostEstimate(flops=10**10, bytes_accessed=10**7, transcendentals=10**7),
    )(*ins.values())
    grads = [
        ((rows, cw), BF16), ((rows, cw), F32), ((1, cw), F32), ((1, cw), F32),
        ((wide, cw), F32), ((wide, cw), F32), ((wide, cw), F32), ((cw, wide), F32),
        ((wide, cw), F32), ((1, cw), F32), ((1, cw), F32), ((1, cw), F32), ((wide, cw), F32), ((1, cw), F32),
        ((cw, units), F32), ((units, cw), F32),
    ]
    done = pl.pallas_call(
        functools.partial(final_kernel, heads),
        out_shape=[jax.ShapeDtypeStruct(shape, kind) for shape, kind in grads],
        in_specs=[vmem] * len(outs),
        out_specs=[vmem] * len(grads),
        compiler_params=pltpu.CompilerParams(vmem_limit_bytes=VMEM_LIMIT),
    )(*results)
    return tuple(a[0] if a.shape[0] == 1 else a for a in done)


def solution(mesh):
    cols = P(None, "width")
    vec = P("width")
    in_specs = (
        P(("batch", "hidden"), "width"), vec, vec, cols, cols, cols, P("width", None), cols, vec, vec, vec,
        cols, vec, P("width", "hidden"), P("hidden", "width"), P("batch", None),
        P(("batch", "hidden"), "width"),
    )
    out_specs = (
        P(("batch", "hidden"), "width"), P(("batch", "hidden"), "width"), vec, vec, cols, cols, cols,
        P("width", None), cols, vec, vec, vec, cols, vec, P("width", "hidden"), P("hidden", "width"),
    )
    return jax.shard_map(local, mesh=mesh, in_specs=in_specs, out_specs=out_specs, check_vma=False)
```

```python
import functools
import types

import jax
import jax.numpy as jnp
from jax import lax
from jax.experimental import pallas as pl
from jax.experimental.pallas import tpu as pltpu
from jax.sharding import PartitionSpec as P

HD = 64
EPSILON = 1e-05
MESH = pl.DeviceIdType.MESH
F32 = jnp.float32
BF16 = jnp.bfloat16
NEG = -1e30
VMEM_LIMIT = 62 * 1024 * 1024
HALVING = False
PLAN = {
    "begin": ("a1",), "row0": (), "col0": ("bx",), "row1": (), "col1": ("bz",), "row2": ("a2",), "col2": (),
    "loop": ("a3", "bg"), "whole": (), "sent": (), "proj": ("cy", "a4", "a5"), "half": ("cz",),
    "norm": ("bb",), "vec": ("cg", "a6"), "rows": (), "last": ("bc", "cb"), "end": ("cc",),
}
SCALE = HD**-0.5


def nn(a, b):
    return lax.dot_general(a, b, (((1,), (0,)), ((), ())), preferred_element_type=F32)


def nt(a, b):
    return lax.dot_general(a, b, (((1,), (1,)), ((), ())), preferred_element_type=F32)


def flip(a):
    return a.astype(F32).T.astype(BF16)


def remote(src, dst, send, recv, dev):
    return pltpu.make_async_remote_copy(
        src_ref=src, dst_ref=dst, send_sem=send, recv_sem=recv, device_id=dev, device_id_type=MESH
    )


def await_copy(ref, sem):
    pltpu.make_async_copy(ref, ref, sem).wait()


def at(index, size):
    return pl.ds(pl.multiple_of(index * size, size), size)


def sub_row(index, sub, dph):
    return jnp.where(lax.rem(index, 2) == 0, sub, dph - 1 - sub)


def segments(pos, ends):
    total = jnp.zeros(pos.shape, jnp.int32)
    for end in ends:
        total = total + (pos >= end).astype(jnp.int32)
    return total


def allowed_mask(key_base, query_base, keys, queries, ends):
    key_pos = key_base + lax.broadcasted_iota(jnp.int32, (keys, 1), 0)
    query_pos = query_base + lax.broadcasted_iota(jnp.int32, (1, queries), 1)
    same = segments(key_pos, ends) == segments(query_pos, ends)
    return same & (key_pos <= query_pos)


def sigmoid(x):
    return 1.0 / (1.0 + jnp.exp(-x))


class Sends:
    def __init__(self):
        self.items = []

    def start(self, copy):
        copy.start()
        self.items.append((None, copy))

    def start_if(self, cond, copy):
        @pl.when(cond)
        def _():
            copy.start()

        self.items.append((cond, copy))

    def finish(self):
        for cond, copy in self.items:
            if cond is None:
                copy.wait_send()
            else:

                @pl.when(cond)
                def _(copy=copy):
                    copy.wait_send()


def layer_kernel(names, sizes, *refs):
    r = types.SimpleNamespace(**dict(zip(names, refs)))
    nb, nh, rows, cw, units, heads, dph, tq = sizes
    half, wide, nz = rows // 2, 2 * cw, nh // 2
    per = half // tq
    pairs = nb // 2
    hops = nz.bit_length() - 1
    b, h, w = lax.axis_index("batch"), lax.axis_index("hidden"), lax.axis_index("width")
    group, sub = lax.div(h, dph), lax.rem(h, dph)
    z, c, bp = lax.div(h, 2), lax.rem(h, 2), lax.rem(b, 2)
    x_dev = (b, h, 1 - w)
    c_dev = (b, h + 1 - 2 * c, w)
    y_dev = (b + 1 - 2 * bp, h, w)

    def z_dev(k):
        zz = lax.rem(z + k, nz)
        return zz, (b, 2 * zz + c, w)

    own, other = at(w, cw), at(1 - w, cw)
    mine, theirs = at(w, half), at(1 - w, half)
    lanes = at(c, half)
    ends = [
        r.lens[0, 0],
        r.lens[0, 0] + r.lens[0, 1],
        r.lens[0, 0] + r.lens[0, 1] + r.lens[0, 2],
    ]
    sends = Sends()

    barrier = pltpu.get_barrier_semaphore()
    count = 0
    for dw in range(2):
        for dh in range(nh):
            if dh or dw:
                dev = (b, lax.rem(h + dh, nh), lax.rem(w + dw, 2))
                pl.semaphore_signal(barrier, inc=1, device_id=dev, device_id_type=MESH)
                count += 1
    for db in range(1, nb):
        dev = (lax.rem(b + db, nb), h, w)
        pl.semaphore_signal(barrier, inc=1, device_id=dev, device_id_type=MESH)
        count += 1
    pl.semaphore_wait(barrier, count)

    for i, vec in enumerate((r.v0, r.v1, r.v2, r.v3, r.v4, r.v5)):
        r.vsrc[i : i + 1, :] = vec[...]
    vcopy = remote(r.vsrc, r.vecf.at[:, own], r.xs.at[0], r.xr.at[0], x_dev)
    sends.start(vcopy)
    tcopies = []
    for k in range(2):
        part = pl.ds(k * half, half)
        copy = remote(r.tok.at[part], r.tokf.at[part, own], r.xs.at[1 + k], r.xr.at[1 + k], x_dev)
        sends.start(copy)
        tcopies.append(copy)
    r.wup[z, c, w] = r.wu[...]
    r.wdn[z, c, w] = r.wd[...]

    def weight_blocks(distance):
        for kind, buf in enumerate((r.wup, r.wdn)):
            for step in (1, -1) if distance else (1,):
                zz = z - step * distance
                index = jnp.clip(zz, 0, nz - 1)
                yield (zz >= 0) & (zz < nz) & (bp == kind), index, buf, step

    def weight_hop(k, ending=False):
        for here, index, buf, step in weight_blocks(k - 1):
            for way in (1, -1) if k == 1 else (step,):
                onward = (z + way >= 0) & (z + way < nz)
                going = here & (jnp.logical_not(onward) if ending else onward)
                block = buf.at[index, c, w]
                if k > 1:

                    @pl.when(going)
                    def _(block=block, index=index):
                        await_copy(block, r.wzr.at[index])
                        remote(block, block, r.wxs.at[index], r.wxr.at[index], x_dev).start()
                        remote(block, block, r.wys.at[index, w], r.wyr.at[index, w], y_dev).start()

                if not ending:
                    dev = (b, 2 * jnp.clip(z + way, 0, nz - 1) + c, w)
                    copy = remote(block, block, r.wzs.at[(1 - way) // 2, k], r.wzr.at[index], dev)
                    sends.start_if(going, copy)

    def weight_cross(distance):
        for here, index, buf, _ in weight_blocks(distance):

            @pl.when(here)
            def _(index=index, buf=buf):
                block = buf.at[index, c, 1 - w]
                await_copy(block, r.wxr.at[index])
                remote(block, block, r.wys.at[index, 1 - w], r.wyr.at[index, 1 - w], y_dev).start()

    for here, index, buf, _ in weight_blocks(0):
        block = buf.at[index, c, w]
        copy = remote(block, block, r.wxs.at[index], r.wxr.at[index], x_dev)

        @pl.when(here)
        def _(copy=copy):
            copy.start()

    weight_hop(1)
    gates = ((r.wg1, r.g1f), (r.wg2, r.g2f), (r.wo, r.wof))
    for src, dst in gates:
        dst[w] = src[...]
    ccopy = remote(r.cot.at[theirs], r.cotr.at[:, own], r.xs.at[3], r.xr.at[3], x_dev)
    r.vecf[:, own] = r.vsrc[...]
    r.tokf[:, own] = r.tok[...]
    r.cotr[:, own] = r.cot[mine, :]

    for i, weight in enumerate((r.wq, r.wk, r.wv)):
        turned = flip(weight[...])
        for t in range(heads):
            r.wt[t, i * HD : (i + 1) * HD, :] = turned[t * HD : (t + 1) * HD]

    vcopy.wait_recv()
    gain, shift = r.vecf[0:1, :], r.vecf[1:2, :]

    def project(k):
        part = slice(k * half, (k + 1) * half)
        tcopies[k].wait_recv()
        x = r.tokf[part, :].astype(F32)
        centre = x - jnp.mean(x, -1, keepdims=True)
        spread = jnp.mean(centre * centre, -1, keepdims=True)
        n = (centre * lax.rsqrt(spread + EPSILON) * gain + shift).astype(BF16)
        r.npair[c, part, :] = n
        for t in range(heads):
            qkv = nt(r.wt[t], n).astype(BF16)
            r.qsrc[t, :, part] = qkv[:HD]
            r.kvsrc[t, :, part] = qkv[HD:]

    def head_copies(step, k):
        t = lax.rem(group + step, heads)
        span = pl.ds(k * half, half)
        src, dst = r.kvsrc.at[t, :, span], r.kvt.at[h, :, span]
        if step:
            yield None, remote(src, dst, r.ks.at[step, k], r.kr.at[h, k], (b, t * dph + sub, w))
        else:
            yield None, pltpu.make_async_copy(src, dst, r.kr.at[h, k])
        for i in range(per):
            row = k * per + i
            target = sub_row(h, row, dph)
            src, dst = r.qsrc.at[t, :, pl.ds(row * tq, tq)], r.qt.at[h]
            copy = remote(src, dst, r.qs.at[step, row], r.qr.at[h], (b, t * dph + target, w))
            if step:
                yield None, copy
            else:
                yield target != sub, copy
                yield target == sub, pltpu.make_async_copy(src, dst, r.qr.at[h])

    def send_heads(step, k):
        for cond, copy in head_copies(step, k):
            if cond is None:
                copy.start()
            else:

                @pl.when(cond)
                def _(copy=copy):
                    copy.start()

    def heads_sent():
        for k in range(2):
            for step in range(1, heads):
                for _, copy in head_copies(step, k):
                    copy.wait_send()
            for i in range(per):
                row = k * per + i

                @pl.when(sub_row(h, row, dph) != sub)
                def _(row=row):
                    await_copy(r.qt.at[h], r.qs.at[0, row])

    project(0)
    weight_hop(2)
    weight_hop(2, ending=True)
    send_heads(heads - 1, 0)
    project(1)
    send_heads(heads - 1, 1)
    for k in range(2):
        send_heads(0, k)

    def weights_over_core():
        for kind, buf in enumerate((r.wup, r.wdn)):

            @pl.when(bp != kind)
            def _(buf=buf):
                for k in range(nz):
                    zz, _ = z_dev(k)
                    if k:
                        await_copy(buf.at[zz, c, w], r.wyr.at[zz, w])
                    await_copy(buf.at[zz, c, 1 - w], r.wyr.at[zz, 1 - w])

            block = buf.at[:, c]
            sends.start(remote(block, block, r.wcs.at[kind], r.wcr.at[kind], c_dev))

    def gates_over_core():
        for i, (src, dst) in enumerate(gates):
            piece = dst.at[1 - w, at(c, src.shape[0] // 2)]
            await_copy(piece, r.gxr.at[i])
            remote(piece, piece, r.gcs.at[i], r.gcr.at[i], c_dev).start()

    def weights_sent():
        for kind, buf in enumerate((r.wup, r.wdn)):

            @pl.when(bp == kind)
            def _(buf=buf):
                block = buf.at[z, c, w]
                for k in range(nz):
                    zz, _ = z_dev(k)
                    await_copy(block, r.wxs.at[zz])
                    await_copy(block, r.wys.at[zz, 1 - w])
                    if k:
                        await_copy(block, r.wys.at[zz, w])

        for i, (src, dst) in enumerate(gates):
            await_copy(dst.at[1 - w, at(c, src.shape[0] // 2)], r.gcs.at[i])

    def pass_on(s):
        @pl.when(lax.rem(s, dph) == sub)
        def _():
            for k in range(2):
                await_copy(r.kvt.at[s, :, pl.ds(k * half, half)], r.kr.at[s, k])
            for k in range(1, dph):
                dev = (b, group * dph + lax.rem(sub + k, dph), w)
                remote(r.kvt.at[s], r.kvt.at[s], r.fs.at[s, k], r.fr.at[s], dev).start()

    def arrive(s):
        @pl.when(lax.rem(s, dph) != sub)
        def _():
            await_copy(r.kvt.at[s], r.fr.at[s])

        r.kvn[s] = flip(r.kvt[s])
        await_copy(r.qt.at[s], r.qr.at[s])
        q = r.qt[s].astype(F32) * SCALE
        r.qlow[s] = jnp.concatenate([q, jnp.zeros_like(q)], 0).astype(BF16)

    def masked(scores, i, j):
        query_base = i * rows + sub_row(i, sub, dph) * tq
        return jnp.where(allowed_mask(j * rows, query_base, rows, tq, ends), scores, NEG)

    def bias(scores, j):
        key_pos = j * rows + lax.broadcasted_iota(jnp.int32, (rows, 1), 0)
        return scores + jnp.where(key_pos < ends[0], NEG, 0.0)

    def absorb(i, blocks):
        top = r.top[i]
        new_top = top
        for scores, _ in blocks:
            new_top = jnp.maximum(new_top, jnp.max(scores, 0, keepdims=True))
        fade = jnp.exp(top - new_top)
        total, mixed = r.total[i] * fade, r.ot[i] * fade
        for scores, j in blocks:
            weights = jnp.exp(scores - new_top)
            total = total + jnp.sum(weights, 0, keepdims=True)
            mixed = mixed + nn(r.kvt[j, HD:, :], weights.astype(BF16))
        r.top[i], r.total[i], r.ot[i] = new_top, total, mixed

    def send_attended(s):
        row = sub_row(s, sub, dph)
        total = r.total[s]
        mixed = r.ot[s] / total
        r.ot[s] = mixed
        r.lse[s] = r.top[s] + jnp.log(total)
        r.osend[s] = mixed.astype(BF16)
        row_w = lax.div(row * tq, half)
        lane = lax.rem(row * tq, half)
        dst = r.att.at[at(w * heads + group, HD), pl.ds(pl.multiple_of(lane, tq), tq)]
        slot = r.orc.at[w * heads + group, lax.div(lane, tq)]
        here = (s == h) & (row_w == w)

        @pl.when(here)
        def _():
            pltpu.make_async_copy(r.osend.at[s], dst, slot).start()

        @pl.when(jnp.logical_not(here))
        def _():
            remote(r.osend.at[s], dst, r.osd.at[s], slot, (b, s, row_w)).start()

    def own_chip(n):
        i = 2 * n
        first = masked(nn(r.kvn[i], r.qlow[i]), i, i)
        low = masked(nn(r.kvn[i], r.qlow[i + 1]), i + 1, i)
        high = masked(nn(r.kvn[i + 1], r.qlow[i + 1]), i + 1, i + 1)
        absorb(i, [(first, i)])
        absorb(i + 1, [(low, i), (high, i + 1)])

    def two_chips(hi, lo, last):
        queries, keys = (2 * hi, 2 * hi + 1), (2 * lo, 2 * lo + 1)
        scores = [[nn(r.kvn[j], r.qlow[i]) for j in keys] for i in queries]
        for a, i in enumerate(queries):
            if last and a:
                blocks = [(masked(x, i, j), j) for x, j in zip(scores[a], keys)]
            else:
                blocks = [(bias(scores[a][0], keys[0]), keys[0]), (scores[a][1], keys[1])]
            absorb(i, blocks)

    def completes(chip):
        return jnp.where(z == 0, chip, nz - z + jnp.minimum(chip, z - 1))

    def chip_at(d):
        return lax.rem(z + d, nz)

    def stage_passes(d):
        pass_on(2 * chip_at(d))
        pass_on(2 * chip_at(d) + 1)

    def stage_computes(d):
        n = chip_at(d)
        arrive(2 * n)
        arrive(2 * n + 1)
        own_chip(n)

        def with_earlier(e, _):
            m = lax.rem(z + e, nz)
            hi, lo = jnp.maximum(n, m), jnp.minimum(n, m)

            @pl.when(hi == nz - 1)
            def _():
                two_chips(hi, lo, True)

            @pl.when(hi != nz - 1)
            def _():
                two_chips(hi, lo, False)

            @pl.when((m > n) & (completes(m) == d))
            def _():
                send_attended(2 * m)
                send_attended(2 * m + 1)

            return 0

        lax.fori_loop(0, d, with_earlier, 0)

        @pl.when(completes(n) == d)
        def _():
            send_attended(2 * n)
            send_attended(2 * n + 1)

    def late_stage(d, _):
        stage_passes(d)

        @pl.when(d == 2)
        def _():
            for distance in range(2):
                weight_cross(distance)

        @pl.when(d == nz - 1)
        def _():
            weight_hop(nz, ending=True)
            for distance in range(2, nz - 1):
                weight_cross(distance)

        stage_computes(d)
        return 0

    r.top[...] = jnp.full_like(r.top, NEG)
    r.total[...] = jnp.zeros_like(r.total)
    r.ot[...] = jnp.zeros_like(r.ot)
    stage_passes(0)
    stage_computes(0)
    for k in range(2):
        send_heads(2, k)
    for i, (src, dst) in enumerate(gates):
        piece = at(c, src.shape[0] // 2)
        sends.start(remote(src.at[piece], dst.at[w, piece], r.gxs.at[i], r.gxr.at[i], x_dev))
    sends.start(remote(r.npair.at[c], r.npair.at[c], r.cs.at[0], r.cr.at[0], c_dev))
    stage_passes(1)
    for k in range(3, nz):
        weight_hop(k)
    for k in range(3, nz):
        weight_hop(k, ending=True)
    for k in range(2):
        send_heads(1, k)
    stage_computes(1)
    sends.start(ccopy)
    lax.fori_loop(2, nz, late_stage, 0)
    weight_cross(nz - 1)
    gates_over_core()
    weights_over_core()

    for i, (src, dst) in enumerate(gates):
        await_copy(dst.at[1 - w, at(1 - c, src.shape[0] // 2)], r.gcr.at[i])

    def two(a, weight):
        return jnp.concatenate([nn(a, weight[0]), nn(a, weight[1])], 1)

    def two_back(g, weight):
        return nt(g[:, :cw], weight[0]) + nt(g[:, cw:], weight[1])

    tok = r.tokf[mine, :].astype(F32)
    n1 = r.npair[c, mine, :]
    gate_one = sigmoid(two(n1, r.g1f) + r.vecf[2:3, :])
    for g in range(2 * heads):
        for i in range(per):
            await_copy(r.att.at[pl.ds(g * HD, HD), pl.ds(i * tq, tq)], r.orc.at[g, i])
    wof = r.wof[...].reshape(wide, wide)
    branch_one = nn(flip(r.att[...]), wof)
    middle = tok + gate_one * (branch_one - tok)
    centre = middle - jnp.mean(middle, -1, keepdims=True)
    rstd = lax.rsqrt(jnp.mean(centre * centre, -1, keepdims=True) + EPSILON)
    n2 = centre * rstd
    gain_two = r.vecf[3:4, :]
    normed_two = (n2 * gain_two + r.vecf[4:5, :]).astype(BF16)
    gate_two = sigmoid(two(normed_two, r.g2f) + r.vecf[5:6, :])
    for kind, buf in enumerate((r.wup, r.wdn)):
        await_copy(buf.at[:, 1 - c], r.wcr.at[kind])

    def units_of(i2, p):
        return i2, lax.rem(c + p, 2)

    def up(i2, branch):
        for p in range(2):
            i, q = units_of(i2, p)
            pre = nn(normed_two, r.wup[i, q].reshape(wide, units))
            r.pre[i2, p] = pre
            act = jax.nn.gelu(pre).astype(BF16)
            branch = branch + jnp.concatenate([nn(act, r.wdn[i, q, 0]), nn(act, r.wdn[i, q, 1])], 1)
            if p:
                r.acts[i2] = act
                dst = r.actp.at[i2, lanes, :]
                remote(r.acts.at[i2], dst, r.as_.at[i2], r.ar.at[i2], c_dev).start()
            else:
                r.actp[i2, lanes, :] = act
        return branch

    branch_two = lax.fori_loop(0, nz, up, jnp.zeros(middle.shape, F32))
    delta = branch_two - middle
    r.outr[...] = (middle + gate_two * delta).astype(BF16)
    ocopy = remote(r.outr.at[:, other], r.out_c.at[mine, :], r.xs.at[4], r.xr.at[4], x_dev)
    sends.start(ocopy)
    ccopy.wait_recv()
    grad = r.cotr[...].astype(F32)
    gb2 = (grad * gate_two).astype(BF16)
    gl2 = (grad * delta * gate_two * (1.0 - gate_two)).astype(BF16)
    gmid = grad * (1.0 - gate_two)

    def down(i2, total):
        for p in range(2):
            i, q = units_of(i2, p)
            ghid = nt(gb2[:, :cw], r.wdn[i, q, 0]) + nt(gb2[:, cw:], r.wdn[i, q, 1])
            pre = r.pre[i2, p]
            k = 0.7978845608028654
            t = jnp.tanh(k * (pre + 0.044715 * pre * pre * pre))
            slope = 0.5 * (1.0 + t) + 0.5 * pre * (1.0 - t * t) * (k * (1.0 + 3 * 0.044715 * pre * pre))
            gpre = (ghid * slope).astype(BF16)
            total = total + nt(gpre, r.wup[i, q].reshape(wide, units))
            if p:
                r.gpres[i2] = gpre
                dst = r.gprep.at[i2, lanes, :]
                remote(r.gpres.at[i2], dst, r.ps_.at[i2], r.pr.at[i2], c_dev).start()
            else:
                r.gprep[i2, lanes, :] = gpre
        return total

    gnorm = lax.fori_loop(0, nz, down, two_back(gl2, r.g2f))
    e = gnorm * gain_two
    gmid = gmid + rstd * (
        e - jnp.mean(e, -1, keepdims=True) - n2 * jnp.mean(e * n2, -1, keepdims=True)
    )
    gb1 = (gmid * gate_one).astype(BF16)
    r.gatt[...] = nt(wof, gb1).astype(BF16)
    for dw in (1, 0):
        wt = lax.rem(w + dw, 2)
        for step in range(heads - 1, -1, -1):
            t = lax.rem(group + step, heads)
            for i in range(per):
                target = sub_row(h, w * per + i, dph)
                src = r.gatt.at[at(wt * heads + t, HD), pl.ds(i * tq, tq)]
                dst = r.dot.at[h]
                dev = (b, t * dph + target, wt)
                copy = remote(src, dst, r.ds.at[dw, step, i], r.dr.at[h], dev)
                if step or dw:
                    sends.start(copy)
                else:
                    sends.start_if(target != sub, copy)

                    @pl.when(target == sub)
                    def _(src=src, dst=dst):
                        pltpu.make_async_copy(src, dst, r.dr.at[h]).start()

    gl1 = (gmid * (branch_one - tok) * gate_one * (1.0 - gate_one)).astype(BF16)
    r.ginp[...] = gmid * (1.0 - gate_one)
    r.npt[:, lanes] = flip(normed_two)
    sends.start(remote(r.npt.at[:, lanes], r.npt.at[:, lanes], r.cs.at[1], r.cr.at[1], c_dev))
    r.gbt[:, lanes] = flip(gb2)
    sends.start(remote(r.gbt.at[:, lanes], r.gbt.at[:, lanes], r.cs.at[2], r.cr.at[2], c_dev))
    quarter = half // 2
    r.lsrc[0] = r.att[...]
    r.lsrc[1] = flip(gl1)
    r.lsrc[2] = flip(gl2)
    for m, right in enumerate((gb1, n1, normed_two)):
        r.bpair[m, lanes, :] = right
        block = r.bpair.at[m, lanes, :]
        sends.start(remote(block, block, r.cs.at[3 + m], r.cr.at[3 + m], c_dev))
        for v in range(2):
            src = r.lsrc.at[m, at(2 * v + 1 - c, quarter), :]
            dst = r.apair.at[m, v, :, lanes]
            sends.start(remote(src, dst, r.cs.at[6 + 2 * m + v], r.cr.at[6 + 2 * m + v], c_dev))
            r.apair[m, v, :, lanes] = r.lsrc[m, at(2 * v + c, quarter), :]
    r.gterm[...] = two_back(gl1, r.g1f)
    r.vsum[...] = jnp.zeros_like(r.vsum)
    r.vsum[2:3, :] = jnp.sum(gl1.astype(F32), 0, keepdims=True)
    r.vsum[3:4, :] = jnp.sum(gnorm * n2, 0, keepdims=True)
    r.vsum[4:5, :] = jnp.sum(gnorm, 0, keepdims=True)
    r.vsum[5:6, :] = jnp.sum(gl2.astype(F32), 0, keepdims=True)
    r.out_c[mine, :] = r.outr[:, own]

    eighth = quarter // 2
    for m in range(3):
        await_copy(r.bpair.at[m, lanes, :], r.cr.at[3 + m])
        for v in range(2):
            await_copy(r.apair.at[m, v, :, lanes], r.cr.at[6 + 2 * m + v])
            block = nn(r.apair[m, v], r.bpair[m]).astype(BF16)
            for y in range(2):
                r.gb[v, y, m] = block[y * eighth : (y + 1) * eighth]
    for m in range(3):
        sends.start(remote(r.gb.at[:, 1 - bp, m], r.ybin.at[:, m], r.sys.at[m], r.syr.at[m], y_dev))
    await_copy(r.npt.at[:, lanes], r.cr.at[1])
    await_copy(r.gbt.at[:, lanes], r.cr.at[2])

    def weight_grads(i2, _):
        await_copy(r.gprep.at[i2, lanes, :], r.pr.at[i2])
        await_copy(r.actp.at[i2, lanes, :], r.ar.at[i2])
        r.ga[0, i2] = nn(r.npt[...], r.gprep[i2]).astype(BF16).reshape(2, 2, quarter, units)
        r.ga[1, i2] = nn(r.gbt[...], r.actp[i2]).astype(BF16).reshape(2, 2, quarter, units)
        return 0

    lax.fori_loop(0, nz, weight_grads, 0)
    sends.start(remote(r.ga.at[0, :, 1 - w], r.xin0, r.xs.at[5], r.xr.at[5], x_dev))


    def z_block(q, flip_bit, v):
        bit = lax.rem(lax.div(z, 1 << q), 2)
        bit = 1 - bit if flip_bit else bit
        return lax.rem(z, 1 << q) + bit * (1 << q) + v * (2 << q)

    def ffn_first():
        remote(r.ga.at[1, :, :, 1 - bp], r.yin1, r.ys.at[1], r.yr.at[1], y_dev).start()

    def ffn_second():
        await_copy(r.xin0, r.xr.at[5])
        r.ga[0, :, w] = (r.ga[0, :, w].astype(F32) + r.xin0[...].astype(F32)).astype(BF16)
        remote(r.ga.at[0, :, w, 1 - bp], r.yin0, r.ys.at[2], r.yr.at[2], y_dev).start()
        await_copy(r.yin1, r.yr.at[1])
        r.ga[1, :, :, bp] = (r.ga[1, :, :, bp].astype(F32) + r.yin1[...].astype(F32)).astype(BF16)
        remote(r.ga.at[1, :, 1 - w, bp], r.xin1, r.xs.at[6], r.xr.at[6], x_dev).start()

    def ffn_third():
        await_copy(r.yin0, r.yr.at[2])
        await_copy(r.xin1, r.xr.at[6])
        r.zs[:, 0] = (r.ga[0, :, w, bp].astype(F32) + r.yin0[...].astype(F32)).astype(BF16)
        r.zs[:, 1] = (r.ga[1, :, w, bp].astype(F32) + r.xin1[...].astype(F32)).astype(BF16)
        ffn_hop(0)

    def ffn_hop(q):
        if q:
            ffn_add(q - 1)
        bit = lax.rem(lax.div(z, 1 << q), 2)
        dev = (b, 2 * (z + (1 << q) * (1 - 2 * bit)) + c, w)
        for v in range(nz >> (q + 1)):
            slot = nz - (nz >> q) + v
            remote(r.zs.at[z_block(q, True, v)], r.zin.at[slot], r.zss.at[slot], r.zsr.at[slot], dev).start()

    def ffn_add(q):
        for v in range(nz >> (q + 1)):
            slot = nz - (nz >> q) + v
            await_copy(r.zin.at[slot], r.zsr.at[slot])
            kept = z_block(q, False, v)
            r.zs[kept] = (r.zs[kept].astype(F32) + r.zin[slot].astype(F32)).astype(BF16)

    def ffn_fourth():
        ffn_add(hops - 1)
        total = r.zs[z].astype(F32)
        if pairs > 1:
            mypair = lax.div(b, 2)
            r.pin[mypair] = total.astype(BF16)
            for k in range(1, pairs):
                dev = (lax.rem(b + 2 * k, nb), h, w)
                block = r.pin.at[mypair]
                remote(block, block, r.pas.at[k], r.par.at[mypair], dev).start()
            for k in range(1, pairs):
                pp = lax.rem(mypair + k, pairs)
                await_copy(r.pin.at[pp], r.par.at[pp])
            total = r.pin[0].astype(F32)
            for k in range(1, pairs):
                total = total + r.pin[k].astype(F32)
        r.red_a[bp] = total.astype(BF16)
        block = r.red_a.at[bp]
        remote(block, block, r.ys.at[3], r.yr.at[3], y_dev).start()

    def ffn_sent():
        await_copy(r.red_a.at[bp], r.ys.at[3])
        for k in range(1, pairs):
            await_copy(r.pin.at[0], r.pas.at[k])
        await_copy(r.yin1, r.ys.at[1])
        await_copy(r.yin0, r.ys.at[2])
        await_copy(r.xin1, r.xs.at[6])
        for k in range(nz - 1):
            await_copy(r.zin.at[k], r.zss.at[k])

    zr = HD * 4 // nz

    def z_part(zz):
        return pl.ds(pl.multiple_of(lax.div(zz, 4) * zr, zr), zr), at(lax.rem(zz, 4), 128)

    def square_x():
        for p in range(3):
            await_copy(r.ybin.at[:, p], r.syr.at[p])
            r.gb[:, bp, p] = (r.gb[:, bp, p].astype(F32) + r.ybin[:, p].astype(F32)).astype(BF16)
            remote(r.gb.at[1 - w, bp, p], r.xbin.at[p], r.sxs.at[p], r.sxr.at[p], x_dev).start()

    def z_peer(q):
        return (b, 2 * (z + (1 << q) * (1 - 2 * lax.rem(lax.div(z, 1 << q), 2))) + c, w)

    def z_slots(q):
        return [(nz - (nz >> q) + v, v) for v in range(nz >> (q + 1))]

    def square_add(which, p, q):
        for slot, v in z_slots(q):
            await_copy(r.sqin.at[which, p, slot], r.sqr.at[which, p, slot])
            kept = (which, p) + z_part(z_block(q, False, v))
            r.sq[kept] = (r.sq[kept].astype(F32) + r.sqin[which, p, slot].astype(F32)).astype(BF16)

    def square_hop(which, q):
        for p in range(3):
            if q == 0:
                await_copy(r.xbin.at[p], r.sxr.at[p])
                r.sq[which, p] = (r.gb[w, bp, p].astype(F32) + r.xbin[p].astype(F32)).astype(BF16)
            else:
                square_add(which, p, q - 1)
            for slot, v in z_slots(q):
                src = r.sq.at[(which, p) + z_part(z_block(q, True, v))]
                dst = r.sqin.at[which, p, slot]
                remote(src, dst, r.sqs.at[which, p, slot], r.sqr.at[which, p, slot], z_peer(q)).start()

    def spread_part(which, p, q):
        for slot, v in z_slots(q):
            block = r.red_s.at[(which, c, bp, p) + z_part(z_block(q, False, v))]
            remote(block, block, r.sgs.at[which, p, slot], r.sgr.at[which, p, slot], z_peer(q)).start()

    def spread_await(which, p, q):
        for slot, v in z_slots(q):
            block = r.red_s.at[(which, c, bp, p) + z_part(z_block(q, True, v))]
            await_copy(block, r.sgr.at[which, p, slot])

    def over_pairs(which, p, total):
        if pairs == 1:
            return total
        mypair = lax.div(b, 2)
        r.sqpair[which, p, mypair] = total
        for k in range(1, pairs):
            dev = (lax.rem(b + 2 * k, nb), h, w)
            block = r.sqpair.at[which, p, mypair]
            remote(block, block, r.sqps.at[which, p, k], r.sqpr.at[which, p, mypair], dev).start()
        for k in range(1, pairs):
            pp = lax.rem(mypair + k, pairs)
            await_copy(r.sqpair.at[which, p, pp], r.sqpr.at[which, p, pp])
        total = r.sqpair[which, p, 0].astype(F32)
        for k in range(1, pairs):
            total = total + r.sqpair[which, p, k].astype(F32)
        return total.astype(BF16)

    def square_turn(which):
        for p in range(3):
            square_add(which, p, hops - 1)
            total = over_pairs(which, p, r.sq[(which, p) + z_part(z)])
            r.red_s[(which, c, bp, p) + z_part(z)] = total
            spread_part(which, p, hops - 1)

    def square_spread(which, q):
        for p in range(3):
            spread_await(which, p, q + 1)
            spread_part(which, p, q)

    def square_back(which):
        for p in range(3):
            spread_await(which, p, 0)
            block = r.red_s.at[which, c, bp, p]
            remote(block, block, r.sbs.at[which, p], r.sbr.at[which, p], y_dev).start()

    def square_core(which):
        for p in range(3):
            await_copy(r.red_s.at[which, c, 1 - bp, p], r.sbr.at[which, p])
            block = r.red_s.at[which, c, :, p]
            remote(block, block, r.scs.at[which, p], r.scr.at[which, p], c_dev).start()

    def scatter(which):
        for p in range(3):
            if which:
                await_copy(r.ycin.at[p], r.pyr.at[p])
                r.sq[1, p] = (r.gc[bp, p].astype(F32) + r.ycin[p].astype(F32)).astype(BF16)
            else:
                await_copy(r.xbin.at[p], r.sxr.at[p])
                r.sq[0, p] = (r.gb[w, bp, p].astype(F32) + r.xbin[p].astype(F32)).astype(BF16)
            for k in range(nz - 1, 0, -1):
                zz, dev = z_dev(k)
                src, dst = r.sq.at[(which, p) + z_part(zz)], r.pzin.at[which, p, z]
                remote(src, dst, r.pzs.at[which, p, k], r.pzr.at[which, p, z], dev).start()

    def gather(which):
        for p in range(3):
            total = r.sq[(which, p) + z_part(z)].astype(F32)
            for k in range(1, nz):
                zz, _ = z_dev(k)
                await_copy(r.pzin.at[which, p, zz], r.pzr.at[which, p, zz])
                total = total + r.pzin[which, p, zz].astype(F32)
            block = (which, c, bp, p) + z_part(z)
            r.red_s[block] = over_pairs(which, p, total.astype(BF16))
            for k in range(nz - 1, 0, -1):
                _, dev = z_dev(k)
                ref = r.red_s.at[block]
                remote(ref, ref, r.pgs.at[which, p, k], r.pgr.at[which, p, z], dev).start()

    def back(which):
        for p in range(3):
            for k in range(1, nz):
                zz, _ = z_dev(k)
                await_copy(r.red_s.at[(which, c, bp, p) + z_part(zz)], r.pgr.at[which, p, zz])
            block = r.red_s.at[which, c, bp, p]
            remote(block, block, r.sbs.at[which, p], r.sbr.at[which, p], y_dev).start()

    def proj_y():
        for p in range(3):
            remote(r.gc.at[1 - bp, p], r.ycin.at[p], r.pys.at[p], r.pyr.at[p], y_dev).start()

    def square_end(which):
        for p in range(3):
            await_copy(r.red_s.at[which, 1 - c, :, p], r.scr.at[which, p])
            await_copy(r.red_s.at[which, c, :, p], r.scs.at[which, p])
            await_copy(r.xbin.at[p], r.sbs.at[which, p])
            if which == 0:
                await_copy(r.xbin.at[p], r.sxs.at[p])
            else:
                await_copy(r.ycin.at[p], r.pys.at[p])
            if which == 0 and HALVING:
                for slot in range(nz - 1):
                    await_copy(r.sqin.at[which, p, slot], r.sqs.at[which, p, slot])
                    await_copy(r.sqin.at[which, p, slot], r.sgs.at[which, p, slot])
            else:
                for k in range(1, nz):
                    await_copy(r.pzin.at[which, p, z], r.pzs.at[which, p, k])
                    await_copy(r.pzin.at[which, p, z], r.pgs.at[which, p, k])
            for k in range(1, pairs):
                await_copy(r.sqpair.at[which, p, 0], r.sqps.at[which, p, k])

    def each(step, *args):
        return lambda: [step(*(a if isinstance(a, tuple) else (a,))) for a in args]

    later = list(range(2, hops))
    down_again = list(range(hops - 2, -1, -1))
    steps = dict(
        a1=ffn_first, a2=ffn_second, a3=ffn_third, a4=lambda: ffn_hop(1), a5=each(ffn_hop, *later), a6=ffn_fourth,
        bx=square_x, cy=proj_y, cz=lambda: scatter(1), cg=lambda: gather(1), cb=lambda: back(1),
        cc=lambda: square_core(1), bc=lambda: square_core(0),
    )
    if HALVING:
        steps.update(
            bz0=lambda: square_hop(0, 0), bz1=lambda: square_hop(0, 1), bz2=each(square_hop, *[(0, q) for q in later]),
            bt=lambda: square_turn(0), bs=each(square_spread, *[(0, q) for q in down_again]),
            bb=lambda: square_back(0),
        )
    else:
        steps.update(bz=lambda: scatter(0), bg=lambda: gather(0), bb=lambda: back(0))

    def take(point):
        for name in PLAN[point]:
            steps[name]()

    r.acc[...] = jnp.zeros_like(r.acc)

    def finish(s):
        @pl.when(lax.rem(s, dph) == sub)
        def _():
            total = r.acc[s]
            for k in range(1, dph):
                slot = r.pin_kv.at[lax.div(s, dph), k - 1]
                await_copy(slot, r.pkr.at[lax.div(s, dph), k - 1])
                total = total + r.pin_kv[lax.div(s, dph), k - 1]
            r.dkvsend[s, :HD] = (total[:HD] * SCALE).astype(BF16)
            r.dkvsend[s, HD:] = total[HD:].astype(BF16)
            dst = r.dqkv.at[group, pl.ds(HD, 2 * HD), :]

            @pl.when(s == h)
            def _():
                pltpu.make_async_copy(r.dkvsend.at[s], dst, r.dkr.at[group]).start()

            @pl.when(s != h)
            def _():
                remote(r.dkvsend.at[s], dst, r.dks.at[s], r.dkr.at[group], (b, s, w)).start()

    def pairs_backward(where, full):
        scores = [nn(r.kvn[j], r.qlow[i]) for i, j in where]
        gprobs = [nn(r.kvn[j], r.dhigh[i]) for i, j in where]
        for x, gp, (i, j), whole in zip(scores, gprobs, where, full):
            x = masked(x, i, j) if whole else bias(x, j)
            probs = jnp.exp(x - r.lse[i])
            gscores = (probs * (gp - r.centre[i])).astype(BF16)
            r.acc[j, HD:, :] += nt(r.dhigh[i, HD:, :], probs.astype(BF16))
            r.acc[j, :HD, :] += nt(r.qt[i], gscores)
            r.dqa[i] += nn(r.kvt[j, :HD, :], gscores)

    def choose(kinds, where):
        taken = False
        for cond, full in kinds:

            @pl.when(jnp.logical_and(cond, jnp.logical_not(taken)))
            def _(full=full):
                pairs_backward(where, full)

            taken = jnp.logical_or(taken, cond)

    def pair_at(t, u):
        lo, hi = t, nh - 1 - t
        n = hi - lo + 1
        return jnp.where(u < n, hi, lo + u - n), jnp.where(u < n, lo + u, lo)

    def out_arrives(s):
        await_copy(r.dot.at[s], r.dr.at[s])
        dout = r.dot[s]
        r.dhigh[s] = jnp.concatenate([jnp.zeros((HD, tq), BF16), dout], 0)
        r.centre[s] = jnp.sum(r.ot[s] * dout.astype(F32), 0, keepdims=True)

    def send_block(s):
        row = sub_row(s, sub, dph)
        r.dqsend[s] = (r.dqa[s] * SCALE).astype(BF16)
        dst = r.dqkv.at[group, pl.ds(0, HD), pl.ds(pl.multiple_of(row * tq, tq), tq)]

        @pl.when(s == h)
        def _():
            pltpu.make_async_copy(r.dqsend.at[s], dst, r.dqr.at[group, row]).start()

        @pl.when(s != h)
        def _():
            remote(r.dqsend.at[s], dst, r.dqs.at[s], r.dqr.at[group, row], (b, s, w)).start()

        owner = lax.rem(s, dph)

        @pl.when(owner != sub)
        def _():
            k = lax.rem(sub - owner + dph, dph)
            dev = (b, group * dph + owner, w)
            slot = lax.div(s, dph)
            remote(r.acc.at[s], r.pin_kv.at[slot, k - 1], r.pks.at[s], r.pkr.at[slot, k - 1], dev).start()

    def round_backward(t, _):
        lo, hi = t, nh - 1 - t
        n = hi - lo + 1

        rowed = lax.div(n, 2)
        columned = rowed - 1

        def row_step(v, _):
            where = [pair_at(t, 2 * v), pair_at(t, 2 * v + 1)]
            choose([(t == 0, (True, True)), (v == rowed - 1, (False, True)), (True, (False, False))], where)

            @pl.when((t > 0) & (v == jnp.minimum(1, rowed - 1)))
            def _():
                finish(lo - 1)

            return 0

        lax.fori_loop(0, rowed, row_step, 0)
        send_block(hi)

        @pl.when(t == 0)
        def _():
            lax.fori_loop(0, nh - 1, lambda s, z: (out_arrives(s), z)[1], 0)

        for at_round, point in ((0, "row0"), (nh // 8, "row1"), (nh // 4, "row2")):
            if PLAN[point]:

                @pl.when(t == at_round)
                def _(point=point):
                    take(point)

        def column_step(v, _):
            where = [pair_at(t, n + 2 * v), pair_at(t, n + 2 * v + 1)]
            choose([(v == 0, (True, False)), (True, (False, False))], where)

            @pl.when(v == jnp.minimum(1, columned - 1))
            def _():
                finish(hi)

            return 0

        lax.fori_loop(0, columned, column_step, 0)
        pairs_backward([pair_at(t, 2 * n - 2)], (True,))
        send_block(lo)

        @pl.when(columned == 0)
        def _():
            finish(hi)

        for at_round, point in ((0, "col0"), (nh // 8, "col1"), (nh // 4, "col2")):
            if PLAN[point]:

                @pl.when(t == at_round)
                def _(point=point):
                    take(point)

        return 0

    r.dqa[...] = jnp.zeros_like(r.dqa)
    out_arrives(nh - 1)
    take("begin")
    lax.fori_loop(0, nh // 2, round_backward, 0)
    finish(nh // 2 - 1)
    take("loop")

    for t in range(heads):
        await_copy(r.dqkv.at[t, pl.ds(HD, 2 * HD), :], r.dkr.at[t])
        for i in range(dph):
            await_copy(r.dqkv.at[t, pl.ds(0, HD), pl.ds(i * tq, tq)], r.dqr.at[t, i])
        sends.start_if(
            t % 2 != c, remote(r.dqkv.at[t], r.dsib.at[t // 2], r.ts.at[t], r.tr.at[t // 2], c_dev)
        )
    take("whole")
    wts = r.wt[...].reshape(heads * 3 * HD, wide)

    def grad_normed(span):
        return nn(flip(r.dqkv[:, :, span].reshape(heads * 3 * HD, half)), wts)

    r.psend[...] = grad_normed(theirs).astype(BF16)
    pcopy = remote(r.psend, r.precv, r.xs.at[8], r.xr.at[8], x_dev)
    sends.start(pcopy)
    take("sent")
    await_copy(r.npair.at[1 - c], r.cr.at[0])
    for j in range(heads // 2):
        await_copy(r.dsib.at[j], r.tr.at[j])
        part = nn(r.dqkv[2 * j + c], r.npair[c]) + nn(r.dsib[j], r.npair[1 - c])
        for p in range(3):
            r.gc[j, p] = part[p * HD : (p + 1) * HD].astype(BF16)
    take("proj")
    gnorm = grad_normed(mine) + r.gterm[...]
    x = r.tokf[mine, :].astype(F32)
    centre = x - jnp.mean(x, -1, keepdims=True)
    rstd = lax.rsqrt(jnp.mean(centre * centre, -1, keepdims=True) + EPSILON)
    n = centre * rstd
    take("half")
    pcopy.wait_recv()
    gnorm = gnorm + r.precv[...].astype(F32)
    e = gnorm * r.vecf[0:1, :]
    result = r.ginp[...] + rstd * (
        e - jnp.mean(e, -1, keepdims=True) - n * jnp.mean(e * n, -1, keepdims=True)
    )
    r.tsend[...] = result.astype(BF16)
    tcopy = remote(r.tsend.at[:, other], r.trecv, r.xs.at[9], r.xr.at[9], x_dev)
    sends.start(tcopy)
    r.vsum[0:1, :] = jnp.sum(gnorm * n, 0, keepdims=True)
    r.vsum[1:2, :] = jnp.sum(gnorm, 0, keepdims=True)
    me4 = 2 * c + w
    r.vin4[me4] = r.vsum[...]
    k = 0
    for dc in range(2):
        for dw in range(2):
            if dc or dw:
                cc, ww = lax.rem(c + dc, 2), lax.rem(w + dw, 2)
                dev = (b, 2 * z + cc, ww)
                sends.start(remote(r.vin4.at[me4], r.vin4.at[me4], r.v4s.at[k], r.v4r.at[me4], dev))
                k += 1
    r.gtok[mine, :] = jnp.where(w == 0, result[:, :cw], result[:, cw:])
    take("norm")
    for dc in range(2):
        for dw in range(2):
            if dc or dw:
                peer = 2 * lax.rem(c + dc, 2) + lax.rem(w + dw, 2)
                await_copy(r.vin4.at[peer], r.v4r.at[peer])
    r.vinz[z] = r.vin4[0] + r.vin4[1] + r.vin4[2] + r.vin4[3]
    for k in range(1, nz):
        _, dev = z_dev(k)
        sends.start(remote(r.vinz.at[z], r.vinz.at[z], r.vzs.at[k], r.vzr.at[z], dev))
    take("vec")
    tcopy.wait_recv()
    r.gtok[theirs, :] = r.trecv[...].astype(F32)
    ocopy.wait_recv()
    take("rows")
    for k in range(1, nz):
        zz, _ = z_dev(k)
        await_copy(r.vinz.at[zz], r.vzr.at[zz])
    total = r.vinz[0]
    for k in range(1, nz):
        total = total + r.vinz[k]
    r.vinb[b] = total
    for k in range(1, nb):
        dev = (lax.rem(b + k, nb), h, w)
        sends.start(remote(r.vinb.at[b], r.vinb.at[b], r.vbs.at[k], r.vbr.at[b], dev))
    take("last")
    for k in range(1, nb):
        bb = lax.rem(b + k, nb)
        await_copy(r.vinb.at[bb], r.vbr.at[bb])
    total = r.vinb[0]
    for k in range(1, nb):
        total = total + r.vinb[k]
    r.red_v[...] = jnp.where(w == 0, total[:, :cw], total[:, cw:])
    take("end")
    await_copy(r.red_a.at[1 - bp], r.yr.at[3])

    def sent(s, _):
        row = sub_row(s, sub, dph)
        here = (s == h) & (lax.div(row * tq, half) == w)

        @pl.when(jnp.logical_not(here))
        def _():
            await_copy(r.osend.at[s], r.osd.at[s])

        @pl.when(lax.rem(s, dph) == sub)
        def _():
            for k in range(1, dph):
                await_copy(r.kvt.at[s], r.fs.at[s, k])

        @pl.when(s != h)
        def _():
            await_copy(r.dqsend.at[s], r.dqs.at[s])

        @pl.when((s != h) & (lax.rem(s, dph) == sub))
        def _():
            await_copy(r.dkvsend.at[s], r.dks.at[s])

        @pl.when(lax.rem(s, dph) != sub)
        def _():
            await_copy(r.acc.at[s], r.pks.at[s])

        return 0

    lax.fori_loop(0, nh, sent, 0)
    weights_sent()
    heads_sent()
    for i2 in range(nz):
        await_copy(r.acts.at[i2], r.as_.at[i2])
        await_copy(r.gpres.at[i2], r.ps_.at[i2])
    ffn_sent()
    sends.finish()
    square_end(0)
    square_end(1)


def final_kernel(heads, *refs):
    (
        out_c, gtok, red_a, red_s, red_v,
        o_out, o_tok, o_g1, o_b1, o_wq, o_wk, o_wv, o_wo, o_gw1, o_gb1, o_g2, o_b2, o_gw2, o_gb2, o_up, o_dn,
    ) = refs
    o_out[...] = out_c[...]
    o_tok[...] = gtok[...]
    for i, ref in enumerate((o_g1, o_b1, o_gb1, o_g2, o_b2, o_gb2)):
        ref[...] = red_v[i : i + 1, :]
    _, quarter, units = red_a.shape[1:]
    o_up[:quarter, :] = red_a[0, 0].astype(F32)
    o_up[quarter:, :] = red_a[1, 0].astype(F32)
    o_dn[:, :quarter] = red_a[0, 1].astype(F32).T
    o_dn[:, quarter:] = red_a[1, 1].astype(F32).T
    eighth = quarter // 2
    for core in range(2):
        for y in range(2):
            base = (2 * core + y) * eighth
            o_wo[base : base + eighth, :] = red_s[0, core, y, 0].astype(F32)
    for m, ref in ((1, o_gw1), (2, o_gw2)):
        full = [red_s[0, core, y, m] for core in range(2) for y in range(2)]
        ref[...] = jnp.concatenate(full, 0).astype(F32).T
    for i, ref in enumerate((o_wq, o_wk, o_wv)):
        full = []
        for t in range(heads):
            full.append(red_s[1, t % 2, t // 2, i])
        ref[...] = jnp.concatenate(full, 0).astype(F32).T


def local(
    tokens, ln1_gain, ln1_bias, w_query, w_key, w_value, w_out, gate1_weight, gate1_bias,
    ln2_gain, ln2_bias, gate2_weight, gate2_bias, w_up, w_down, lengths, cotangent,
):
    nb, nh = lax.axis_size("batch"), lax.axis_size("hidden")
    rows, cw = tokens.shape
    units = w_up.shape[1]
    heads = cw // HD
    dph = nh // heads
    tq, half, wide, nz, pairs = rows // dph, rows // 2, 2 * cw, nh // 2, nb // 2
    quarter = half // 2
    zr = HD * 4 // nz
    per = half // tq
    sizes = (nb, nh, rows, cw, units, heads, dph, tq)

    ins = dict(
        lens=lengths, tok=tokens, cot=cotangent, v0=ln1_gain[None], v1=ln1_bias[None], v2=gate1_bias[None],
        v3=ln2_gain[None], v4=ln2_bias[None], v5=gate2_bias[None], wq=w_query, wk=w_key, wv=w_value,
        wo=w_out, wg1=gate1_weight, wg2=gate2_weight, wu=w_up, wd=w_down,
    )
    outs = dict(
        out_c=((rows, cw), BF16),
        gtok=((rows, cw), F32),
        red_a=((2, 2, quarter, units), BF16),
        red_s=((2, 2, 2, 3, HD, wide), BF16),
        red_v=((8, cw), F32),
    )
    bufs = dict(
        vsrc=((8, cw), F32), vecf=((8, wide), F32), tokf=((rows, wide), BF16), cotr=((half, wide), BF16),
        g1f=((2, wide, cw), BF16), g2f=((2, wide, cw), BF16), wof=((2, cw, wide), BF16),
        wup=((nz, 2, 2, cw, units), BF16), wdn=((nz, 2, 2, units, cw), BF16),
        wt=((heads, 3 * HD, wide), BF16), npair=((2, rows, wide), BF16),
        qsrc=((heads, HD, rows), BF16), kvsrc=((heads, 2 * HD, rows), BF16),
        kvt=((nh, 2 * HD, rows), BF16), kvn=((nh, rows, 2 * HD), BF16), qt=((nh, HD, tq), BF16),
        qlow=((nh, 2 * HD, tq), BF16), dhigh=((nh, 2 * HD, tq), BF16), top=((nh, 1, tq), F32), total=((nh, 1, tq), F32),
        centre=((nh, 1, tq), F32), dqa=((nh, HD, tq), F32), ot=((nh, HD, tq), F32), lse=((nh, 1, tq), F32), osend=((nh, HD, tq), BF16),
        att=((2 * heads * HD, half), BF16),
        pre=((nz, 2, half, units), F32), acts=((nz, half, units), BF16), actp=((nz, rows, units), BF16),
        gpres=((nz, half, units), BF16), gprep=((nz, rows, units), BF16),
        outr=((half, wide), BF16), gatt=((wide, half), BF16), dot=((nh, HD, tq), BF16),
        ginp=((half, wide), F32), gterm=((half, wide), F32), npt=((wide, rows), BF16), gbt=((wide, rows), BF16),
        lsrc=((3, wide, half), BF16), bpair=((3, rows, wide), BF16), apair=((3, 2, quarter, rows), BF16),
        vsum=((8, wide), F32),
        gb=((2, 2, 3, HD, wide), BF16), ybin=((2, 3, HD, wide), BF16), xbin=((3, HD, wide), BF16),
        ga=((2, nz, 2, 2, quarter, units), BF16), xin0=((nz, 2, quarter, units), BF16),
        yin1=((nz, 2, quarter, units), BF16), yin0=((nz, quarter, units), BF16), xin1=((nz, quarter, units), BF16),
        zs=((nz, 2, quarter, units), BF16), zin=((nz, 2, quarter, units), BF16),
        pin=((pairs, 2, quarter, units), BF16),
        gc=((2, 3, HD, wide), BF16), ycin=((3, HD, wide), BF16), sq=((2, 3, HD, wide), BF16),
        sqin=((1, 3, nz - 1, zr, 128), BF16), pzin=((2, 3, nz, zr, 128), BF16), sqpair=((2, 3, pairs, zr, 128), BF16),
        acc=((nh, 2 * HD, rows), F32), pin_kv=((nh // dph, max(dph - 1, 1), 2 * HD, rows), F32),
        dkvsend=((nh, 2 * HD, rows), BF16), dqsend=((nh, HD, tq), BF16),
        dqkv=((heads, 3 * HD, rows), BF16), dsib=((heads // 2, 3 * HD, rows), BF16),
        psend=((half, wide), BF16), precv=((half, wide), BF16),
        tsend=((half, wide), BF16), trecv=((half, cw), BF16),
        vin4=((4, 8, wide), F32), vinz=((nz, 8, wide), F32), vinb=((nb, 8, wide), F32),
    )
    sems = dict(
        xs=(10,), xr=(10,), wzs=(2, nz), wzr=(nz,), gxs=(3,), gxr=(3,), gcs=(3,), gcr=(3,),
        ks=(heads, 2), kr=(nh, 2), qs=(heads, dph), qr=(nh,), cs=(12,), cr=(12,),
        wxs=(nz,), wxr=(nz,), wys=(nz, 2), wyr=(nz, 2), wcs=(2,), wcr=(2,),
        fs=(nh, dph), fr=(nh,), osd=(nh,), orc=(2 * heads, per),
        as_=(nz,), ar=(nz,), ps_=(nz,), pr=(nz,), ds=(2, heads, per), dr=(nh,),
        ys=(5,), yr=(5,), zss=(nz,), zsr=(nz,), pas=(pairs,), par=(pairs,),
        sqs=(1, 3, nz), sqr=(1, 3, nz), sqps=(2, 3, pairs), sqpr=(2, 3, pairs), sgs=(1, 3, nz), sgr=(1, 3, nz),
        pys=(3,), pyr=(3,), pzs=(2, 3, nz), pzr=(2, 3, nz), pgs=(2, 3, nz), pgr=(2, 3, nz),
        sxs=(3,), sxr=(3,), sys=(3,), syr=(3,), sbs=(2, 3), sbr=(2, 3), scs=(2, 3), scr=(2, 3),
        pks=(nh,), pkr=(nh // dph, max(dph - 1, 1)), dqs=(nh,), dqr=(heads, dph), dks=(nh,), dkr=(heads,),
        ts=(heads,), tr=(heads // 2,), v4s=(3,), v4r=(4,), vzs=(nz,), vzr=(nz,), vbs=(nb,), vbr=(nb,),
    )
    names = list(ins) + list(outs) + list(bufs) + list(sems)
    vmem = pl.BlockSpec(memory_space=pltpu.VMEM)
    results = pl.pallas_call(
        functools.partial(layer_kernel, names, sizes),
        out_shape=[jax.ShapeDtypeStruct(shape, kind) for shape, kind in outs.values()],
        in_specs=[pl.BlockSpec(memory_space=pltpu.SMEM)] + [vmem] * (len(ins) - 1),
        out_specs=[vmem] * len(outs),
        scratch_shapes=[pltpu.VMEM(shape, kind) for shape, kind in bufs.values()]
        + [pltpu.SemaphoreType.DMA(shape) for shape in sems.values()],
        compiler_params=pltpu.CompilerParams(
            collective_id=1, has_side_effects=True, vmem_limit_bytes=VMEM_LIMIT
        ),
        cost_estimate=pl.CostEstimate(flops=10**10, bytes_accessed=10**7, transcendentals=10**7),
    )(*ins.values())
    grads = [
        ((rows, cw), BF16), ((rows, cw), F32), ((1, cw), F32), ((1, cw), F32),
        ((wide, cw), F32), ((wide, cw), F32), ((wide, cw), F32), ((cw, wide), F32),
        ((wide, cw), F32), ((1, cw), F32), ((1, cw), F32), ((1, cw), F32), ((wide, cw), F32), ((1, cw), F32),
        ((cw, units), F32), ((units, cw), F32),
    ]
    done = pl.pallas_call(
        functools.partial(final_kernel, heads),
        out_shape=[jax.ShapeDtypeStruct(shape, kind) for shape, kind in grads],
        in_specs=[vmem] * len(outs),
        out_specs=[vmem] * len(grads),
        compiler_params=pltpu.CompilerParams(vmem_limit_bytes=VMEM_LIMIT),
    )(*results)
    return tuple(a[0] if a.shape[0] == 1 else a for a in done)


def solution(mesh):
    cols = P(None, "width")
    vec = P("width")
    in_specs = (
        P(("batch", "hidden"), "width"), vec, vec, cols, cols, cols, P("width", None), cols, vec, vec, vec,
        cols, vec, P("width", "hidden"), P("hidden", "width"), P("batch", None),
        P(("batch", "hidden"), "width"),
    )
    out_specs = (
        P(("batch", "hidden"), "width"), P(("batch", "hidden"), "width"), vec, vec, cols, cols, cols,
        P("width", None), cols, vec, vec, vec, cols, vec, P("width", "hidden"), P("hidden", "width"),
    )
    return jax.shard_map(local, mesh=mesh, in_specs=in_specs, out_specs=out_specs, check_vma=False)
```

```python
import functools
import math
import types

import jax
import jax.numpy as jnp
from jax import lax
from jax.experimental import pallas as pl
from jax.experimental.pallas import tpu as pltpu
from jax.sharding import PartitionSpec as P

HD = 64
EPSILON = 1e-05
MESH = pl.DeviceIdType.MESH
F32 = jnp.float32
BF16 = jnp.bfloat16
NEG = -1e30
VMEM_LIMIT = 62 * 1024 * 1024
PLAN = {
    "begin": ("a1",), "row0": (), "col0": ("bx",), "row1": (), "col1": ("bz",), "row2": ("a2",), "col2": (),
    "loop": ("a3", "bg"), "whole": (), "sent": (), "proj": ("cy", "a4"), "half": ("cz",),
    "norm": ("bb",), "vec": ("cg", "a5"), "rows": (), "last": ("bc", "cb"), "end": ("cc",),
}
SCALE = HD**-0.5


def nn(a, b):
    return lax.dot_general(a, b, (((1,), (0,)), ((), ())), preferred_element_type=F32)


def nt(a, b):
    return lax.dot_general(a, b, (((1,), (1,)), ((), ())), preferred_element_type=F32)


def flip(a):
    return a.astype(F32).T.astype(BF16)


def remote(src, dst, send, recv, dev):
    return pltpu.make_async_remote_copy(
        src_ref=src, dst_ref=dst, send_sem=send, recv_sem=recv, device_id=dev, device_id_type=MESH
    )


def await_copy(ref, sem):
    pltpu.make_async_copy(ref, ref, sem).wait()


def at(index, size):
    return pl.ds(pl.multiple_of(index * size, size), size)


def sub_row(index, sub, dph):
    return jnp.where(lax.rem(index, 2) == 0, sub, dph - 1 - sub)


def segments(pos, ends):
    total = jnp.zeros(pos.shape, jnp.int32)
    for end in ends:
        total = total + (pos >= end).astype(jnp.int32)
    return total


def allowed_mask(key_base, query_base, keys, queries, ends):
    key_pos = key_base + lax.broadcasted_iota(jnp.int32, (keys, 1), 0)
    query_pos = query_base + lax.broadcasted_iota(jnp.int32, (1, queries), 1)
    same = segments(key_pos, ends) == segments(query_pos, ends)
    return same & (key_pos <= query_pos)


def sigmoid(x):
    return 1.0 / (1.0 + jnp.exp(-x))


def nbytes(ref):
    return math.prod(ref.shape) * ref.dtype.itemsize


class Sends:
    def __init__(self, sems, tally):
        self.sems, self.tally = sems, tally
        self.bytes = {}
        self.items = []

    def sem(self, group):
        return self.sems.at[group]

    def count(self, group, *sizes):
        self.bytes[group] = self.bytes.get(group, 0) + sum(sizes)

    def go(self, src, dst, recv, dev, group=0):
        copy = remote(src, dst, self.sem(group), recv, dev)
        copy.start()
        self.count(group, nbytes(src))
        return copy

    def start_if(self, cond, copy):
        @pl.when(cond)
        def _():
            copy.start()

        self.items.append((cond, copy))

    def wait(self, group, size):
        await_copy(self.tally.at[pl.ds(0, size // 512)], self.sem(group))

    def finish(self):
        for group, size in self.bytes.items():
            self.wait(group, size)
        for cond, copy in self.items:

            @pl.when(cond)
            def _(copy=copy):
                copy.wait_send()


def layer_kernel(names, sizes, *refs):
    r = types.SimpleNamespace(**dict(zip(names, refs)))
    nb, nh, rows, cw, units, heads, dph, tq = sizes
    half, wide, nz = rows // 2, 2 * cw, nh // 2
    per = half // tq
    pairs = nb // 2
    hops = nz.bit_length() - 1
    b, h, w = lax.axis_index("batch"), lax.axis_index("hidden"), lax.axis_index("width")
    group, sub = lax.div(h, dph), lax.rem(h, dph)
    z, c, bp = lax.div(h, 2), lax.rem(h, 2), lax.rem(b, 2)
    x_dev = (b, h, 1 - w)
    c_dev = (b, h + 1 - 2 * c, w)
    y_dev = (b + 1 - 2 * bp, h, w)

    def z_dev(k):
        zz = lax.rem(z + k, nz)
        return zz, (b, 2 * zz + c, w)

    own, other = at(w, cw), at(1 - w, cw)
    mine, theirs = at(w, half), at(1 - w, half)
    lanes = at(c, half)
    ends = [
        r.lens[0, 0],
        r.lens[0, 0] + r.lens[0, 1],
        r.lens[0, 0] + r.lens[0, 1] + r.lens[0, 2],
    ]
    sends = Sends(r.snd, r.tally)
    SUMS, LOOPS, ROWS, WEIGHTS, BACK = 3, 4, 5, 6, 7

    barrier = pltpu.get_barrier_semaphore()
    count = 0
    for dw in range(2):
        for dh in range(nh):
            if dh or dw:
                dev = (b, lax.rem(h + dh, nh), lax.rem(w + dw, 2))
                pl.semaphore_signal(barrier, inc=1, device_id=dev, device_id_type=MESH)
                count += 1
    for db in range(1, nb):
        dev = (lax.rem(b + db, nb), h, w)
        pl.semaphore_signal(barrier, inc=1, device_id=dev, device_id_type=MESH)
        count += 1
    loads = dict(
        tok0=(r.tok.at[pl.ds(0, half)], r.tokf.at[pl.ds(0, half), own]),
        tok1=(r.tok.at[pl.ds(half, half)], r.tokf.at[pl.ds(half, half), own]),
        wu=(r.wu, r.wup.at[z, c, w]), wd=(r.wd, r.wdn.at[z, c, w]),
        wq=(r.wq, r.wqkv.at[0]), wk=(r.wk, r.wqkv.at[1]), wv=(r.wv, r.wqkv.at[2]),
        wg1=(r.wg1, r.g1f.at[w]), wg2=(r.wg2, r.g2f.at[w]), wo=(r.wo, r.wof.at[w]),
        cot=(r.cot.at[mine], r.cotr.at[:, own]),
    )
    shared = dict(tok0=0, tok1=1, wu=2, wd=2, wq=3, wk=3, wv=3, wg1=4, wg2=4, wo=4, cot=5)
    for name, (src, dst) in loads.items():
        pltpu.make_async_copy(src, dst, r.ls.at[shared[name]]).start()
    for i, vec in enumerate((r.v0, r.v1, r.v2, r.v3, r.v4, r.v5)):
        r.vsrc[i : i + 1, :] = vec[...]
    pl.semaphore_wait(barrier, count)

    vcopy = sends.go(r.vsrc, r.vecf.at[:, own], r.xr.at[0], x_dev)
    tcopies = []
    for k in range(2):
        block = r.tokf.at[pl.ds(k * half, half), own]
        await_copy(block, r.ls.at[k])
        tcopies.append(sends.go(block, block, r.xr.at[1 + k], x_dev))
    await_copy(r.wup.at[z, c], r.ls.at[2])

    def weight_blocks(distance):
        for kind, buf in enumerate((r.wup, r.wdn)):
            for step in (1, -1) if distance else (1,):
                zz = z - step * distance
                index = jnp.clip(zz, 0, nz - 1)
                yield (zz >= 0) & (zz < nz) & (bp == kind), index, buf, step

    def weight_hop(k, ending=False):
        for here, index, buf, step in weight_blocks(k - 1):
            for way in (1, -1) if k == 1 else (step,):
                onward = (z + way >= 0) & (z + way < nz)
                going = here & (jnp.logical_not(onward) if ending else onward)
                block = buf.at[index, c, w]
                if k > 1:

                    @pl.when(going)
                    def _(block=block, index=index):
                        await_copy(block, r.wzr.at[index])
                        remote(block, block, sends.sem(WEIGHTS), r.wxr.at[index], x_dev).start()
                        remote(block, block, sends.sem(WEIGHTS), r.wyr.at[0], y_dev).start()

                if not ending:
                    dev = (b, 2 * jnp.clip(z + way, 0, nz - 1) + c, w)
                    copy = remote(block, block, r.wzs.at[(1 - way) // 2, k], r.wzr.at[index], dev)
                    sends.start_if(going, copy)

    def weight_cross(distance):
        for here, index, buf, _ in weight_blocks(distance):

            @pl.when(here)
            def _(index=index, buf=buf):
                block = buf.at[index, c, 1 - w]
                await_copy(block, r.wxr.at[index])
                remote(block, block, sends.sem(WEIGHTS), r.wyr.at[0], y_dev).start()

    for here, index, buf, _ in weight_blocks(0):
        block = buf.at[index, c, w]
        copy = remote(block, block, sends.sem(WEIGHTS), r.wxr.at[index], x_dev)

        @pl.when(here)
        def _(copy=copy):
            copy.start()

    weight_hop(1)
    gates = ((r.wg1, r.g1f), (r.wg2, r.g2f), (r.wo, r.wof))
    r.vecf[:, own] = r.vsrc[...]

    await_copy(r.wqkv, r.ls.at[3])
    for i in range(3):
        turned = flip(r.wqkv[i])
        for t in range(heads):
            r.wt[t, i * HD : (i + 1) * HD, :] = turned[t * HD : (t + 1) * HD]

    vcopy.wait_recv()
    gain, shift = r.vecf[0:1, :], r.vecf[1:2, :]

    def project(k):
        part = slice(k * half, (k + 1) * half)
        tcopies[k].wait_recv()
        x = r.tokf[part, :].astype(F32)
        centre = x - jnp.mean(x, -1, keepdims=True)
        spread = jnp.mean(centre * centre, -1, keepdims=True)
        n = (centre * lax.rsqrt(spread + EPSILON) * gain + shift).astype(BF16)
        r.npair[c, part, :] = n
        for t in range(heads):
            qkv = nt(r.wt[t], n).astype(BF16)
            r.qsrc[t, :, part] = qkv[:HD]
            r.kvsrc[t, :, part] = qkv[HD:]

    def head_copies(step, k):
        t = lax.rem(group + step, heads)
        span = pl.ds(k * half, half)
        src, dst = r.kvsrc.at[t, :, span], r.kvt.at[h, :, span]
        if step:
            yield None, remote(src, dst, sends.sem(LOOPS), r.kr.at[h], (b, t * dph + sub, w))
        else:
            yield None, pltpu.make_async_copy(src, dst, r.kr.at[h])
        for i in range(per):
            row = k * per + i
            target = sub_row(h, row, dph)
            src, dst = r.qsrc.at[t, :, pl.ds(row * tq, tq)], r.qt.at[h]
            copy = remote(src, dst, sends.sem(LOOPS), r.qr.at[h], (b, t * dph + target, w))
            if step:
                yield None, copy
            else:
                yield target != sub, copy
                yield target == sub, pltpu.make_async_copy(src, dst, r.qr.at[h])

    def send_heads(step, k):
        for cond, copy in head_copies(step, k):
            if cond is None:
                copy.start()
            else:

                @pl.when(cond)
                def _(copy=copy):
                    copy.start()

    project(0)
    weight_hop(2)
    weight_hop(2, ending=True)
    send_heads(heads - 1, 0)
    project(1)
    send_heads(heads - 1, 1)
    for k in range(2):
        send_heads(0, k)

    def sends_of(count, buf, sem):
        await_copy(r.tally.at[pl.ds(0, count * nbytes(buf.at[0, 0, 0]) // 512)], sem)

    def weights_over_core():
        for kind, buf in enumerate((r.wup, r.wdn)):

            @pl.when(bp != kind)
            def _(buf=buf):
                sends_of(2 * nz - 1, buf, r.wyr.at[0])

            block = buf.at[:, c]
            sends.go(block, block, r.wcr.at[kind], c_dev, 1)

    def gates_over_core():
        for i, (src, dst) in enumerate(gates):
            piece = dst.at[1 - w, at(c, src.shape[0] // 2)]
            if i == 0:
                await_copy(r.tally.at[pl.ds(0, 3 * nbytes(piece) // 512)], r.gxr.at[0])
            sends.go(piece, piece, r.gcr.at[0], c_dev)

    def weights_sent():
        sends.wait(WEIGHTS, (3 * nz - 1) * nbytes(r.wu))

    def pass_on(s):
        @pl.when(lax.rem(s, dph) == sub)
        def _():
            await_copy(r.kvt.at[s], r.kr.at[s])
            for k in range(1, dph):
                dev = (b, group * dph + lax.rem(sub + k, dph), w)
                remote(r.kvt.at[s], r.kvt.at[s], sends.sem(LOOPS), r.fr.at[s], dev).start()

    def arrive(s):
        @pl.when(lax.rem(s, dph) != sub)
        def _():
            await_copy(r.kvt.at[s], r.fr.at[s])

        r.kvn[s] = flip(r.kvt[s])
        await_copy(r.qt.at[s], r.qr.at[s])
        q = r.qt[s].astype(F32) * SCALE
        r.qlow[s] = jnp.concatenate([q, jnp.zeros_like(q)], 0).astype(BF16)

    def masked(scores, i, j):
        query_base = i * rows + sub_row(i, sub, dph) * tq
        return jnp.where(allowed_mask(j * rows, query_base, rows, tq, ends), scores, NEG)

    def bias(scores, j):
        key_pos = j * rows + lax.broadcasted_iota(jnp.int32, (rows, 1), 0)
        return scores + jnp.where(key_pos < ends[0], NEG, 0.0)

    def absorb(i, blocks):
        top = r.top[i]
        new_top = top
        for scores, _ in blocks:
            new_top = jnp.maximum(new_top, jnp.max(scores, 0, keepdims=True))
        fade = jnp.exp(top - new_top)
        total, mixed = r.total[i] * fade, r.ot[i] * fade
        for scores, j in blocks:
            weights = jnp.exp(scores - new_top)
            total = total + jnp.sum(weights, 0, keepdims=True)
            mixed = mixed + nn(r.kvt[j, HD:, :], weights.astype(BF16))
        r.top[i], r.total[i], r.ot[i] = new_top, total, mixed

    def send_attended(s):
        row = sub_row(s, sub, dph)
        total = r.total[s]
        mixed = r.ot[s] / total
        r.ot[s] = mixed
        r.lse[s] = r.top[s] + jnp.log(total)
        r.osend[s] = mixed.astype(BF16)
        row_w = lax.div(row * tq, half)
        lane = lax.rem(row * tq, half)
        dst = r.att.at[at(w * heads + group, HD), pl.ds(pl.multiple_of(lane, tq), tq)]
        slot = r.orc.at[0]
        here = (s == h) & (row_w == w)

        @pl.when(here)
        def _():
            pltpu.make_async_copy(r.osend.at[s], dst, slot).start()

        @pl.when(jnp.logical_not(here))
        def _():
            remote(r.osend.at[s], dst, sends.sem(ROWS), slot, (b, s, row_w)).start()

    def own_chip(n):
        i = 2 * n
        first = masked(nn(r.kvn[i], r.qlow[i]), i, i)
        low = masked(nn(r.kvn[i], r.qlow[i + 1]), i + 1, i)
        high = masked(nn(r.kvn[i + 1], r.qlow[i + 1]), i + 1, i + 1)
        absorb(i, [(first, i)])
        absorb(i + 1, [(low, i), (high, i + 1)])

    def two_chips(hi, lo, last):
        queries, keys = (2 * hi, 2 * hi + 1), (2 * lo, 2 * lo + 1)
        scores = [[nn(r.kvn[j], r.qlow[i]) for j in keys] for i in queries]
        for a, i in enumerate(queries):
            if last and a:
                blocks = [(masked(x, i, j), j) for x, j in zip(scores[a], keys)]
            else:
                blocks = [(bias(scores[a][0], keys[0]), keys[0]), (scores[a][1], keys[1])]
            absorb(i, blocks)

    def completes(chip):
        return jnp.where(z == 0, chip, nz - z + jnp.minimum(chip, z - 1))

    def chip_at(d):
        return lax.rem(z + d, nz)

    def stage_passes(d):
        pass_on(2 * chip_at(d))
        pass_on(2 * chip_at(d) + 1)

    def stage_computes(d):
        n = chip_at(d)
        arrive(2 * n)
        arrive(2 * n + 1)
        own_chip(n)

        def with_earlier(e, _):
            @pl.when((d == nz - 1) & (e == 1))
            def _():
                weight_cross(nz - 1)

            m = lax.rem(z + e, nz)
            hi, lo = jnp.maximum(n, m), jnp.minimum(n, m)

            @pl.when(hi == nz - 1)
            def _():
                two_chips(hi, lo, True)

            @pl.when(hi != nz - 1)
            def _():
                two_chips(hi, lo, False)

            @pl.when((m > n) & (completes(m) == d))
            def _():
                send_attended(2 * m)
                send_attended(2 * m + 1)

            return 0

        lax.fori_loop(0, d, with_earlier, 0)

        @pl.when(completes(n) == d)
        def _():
            send_attended(2 * n)
            send_attended(2 * n + 1)

    def late_stage(d, _):
        stage_passes(d)

        @pl.when(d == 2)
        def _():
            for distance in range(2):
                weight_cross(distance)

        @pl.when(d == nz - 1)
        def _():
            weight_hop(nz, ending=True)
            for distance in range(2, nz - 1):
                weight_cross(distance)

        stage_computes(d)
        return 0

    r.top[...] = jnp.full_like(r.top, NEG)
    r.total[...] = jnp.zeros_like(r.total)
    r.ot[...] = jnp.zeros_like(r.ot)
    stage_passes(0)
    stage_computes(0)
    for k in range(2):
        send_heads(2, k)
    await_copy(r.wqkv, r.ls.at[4])
    for src, dst in gates:
        block = dst.at[w, at(c, src.shape[0] // 2)]
        sends.go(block, block, r.gxr.at[0], x_dev)
    sends.go(r.npair.at[c], r.npair.at[c], r.cr.at[0], c_dev)
    stage_passes(1)
    for k in range(3, nz):
        weight_hop(k)
    for k in range(3, nz):
        weight_hop(k, ending=True)
    for k in range(2):
        send_heads(1, k)
    stage_computes(1)
    await_copy(r.cotr.at[:, own], r.ls.at[5])
    sends.go(r.cot.at[theirs], r.cotr.at[:, own], r.xr.at[3], x_dev)
    lax.fori_loop(2, nz, late_stage, 0)
    gates_over_core()
    weights_over_core()

    await_copy(r.tally.at[pl.ds(0, 3 * nbytes(r.wg1) // 1024)], r.gcr.at[0])

    def two(a, weight):
        return jnp.concatenate([nn(a, weight[0]), nn(a, weight[1])], 1)

    def two_back(g, weight):
        return nt(g[:, :cw], weight[0]) + nt(g[:, cw:], weight[1])

    tok = r.tokf[mine, :].astype(F32)
    n1 = r.npair[c, mine, :]
    gate_one = sigmoid(two(n1, r.g1f) + r.vecf[2:3, :])
    await_copy(r.att, r.orc.at[0])
    wof = r.wof[...].reshape(wide, wide)
    branch_one = nn(flip(r.att[...]), wof)
    middle = tok + gate_one * (branch_one - tok)
    centre = middle - jnp.mean(middle, -1, keepdims=True)
    rstd = lax.rsqrt(jnp.mean(centre * centre, -1, keepdims=True) + EPSILON)
    n2 = centre * rstd
    gain_two = r.vecf[3:4, :]
    normed_two = (n2 * gain_two + r.vecf[4:5, :]).astype(BF16)
    gate_two = sigmoid(two(normed_two, r.g2f) + r.vecf[5:6, :])
    for kind, buf in enumerate((r.wup, r.wdn)):
        await_copy(buf.at[:, 1 - c], r.wcr.at[kind])

    def units_of(i2, p):
        return i2, lax.rem(c + p, 2)

    def up(i2, branch):
        for p in range(2):
            i, q = units_of(i2, p)
            pre = nn(normed_two, r.wup[i, q].reshape(wide, units))
            r.pre[i2, p] = pre
            act = jax.nn.gelu(pre).astype(BF16)
            r.actall[:, pl.ds(pl.multiple_of((2 * i + q) * units, units), units)] = act
            if p:
                r.acts[i2] = act
                dst = r.actp.at[i2, lanes, :]
                remote(r.acts.at[i2], dst, sends.sem(LOOPS), r.ar.at[0], c_dev).start()
            else:
                r.actp[i2, lanes, :] = act
        return branch

    lax.fori_loop(0, nz, up, 0)
    deep = nh * units
    branch_two = jnp.concatenate([nn(r.actall[...], r.wdn[:, :, v].reshape(deep, cw)) for v in range(2)], 1)
    delta = branch_two - middle
    r.outr[...] = (middle + gate_two * delta).astype(BF16)
    ocopy = sends.go(r.outr.at[:, other], r.out_c.at[mine, :], r.xr.at[4], x_dev)
    await_copy(r.cotr.at[:, own], r.xr.at[3])
    grad = r.cotr[...].astype(F32)
    gb2 = (grad * gate_two).astype(BF16)
    gl2 = (grad * delta * gate_two * (1.0 - gate_two)).astype(BF16)
    gmid = grad * (1.0 - gate_two)

    def down(i2, total):
        for p in range(2):
            i, q = units_of(i2, p)
            ghid = nt(gb2[:, :cw], r.wdn[i, q, 0]) + nt(gb2[:, cw:], r.wdn[i, q, 1])
            pre = r.pre[i2, p]
            k = 0.7978845608028654
            t = jnp.tanh(k * (pre + 0.044715 * pre * pre * pre))
            slope = 0.5 * (1.0 + t) + 0.5 * pre * (1.0 - t * t) * (k * (1.0 + 3 * 0.044715 * pre * pre))
            gpre = (ghid * slope).astype(BF16)
            total = total + nt(gpre, r.wup[i, q].reshape(wide, units))
            if p:
                r.gpres[i2] = gpre
                dst = r.gprep.at[i2, lanes, :]
                remote(r.gpres.at[i2], dst, sends.sem(LOOPS), r.pr.at[0], c_dev).start()
            else:
                r.gprep[i2, lanes, :] = gpre
        return total

    gnorm = lax.fori_loop(0, nz, down, two_back(gl2, r.g2f))
    e = gnorm * gain_two
    gmid = gmid + rstd * (
        e - jnp.mean(e, -1, keepdims=True) - n2 * jnp.mean(e * n2, -1, keepdims=True)
    )
    gb1 = (gmid * gate_one).astype(BF16)
    r.gatt[...] = nt(wof, gb1).astype(BF16)
    for dw in (1, 0):
        wt = lax.rem(w + dw, 2)
        for step in range(heads - 1, -1, -1):
            t = lax.rem(group + step, heads)
            for i in range(per):
                target = sub_row(h, w * per + i, dph)
                src = r.gatt.at[at(wt * heads + t, HD), pl.ds(i * tq, tq)]
                dst = r.dot.at[h]
                dev = (b, t * dph + target, wt)
                slot = r.dr.at[jnp.where(h == nh - 1, 1, 0)]
                copy = remote(src, dst, sends.sem(ROWS), slot, dev)
                if step or dw:
                    copy.start()
                else:

                    @pl.when(target != sub)
                    def _(copy=copy):
                        copy.start()

                    @pl.when(target == sub)
                    def _(src=src, dst=dst, slot=slot):
                        pltpu.make_async_copy(src, dst, slot).start()

    gl1 = (gmid * (branch_one - tok) * gate_one * (1.0 - gate_one)).astype(BF16)
    r.ginp[...] = gmid * (1.0 - gate_one)
    r.npt[:, lanes] = flip(normed_two)
    sends.go(r.npt.at[:, lanes], r.npt.at[:, lanes], r.cr.at[1], c_dev)
    r.gbt[:, lanes] = flip(gb2)
    sends.go(r.gbt.at[:, lanes], r.gbt.at[:, lanes], r.cr.at[1], c_dev)
    quarter = half // 2
    r.lsrc[0] = r.att[...]
    r.lsrc[1] = flip(gl1)
    r.lsrc[2] = flip(gl2)
    for m, right in enumerate((gb1, n1, normed_two)):
        r.bpair[m, lanes, :] = right
        block = r.bpair.at[m, lanes, :]
        sends.go(block, block, r.cr.at[2], c_dev, 2)
        for v in range(2):
            src = r.lsrc.at[m, at(2 * v + 1 - c, quarter), :]
            dst = r.apair.at[m, v, :, lanes]
            sends.go(src, dst, r.cr.at[2], c_dev, 2)
            r.apair[m, v, :, lanes] = r.lsrc[m, at(2 * v + c, quarter), :]
    r.gterm[...] = two_back(gl1, r.g1f)
    r.vsum[...] = jnp.zeros_like(r.vsum)
    r.vsum[2:3, :] = jnp.sum(gl1.astype(F32), 0, keepdims=True)
    r.vsum[3:4, :] = jnp.sum(gnorm * n2, 0, keepdims=True)
    r.vsum[4:5, :] = jnp.sum(gnorm, 0, keepdims=True)
    r.vsum[5:6, :] = jnp.sum(gl2.astype(F32), 0, keepdims=True)
    r.out_c[mine, :] = r.outr[:, own]

    eighth = quarter // 2
    await_copy(r.npt, r.cr.at[1])
    await_copy(r.gpres, r.pr.at[0])
    await_copy(r.acts, r.ar.at[0])

    def weight_grads(i2, _):
        r.ga[0, i2] = nn(r.npt[...], r.gprep[i2]).astype(BF16).reshape(2, 2, quarter, units)
        r.ga[1, i2] = nn(r.gbt[...], r.actp[i2]).astype(BF16).reshape(2, 2, quarter, units)
        return 0

    lax.fori_loop(0, nz, weight_grads, 0)
    sends.go(r.ga.at[0, :, 1 - w], r.xin0, r.xr.at[5], x_dev, 2)
    pair_bytes = 3 * (nbytes(r.bpair.at[0, lanes, :]) + 2 * nbytes(r.apair.at[0, 0, :, lanes]))
    await_copy(r.tally.at[pl.ds(0, pair_bytes // 512)], r.cr.at[2])
    for m in range(3):
        for v in range(2):
            block = nn(r.apair[m, v], r.bpair[m]).astype(BF16)
            for y in range(2):
                r.gb[v, y, m] = block[y * eighth : (y + 1) * eighth]
    for m in range(3):
        sends.go(r.gb.at[:, 1 - bp, m], r.ybin.at[:, m], r.syr.at[0], y_dev, 2)


    def z_block(q, flip_bit, v):
        bit = lax.rem(lax.div(z, 1 << q), 2)
        bit = 1 - bit if flip_bit else bit
        return lax.rem(z, 1 << q) + bit * (1 << q) + v * (2 << q)

    def ffn_first():
        remote(r.ga.at[1, :, :, 1 - bp], r.yin1, sends.sem(SUMS), r.yr.at[1], y_dev).start()

    def ffn_second():
        await_copy(r.xin0, r.xr.at[5])
        r.ga[0, :, w] = (r.ga[0, :, w].astype(F32) + r.xin0[...].astype(F32)).astype(BF16)
        remote(r.ga.at[0, :, w, 1 - bp], r.yin0, sends.sem(SUMS), r.yr.at[2], y_dev).start()
        await_copy(r.yin1, r.yr.at[1])
        r.ga[1, :, :, bp] = (r.ga[1, :, :, bp].astype(F32) + r.yin1[...].astype(F32)).astype(BF16)
        remote(r.ga.at[1, :, 1 - w, bp], r.xin1, sends.sem(SUMS), r.xr.at[6], x_dev).start()

    def ffn_third():
        await_copy(r.yin0, r.yr.at[2])
        await_copy(r.xin1, r.xr.at[6])
        r.zs[:, 0] = (r.ga[0, :, w, bp].astype(F32) + r.yin0[...].astype(F32)).astype(BF16)
        r.zs[:, 1] = (r.ga[1, :, w, bp].astype(F32) + r.xin1[...].astype(F32)).astype(BF16)
        ffn_hop(0)

    def ffn_hop(q):
        if q:
            ffn_add(q - 1)
        bit = lax.rem(lax.div(z, 1 << q), 2)
        dev = (b, 2 * (z + (1 << q) * (1 - 2 * bit)) + c, w)
        for v in range(nz >> (q + 1)):
            slot = nz - (nz >> q) + v
            remote(r.zs.at[z_block(q, True, v)], r.zin.at[slot], sends.sem(SUMS), r.zsr.at[slot], dev).start()

    def ffn_add(q):
        for v in range(nz >> (q + 1)):
            slot = nz - (nz >> q) + v
            await_copy(r.zin.at[slot], r.zsr.at[slot])
            kept = z_block(q, False, v)
            r.zs[kept] = (r.zs[kept].astype(F32) + r.zin[slot].astype(F32)).astype(BF16)

    def ffn_fourth():
        ffn_add(hops - 1)
        total = r.zs[z].astype(F32)
        if pairs > 1:
            mypair = lax.div(b, 2)
            r.pin[mypair] = total.astype(BF16)
            for k in range(1, pairs):
                dev = (lax.rem(b + 2 * k, nb), h, w)
                block = r.pin.at[mypair]
                remote(block, block, sends.sem(SUMS), r.par.at[mypair], dev).start()
            for k in range(1, pairs):
                pp = lax.rem(mypair + k, pairs)
                await_copy(r.pin.at[pp], r.par.at[pp])
            total = r.pin[0].astype(F32)
            for k in range(1, pairs):
                total = total + r.pin[k].astype(F32)
        r.red_a[bp] = total.astype(BF16)
        block = r.red_a.at[bp]
        remote(block, block, sends.sem(SUMS), r.yr.at[3], y_dev).start()

    def sums_sent():
        sends.count(SUMS, nbytes(r.yin1), nbytes(r.yin0), nbytes(r.xin1), nbytes(r.red_a.at[0]))
        sends.count(SUMS, (nz - 1) * nbytes(r.zin.at[0]), (pairs - 1) * nbytes(r.pin.at[0]))
        sends.count(SUMS, nbytes(r.xbin), nbytes(r.ycin), 2 * nbytes(r.ycin), nbytes(r.red_s) // 2)
        sends.count(SUMS, 6 * (2 * (nz - 1) + pairs - 1) * nbytes(r.pzin.at[0, 0, 0]))

    zr = HD * 4 // nz

    def z_part(zz):
        return pl.ds(pl.multiple_of(lax.div(zz, 4) * zr, zr), zr), at(lax.rem(zz, 4), 128)

    def square_x():
        await_copy(r.ybin, r.syr.at[0])
        for p in range(3):
            r.gb[:, bp, p] = (r.gb[:, bp, p].astype(F32) + r.ybin[:, p].astype(F32)).astype(BF16)
            remote(r.gb.at[1 - w, bp, p], r.xbin.at[p], sends.sem(SUMS), r.sxr.at[0], x_dev).start()

    def over_pairs(which, p, total):
        if pairs == 1:
            return total
        mypair = lax.div(b, 2)
        r.sqpair[which, p, mypair] = total
        for k in range(1, pairs):
            dev = (lax.rem(b + 2 * k, nb), h, w)
            block = r.sqpair.at[which, p, mypair]
            remote(block, block, sends.sem(SUMS), r.sqpr.at[which, p, mypair], dev).start()
        for k in range(1, pairs):
            pp = lax.rem(mypair + k, pairs)
            await_copy(r.sqpair.at[which, p, pp], r.sqpr.at[which, p, pp])
        total = r.sqpair[which, p, 0].astype(F32)
        for k in range(1, pairs):
            total = total + r.sqpair[which, p, k].astype(F32)
        return total.astype(BF16)

    def scatter(which):
        for p in range(3):
            if which:
                await_copy(r.ycin.at[p], r.pyr.at[p])
                r.sq[1, p] = (r.gc[bp, p].astype(F32) + r.ycin[p].astype(F32)).astype(BF16)
            else:
                if p == 0:
                    await_copy(r.xbin, r.sxr.at[0])
                r.sq[0, p] = (r.gb[w, bp, p].astype(F32) + r.xbin[p].astype(F32)).astype(BF16)
            for k in range(nz - 1, 0, -1):
                zz, dev = z_dev(k)
                src, dst = r.sq.at[(which, p) + z_part(zz)], r.pzin.at[which, p, z]
                remote(src, dst, sends.sem(SUMS), r.pzr.at[which, p], dev).start()

    def gather(which):
        for p in range(3):
            total = r.sq[(which, p) + z_part(z)].astype(F32)
            await_copy(r.pzin.at[which, p, pl.ds(0, nz - 1)], r.pzr.at[which, p])
            for k in range(1, nz):
                zz, _ = z_dev(k)
                total = total + r.pzin[which, p, zz].astype(F32)
            block = (which, c, bp, p) + z_part(z)
            r.red_s[block] = over_pairs(which, p, total.astype(BF16))
            for k in range(nz - 1, 0, -1):
                _, dev = z_dev(k)
                ref = r.red_s.at[block]
                remote(ref, ref, sends.sem(SUMS), r.pgr.at[which, p], dev).start()

    def back(which):
        for p in range(3):
            await_copy(r.pzin.at[which, p, pl.ds(0, nz - 1)], r.pgr.at[which, p])
            block = r.red_s.at[which, c, bp, p]
            remote(block, block, sends.sem(SUMS), r.sbr.at[which, p], y_dev).start()

    def square_core(which):
        for p in range(3):
            await_copy(r.red_s.at[which, c, 1 - bp, p], r.sbr.at[which, p])
            block = r.red_s.at[which, c, :, p]
            remote(block, block, sends.sem(SUMS), r.scr.at[which], c_dev).start()

    def proj_y():
        for p in range(3):
            remote(r.gc.at[1 - bp, p], r.ycin.at[p], sends.sem(SUMS), r.pyr.at[p], y_dev).start()

    steps = dict(
        a1=ffn_first, a2=ffn_second, a3=ffn_third, a4=lambda: [ffn_hop(q) for q in range(1, hops)], a5=ffn_fourth,
        bx=square_x, bz=lambda: scatter(0), bg=lambda: gather(0), bb=lambda: back(0), bc=lambda: square_core(0),
        cy=proj_y, cz=lambda: scatter(1), cg=lambda: gather(1), cb=lambda: back(1), cc=lambda: square_core(1),
    )

    def take(point):
        for name in PLAN[point]:
            steps[name]()

    r.acc[...] = jnp.zeros_like(r.acc)

    def finish(s):
        @pl.when(lax.rem(s, dph) == sub)
        def _():
            total = r.acc[s]
            for k in range(1, dph):
                slot = r.pin_kv.at[lax.div(s, dph), k - 1]
                await_copy(slot, r.pkr.at[lax.div(s, dph), k - 1])
                total = total + r.pin_kv[lax.div(s, dph), k - 1]
            r.dkvsend[s, :HD] = (total[:HD] * SCALE).astype(BF16)
            r.dkvsend[s, HD:] = total[HD:].astype(BF16)
            dst = r.dqkv.at[group, pl.ds(HD, 2 * HD), :]

            @pl.when(s == h)
            def _():
                pltpu.make_async_copy(r.dkvsend.at[s], dst, r.dkr.at[group]).start()

            @pl.when(s != h)
            def _():
                remote(r.dkvsend.at[s], dst, sends.sem(BACK), r.dkr.at[group], (b, s, w)).start()

    def pairs_backward(where, full):
        scores = [nn(r.kvn[j], r.qlow[i]) for i, j in where]
        gprobs = [nn(r.kvn[j], r.dhigh[i]) for i, j in where]
        for x, gp, (i, j), whole in zip(scores, gprobs, where, full):
            x = masked(x, i, j) if whole else bias(x, j)
            probs = jnp.exp(x - r.lse[i])
            gscores = (probs * (gp - r.centre[i])).astype(BF16)
            r.acc[j, HD:, :] += nt(r.dhigh[i, HD:, :], probs.astype(BF16))
            r.acc[j, :HD, :] += nt(r.qt[i], gscores)
            r.dqa[i] += nn(r.kvt[j, :HD, :], gscores)

    def choose(kinds, where):
        taken = False
        for cond, full in kinds:

            @pl.when(jnp.logical_and(cond, jnp.logical_not(taken)))
            def _(full=full):
                pairs_backward(where, full)

            taken = jnp.logical_or(taken, cond)

    def pair_at(t, u):
        lo, hi = t, nh - 1 - t
        n = hi - lo + 1
        return jnp.where(u < n, hi, lo + u - n), jnp.where(u < n, lo + u, lo)

    def out_arrives(s):
        dout = r.dot[s]
        r.dhigh[s] = jnp.concatenate([jnp.zeros((HD, tq), BF16), dout], 0)
        r.centre[s] = jnp.sum(r.ot[s] * dout.astype(F32), 0, keepdims=True)

    def send_block(s):
        row = sub_row(s, sub, dph)
        r.dqsend[s] = (r.dqa[s] * SCALE).astype(BF16)
        dst = r.dqkv.at[group, pl.ds(0, HD), pl.ds(pl.multiple_of(row * tq, tq), tq)]

        @pl.when(s == h)
        def _():
            pltpu.make_async_copy(r.dqsend.at[s], dst, r.dkr.at[group]).start()

        @pl.when(s != h)
        def _():
            remote(r.dqsend.at[s], dst, sends.sem(BACK), r.dkr.at[group], (b, s, w)).start()

        owner = lax.rem(s, dph)

        @pl.when(owner != sub)
        def _():
            k = lax.rem(sub - owner + dph, dph)
            dev = (b, group * dph + owner, w)
            slot = lax.div(s, dph)
            remote(r.acc.at[s], r.pin_kv.at[slot, k - 1], sends.sem(BACK), r.pkr.at[slot, k - 1], dev).start()

    def round_backward(t, _):
        lo, hi = t, nh - 1 - t
        n = hi - lo + 1

        rowed = lax.div(n, 2)
        columned = rowed - 1

        def row_step(v, _):
            where = [pair_at(t, 2 * v), pair_at(t, 2 * v + 1)]
            choose([(t == 0, (True, True)), (v == rowed - 1, (False, True)), (True, (False, False))], where)

            @pl.when((t > 0) & (v == jnp.minimum(1, rowed - 1)))
            def _():
                finish(lo - 1)

            return 0

        lax.fori_loop(0, rowed, row_step, 0)
        send_block(hi)

        @pl.when(t == 0)
        def _():
            await_copy(r.dot.at[pl.ds(0, nh - 1)], r.dr.at[0])
            lax.fori_loop(0, nh - 1, lambda s, z: (out_arrives(s), z)[1], 0)

        for at_round, point in ((0, "row0"), (nh // 8, "row1"), (nh // 4, "row2")):
            if PLAN[point]:

                @pl.when(t == at_round)
                def _(point=point):
                    take(point)

        def column_step(v, _):
            where = [pair_at(t, n + 2 * v), pair_at(t, n + 2 * v + 1)]
            choose([(v == 0, (True, False)), (True, (False, False))], where)

            @pl.when(v == jnp.minimum(1, columned - 1))
            def _():
                finish(hi)

            return 0

        lax.fori_loop(0, columned, column_step, 0)
        pairs_backward([pair_at(t, 2 * n - 2)], (True,))
        send_block(lo)

        @pl.when(columned == 0)
        def _():
            finish(hi)

        for at_round, point in ((0, "col0"), (nh // 8, "col1"), (nh // 4, "col2")):
            if PLAN[point]:

                @pl.when(t == at_round)
                def _(point=point):
                    take(point)

        return 0

    r.dqa[...] = jnp.zeros_like(r.dqa)
    await_copy(r.dot.at[nh - 1], r.dr.at[1])
    out_arrives(nh - 1)
    take("begin")
    lax.fori_loop(0, nh // 2, round_backward, 0)
    finish(nh // 2 - 1)
    take("loop")

    def write(i, src, dst):
        pltpu.make_async_copy(src, dst, r.os.at[i]).start()

    ocopy.wait_recv()
    write(0, r.out_c, r.h_out_c)

    for t in range(heads):
        await_copy(r.dqkv.at[t], r.dkr.at[t])

        @pl.when(t % 2 != c)
        def _(t=t):
            remote(r.dqkv.at[t], r.dsib.at[t // 2], sends.sem(BACK), r.tr.at[0], c_dev).start()

    take("whole")
    wts = r.wt[...].reshape(heads * 3 * HD, wide)

    def grad_normed(span):
        return nn(flip(r.dqkv[:, :, span].reshape(heads * 3 * HD, half)), wts)

    r.psend[...] = grad_normed(theirs).astype(BF16)
    pcopy = sends.go(r.psend, r.precv, r.xr.at[8], x_dev)
    take("sent")
    await_copy(r.npair.at[1 - c], r.cr.at[0])
    await_copy(r.dsib, r.tr.at[0])
    for j in range(heads // 2):
        part = nn(r.dqkv[2 * j + c], r.npair[c]) + nn(r.dsib[j], r.npair[1 - c])
        for p in range(3):
            r.gc[j, p] = part[p * HD : (p + 1) * HD].astype(BF16)
    take("proj")
    gnorm = grad_normed(mine) + r.gterm[...]
    x = r.tokf[mine, :].astype(F32)
    centre = x - jnp.mean(x, -1, keepdims=True)
    rstd = lax.rsqrt(jnp.mean(centre * centre, -1, keepdims=True) + EPSILON)
    n = centre * rstd
    take("half")
    pcopy.wait_recv()
    gnorm = gnorm + r.precv[...].astype(F32)
    e = gnorm * r.vecf[0:1, :]
    result = r.ginp[...] + rstd * (
        e - jnp.mean(e, -1, keepdims=True) - n * jnp.mean(e * n, -1, keepdims=True)
    )
    r.tsend[...] = result.astype(BF16)
    tcopy = sends.go(r.tsend.at[:, other], r.trecv, r.xr.at[9], x_dev)
    r.vsum[0:1, :] = jnp.sum(gnorm * n, 0, keepdims=True)
    r.vsum[1:2, :] = jnp.sum(gnorm, 0, keepdims=True)
    me4 = 2 * c + w
    r.vin4[me4] = r.vsum[...]
    for dc in range(2):
        for dw in range(2):
            if dc or dw:
                cc, ww = lax.rem(c + dc, 2), lax.rem(w + dw, 2)
                dev = (b, 2 * z + cc, ww)
                sends.go(r.vin4.at[me4], r.vin4.at[me4], r.vr.at[0], dev)
    r.gtok[mine, :] = jnp.where(w == 0, result[:, :cw], result[:, cw:])
    write(1, r.gtok.at[mine], r.h_gtok.at[mine])
    take("norm")
    await_copy(r.vin4.at[pl.ds(0, 3)], r.vr.at[0])
    r.vinz[z] = r.vin4[0] + r.vin4[1] + r.vin4[2] + r.vin4[3]
    for k in range(1, nz):
        _, dev = z_dev(k)
        sends.go(r.vinz.at[z], r.vinz.at[z], r.vr.at[1], dev)
    take("vec")
    tcopy.wait_recv()
    r.gtok[theirs, :] = r.trecv[...].astype(F32)
    write(1, r.gtok.at[theirs], r.h_gtok.at[theirs])
    take("rows")
    await_copy(r.vinz.at[pl.ds(0, nz - 1)], r.vr.at[1])
    total = r.vinz[0]
    for k in range(1, nz):
        total = total + r.vinz[k]
    r.vinb[b] = total
    for k in range(1, nb):
        dev = (lax.rem(b + k, nb), h, w)
        sends.go(r.vinb.at[b], r.vinb.at[b], r.vr.at[2], dev)
    take("last")
    await_copy(r.vinb.at[pl.ds(0, nb - 1)], r.vr.at[2])
    total = r.vinb[0]
    for k in range(1, nb):
        total = total + r.vinb[k]
    r.red_v[...] = jnp.where(w == 0, total[:, :cw], total[:, cw:])
    write(2, r.red_v, r.h_red_v)
    write(3, r.red_s.at[0, c], r.h_red_s.at[0, c])
    take("end")
    write(3, r.red_s.at[1, c], r.h_red_s.at[1, c])
    await_copy(r.red_a.at[1 - bp], r.yr.at[3])
    write(4, r.red_a, r.h_red_a)
    for which in range(2):
        await_copy(r.red_s.at[which, 1 - c], r.scr.at[which])
        write(3, r.red_s.at[which, 1 - c], r.h_red_s.at[which, 1 - c])

    own_blocks = nh // dph
    loops = [(heads - 1) * nbytes(r.kvt.at[0]), (nh - 1) * nbytes(r.qt.at[0]), (dph - 1) * own_blocks * nbytes(r.kvt.at[0])]
    sends.count(LOOPS, *loops, nbytes(r.acts), nbytes(r.gpres))
    sends.count(BACK, (nh - 1) * nbytes(r.dqsend.at[0]), heads // 2 * nbytes(r.dqkv.at[0]))
    sends.count(BACK, (own_blocks - 1) * nbytes(r.dkvsend.at[0]), (nh - own_blocks) * nbytes(r.acc.at[0]))
    rowed = (nh + 2 * heads * per) * nbytes(r.osend.at[0])
    local_row = lax.div(sub_row(h, sub, dph) * tq, half) == w

    @pl.when(local_row)
    def _():
        sends.wait(ROWS, rowed - 2 * nbytes(r.osend.at[0]))

    @pl.when(jnp.logical_not(local_row))
    def _():
        sends.wait(ROWS, rowed)

    weights_sent()
    sums_sent()
    sends.finish()
    for i, ref in enumerate((r.out_c, r.gtok, r.red_v, r.red_s, r.red_a)):
        await_copy(ref, r.os.at[i])


def final_kernel(heads, *refs):
    (
        out_c, gtok, red_a, red_s, red_v,
        o_out, o_tok, o_g1, o_b1, o_wq, o_wk, o_wv, o_wo, o_gw1, o_gb1, o_g2, o_b2, o_gw2, o_gb2, o_up, o_dn,
    ) = refs
    o_out[...] = out_c[...]
    o_tok[...] = gtok[...]
    for i, ref in enumerate((o_g1, o_b1, o_gb1, o_g2, o_b2, o_gb2)):
        ref[...] = red_v[i : i + 1, :]
    _, quarter, units = red_a.shape[1:]
    o_up[:quarter, :] = red_a[0, 0].astype(F32)
    o_up[quarter:, :] = red_a[1, 0].astype(F32)
    o_dn[:, :quarter] = red_a[0, 1].astype(F32).T
    o_dn[:, quarter:] = red_a[1, 1].astype(F32).T
    eighth = quarter // 2
    for core in range(2):
        for y in range(2):
            base = (2 * core + y) * eighth
            o_wo[base : base + eighth, :] = red_s[0, core, y, 0].astype(F32)
    for m, ref in ((1, o_gw1), (2, o_gw2)):
        full = [red_s[0, core, y, m] for core in range(2) for y in range(2)]
        ref[...] = jnp.concatenate(full, 0).astype(F32).T
    for i, ref in enumerate((o_wq, o_wk, o_wv)):
        full = []
        for t in range(heads):
            full.append(red_s[1, t % 2, t // 2, i])
        ref[...] = jnp.concatenate(full, 0).astype(F32).T


def local(
    tokens, ln1_gain, ln1_bias, w_query, w_key, w_value, w_out, gate1_weight, gate1_bias,
    ln2_gain, ln2_bias, gate2_weight, gate2_bias, w_up, w_down, lengths, cotangent,
):
    nb, nh = lax.axis_size("batch"), lax.axis_size("hidden")
    rows, cw = tokens.shape
    units = w_up.shape[1]
    heads = cw // HD
    dph = nh // heads
    tq, half, wide, nz, pairs = rows // dph, rows // 2, 2 * cw, nh // 2, nb // 2
    quarter = half // 2
    zr = HD * 4 // nz
    per = half // tq
    sizes = (nb, nh, rows, cw, units, heads, dph, tq)

    ins = dict(
        lens=lengths, tok=tokens, cot=cotangent, v0=ln1_gain[None], v1=ln1_bias[None], v2=gate1_bias[None],
        v3=ln2_gain[None], v4=ln2_bias[None], v5=gate2_bias[None], wq=w_query, wk=w_key, wv=w_value,
        wo=w_out, wg1=gate1_weight, wg2=gate2_weight, wu=w_up, wd=w_down,
    )
    results = dict(
        out_c=((rows, cw), BF16),
        gtok=((rows, cw), F32),
        red_a=((2, 2, quarter, units), BF16),
        red_s=((2, 2, 2, 3, HD, wide), BF16),
        red_v=((8, cw), F32),
    )
    outs = {"h_" + name: spec for name, spec in results.items()}
    bufs = dict(
        **results, tally=((8192, 128), F32), wqkv=((3, wide, cw), BF16),
        vsrc=((8, cw), F32), vecf=((8, wide), F32), tokf=((rows, wide), BF16), cotr=((half, wide), BF16),
        g1f=((2, wide, cw), BF16), g2f=((2, wide, cw), BF16), wof=((2, cw, wide), BF16),
        wup=((nz, 2, 2, cw, units), BF16), wdn=((nz, 2, 2, units, cw), BF16),
        wt=((heads, 3 * HD, wide), BF16), npair=((2, rows, wide), BF16),
        qsrc=((heads, HD, rows), BF16), kvsrc=((heads, 2 * HD, rows), BF16),
        kvt=((nh, 2 * HD, rows), BF16), kvn=((nh, rows, 2 * HD), BF16), qt=((nh, HD, tq), BF16),
        qlow=((nh, 2 * HD, tq), BF16), dhigh=((nh, 2 * HD, tq), BF16), top=((nh, 1, tq), F32), total=((nh, 1, tq), F32),
        centre=((nh, 1, tq), F32), dqa=((nh, HD, tq), F32), ot=((nh, HD, tq), F32), lse=((nh, 1, tq), F32), osend=((nh, HD, tq), BF16),
        att=((2 * heads * HD, half), BF16),
        pre=((nz, 2, half, units), F32), actall=((half, nh * units), BF16), acts=((nz, half, units), BF16), actp=((nz, rows, units), BF16),
        gpres=((nz, half, units), BF16), gprep=((nz, rows, units), BF16),
        outr=((half, wide), BF16), gatt=((wide, half), BF16), dot=((nh, HD, tq), BF16),
        ginp=((half, wide), F32), gterm=((half, wide), F32), npt=((wide, rows), BF16), gbt=((wide, rows), BF16),
        lsrc=((3, wide, half), BF16), bpair=((3, rows, wide), BF16), apair=((3, 2, quarter, rows), BF16),
        vsum=((8, wide), F32),
        gb=((2, 2, 3, HD, wide), BF16), ybin=((2, 3, HD, wide), BF16), xbin=((3, HD, wide), BF16),
        ga=((2, nz, 2, 2, quarter, units), BF16), xin0=((nz, 2, quarter, units), BF16),
        yin1=((nz, 2, quarter, units), BF16), yin0=((nz, quarter, units), BF16), xin1=((nz, quarter, units), BF16),
        zs=((nz, 2, quarter, units), BF16), zin=((nz, 2, quarter, units), BF16),
        pin=((pairs, 2, quarter, units), BF16),
        gc=((2, 3, HD, wide), BF16), ycin=((3, HD, wide), BF16), sq=((2, 3, HD, wide), BF16),
        pzin=((2, 3, nz, zr, 128), BF16), sqpair=((2, 3, pairs, zr, 128), BF16),
        acc=((nh, 2 * HD, rows), F32), pin_kv=((nh // dph, max(dph - 1, 1), 2 * HD, rows), F32),
        dkvsend=((nh, 2 * HD, rows), BF16), dqsend=((nh, HD, tq), BF16),
        dqkv=((heads, 3 * HD, rows), BF16), dsib=((heads // 2, 3 * HD, rows), BF16),
        psend=((half, wide), BF16), precv=((half, wide), BF16),
        tsend=((half, wide), BF16), trecv=((half, cw), BF16),
        vin4=((4, 8, wide), F32), vinz=((nz, 8, wide), F32), vinb=((nb, 8, wide), F32),
    )
    sems = dict(
        ls=(6,), os=(5,), snd=(8,), xr=(10,), wzs=(2, nz), wzr=(nz,), gxr=(1,), gcr=(1,), kr=(nh,), qr=(nh,), cr=(3,),
        wxr=(nz,), wyr=(1,), wcr=(2,), fr=(nh,), orc=(1,), ar=(1,), pr=(1,), dr=(2,), yr=(4,), zsr=(nz,), par=(pairs,),
        sqpr=(2, 3, pairs) if pairs > 1 else (1,), pyr=(3,), pzr=(2, 3), pgr=(2, 3), sxr=(1,), syr=(1,), sbr=(2, 3),
        scr=(2,), pkr=(nh // dph, max(dph - 1, 1)), dkr=(heads,), tr=(1,), vr=(3,),
    )
    names = list(ins) + list(outs) + list(bufs) + list(sems)
    vmem = pl.BlockSpec(memory_space=pltpu.VMEM)
    any_space = pl.BlockSpec(memory_space=pl.ANY)
    in_specs = [vmem if name[0] == "v" else any_space for name in list(ins)[1:]]
    sums = pl.pallas_call(
        functools.partial(layer_kernel, names, sizes),
        out_shape=[jax.ShapeDtypeStruct(shape, kind) for shape, kind in outs.values()],
        in_specs=[pl.BlockSpec(memory_space=pltpu.SMEM)] + in_specs,
        out_specs=[any_space] * len(outs),
        scratch_shapes=[pltpu.VMEM(shape, kind) for shape, kind in bufs.values()]
        + [pltpu.SemaphoreType.DMA(shape) for shape in sems.values()],
        compiler_params=pltpu.CompilerParams(
            collective_id=1, has_side_effects=True, vmem_limit_bytes=VMEM_LIMIT
        ),
        cost_estimate=pl.CostEstimate(flops=10**10, bytes_accessed=10**7, transcendentals=10**7),
    )(*ins.values())
    grads = [
        ((rows, cw), BF16), ((rows, cw), F32), ((1, cw), F32), ((1, cw), F32),
        ((wide, cw), F32), ((wide, cw), F32), ((wide, cw), F32), ((cw, wide), F32),
        ((wide, cw), F32), ((1, cw), F32), ((1, cw), F32), ((1, cw), F32), ((wide, cw), F32), ((1, cw), F32),
        ((cw, units), F32), ((units, cw), F32),
    ]
    done = pl.pallas_call(
        functools.partial(final_kernel, heads),
        out_shape=[jax.ShapeDtypeStruct(shape, kind) for shape, kind in grads],
        in_specs=[vmem] * len(outs),
        out_specs=[vmem] * len(grads),
        compiler_params=pltpu.CompilerParams(vmem_limit_bytes=VMEM_LIMIT),
    )(*sums)
    return tuple(a[0] if a.shape[0] == 1 else a for a in done)


def solution(mesh):
    cols = P(None, "width")
    vec = P("width")
    in_specs = (
        P(("batch", "hidden"), "width"), vec, vec, cols, cols, cols, P("width", None), cols, vec, vec, vec,
        cols, vec, P("width", "hidden"), P("hidden", "width"), P("batch", None),
        P(("batch", "hidden"), "width"),
    )
    out_specs = (
        P(("batch", "hidden"), "width"), P(("batch", "hidden"), "width"), vec, vec, cols, cols, cols,
        P("width", None), cols, vec, vec, vec, cols, vec, P("width", "hidden"), P("hidden", "width"),
    )
    return jax.shard_map(local, mesh=mesh, in_specs=in_specs, out_specs=out_specs, check_vma=False)
```

```python
import functools
import math
import types

import jax
import jax.numpy as jnp
from jax import lax
from jax.experimental import pallas as pl
from jax.experimental.pallas import tpu as pltpu
from jax.sharding import PartitionSpec as P

HD = 64
EPSILON = 1e-05
MESH = pl.DeviceIdType.MESH
F32 = jnp.float32
BF16 = jnp.bfloat16
NEG = -1e30
VMEM_LIMIT = 62 * 1024 * 1024
PLAN = {
    "begin": ("a1",), "row0": (), "col0": ("bx",), "row1": (), "col1": ("bz",), "row2": ("a2",), "col2": (),
    "loop": ("a3",), "whole": (), "sent": ("bg",), "proj": ("cy", "a4"), "half": ("cz",),
    "norm": ("bb",), "vec": ("cg",), "rows": ("a5",), "last": ("bc", "cb"), "end": ("cc",),
}
SCALE = HD**-0.5


def nn(a, b):
    return lax.dot_general(a, b, (((1,), (0,)), ((), ())), preferred_element_type=F32)


def nt(a, b):
    return lax.dot_general(a, b, (((1,), (1,)), ((), ())), preferred_element_type=F32)


def flip(a):
    return a.astype(F32).T.astype(BF16)


def remote(src, dst, send, recv, dev):
    return pltpu.make_async_remote_copy(
        src_ref=src, dst_ref=dst, send_sem=send, recv_sem=recv, device_id=dev, device_id_type=MESH
    )


def await_copy(ref, sem):
    pltpu.make_async_copy(ref, ref, sem).wait()


def at(index, size):
    return pl.ds(pl.multiple_of(index * size, size), size)


def sub_row(index, sub, dph):
    return jnp.where(lax.rem(index, 2) == 0, sub, dph - 1 - sub)


def segments(pos, ends):
    total = jnp.zeros(pos.shape, jnp.int32)
    for end in ends:
        total = total + (pos >= end).astype(jnp.int32)
    return total


def allowed_mask(key_base, query_base, keys, queries, ends):
    key_pos = key_base + lax.broadcasted_iota(jnp.int32, (keys, 1), 0)
    query_pos = query_base + lax.broadcasted_iota(jnp.int32, (1, queries), 1)
    same = segments(key_pos, ends) == segments(query_pos, ends)
    return same & (key_pos <= query_pos)


def sigmoid(x):
    return 1.0 / (1.0 + jnp.exp(-x))


def nbytes(ref):
    return math.prod(ref.shape) * ref.dtype.itemsize


class Sends:
    def __init__(self, sems, tally):
        self.sems, self.tally = sems, tally
        self.bytes = {}
        self.items = []

    def sem(self, group):
        return self.sems.at[group]

    def count(self, group, *sizes):
        self.bytes[group] = self.bytes.get(group, 0) + sum(sizes)

    def go(self, src, dst, recv, dev, group=0):
        copy = remote(src, dst, self.sem(group), recv, dev)
        copy.start()
        self.count(group, nbytes(src))
        return copy

    def start_if(self, cond, copy):
        @pl.when(cond)
        def _():
            copy.start()

        self.items.append((cond, copy))

    def wait(self, group, size):
        await_copy(self.tally.at[pl.ds(0, size // 512)], self.sem(group))

    def finish(self):
        for group, size in self.bytes.items():
            self.wait(group, size)
        for cond, copy in self.items:

            @pl.when(cond)
            def _(copy=copy):
                copy.wait_send()


def layer_kernel(names, sizes, *refs):
    r = types.SimpleNamespace(**dict(zip(names, refs)))
    nb, nh, rows, cw, units, heads, dph, tq = sizes
    half, wide, nz = rows // 2, 2 * cw, nh // 2
    per = half // tq
    pairs = nb // 2
    hops = nz.bit_length() - 1
    b, h, w = lax.axis_index("batch"), lax.axis_index("hidden"), lax.axis_index("width")
    group, sub = lax.div(h, dph), lax.rem(h, dph)
    z, c, bp = lax.div(h, 2), lax.rem(h, 2), lax.rem(b, 2)
    x_dev = (b, h, 1 - w)
    c_dev = (b, h + 1 - 2 * c, w)
    y_dev = (b + 1 - 2 * bp, h, w)

    def z_dev(k):
        zz = lax.rem(z + k, nz)
        return zz, (b, 2 * zz + c, w)

    own, other = at(w, cw), at(1 - w, cw)
    mine, theirs = at(w, half), at(1 - w, half)
    lanes = at(c, half)
    ends = [
        r.lens[0, 0],
        r.lens[0, 0] + r.lens[0, 1],
        r.lens[0, 0] + r.lens[0, 1] + r.lens[0, 2],
    ]
    sends = Sends(r.snd, r.tally)
    SUMS, LOOPS, ROWS, WEIGHTS, BACK = 3, 4, 5, 6, 7

    barrier = pltpu.get_barrier_semaphore()
    count = 0
    for dw in range(2):
        for dh in range(nh):
            if dh or dw:
                dev = (b, lax.rem(h + dh, nh), lax.rem(w + dw, 2))
                pl.semaphore_signal(barrier, inc=1, device_id=dev, device_id_type=MESH)
                count += 1
    for db in range(1, nb):
        dev = (lax.rem(b + db, nb), h, w)
        pl.semaphore_signal(barrier, inc=1, device_id=dev, device_id_type=MESH)
        count += 1
    loads = dict(
        tok0=(r.tok.at[pl.ds(0, half)], r.tokf.at[pl.ds(0, half), own]),
        tok1=(r.tok.at[pl.ds(half, half)], r.tokf.at[pl.ds(half, half), own]),
        wu=(r.wu, r.wup.at[z, c, w]), wd=(r.wd, r.wdn.at[z, c, w]),
        wq=(r.wq, r.wqkv.at[0]), wk=(r.wk, r.wqkv.at[1]), wv=(r.wv, r.wqkv.at[2]),
        wg1=(r.wg1, r.g1f.at[w]), wg2=(r.wg2, r.g2f.at[w]), wo=(r.wo, r.wof.at[w]),
        cot=(r.cot.at[mine], r.cotr.at[:, own]),
    )
    shared = dict(tok0=0, tok1=1, wu=2, wd=2, wq=3, wk=3, wv=3, wg1=4, wg2=4, wo=4, cot=5)
    for name, (src, dst) in loads.items():
        pltpu.make_async_copy(src, dst, r.ls.at[shared[name]]).start()
    for i, vec in enumerate((r.v0, r.v1, r.v2, r.v3, r.v4, r.v5)):
        r.vsrc[i : i + 1, :] = vec[...]
    pl.semaphore_wait(barrier, count)

    vcopy = sends.go(r.vsrc, r.vecf.at[:, own], r.xr.at[0], x_dev)
    tcopies = []
    for k in range(2):
        block = r.tokf.at[pl.ds(k * half, half), own]
        await_copy(block, r.ls.at[k])
        tcopies.append(sends.go(block, block, r.xr.at[1 + k], x_dev))
    await_copy(r.wup.at[z, c], r.ls.at[2])

    def weight_blocks(distance):
        for kind, buf in enumerate((r.wup, r.wdn)):
            for step in (1, -1) if distance else (1,):
                zz = z - step * distance
                index = jnp.clip(zz, 0, nz - 1)
                yield (zz >= 0) & (zz < nz) & (bp == kind), index, buf, step

    def weight_hop(k, ending=False):
        for here, index, buf, step in weight_blocks(k - 1):
            for way in (1, -1) if k == 1 else (step,):
                onward = (z + way >= 0) & (z + way < nz)
                going = here & (jnp.logical_not(onward) if ending else onward)
                block = buf.at[index, c, w]
                if k > 1:

                    @pl.when(going)
                    def _(block=block, index=index):
                        await_copy(block, r.wzr.at[index])
                        remote(block, block, sends.sem(WEIGHTS), r.wxr.at[index], x_dev).start()
                        remote(block, block, sends.sem(WEIGHTS), r.wyr.at[0], y_dev).start()

                if not ending:
                    dev = (b, 2 * jnp.clip(z + way, 0, nz - 1) + c, w)
                    copy = remote(block, block, r.wzs.at[(1 - way) // 2, k], r.wzr.at[index], dev)
                    sends.start_if(going, copy)

    def weight_cross(distance):
        for here, index, buf, _ in weight_blocks(distance):

            @pl.when(here)
            def _(index=index, buf=buf):
                block = buf.at[index, c, 1 - w]
                await_copy(block, r.wxr.at[index])
                remote(block, block, sends.sem(WEIGHTS), r.wyr.at[0], y_dev).start()

    for here, index, buf, _ in weight_blocks(0):
        block = buf.at[index, c, w]
        copy = remote(block, block, sends.sem(WEIGHTS), r.wxr.at[index], x_dev)

        @pl.when(here)
        def _(copy=copy):
            copy.start()

    weight_hop(1)
    gates = ((r.wg1, r.g1f), (r.wg2, r.g2f), (r.wo, r.wof))
    r.vecf[:, own] = r.vsrc[...]

    await_copy(r.wqkv, r.ls.at[3])
    for i in range(3):
        turned = flip(r.wqkv[i])
        for t in range(heads):
            r.wt[t, i * HD : (i + 1) * HD, :] = turned[t * HD : (t + 1) * HD]

    vcopy.wait_recv()
    gain, shift = r.vecf[0:1, :], r.vecf[1:2, :]

    def project(k):
        part = slice(k * half, (k + 1) * half)
        tcopies[k].wait_recv()
        x = r.tokf[part, :].astype(F32)
        centre = x - jnp.mean(x, -1, keepdims=True)
        spread = jnp.mean(centre * centre, -1, keepdims=True)
        n = (centre * lax.rsqrt(spread + EPSILON) * gain + shift).astype(BF16)
        r.npair[c, part, :] = n
        for t in range(heads):
            qkv = nt(r.wt[t], n).astype(BF16)
            r.qsrc[t, :, part] = qkv[:HD]
            r.kvsrc[t, :, part] = qkv[HD:]

    def head_copies(step, k):
        t = lax.rem(group + step, heads)
        span = pl.ds(k * half, half)
        src, dst = r.kvsrc.at[t, :, span], r.kvt.at[h, :, span]
        if step:
            yield None, remote(src, dst, sends.sem(LOOPS), r.kr.at[h], (b, t * dph + sub, w))
        else:
            yield None, pltpu.make_async_copy(src, dst, r.kr.at[h])
        for i in range(per):
            row = k * per + i
            target = sub_row(h, row, dph)
            src, dst = r.qsrc.at[t, :, pl.ds(row * tq, tq)], r.qt.at[h]
            copy = remote(src, dst, sends.sem(LOOPS), r.qr.at[h], (b, t * dph + target, w))
            if step:
                yield None, copy
            else:
                yield target != sub, copy
                yield target == sub, pltpu.make_async_copy(src, dst, r.qr.at[h])

    def send_heads(step, k):
        for cond, copy in head_copies(step, k):
            if cond is None:
                copy.start()
            else:

                @pl.when(cond)
                def _(copy=copy):
                    copy.start()

    project(0)
    weight_hop(2)
    weight_hop(2, ending=True)
    send_heads(heads - 1, 0)
    project(1)
    send_heads(heads - 1, 1)
    for k in range(2):
        send_heads(0, k)

    def sends_of(count, buf, sem):
        await_copy(r.tally.at[pl.ds(0, count * nbytes(buf.at[0, 0, 0]) // 512)], sem)

    def weights_over_core():
        for kind, buf in enumerate((r.wup, r.wdn)):

            @pl.when(bp != kind)
            def _(buf=buf):
                sends_of(2 * nz - 1, buf, r.wyr.at[0])

            block = buf.at[:, c]
            sends.go(block, block, r.wcr.at[kind], c_dev, 1)

    def gates_over_core():
        for i, (src, dst) in enumerate(gates):
            piece = dst.at[1 - w, at(c, src.shape[0] // 2)]
            if i == 0:
                await_copy(r.tally.at[pl.ds(0, 3 * nbytes(piece) // 512)], r.gxr.at[0])
            sends.go(piece, piece, r.gcr.at[0], c_dev)

    def weights_sent():
        sends.wait(WEIGHTS, (3 * nz - 1) * nbytes(r.wu))

    def pass_on(s):
        @pl.when(lax.rem(s, dph) == sub)
        def _():
            await_copy(r.kvt.at[s], r.kr.at[s])
            for k in range(1, dph):
                dev = (b, group * dph + lax.rem(sub + k, dph), w)
                remote(r.kvt.at[s], r.kvt.at[s], sends.sem(LOOPS), r.fr.at[s], dev).start()

    def arrive(s):
        @pl.when(lax.rem(s, dph) != sub)
        def _():
            await_copy(r.kvt.at[s], r.fr.at[s])

        r.kvn[s] = flip(r.kvt[s])
        await_copy(r.qt.at[s], r.qr.at[s])
        q = r.qt[s].astype(F32) * SCALE
        r.qlow[s] = jnp.concatenate([q, jnp.zeros_like(q)], 0).astype(BF16)

    def masked(scores, i, j):
        query_base = i * rows + sub_row(i, sub, dph) * tq
        return jnp.where(allowed_mask(j * rows, query_base, rows, tq, ends), scores, NEG)

    def bias(scores, j):
        key_pos = j * rows + lax.broadcasted_iota(jnp.int32, (rows, 1), 0)
        return scores + jnp.where(key_pos < ends[0], NEG, 0.0)

    def absorb(i, blocks):
        top = r.top[i]
        new_top = top
        for scores, _ in blocks:
            new_top = jnp.maximum(new_top, jnp.max(scores, 0, keepdims=True))
        fade = jnp.exp(top - new_top)
        total, mixed = r.total[i] * fade, r.ot[i] * fade
        for scores, j in blocks:
            weights = jnp.exp(scores - new_top)
            total = total + jnp.sum(weights, 0, keepdims=True)
            mixed = mixed + nn(r.kvt[j, HD:, :], weights.astype(BF16))
        r.top[i], r.total[i], r.ot[i] = new_top, total, mixed

    def send_attended(s):
        row = sub_row(s, sub, dph)
        total = r.total[s]
        mixed = r.ot[s] / total
        r.ot[s] = mixed
        r.lse[s] = r.top[s] + jnp.log(total)
        r.osend[s] = mixed.astype(BF16)
        row_w = lax.div(row * tq, half)
        lane = lax.rem(row * tq, half)
        dst = r.att.at[at(w * heads + group, HD), pl.ds(pl.multiple_of(lane, tq), tq)]
        slot = r.orc.at[0]
        here = (s == h) & (row_w == w)

        @pl.when(here)
        def _():
            pltpu.make_async_copy(r.osend.at[s], dst, slot).start()

        @pl.when(jnp.logical_not(here))
        def _():
            remote(r.osend.at[s], dst, sends.sem(ROWS), slot, (b, s, row_w)).start()

    def own_chip(n):
        i = 2 * n
        first = masked(nn(r.kvn[i], r.qlow[i]), i, i)
        low = masked(nn(r.kvn[i], r.qlow[i + 1]), i + 1, i)
        high = masked(nn(r.kvn[i + 1], r.qlow[i + 1]), i + 1, i + 1)
        absorb(i, [(first, i)])
        absorb(i + 1, [(low, i), (high, i + 1)])

    def two_chips(hi, lo, last):
        queries, keys = (2 * hi, 2 * hi + 1), (2 * lo, 2 * lo + 1)
        scores = [[nn(r.kvn[j], r.qlow[i]) for j in keys] for i in queries]
        for a, i in enumerate(queries):
            if last and a:
                blocks = [(masked(x, i, j), j) for x, j in zip(scores[a], keys)]
            else:
                blocks = [(bias(scores[a][0], keys[0]), keys[0]), (scores[a][1], keys[1])]
            absorb(i, blocks)

    def completes(chip):
        return jnp.where(z == 0, chip, nz - z + jnp.minimum(chip, z - 1))

    def chip_at(d):
        return lax.rem(z + d, nz)

    def stage_passes(d):
        pass_on(2 * chip_at(d))
        pass_on(2 * chip_at(d) + 1)

    def stage_computes(d):
        n = chip_at(d)
        arrive(2 * n)
        arrive(2 * n + 1)
        own_chip(n)

        def with_earlier(e, _):
            @pl.when((d == nz - 1) & (e == 1))
            def _():
                weight_cross(nz - 1)

            m = lax.rem(z + e, nz)
            hi, lo = jnp.maximum(n, m), jnp.minimum(n, m)

            @pl.when(hi == nz - 1)
            def _():
                two_chips(hi, lo, True)

            @pl.when(hi != nz - 1)
            def _():
                two_chips(hi, lo, False)

            @pl.when((m > n) & (completes(m) == d))
            def _():
                send_attended(2 * m)
                send_attended(2 * m + 1)

            return 0

        lax.fori_loop(0, d, with_earlier, 0)

        @pl.when(completes(n) == d)
        def _():
            send_attended(2 * n)
            send_attended(2 * n + 1)

    def late_stage(d, _):
        stage_passes(d)

        @pl.when(d == 2)
        def _():
            for k in range(2):
                send_heads(1, k)
            for distance in range(2):
                weight_cross(distance)

        @pl.when(d == nz - 1)
        def _():
            weight_hop(nz, ending=True)
            for distance in range(2, nz - 1):
                weight_cross(distance)

        stage_computes(d)
        return 0

    r.top[...] = jnp.full_like(r.top, NEG)
    r.total[...] = jnp.zeros_like(r.total)
    r.ot[...] = jnp.zeros_like(r.ot)
    stage_passes(0)
    stage_computes(0)
    await_copy(r.wqkv, r.ls.at[4])
    for src, dst in gates:
        block = dst.at[w, at(c, src.shape[0] // 2)]
        sends.go(block, block, r.gxr.at[0], x_dev)
    sends.go(r.npair.at[c], r.npair.at[c], r.cr.at[0], c_dev)
    stage_passes(1)
    for k in range(3, nz):
        weight_hop(k)
    for k in range(2):
        send_heads(2, k)
    for k in range(3, nz):
        weight_hop(k, ending=True)
    stage_computes(1)
    await_copy(r.cotr.at[:, own], r.ls.at[5])
    sends.go(r.cot.at[theirs], r.cotr.at[:, own], r.xr.at[3], x_dev)
    lax.fori_loop(2, nz, late_stage, 0)
    gates_over_core()
    weights_over_core()

    await_copy(r.tally.at[pl.ds(0, 3 * nbytes(r.wg1) // 1024)], r.gcr.at[0])

    def two(a, weight):
        return jnp.concatenate([nn(a, weight[0]), nn(a, weight[1])], 1)

    def two_back(g, weight):
        return nt(g[:, :cw], weight[0]) + nt(g[:, cw:], weight[1])

    tok = r.tokf[mine, :].astype(F32)
    n1 = r.npair[c, mine, :]
    gate_one = sigmoid(two(n1, r.g1f) + r.vecf[2:3, :])
    await_copy(r.att, r.orc.at[0])
    wof = r.wof[...].reshape(wide, wide)
    branch_one = nn(flip(r.att[...]), wof)
    middle = tok + gate_one * (branch_one - tok)
    centre = middle - jnp.mean(middle, -1, keepdims=True)
    rstd = lax.rsqrt(jnp.mean(centre * centre, -1, keepdims=True) + EPSILON)
    n2 = centre * rstd
    gain_two = r.vecf[3:4, :]
    normed_two = (n2 * gain_two + r.vecf[4:5, :]).astype(BF16)
    gate_two = sigmoid(two(normed_two, r.g2f) + r.vecf[5:6, :])
    for kind, buf in enumerate((r.wup, r.wdn)):
        await_copy(buf.at[:, 1 - c], r.wcr.at[kind])

    def units_of(i2, p):
        return i2, lax.rem(c + p, 2)

    def up(i2, branch):
        for p in range(2):
            i, q = units_of(i2, p)
            pre = nn(normed_two, r.wup[i, q].reshape(wide, units))
            r.pre[i2, p] = pre
            act = jax.nn.gelu(pre).astype(BF16)
            r.actall[:, pl.ds(pl.multiple_of((2 * i + q) * units, units), units)] = act
            if p:
                r.acts[i2] = act
                dst = r.actp.at[i2, lanes, :]
                remote(r.acts.at[i2], dst, sends.sem(LOOPS), r.ar.at[0], c_dev).start()
            else:
                r.actp[i2, lanes, :] = act
        return branch

    lax.fori_loop(0, nz, up, 0)
    deep = nh * units
    branch_two = jnp.concatenate([nn(r.actall[...], r.wdn[:, :, v].reshape(deep, cw)) for v in range(2)], 1)
    delta = branch_two - middle
    r.outr[...] = (middle + gate_two * delta).astype(BF16)
    ocopy = sends.go(r.outr.at[:, other], r.out_c.at[mine, :], r.xr.at[4], x_dev)
    await_copy(r.cotr.at[:, own], r.xr.at[3])
    grad = r.cotr[...].astype(F32)
    gb2 = (grad * gate_two).astype(BF16)
    gl2 = (grad * delta * gate_two * (1.0 - gate_two)).astype(BF16)
    gmid = grad * (1.0 - gate_two)

    def down(i2, total):
        for p in range(2):
            i, q = units_of(i2, p)
            ghid = nt(gb2[:, :cw], r.wdn[i, q, 0]) + nt(gb2[:, cw:], r.wdn[i, q, 1])
            pre = r.pre[i2, p]
            k = 0.7978845608028654
            t = jnp.tanh(k * (pre + 0.044715 * pre * pre * pre))
            slope = 0.5 * (1.0 + t) + 0.5 * pre * (1.0 - t * t) * (k * (1.0 + 3 * 0.044715 * pre * pre))
            gpre = (ghid * slope).astype(BF16)
            total = total + nt(gpre, r.wup[i, q].reshape(wide, units))
            if p:
                r.gpres[i2] = gpre
                dst = r.gprep.at[i2, lanes, :]
                remote(r.gpres.at[i2], dst, sends.sem(LOOPS), r.pr.at[0], c_dev).start()
            else:
                r.gprep[i2, lanes, :] = gpre
        return total

    gnorm = lax.fori_loop(0, nz, down, two_back(gl2, r.g2f))
    e = gnorm * gain_two
    gmid = gmid + rstd * (
        e - jnp.mean(e, -1, keepdims=True) - n2 * jnp.mean(e * n2, -1, keepdims=True)
    )
    gb1 = (gmid * gate_one).astype(BF16)
    r.gatt[...] = nt(wof, gb1).astype(BF16)
    for dw in (1, 0):
        wt = lax.rem(w + dw, 2)
        for step in range(heads - 1, -1, -1):
            t = lax.rem(group + step, heads)
            for i in range(per):
                target = sub_row(h, w * per + i, dph)
                src = r.gatt.at[at(wt * heads + t, HD), pl.ds(i * tq, tq)]
                dst = r.dot.at[h]
                dev = (b, t * dph + target, wt)
                slot = r.dr.at[jnp.where(h == nh - 1, 1, 0)]
                copy = remote(src, dst, sends.sem(ROWS), slot, dev)
                if step or dw:
                    copy.start()
                else:

                    @pl.when(target != sub)
                    def _(copy=copy):
                        copy.start()

                    @pl.when(target == sub)
                    def _(src=src, dst=dst, slot=slot):
                        pltpu.make_async_copy(src, dst, slot).start()

    gl1 = (gmid * (branch_one - tok) * gate_one * (1.0 - gate_one)).astype(BF16)
    r.ginp[...] = gmid * (1.0 - gate_one)
    r.npt[:, lanes] = flip(normed_two)
    sends.go(r.npt.at[:, lanes], r.npt.at[:, lanes], r.cr.at[1], c_dev)
    r.gbt[:, lanes] = flip(gb2)
    sends.go(r.gbt.at[:, lanes], r.gbt.at[:, lanes], r.cr.at[1], c_dev)
    quarter = half // 2
    r.lsrc[0] = r.att[...]
    r.lsrc[1] = flip(gl1)
    r.lsrc[2] = flip(gl2)
    for m, right in enumerate((gb1, n1, normed_two)):
        r.bpair[m, lanes, :] = right
        block = r.bpair.at[m, lanes, :]
        sends.go(block, block, r.cr.at[2], c_dev, 2)
        for v in range(2):
            src = r.lsrc.at[m, at(2 * v + 1 - c, quarter), :]
            dst = r.apair.at[m, v, :, lanes]
            sends.go(src, dst, r.cr.at[2], c_dev, 2)
            r.apair[m, v, :, lanes] = r.lsrc[m, at(2 * v + c, quarter), :]
    r.gterm[...] = two_back(gl1, r.g1f)
    r.vsum[...] = jnp.zeros_like(r.vsum)
    r.vsum[2:3, :] = jnp.sum(gl1.astype(F32), 0, keepdims=True)
    r.vsum[3:4, :] = jnp.sum(gnorm * n2, 0, keepdims=True)
    r.vsum[4:5, :] = jnp.sum(gnorm, 0, keepdims=True)
    r.vsum[5:6, :] = jnp.sum(gl2.astype(F32), 0, keepdims=True)
    r.out_c[mine, :] = r.outr[:, own]

    eighth = quarter // 2
    await_copy(r.npt, r.cr.at[1])
    await_copy(r.gpres, r.pr.at[0])
    await_copy(r.acts, r.ar.at[0])

    def weight_grads(i2, _):
        r.ga[0, i2] = nn(r.npt[...], r.gprep[i2]).astype(BF16).reshape(2, 2, quarter, units)
        r.ga[1, i2] = nn(r.gbt[...], r.actp[i2]).astype(BF16).reshape(2, 2, quarter, units)
        return 0

    lax.fori_loop(0, nz, weight_grads, 0)
    sends.go(r.ga.at[0, :, 1 - w], r.xin0, r.xr.at[5], x_dev, 2)
    pair_bytes = 3 * (nbytes(r.bpair.at[0, lanes, :]) + 2 * nbytes(r.apair.at[0, 0, :, lanes]))
    await_copy(r.tally.at[pl.ds(0, pair_bytes // 512)], r.cr.at[2])
    for m in range(3):
        for v in range(2):
            block = nn(r.apair[m, v], r.bpair[m]).astype(BF16)
            for y in range(2):
                r.gb[v, y, m] = block[y * eighth : (y + 1) * eighth]
    for m in range(3):
        sends.go(r.gb.at[:, 1 - bp, m], r.ybin.at[:, m], r.syr.at[0], y_dev, 2)


    def z_block(q, flip_bit, v):
        bit = lax.rem(lax.div(z, 1 << q), 2)
        bit = 1 - bit if flip_bit else bit
        return lax.rem(z, 1 << q) + bit * (1 << q) + v * (2 << q)

    def ffn_first():
        remote(r.ga.at[1, :, :, 1 - bp], r.yin1, sends.sem(SUMS), r.yr.at[1], y_dev).start()

    def ffn_second():
        await_copy(r.xin0, r.xr.at[5])
        r.ga[0, :, w] = (r.ga[0, :, w].astype(F32) + r.xin0[...].astype(F32)).astype(BF16)
        remote(r.ga.at[0, :, w, 1 - bp], r.yin0, sends.sem(SUMS), r.yr.at[2], y_dev).start()
        await_copy(r.yin1, r.yr.at[1])
        r.ga[1, :, :, bp] = (r.ga[1, :, :, bp].astype(F32) + r.yin1[...].astype(F32)).astype(BF16)
        remote(r.ga.at[1, :, 1 - w, bp], r.xin1, sends.sem(SUMS), r.xr.at[6], x_dev).start()

    def ffn_third():
        await_copy(r.yin0, r.yr.at[2])
        await_copy(r.xin1, r.xr.at[6])
        r.zs[:, 0] = (r.ga[0, :, w, bp].astype(F32) + r.yin0[...].astype(F32)).astype(BF16)
        r.zs[:, 1] = (r.ga[1, :, w, bp].astype(F32) + r.xin1[...].astype(F32)).astype(BF16)
        ffn_hop(0)

    def ffn_hop(q):
        if q:
            ffn_add(q - 1)
        bit = lax.rem(lax.div(z, 1 << q), 2)
        dev = (b, 2 * (z + (1 << q) * (1 - 2 * bit)) + c, w)
        for v in range(nz >> (q + 1)):
            slot = nz - (nz >> q) + v
            remote(r.zs.at[z_block(q, True, v)], r.zin.at[slot], sends.sem(SUMS), r.zsr.at[slot], dev).start()

    def ffn_add(q):
        for v in range(nz >> (q + 1)):
            slot = nz - (nz >> q) + v
            await_copy(r.zin.at[slot], r.zsr.at[slot])
            kept = z_block(q, False, v)
            r.zs[kept] = (r.zs[kept].astype(F32) + r.zin[slot].astype(F32)).astype(BF16)

    def ffn_fourth():
        ffn_add(hops - 1)
        total = r.zs[z].astype(F32)
        if pairs > 1:
            mypair = lax.div(b, 2)
            r.pin[mypair] = total.astype(BF16)
            for k in range(1, pairs):
                dev = (lax.rem(b + 2 * k, nb), h, w)
                block = r.pin.at[mypair]
                remote(block, block, sends.sem(SUMS), r.par.at[mypair], dev).start()
            for k in range(1, pairs):
                pp = lax.rem(mypair + k, pairs)
                await_copy(r.pin.at[pp], r.par.at[pp])
            total = r.pin[0].astype(F32)
            for k in range(1, pairs):
                total = total + r.pin[k].astype(F32)
        r.red_a[bp] = total.astype(BF16)
        block = r.red_a.at[bp]
        remote(block, block, sends.sem(SUMS), r.yr.at[3], y_dev).start()

    def sums_sent():
        sends.count(SUMS, nbytes(r.yin1), nbytes(r.yin0), nbytes(r.xin1), nbytes(r.red_a.at[0]))
        sends.count(SUMS, (nz - 1) * nbytes(r.zin.at[0]), (pairs - 1) * nbytes(r.pin.at[0]))
        sends.count(SUMS, nbytes(r.xbin), nbytes(r.ycin), 2 * nbytes(r.ycin), nbytes(r.red_s) // 2)
        sends.count(SUMS, 6 * (2 * (nz - 1) + pairs - 1) * nbytes(r.pzin.at[0, 0, 0]))

    zr = HD * 4 // nz

    def z_part(zz):
        return pl.ds(pl.multiple_of(lax.div(zz, 4) * zr, zr), zr), at(lax.rem(zz, 4), 128)

    def square_x():
        await_copy(r.ybin, r.syr.at[0])
        for p in range(3):
            r.gb[:, bp, p] = (r.gb[:, bp, p].astype(F32) + r.ybin[:, p].astype(F32)).astype(BF16)
            remote(r.gb.at[1 - w, bp, p], r.xbin.at[p], sends.sem(SUMS), r.sxr.at[0], x_dev).start()

    def over_pairs(which, p, total):
        if pairs == 1:
            return total
        mypair = lax.div(b, 2)
        r.sqpair[which, p, mypair] = total
        for k in range(1, pairs):
            dev = (lax.rem(b + 2 * k, nb), h, w)
            block = r.sqpair.at[which, p, mypair]
            remote(block, block, sends.sem(SUMS), r.sqpr.at[which, p, mypair], dev).start()
        for k in range(1, pairs):
            pp = lax.rem(mypair + k, pairs)
            await_copy(r.sqpair.at[which, p, pp], r.sqpr.at[which, p, pp])
        total = r.sqpair[which, p, 0].astype(F32)
        for k in range(1, pairs):
            total = total + r.sqpair[which, p, k].astype(F32)
        return total.astype(BF16)

    def scatter(which):
        for p in range(3):
            if which:
                await_copy(r.ycin.at[p], r.pyr.at[p])
                r.sq[1, p] = (r.gc[bp, p].astype(F32) + r.ycin[p].astype(F32)).astype(BF16)
            else:
                if p == 0:
                    await_copy(r.xbin, r.sxr.at[0])
                r.sq[0, p] = (r.gb[w, bp, p].astype(F32) + r.xbin[p].astype(F32)).astype(BF16)
            for k in range(nz - 1, 0, -1):
                zz, dev = z_dev(k)
                src, dst = r.sq.at[(which, p) + z_part(zz)], r.pzin.at[which, p, z]
                remote(src, dst, sends.sem(SUMS), r.pzr.at[which, p], dev).start()

    def gather(which):
        for p in range(3):
            total = r.sq[(which, p) + z_part(z)].astype(F32)
            await_copy(r.pzin.at[which, p, pl.ds(0, nz - 1)], r.pzr.at[which, p])
            for k in range(1, nz):
                zz, _ = z_dev(k)
                total = total + r.pzin[which, p, zz].astype(F32)
            block = (which, c, bp, p) + z_part(z)
            r.red_s[block] = over_pairs(which, p, total.astype(BF16))
            for k in range(nz - 1, 0, -1):
                _, dev = z_dev(k)
                ref = r.red_s.at[block]
                remote(ref, ref, sends.sem(SUMS), r.pgr.at[which, p], dev).start()

    def back(which):
        for p in range(3):
            await_copy(r.pzin.at[which, p, pl.ds(0, nz - 1)], r.pgr.at[which, p])
            block = r.red_s.at[which, c, bp, p]
            remote(block, block, sends.sem(SUMS), r.sbr.at[which, p], y_dev).start()

    def square_core(which):
        for p in range(3):
            await_copy(r.red_s.at[which, c, 1 - bp, p], r.sbr.at[which, p])
            block = r.red_s.at[which, c, :, p]
            remote(block, block, sends.sem(SUMS), r.scr.at[which], c_dev).start()

    def proj_y():
        for p in range(3):
            remote(r.gc.at[1 - bp, p], r.ycin.at[p], sends.sem(SUMS), r.pyr.at[p], y_dev).start()

    steps = dict(
        a1=ffn_first, a2=ffn_second, a3=ffn_third, a4=lambda: [ffn_hop(q) for q in range(1, hops)], a5=ffn_fourth,
        bx=square_x, bz=lambda: scatter(0), bg=lambda: gather(0), bb=lambda: back(0), bc=lambda: square_core(0),
        cy=proj_y, cz=lambda: scatter(1), cg=lambda: gather(1), cb=lambda: back(1), cc=lambda: square_core(1),
    )

    def take(point):
        for name in PLAN[point]:
            steps[name]()

    r.acc[...] = jnp.zeros_like(r.acc)

    def finish(s):
        @pl.when(lax.rem(s, dph) == sub)
        def _():
            total = r.acc[s]
            for k in range(1, dph):
                slot = r.pin_kv.at[lax.div(s, dph), k - 1]
                await_copy(slot, r.pkr.at[lax.div(s, dph), k - 1])
                total = total + r.pin_kv[lax.div(s, dph), k - 1]
            r.dkvsend[s, :HD] = (total[:HD] * SCALE).astype(BF16)
            r.dkvsend[s, HD:] = total[HD:].astype(BF16)
            dst = r.dqkv.at[group, pl.ds(HD, 2 * HD), :]

            @pl.when(s == h)
            def _():
                pltpu.make_async_copy(r.dkvsend.at[s], dst, r.dkr.at[group]).start()

            @pl.when(s != h)
            def _():
                remote(r.dkvsend.at[s], dst, sends.sem(BACK), r.dkr.at[group], (b, s, w)).start()

    def pairs_backward(where, full):
        scores = [nn(r.kvn[j], r.qlow[i]) for i, j in where]
        gprobs = [nn(r.kvn[j], r.dhigh[i]) for i, j in where]
        for x, gp, (i, j), whole in zip(scores, gprobs, where, full):
            x = masked(x, i, j) if whole else bias(x, j)
            probs = jnp.exp(x - r.lse[i])
            gscores = (probs * (gp - r.centre[i])).astype(BF16)
            r.acc[j, HD:, :] += nt(r.dhigh[i, HD:, :], probs.astype(BF16))
            r.acc[j, :HD, :] += nt(r.qt[i], gscores)
            r.dqa[i] += nn(r.kvt[j, :HD, :], gscores)

    def choose(kinds, where):
        taken = False
        for cond, full in kinds:

            @pl.when(jnp.logical_and(cond, jnp.logical_not(taken)))
            def _(full=full):
                pairs_backward(where, full)

            taken = jnp.logical_or(taken, cond)

    def pair_at(t, u):
        lo, hi = t, nh - 1 - t
        n = hi - lo + 1
        return jnp.where(u < n, hi, lo + u - n), jnp.where(u < n, lo + u, lo)

    def out_arrives(s):
        dout = r.dot[s]
        r.dhigh[s] = jnp.concatenate([jnp.zeros((HD, tq), BF16), dout], 0)
        r.centre[s] = jnp.sum(r.ot[s] * dout.astype(F32), 0, keepdims=True)

    def send_block(s):
        row = sub_row(s, sub, dph)
        r.dqsend[s] = (r.dqa[s] * SCALE).astype(BF16)
        dst = r.dqkv.at[group, pl.ds(0, HD), pl.ds(pl.multiple_of(row * tq, tq), tq)]

        @pl.when(s == h)
        def _():
            pltpu.make_async_copy(r.dqsend.at[s], dst, r.dkr.at[group]).start()

        @pl.when(s != h)
        def _():
            remote(r.dqsend.at[s], dst, sends.sem(BACK), r.dkr.at[group], (b, s, w)).start()

        owner = lax.rem(s, dph)

        @pl.when(owner != sub)
        def _():
            k = lax.rem(sub - owner + dph, dph)
            dev = (b, group * dph + owner, w)
            slot = lax.div(s, dph)
            remote(r.acc.at[s], r.pin_kv.at[slot, k - 1], sends.sem(BACK), r.pkr.at[slot, k - 1], dev).start()

    def round_backward(t, _):
        lo, hi = t, nh - 1 - t
        n = hi - lo + 1

        rowed = lax.div(n, 2)
        columned = rowed - 1

        def row_step(v, _):
            where = [pair_at(t, 2 * v), pair_at(t, 2 * v + 1)]
            choose([(t == 0, (True, True)), (v == rowed - 1, (False, True)), (True, (False, False))], where)

            @pl.when((t > 0) & (v == jnp.minimum(1, rowed - 1)))
            def _():
                finish(lo - 1)

            return 0

        lax.fori_loop(0, rowed, row_step, 0)
        send_block(hi)

        @pl.when(t == 0)
        def _():
            await_copy(r.dot.at[pl.ds(0, nh - 1)], r.dr.at[0])
            lax.fori_loop(0, nh - 1, lambda s, z: (out_arrives(s), z)[1], 0)

        for at_round, point in ((0, "row0"), (nh // 8, "row1"), (nh // 4, "row2")):
            if PLAN[point]:

                @pl.when(t == at_round)
                def _(point=point):
                    take(point)

        def column_step(v, _):
            where = [pair_at(t, n + 2 * v), pair_at(t, n + 2 * v + 1)]
            choose([(v == 0, (True, False)), (True, (False, False))], where)

            @pl.when(v == jnp.minimum(1, columned - 1))
            def _():
                finish(hi)

            return 0

        lax.fori_loop(0, columned, column_step, 0)
        pairs_backward([pair_at(t, 2 * n - 2)], (True,))
        send_block(lo)

        @pl.when(columned == 0)
        def _():
            finish(hi)

        for at_round, point in ((0, "col0"), (nh // 8, "col1"), (nh // 4, "col2")):
            if PLAN[point]:

                @pl.when(t == at_round)
                def _(point=point):
                    take(point)

        return 0

    r.dqa[...] = jnp.zeros_like(r.dqa)
    await_copy(r.dot.at[nh - 1], r.dr.at[1])
    out_arrives(nh - 1)
    take("begin")
    lax.fori_loop(0, nh // 2, round_backward, 0)
    finish(nh // 2 - 1)
    take("loop")

    def write(i, src, dst):
        pltpu.make_async_copy(src, dst, r.os.at[i]).start()

    ocopy.wait_recv()
    write(0, r.out_c, r.h_out_c)

    for t in range(heads):
        await_copy(r.dqkv.at[t], r.dkr.at[t])

        @pl.when(t % 2 != c)
        def _(t=t):
            remote(r.dqkv.at[t], r.dsib.at[t // 2], sends.sem(BACK), r.tr.at[0], c_dev).start()

    take("whole")
    wts = r.wt[...].reshape(heads * 3 * HD, wide)

    def grad_normed(span):
        return nn(flip(r.dqkv[:, :, span].reshape(heads * 3 * HD, half)), wts)

    r.psend[...] = grad_normed(theirs).astype(BF16)
    pcopy = sends.go(r.psend, r.precv, r.xr.at[8], x_dev)
    take("sent")
    await_copy(r.npair.at[1 - c], r.cr.at[0])
    await_copy(r.dsib, r.tr.at[0])
    for j in range(heads // 2):
        part = nn(r.dqkv[2 * j + c], r.npair[c]) + nn(r.dsib[j], r.npair[1 - c])
        for p in range(3):
            r.gc[j, p] = part[p * HD : (p + 1) * HD].astype(BF16)
    take("proj")
    gnorm = grad_normed(mine) + r.gterm[...]
    x = r.tokf[mine, :].astype(F32)
    centre = x - jnp.mean(x, -1, keepdims=True)
    rstd = lax.rsqrt(jnp.mean(centre * centre, -1, keepdims=True) + EPSILON)
    n = centre * rstd
    take("half")
    pcopy.wait_recv()
    gnorm = gnorm + r.precv[...].astype(F32)
    e = gnorm * r.vecf[0:1, :]
    result = r.ginp[...] + rstd * (
        e - jnp.mean(e, -1, keepdims=True) - n * jnp.mean(e * n, -1, keepdims=True)
    )
    r.tsend[...] = result.astype(BF16)
    tcopy = sends.go(r.tsend.at[:, other], r.trecv, r.xr.at[9], x_dev)
    r.vsum[0:1, :] = jnp.sum(gnorm * n, 0, keepdims=True)
    r.vsum[1:2, :] = jnp.sum(gnorm, 0, keepdims=True)
    me4 = 2 * c + w
    r.vin4[me4] = r.vsum[...]
    for dc in range(2):
        for dw in range(2):
            if dc or dw:
                cc, ww = lax.rem(c + dc, 2), lax.rem(w + dw, 2)
                dev = (b, 2 * z + cc, ww)
                sends.go(r.vin4.at[me4], r.vin4.at[me4], r.vr.at[0], dev)
    r.gtok[mine, :] = jnp.where(w == 0, result[:, :cw], result[:, cw:])
    write(1, r.gtok.at[mine], r.h_gtok.at[mine])
    take("norm")
    await_copy(r.vin4.at[pl.ds(0, 3)], r.vr.at[0])
    r.vinz[z] = r.vin4[0] + r.vin4[1] + r.vin4[2] + r.vin4[3]
    for k in range(1, nz):
        _, dev = z_dev(k)
        sends.go(r.vinz.at[z], r.vinz.at[z], r.vr.at[1], dev)
    take("vec")
    tcopy.wait_recv()
    r.gtok[theirs, :] = r.trecv[...].astype(F32)
    write(1, r.gtok.at[theirs], r.h_gtok.at[theirs])
    take("rows")
    await_copy(r.vinz.at[pl.ds(0, nz - 1)], r.vr.at[1])
    total = r.vinz[0]
    for k in range(1, nz):
        total = total + r.vinz[k]
    r.vinb[b] = total
    for k in range(1, nb):
        dev = (lax.rem(b + k, nb), h, w)
        sends.go(r.vinb.at[b], r.vinb.at[b], r.vr.at[2], dev)
    take("last")
    await_copy(r.vinb.at[pl.ds(0, nb - 1)], r.vr.at[2])
    total = r.vinb[0]
    for k in range(1, nb):
        total = total + r.vinb[k]
    r.red_v[...] = jnp.where(w == 0, total[:, :cw], total[:, cw:])
    write(2, r.red_v, r.h_red_v)
    write(3, r.red_s.at[0, c], r.h_red_s.at[0, c])
    take("end")
    write(3, r.red_s.at[1, c], r.h_red_s.at[1, c])
    await_copy(r.red_a.at[1 - bp], r.yr.at[3])
    write(4, r.red_a, r.h_red_a)
    for which in range(2):
        await_copy(r.red_s.at[which, 1 - c], r.scr.at[which])
        write(3, r.red_s.at[which, 1 - c], r.h_red_s.at[which, 1 - c])

    own_blocks = nh // dph
    loops = [(heads - 1) * nbytes(r.kvt.at[0]), (nh - 1) * nbytes(r.qt.at[0]), (dph - 1) * own_blocks * nbytes(r.kvt.at[0])]
    sends.count(LOOPS, *loops, nbytes(r.acts), nbytes(r.gpres))
    sends.count(BACK, (nh - 1) * nbytes(r.dqsend.at[0]), heads // 2 * nbytes(r.dqkv.at[0]))
    sends.count(BACK, (own_blocks - 1) * nbytes(r.dkvsend.at[0]), (nh - own_blocks) * nbytes(r.acc.at[0]))
    rowed = (nh + 2 * heads * per) * nbytes(r.osend.at[0])
    local_row = lax.div(sub_row(h, sub, dph) * tq, half) == w

    @pl.when(local_row)
    def _():
        sends.wait(ROWS, rowed - 2 * nbytes(r.osend.at[0]))

    @pl.when(jnp.logical_not(local_row))
    def _():
        sends.wait(ROWS, rowed)

    weights_sent()
    sums_sent()
    sends.finish()
    for i, ref in enumerate((r.out_c, r.gtok, r.red_v, r.red_s, r.red_a)):
        await_copy(ref, r.os.at[i])


def final_kernel(heads, *refs):
    (
        out_c, gtok, red_a, red_s, red_v,
        o_out, o_tok, o_g1, o_b1, o_wq, o_wk, o_wv, o_wo, o_gw1, o_gb1, o_g2, o_b2, o_gw2, o_gb2, o_up, o_dn,
    ) = refs
    o_out[...] = out_c[...]
    o_tok[...] = gtok[...]
    for i, ref in enumerate((o_g1, o_b1, o_gb1, o_g2, o_b2, o_gb2)):
        ref[...] = red_v[i : i + 1, :]
    _, quarter, units = red_a.shape[1:]
    o_up[:quarter, :] = red_a[0, 0].astype(F32)
    o_up[quarter:, :] = red_a[1, 0].astype(F32)
    o_dn[:, :quarter] = red_a[0, 1].astype(F32).T
    o_dn[:, quarter:] = red_a[1, 1].astype(F32).T
    eighth = quarter // 2
    for core in range(2):
        for y in range(2):
            base = (2 * core + y) * eighth
            o_wo[base : base + eighth, :] = red_s[0, core, y, 0].astype(F32)
    for m, ref in ((1, o_gw1), (2, o_gw2)):
        full = [red_s[0, core, y, m] for core in range(2) for y in range(2)]
        ref[...] = jnp.concatenate(full, 0).astype(F32).T
    for i, ref in enumerate((o_wq, o_wk, o_wv)):
        full = []
        for t in range(heads):
            full.append(red_s[1, t % 2, t // 2, i])
        ref[...] = jnp.concatenate(full, 0).astype(F32).T


def local(
    tokens, ln1_gain, ln1_bias, w_query, w_key, w_value, w_out, gate1_weight, gate1_bias,
    ln2_gain, ln2_bias, gate2_weight, gate2_bias, w_up, w_down, lengths, cotangent,
):
    nb, nh = lax.axis_size("batch"), lax.axis_size("hidden")
    rows, cw = tokens.shape
    units = w_up.shape[1]
    heads = cw // HD
    dph = nh // heads
    tq, half, wide, nz, pairs = rows // dph, rows // 2, 2 * cw, nh // 2, nb // 2
    quarter = half // 2
    zr = HD * 4 // nz
    per = half // tq
    sizes = (nb, nh, rows, cw, units, heads, dph, tq)

    ins = dict(
        lens=lengths, tok=tokens, cot=cotangent, v0=ln1_gain[None], v1=ln1_bias[None], v2=gate1_bias[None],
        v3=ln2_gain[None], v4=ln2_bias[None], v5=gate2_bias[None], wq=w_query, wk=w_key, wv=w_value,
        wo=w_out, wg1=gate1_weight, wg2=gate2_weight, wu=w_up, wd=w_down,
    )
    results = dict(
        out_c=((rows, cw), BF16),
        gtok=((rows, cw), F32),
        red_a=((2, 2, quarter, units), BF16),
        red_s=((2, 2, 2, 3, HD, wide), BF16),
        red_v=((8, cw), F32),
    )
    outs = {"h_" + name: spec for name, spec in results.items()}
    bufs = dict(
        **results, tally=((8192, 128), F32), wqkv=((3, wide, cw), BF16),
        vsrc=((8, cw), F32), vecf=((8, wide), F32), tokf=((rows, wide), BF16), cotr=((half, wide), BF16),
        g1f=((2, wide, cw), BF16), g2f=((2, wide, cw), BF16), wof=((2, cw, wide), BF16),
        wup=((nz, 2, 2, cw, units), BF16), wdn=((nz, 2, 2, units, cw), BF16),
        wt=((heads, 3 * HD, wide), BF16), npair=((2, rows, wide), BF16),
        qsrc=((heads, HD, rows), BF16), kvsrc=((heads, 2 * HD, rows), BF16),
        kvt=((nh, 2 * HD, rows), BF16), kvn=((nh, rows, 2 * HD), BF16), qt=((nh, HD, tq), BF16),
        qlow=((nh, 2 * HD, tq), BF16), dhigh=((nh, 2 * HD, tq), BF16), top=((nh, 1, tq), F32), total=((nh, 1, tq), F32),
        centre=((nh, 1, tq), F32), dqa=((nh, HD, tq), F32), ot=((nh, HD, tq), F32), lse=((nh, 1, tq), F32), osend=((nh, HD, tq), BF16),
        att=((2 * heads * HD, half), BF16),
        pre=((nz, 2, half, units), F32), actall=((half, nh * units), BF16), acts=((nz, half, units), BF16), actp=((nz, rows, units), BF16),
        gpres=((nz, half, units), BF16), gprep=((nz, rows, units), BF16),
        outr=((half, wide), BF16), gatt=((wide, half), BF16), dot=((nh, HD, tq), BF16),
        ginp=((half, wide), F32), gterm=((half, wide), F32), npt=((wide, rows), BF16), gbt=((wide, rows), BF16),
        lsrc=((3, wide, half), BF16), bpair=((3, rows, wide), BF16), apair=((3, 2, quarter, rows), BF16),
        vsum=((8, wide), F32),
        gb=((2, 2, 3, HD, wide), BF16), ybin=((2, 3, HD, wide), BF16), xbin=((3, HD, wide), BF16),
        ga=((2, nz, 2, 2, quarter, units), BF16), xin0=((nz, 2, quarter, units), BF16),
        yin1=((nz, 2, quarter, units), BF16), yin0=((nz, quarter, units), BF16), xin1=((nz, quarter, units), BF16),
        zs=((nz, 2, quarter, units), BF16), zin=((nz, 2, quarter, units), BF16),
        pin=((pairs, 2, quarter, units), BF16),
        gc=((2, 3, HD, wide), BF16), ycin=((3, HD, wide), BF16), sq=((2, 3, HD, wide), BF16),
        pzin=((2, 3, nz, zr, 128), BF16), sqpair=((2, 3, pairs, zr, 128), BF16),
        acc=((nh, 2 * HD, rows), F32), pin_kv=((nh // dph, max(dph - 1, 1), 2 * HD, rows), F32),
        dkvsend=((nh, 2 * HD, rows), BF16), dqsend=((nh, HD, tq), BF16),
        dqkv=((heads, 3 * HD, rows), BF16), dsib=((heads // 2, 3 * HD, rows), BF16),
        psend=((half, wide), BF16), precv=((half, wide), BF16),
        tsend=((half, wide), BF16), trecv=((half, cw), BF16),
        vin4=((4, 8, wide), F32), vinz=((nz, 8, wide), F32), vinb=((nb, 8, wide), F32),
    )
    sems = dict(
        ls=(6,), os=(5,), snd=(8,), xr=(10,), wzs=(2, nz), wzr=(nz,), gxr=(1,), gcr=(1,), kr=(nh,), qr=(nh,), cr=(3,),
        wxr=(nz,), wyr=(1,), wcr=(2,), fr=(nh,), orc=(1,), ar=(1,), pr=(1,), dr=(2,), yr=(4,), zsr=(nz,), par=(pairs,),
        sqpr=(2, 3, pairs) if pairs > 1 else (1,), pyr=(3,), pzr=(2, 3), pgr=(2, 3), sxr=(1,), syr=(1,), sbr=(2, 3),
        scr=(2,), pkr=(nh // dph, max(dph - 1, 1)), dkr=(heads,), tr=(1,), vr=(3,),
    )
    names = list(ins) + list(outs) + list(bufs) + list(sems)
    vmem = pl.BlockSpec(memory_space=pltpu.VMEM)
    any_space = pl.BlockSpec(memory_space=pl.ANY)
    in_specs = [vmem if name[0] == "v" else any_space for name in list(ins)[1:]]
    sums = pl.pallas_call(
        functools.partial(layer_kernel, names, sizes),
        out_shape=[jax.ShapeDtypeStruct(shape, kind) for shape, kind in outs.values()],
        in_specs=[pl.BlockSpec(memory_space=pltpu.SMEM)] + in_specs,
        out_specs=[any_space] * len(outs),
        scratch_shapes=[pltpu.VMEM(shape, kind) for shape, kind in bufs.values()]
        + [pltpu.SemaphoreType.DMA(shape) for shape in sems.values()],
        compiler_params=pltpu.CompilerParams(
            collective_id=1, has_side_effects=True, vmem_limit_bytes=VMEM_LIMIT
        ),
        cost_estimate=pl.CostEstimate(flops=10**10, bytes_accessed=10**7, transcendentals=10**7),
    )(*ins.values())
    grads = [
        ((rows, cw), BF16), ((rows, cw), F32), ((1, cw), F32), ((1, cw), F32),
        ((wide, cw), F32), ((wide, cw), F32), ((wide, cw), F32), ((cw, wide), F32),
        ((wide, cw), F32), ((1, cw), F32), ((1, cw), F32), ((1, cw), F32), ((wide, cw), F32), ((1, cw), F32),
        ((cw, units), F32), ((units, cw), F32),
    ]
    done = pl.pallas_call(
        functools.partial(final_kernel, heads),
        out_shape=[jax.ShapeDtypeStruct(shape, kind) for shape, kind in grads],
        in_specs=[vmem] * len(outs),
        out_specs=[vmem] * len(grads),
        compiler_params=pltpu.CompilerParams(vmem_limit_bytes=VMEM_LIMIT),
    )(*sums)
    return tuple(a[0] if a.shape[0] == 1 else a for a in done)


def solution(mesh):
    cols = P(None, "width")
    vec = P("width")
    in_specs = (
        P(("batch", "hidden"), "width"), vec, vec, cols, cols, cols, P("width", None), cols, vec, vec, vec,
        cols, vec, P("width", "hidden"), P("hidden", "width"), P("batch", None),
        P(("batch", "hidden"), "width"),
    )
    out_specs = (
        P(("batch", "hidden"), "width"), P(("batch", "hidden"), "width"), vec, vec, cols, cols, cols,
        P("width", None), cols, vec, vec, vec, cols, vec, P("width", "hidden"), P("hidden", "width"),
    )
    return jax.shard_map(local, mesh=mesh, in_specs=in_specs, out_specs=out_specs, check_vma=False)
```

```python
import functools
import math
import types

import jax
import jax.numpy as jnp
from jax import lax
from jax.experimental import pallas as pl
from jax.experimental.pallas import tpu as pltpu
from jax.sharding import PartitionSpec as P

HD = 64
EPSILON = 1e-05
MESH = pl.DeviceIdType.MESH
F32 = jnp.float32
BF16 = jnp.bfloat16
NEG = -1e30
VMEM_LIMIT = 62 * 1024 * 1024
PLAN = {
    "begin": ("a1",), "row0": (), "col0": ("bx",), "row1": (), "col1": ("bz",), "row2": ("a2",), "col2": (),
    "loop": ("a3",), "whole": (), "sent": ("bg",), "proj": ("cy", "a4"), "half": ("cz",),
    "norm": ("bb",), "vec": ("cg",), "rows": ("a5",), "last": ("bc", "cb"), "end": ("cc",),
}
SCALE = HD**-0.5


def nn(a, b):
    return lax.dot_general(a, b, (((1,), (0,)), ((), ())), preferred_element_type=F32)


def nt(a, b):
    return lax.dot_general(a, b, (((1,), (1,)), ((), ())), preferred_element_type=F32)


def flip(a):
    return a.astype(F32).T.astype(BF16)


def remote(src, dst, send, recv, dev):
    return pltpu.make_async_remote_copy(
        src_ref=src, dst_ref=dst, send_sem=send, recv_sem=recv, device_id=dev, device_id_type=MESH
    )


def await_copy(ref, sem):
    pltpu.make_async_copy(ref, ref, sem).wait()


def at(index, size):
    return pl.ds(pl.multiple_of(index * size, size), size)


def sub_row(index, sub, dph):
    return jnp.where(lax.rem(index, 2) == 0, sub, dph - 1 - sub)


def segments(pos, ends):
    total = jnp.zeros(pos.shape, jnp.int32)
    for end in ends:
        total = total + (pos >= end).astype(jnp.int32)
    return total


def allowed_mask(key_base, query_base, keys, queries, ends):
    key_pos = key_base + lax.broadcasted_iota(jnp.int32, (keys, 1), 0)
    query_pos = query_base + lax.broadcasted_iota(jnp.int32, (1, queries), 1)
    same = segments(key_pos, ends) == segments(query_pos, ends)
    return same & (key_pos <= query_pos)


def sigmoid(x):
    return 1.0 / (1.0 + jnp.exp(-x))


def nbytes(ref):
    return math.prod(ref.shape) * ref.dtype.itemsize


class Sends:
    def __init__(self, sems, tally):
        self.sems, self.tally = sems, tally
        self.bytes = {}
        self.items = []

    def sem(self, group):
        return self.sems.at[group]

    def count(self, group, *sizes):
        self.bytes[group] = self.bytes.get(group, 0) + sum(sizes)

    def go(self, src, dst, recv, dev, group=0):
        copy = remote(src, dst, self.sem(group), recv, dev)
        copy.start()
        self.count(group, nbytes(src))
        return copy

    def start_if(self, cond, copy):
        @pl.when(cond)
        def _():
            copy.start()

        self.items.append((cond, copy))

    def wait(self, group, size):
        await_copy(self.tally.at[pl.ds(0, size // 512)], self.sem(group))

    def finish(self):
        for group, size in self.bytes.items():
            self.wait(group, size)
        for cond, copy in self.items:

            @pl.when(cond)
            def _(copy=copy):
                copy.wait_send()


def layer_kernel(names, sizes, *refs):
    r = types.SimpleNamespace(**dict(zip(names, refs)))
    nb, nh, rows, cw, units, heads, dph, tq = sizes
    half, wide, nz = rows // 2, 2 * cw, nh // 2
    per = half // tq
    pairs = nb // 2
    hops = nz.bit_length() - 1
    b, h, w = lax.axis_index("batch"), lax.axis_index("hidden"), lax.axis_index("width")
    group, sub = lax.div(h, dph), lax.rem(h, dph)
    z, c, bp = lax.div(h, 2), lax.rem(h, 2), lax.rem(b, 2)
    x_dev = (b, h, 1 - w)
    c_dev = (b, h + 1 - 2 * c, w)
    y_dev = (b + 1 - 2 * bp, h, w)

    def z_dev(k):
        zz = lax.rem(z + k, nz)
        return zz, (b, 2 * zz + c, w)

    own, other = at(w, cw), at(1 - w, cw)
    mine, theirs = at(w, half), at(1 - w, half)
    lanes = at(c, half)
    ends = [
        r.lens[0, 0],
        r.lens[0, 0] + r.lens[0, 1],
        r.lens[0, 0] + r.lens[0, 1] + r.lens[0, 2],
    ]
    sends = Sends(r.snd, r.tally)
    SUMS, LOOPS, ROWS, WEIGHTS, BACK = 3, 4, 5, 6, 7

    barrier = pltpu.get_barrier_semaphore()
    count = 0
    for dw in range(2):
        for dh in range(nh):
            if dh or dw:
                dev = (b, lax.rem(h + dh, nh), lax.rem(w + dw, 2))
                pl.semaphore_signal(barrier, inc=1, device_id=dev, device_id_type=MESH)
                count += 1
    for db in range(1, nb):
        dev = (lax.rem(b + db, nb), h, w)
        pl.semaphore_signal(barrier, inc=1, device_id=dev, device_id_type=MESH)
        count += 1
    loads = dict(
        tok0=(r.tok.at[pl.ds(0, half)], r.tokf.at[pl.ds(0, half), own]),
        tok1=(r.tok.at[pl.ds(half, half)], r.tokf.at[pl.ds(half, half), own]),
        wu=(r.wu, r.wup.at[z, c, w]), wd=(r.wd, r.wdn.at[z, c, w]),
        wq=(r.wq, r.wqkv.at[0]), wk=(r.wk, r.wqkv.at[1]), wv=(r.wv, r.wqkv.at[2]),
        wg1=(r.wg1, r.g1f.at[w]), wg2=(r.wg2, r.g2f.at[w]), wo=(r.wo, r.wof.at[w]),
        cot=(r.cot.at[mine], r.cotr.at[:, own]),
    )
    shared = dict(tok0=0, tok1=1, wu=2, wd=2, wq=3, wk=3, wv=3, wg1=4, wg2=4, wo=4, cot=5)
    for name, (src, dst) in loads.items():
        pltpu.make_async_copy(src, dst, r.ls.at[shared[name]]).start()
    for i, vec in enumerate((r.v0, r.v1, r.v2, r.v3, r.v4, r.v5)):
        r.vsrc[i : i + 1, :] = vec[...]
    pl.semaphore_wait(barrier, count)

    vcopy = sends.go(r.vsrc, r.vecf.at[:, own], r.xr.at[0], x_dev)
    tcopies = []
    for k in range(2):
        block = r.tokf.at[pl.ds(k * half, half), own]
        await_copy(block, r.ls.at[k])
        tcopies.append(sends.go(block, block, r.xr.at[1 + k], x_dev))
    await_copy(r.wup.at[z, c], r.ls.at[2])

    def weight_blocks(distance):
        for kind, buf in enumerate((r.wup, r.wdn)):
            for step in (1, -1) if distance else (1,):
                zz = z - step * distance
                index = jnp.clip(zz, 0, nz - 1)
                yield (zz >= 0) & (zz < nz) & (bp == kind), index, buf, step

    def weight_hop(k, ending=False):
        for here, index, buf, step in weight_blocks(k - 1):
            for way in (1, -1) if k == 1 else (step,):
                onward = (z + way >= 0) & (z + way < nz)
                going = here & (jnp.logical_not(onward) if ending else onward)
                block = buf.at[index, c, w]
                if k > 1:

                    @pl.when(going)
                    def _(block=block, index=index):
                        await_copy(block, r.wzr.at[index])
                        remote(block, block, sends.sem(WEIGHTS), r.wxr.at[index], x_dev).start()
                        remote(block, block, sends.sem(WEIGHTS), r.wyr.at[0], y_dev).start()

                if not ending:
                    dev = (b, 2 * jnp.clip(z + way, 0, nz - 1) + c, w)
                    copy = remote(block, block, r.wzs.at[(1 - way) // 2, k], r.wzr.at[index], dev)
                    sends.start_if(going, copy)

    def weight_cross(distance):
        for here, index, buf, _ in weight_blocks(distance):

            @pl.when(here)
            def _(index=index, buf=buf):
                block = buf.at[index, c, 1 - w]
                await_copy(block, r.wxr.at[index])
                remote(block, block, sends.sem(WEIGHTS), r.wyr.at[0], y_dev).start()

    for here, index, buf, _ in weight_blocks(0):
        block = buf.at[index, c, w]
        copy = remote(block, block, sends.sem(WEIGHTS), r.wxr.at[index], x_dev)

        @pl.when(here)
        def _(copy=copy):
            copy.start()

    weight_hop(1)
    gates = ((r.wg1, r.g1f), (r.wg2, r.g2f), (r.wo, r.wof))
    r.vecf[:, own] = r.vsrc[...]

    await_copy(r.wqkv, r.ls.at[3])
    for i in range(3):
        turned = flip(r.wqkv[i])
        for t in range(heads):
            r.wt[t, i * HD : (i + 1) * HD, :] = turned[t * HD : (t + 1) * HD]

    vcopy.wait_recv()
    gain, shift = r.vecf[0:1, :], r.vecf[1:2, :]

    def project(k):
        part = slice(k * half, (k + 1) * half)
        tcopies[k].wait_recv()
        x = r.tokf[part, :].astype(F32)
        centre = x - jnp.mean(x, -1, keepdims=True)
        spread = jnp.mean(centre * centre, -1, keepdims=True)
        n = (centre * lax.rsqrt(spread + EPSILON) * gain + shift).astype(BF16)
        r.npair[c, part, :] = n
        for t in range(heads):
            qkv = nt(r.wt[t], n).astype(BF16)
            r.qsrc[t, :, part] = qkv[:HD]
            r.kvsrc[t, :, part] = qkv[HD:]

    def head_copies(step, k):
        t = lax.rem(group + step, heads)
        span = pl.ds(k * half, half)
        src, dst = r.kvsrc.at[t, :, span], r.kvt.at[h, :, span]
        if step:
            yield None, remote(src, dst, sends.sem(LOOPS), r.kr.at[h], (b, t * dph + sub, w))
        else:
            yield None, pltpu.make_async_copy(src, dst, r.kr.at[h])
        for i in range(per):
            row = k * per + i
            target = sub_row(h, row, dph)
            src, dst = r.qsrc.at[t, :, pl.ds(row * tq, tq)], r.qt.at[h]
            copy = remote(src, dst, sends.sem(LOOPS), r.qr.at[h], (b, t * dph + target, w))
            if step:
                yield None, copy
            else:
                yield target != sub, copy
                yield target == sub, pltpu.make_async_copy(src, dst, r.qr.at[h])

    def send_heads(step, k):
        for cond, copy in head_copies(step, k):
            if cond is None:
                copy.start()
            else:

                @pl.when(cond)
                def _(copy=copy):
                    copy.start()

    project(0)
    weight_hop(2)
    weight_hop(2, ending=True)
    send_heads(heads - 1, 0)
    project(1)
    send_heads(heads - 1, 1)
    for k in range(2):
        send_heads(0, k)

    def sends_of(count, buf, sem):
        await_copy(r.tally.at[pl.ds(0, count * nbytes(buf.at[0, 0, 0]) // 512)], sem)

    def weights_over_core():
        for kind, buf in enumerate((r.wup, r.wdn)):

            @pl.when(bp != kind)
            def _(buf=buf):
                sends_of(2 * nz - 1, buf, r.wyr.at[0])

            block = buf.at[:, c]
            sends.go(block, block, r.wcr.at[kind], c_dev, 1)

    def gates_over_core():
        for i, (src, dst) in enumerate(gates):
            piece = dst.at[1 - w, at(c, src.shape[0] // 2)]
            if i == 0:
                await_copy(r.tally.at[pl.ds(0, 3 * nbytes(piece) // 512)], r.gxr.at[0])
            sends.go(piece, piece, r.gcr.at[0], c_dev)

    def weights_sent():
        sends.wait(WEIGHTS, (3 * nz - 1) * nbytes(r.wu))

    def pass_on(s):
        @pl.when(lax.rem(s, dph) == sub)
        def _():
            await_copy(r.kvt.at[s], r.kr.at[s])
            for k in range(1, dph):
                dev = (b, group * dph + lax.rem(sub + k, dph), w)
                remote(r.kvt.at[s], r.kvt.at[s], sends.sem(LOOPS), r.fr.at[s], dev).start()

    def arrive(s):
        @pl.when(lax.rem(s, dph) != sub)
        def _():
            await_copy(r.kvt.at[s], r.fr.at[s])

        r.kvn[s] = flip(r.kvt[s])
        await_copy(r.qt.at[s], r.qr.at[s])
        q = r.qt[s].astype(F32) * SCALE
        r.qlow[s] = jnp.concatenate([q, jnp.zeros_like(q)], 0).astype(BF16)

    def masked(scores, i, j):
        query_base = i * rows + sub_row(i, sub, dph) * tq
        return jnp.where(allowed_mask(j * rows, query_base, scores.shape[0], tq, ends), scores, NEG)

    def bias(scores, j):
        key_pos = j * rows + lax.broadcasted_iota(jnp.int32, (rows, 1), 0)
        return scores + jnp.where(key_pos < ends[0], NEG, 0.0)

    def absorb(i, blocks):
        top = r.top[i]
        new_top = top
        for scores, _ in blocks:
            new_top = jnp.maximum(new_top, jnp.max(scores, 0, keepdims=True))
        fade = jnp.exp(top - new_top)
        total, mixed = r.total[i] * fade, r.ot[i] * fade
        for scores, j in blocks:
            weights = jnp.exp(scores - new_top)
            total = total + jnp.sum(weights, 0, keepdims=True)
            mixed = mixed + nn(r.kvt[j, HD:, : weights.shape[0]], weights.astype(BF16))
        r.top[i], r.total[i], r.ot[i] = new_top, total, mixed

    def send_attended(s):
        row = sub_row(s, sub, dph)
        total = r.total[s]
        mixed = r.ot[s] / total
        r.ot[s] = mixed
        r.lse[s] = r.top[s] + jnp.log(total)
        r.osend[s] = mixed.astype(BF16)
        row_w = lax.div(row * tq, half)
        lane = lax.rem(row * tq, half)
        dst = r.att.at[at(w * heads + group, HD), pl.ds(pl.multiple_of(lane, tq), tq)]
        slot = r.orc.at[0]
        here = (s == h) & (row_w == w)

        @pl.when(here)
        def _():
            pltpu.make_async_copy(r.osend.at[s], dst, slot).start()

        @pl.when(jnp.logical_not(here))
        def _():
            remote(r.osend.at[s], dst, sends.sem(ROWS), slot, (b, s, row_w)).start()

    def short(i):
        return (sub_row(i, sub, dph) + 1) * tq <= half

    def own_chip(n):
        i = 2 * n

        def with_keys(first_keys, second_keys):
            first = masked(nn(r.kvn[i, :first_keys], r.qlow[i]), i, i)
            low = masked(nn(r.kvn[i], r.qlow[i + 1]), i + 1, i)
            high = masked(nn(r.kvn[i + 1, :second_keys], r.qlow[i + 1]), i + 1, i + 1)
            absorb(i, [(first, i)])
            absorb(i + 1, [(low, i), (high, i + 1)])

        @pl.when(short(i))
        def _():
            with_keys(half, rows)

        @pl.when(jnp.logical_not(short(i)))
        def _():
            with_keys(rows, half)

    def two_chips(hi, lo, last):
        queries, keys = (2 * hi, 2 * hi + 1), (2 * lo, 2 * lo + 1)
        scores = [[nn(r.kvn[j], r.qlow[i]) for j in keys] for i in queries]
        for a, i in enumerate(queries):
            if last and a:
                blocks = [(masked(x, i, j), j) for x, j in zip(scores[a], keys)]
            else:
                blocks = [(bias(scores[a][0], keys[0]), keys[0]), (scores[a][1], keys[1])]
            absorb(i, blocks)

    def completes(chip):
        return jnp.where(z == 0, chip, nz - z + jnp.minimum(chip, z - 1))

    def chip_at(d):
        return lax.rem(z + d, nz)

    def stage_passes(d):
        pass_on(2 * chip_at(d))
        pass_on(2 * chip_at(d) + 1)

    def stage_computes(d):
        n = chip_at(d)
        arrive(2 * n)
        arrive(2 * n + 1)
        own_chip(n)

        def with_earlier(e, _):
            @pl.when((d == nz - 1) & (e == 1))
            def _():
                weight_cross(nz - 1)

            m = lax.rem(z + e, nz)
            hi, lo = jnp.maximum(n, m), jnp.minimum(n, m)

            @pl.when(hi == nz - 1)
            def _():
                two_chips(hi, lo, True)

            @pl.when(hi != nz - 1)
            def _():
                two_chips(hi, lo, False)

            @pl.when((m > n) & (completes(m) == d))
            def _():
                send_attended(2 * m)
                send_attended(2 * m + 1)

            return 0

        lax.fori_loop(0, d, with_earlier, 0)

        @pl.when(completes(n) == d)
        def _():
            send_attended(2 * n)
            send_attended(2 * n + 1)

    def late_stage(d, _):
        stage_passes(d)

        @pl.when(d == 2)
        def _():
            for k in range(2):
                send_heads(1, k)
            for distance in range(2):
                weight_cross(distance)

        @pl.when(d == nz // 2)
        def _():
            weight_hop(nz, ending=True)

        @pl.when(d == nz - 1)
        def _():
            for distance in range(2, nz - 1):
                weight_cross(distance)

        stage_computes(d)
        return 0

    r.top[...] = jnp.full_like(r.top, NEG)
    r.total[...] = jnp.zeros_like(r.total)
    r.ot[...] = jnp.zeros_like(r.ot)
    stage_passes(0)
    stage_computes(0)
    await_copy(r.wqkv, r.ls.at[4])
    for src, dst in gates:
        block = dst.at[w, at(c, src.shape[0] // 2)]
        sends.go(block, block, r.gxr.at[0], x_dev)
    sends.go(r.npair.at[c], r.npair.at[c], r.cr.at[0], c_dev)
    stage_passes(1)
    for k in range(3, nz):
        weight_hop(k)
    for k in range(2):
        send_heads(2, k)
    for k in range(3, nz):
        weight_hop(k, ending=True)
    stage_computes(1)
    await_copy(r.cotr.at[:, own], r.ls.at[5])
    sends.go(r.cot.at[theirs], r.cotr.at[:, own], r.xr.at[3], x_dev)
    lax.fori_loop(2, nz, late_stage, 0)
    gates_over_core()
    weights_over_core()

    await_copy(r.tally.at[pl.ds(0, 3 * nbytes(r.wg1) // 1024)], r.gcr.at[0])

    def two(a, weight):
        return jnp.concatenate([nn(a, weight[0]), nn(a, weight[1])], 1)

    def two_back(g, weight):
        return nt(g[:, :cw], weight[0]) + nt(g[:, cw:], weight[1])

    tok = r.tokf[mine, :].astype(F32)
    n1 = r.npair[c, mine, :]
    gate_one = sigmoid(two(n1, r.g1f) + r.vecf[2:3, :])
    await_copy(r.att, r.orc.at[0])
    wof = r.wof[...].reshape(wide, wide)
    branch_one = nn(flip(r.att[...]), wof)
    middle = tok + gate_one * (branch_one - tok)
    centre = middle - jnp.mean(middle, -1, keepdims=True)
    rstd = lax.rsqrt(jnp.mean(centre * centre, -1, keepdims=True) + EPSILON)
    n2 = centre * rstd
    gain_two = r.vecf[3:4, :]
    normed_two = (n2 * gain_two + r.vecf[4:5, :]).astype(BF16)
    gate_two = sigmoid(two(normed_two, r.g2f) + r.vecf[5:6, :])
    for kind, buf in enumerate((r.wup, r.wdn)):
        await_copy(buf.at[:, 1 - c], r.wcr.at[kind])

    def units_of(i2, p):
        return i2, lax.rem(c + p, 2)

    def up(i2, branch):
        for p in range(2):
            i, q = units_of(i2, p)
            pre = nn(normed_two, r.wup[i, q].reshape(wide, units))
            r.pre[i2, p] = pre
            act = jax.nn.gelu(pre).astype(BF16)
            r.actall[:, pl.ds(pl.multiple_of((2 * i + q) * units, units), units)] = act
            if p:
                r.acts[i2] = act
                dst = r.actp.at[i2, lanes, :]
                remote(r.acts.at[i2], dst, sends.sem(LOOPS), r.ar.at[0], c_dev).start()
            else:
                r.actp[i2, lanes, :] = act
        return branch

    lax.fori_loop(0, nz, up, 0)
    deep = nh * units
    branch_two = jnp.concatenate([nn(r.actall[...], r.wdn[:, :, v].reshape(deep, cw)) for v in range(2)], 1)
    delta = branch_two - middle
    r.outr[...] = (middle + gate_two * delta).astype(BF16)
    ocopy = sends.go(r.outr.at[:, other], r.out_c.at[mine, :], r.xr.at[4], x_dev)
    await_copy(r.cotr.at[:, own], r.xr.at[3])
    grad = r.cotr[...].astype(F32)
    gb2 = (grad * gate_two).astype(BF16)
    gl2 = (grad * delta * gate_two * (1.0 - gate_two)).astype(BF16)
    gmid = grad * (1.0 - gate_two)

    def down(i2, total):
        for p in range(2):
            i, q = units_of(i2, p)
            ghid = nt(gb2[:, :cw], r.wdn[i, q, 0]) + nt(gb2[:, cw:], r.wdn[i, q, 1])
            pre = r.pre[i2, p]
            k = 0.7978845608028654
            t = jnp.tanh(k * (pre + 0.044715 * pre * pre * pre))
            slope = 0.5 * (1.0 + t) + 0.5 * pre * (1.0 - t * t) * (k * (1.0 + 3 * 0.044715 * pre * pre))
            gpre = (ghid * slope).astype(BF16)
            total = total + nt(gpre, r.wup[i, q].reshape(wide, units))
            if p:
                r.gpres[i2] = gpre
                dst = r.gprep.at[i2, lanes, :]
                remote(r.gpres.at[i2], dst, sends.sem(LOOPS), r.pr.at[0], c_dev).start()
            else:
                r.gprep[i2, lanes, :] = gpre
        return total

    gnorm = lax.fori_loop(0, nz, down, two_back(gl2, r.g2f))
    e = gnorm * gain_two
    gmid = gmid + rstd * (
        e - jnp.mean(e, -1, keepdims=True) - n2 * jnp.mean(e * n2, -1, keepdims=True)
    )
    gb1 = (gmid * gate_one).astype(BF16)
    r.gatt[...] = nt(wof, gb1).astype(BF16)
    for dw in (1, 0):
        wt = lax.rem(w + dw, 2)
        for step in range(heads - 1, -1, -1):
            t = lax.rem(group + step, heads)
            for i in range(per):
                target = sub_row(h, w * per + i, dph)
                src = r.gatt.at[at(wt * heads + t, HD), pl.ds(i * tq, tq)]
                dst = r.dot.at[h]
                dev = (b, t * dph + target, wt)
                slot = r.dr.at[jnp.where(h == nh - 1, 1, 0)]
                copy = remote(src, dst, sends.sem(ROWS), slot, dev)
                if step or dw:
                    copy.start()
                else:

                    @pl.when(target != sub)
                    def _(copy=copy):
                        copy.start()

                    @pl.when(target == sub)
                    def _(src=src, dst=dst, slot=slot):
                        pltpu.make_async_copy(src, dst, slot).start()

    gl1 = (gmid * (branch_one - tok) * gate_one * (1.0 - gate_one)).astype(BF16)
    r.ginp[...] = gmid * (1.0 - gate_one)
    r.npt[:, lanes] = flip(normed_two)
    sends.go(r.npt.at[:, lanes], r.npt.at[:, lanes], r.cr.at[1], c_dev)
    r.gbt[:, lanes] = flip(gb2)
    sends.go(r.gbt.at[:, lanes], r.gbt.at[:, lanes], r.cr.at[1], c_dev)
    quarter = half // 2
    r.lsrc[0] = r.att[...]
    r.lsrc[1] = flip(gl1)
    r.lsrc[2] = flip(gl2)
    for m, right in enumerate((gb1, n1, normed_two)):
        r.bpair[m, lanes, :] = right
        block = r.bpair.at[m, lanes, :]
        sends.go(block, block, r.cr.at[2], c_dev, 2)
        for v in range(2):
            src = r.lsrc.at[m, at(2 * v + 1 - c, quarter), :]
            dst = r.apair.at[m, v, :, lanes]
            sends.go(src, dst, r.cr.at[2], c_dev, 2)
            r.apair[m, v, :, lanes] = r.lsrc[m, at(2 * v + c, quarter), :]
    r.gterm[...] = two_back(gl1, r.g1f)
    r.vsum[...] = jnp.zeros_like(r.vsum)
    r.vsum[2:3, :] = jnp.sum(gl1.astype(F32), 0, keepdims=True)
    r.vsum[3:4, :] = jnp.sum(gnorm * n2, 0, keepdims=True)
    r.vsum[4:5, :] = jnp.sum(gnorm, 0, keepdims=True)
    r.vsum[5:6, :] = jnp.sum(gl2.astype(F32), 0, keepdims=True)
    r.out_c[mine, :] = r.outr[:, own]

    eighth = quarter // 2
    await_copy(r.npt, r.cr.at[1])
    await_copy(r.gpres, r.pr.at[0])
    await_copy(r.acts, r.ar.at[0])

    def weight_grads(i2, _):
        r.ga[0, i2] = nn(r.npt[...], r.gprep[i2]).astype(BF16).reshape(2, 2, quarter, units)
        r.ga[1, i2] = nn(r.gbt[...], r.actp[i2]).astype(BF16).reshape(2, 2, quarter, units)
        return 0

    lax.fori_loop(0, nz, weight_grads, 0)
    sends.go(r.ga.at[0, :, 1 - w], r.xin0, r.xr.at[5], x_dev, 2)
    pair_bytes = 3 * (nbytes(r.bpair.at[0, lanes, :]) + 2 * nbytes(r.apair.at[0, 0, :, lanes]))
    await_copy(r.tally.at[pl.ds(0, pair_bytes // 512)], r.cr.at[2])
    for m in range(3):
        for v in range(2):
            block = nn(r.apair[m, v], r.bpair[m]).astype(BF16)
            for y in range(2):
                r.gb[v, y, m] = block[y * eighth : (y + 1) * eighth]
    for m in range(3):
        sends.go(r.gb.at[:, 1 - bp, m], r.ybin.at[:, m], r.syr.at[0], y_dev, 2)


    def z_block(q, flip_bit, v):
        bit = lax.rem(lax.div(z, 1 << q), 2)
        bit = 1 - bit if flip_bit else bit
        return lax.rem(z, 1 << q) + bit * (1 << q) + v * (2 << q)

    def ffn_first():
        remote(r.ga.at[1, :, :, 1 - bp], r.yin1, sends.sem(SUMS), r.yr.at[1], y_dev).start()

    def ffn_second():
        await_copy(r.xin0, r.xr.at[5])
        r.ga[0, :, w] = (r.ga[0, :, w].astype(F32) + r.xin0[...].astype(F32)).astype(BF16)
        remote(r.ga.at[0, :, w, 1 - bp], r.yin0, sends.sem(SUMS), r.yr.at[2], y_dev).start()
        await_copy(r.yin1, r.yr.at[1])
        r.ga[1, :, :, bp] = (r.ga[1, :, :, bp].astype(F32) + r.yin1[...].astype(F32)).astype(BF16)
        remote(r.ga.at[1, :, 1 - w, bp], r.xin1, sends.sem(SUMS), r.xr.at[6], x_dev).start()

    def ffn_third():
        await_copy(r.yin0, r.yr.at[2])
        await_copy(r.xin1, r.xr.at[6])
        r.zs[:, 0] = (r.ga[0, :, w, bp].astype(F32) + r.yin0[...].astype(F32)).astype(BF16)
        r.zs[:, 1] = (r.ga[1, :, w, bp].astype(F32) + r.xin1[...].astype(F32)).astype(BF16)
        ffn_hop(0)

    def ffn_hop(q):
        if q:
            ffn_add(q - 1)
        bit = lax.rem(lax.div(z, 1 << q), 2)
        dev = (b, 2 * (z + (1 << q) * (1 - 2 * bit)) + c, w)
        for v in range(nz >> (q + 1)):
            slot = nz - (nz >> q) + v
            remote(r.zs.at[z_block(q, True, v)], r.zin.at[slot], sends.sem(SUMS), r.zsr.at[slot], dev).start()

    def ffn_add(q):
        for v in range(nz >> (q + 1)):
            slot = nz - (nz >> q) + v
            await_copy(r.zin.at[slot], r.zsr.at[slot])
            kept = z_block(q, False, v)
            r.zs[kept] = (r.zs[kept].astype(F32) + r.zin[slot].astype(F32)).astype(BF16)

    def ffn_fourth():
        ffn_add(hops - 1)
        total = r.zs[z].astype(F32)
        if pairs > 1:
            mypair = lax.div(b, 2)
            r.pin[mypair] = total.astype(BF16)
            for k in range(1, pairs):
                dev = (lax.rem(b + 2 * k, nb), h, w)
                block = r.pin.at[mypair]
                remote(block, block, sends.sem(SUMS), r.par.at[mypair], dev).start()
            for k in range(1, pairs):
                pp = lax.rem(mypair + k, pairs)
                await_copy(r.pin.at[pp], r.par.at[pp])
            total = r.pin[0].astype(F32)
            for k in range(1, pairs):
                total = total + r.pin[k].astype(F32)
        r.red_a[bp] = total.astype(BF16)
        block = r.red_a.at[bp]
        remote(block, block, sends.sem(SUMS), r.yr.at[3], y_dev).start()

    def sums_sent():
        sends.count(SUMS, nbytes(r.yin1), nbytes(r.yin0), nbytes(r.xin1), nbytes(r.red_a.at[0]))
        sends.count(SUMS, (nz - 1) * nbytes(r.zin.at[0]), (pairs - 1) * nbytes(r.pin.at[0]))
        sends.count(SUMS, nbytes(r.xbin), nbytes(r.ycin), 2 * nbytes(r.ycin), nbytes(r.red_s) // 2)
        sends.count(SUMS, 6 * (2 * (nz - 1) + pairs - 1) * nbytes(r.pzin.at[0, 0, 0]))

    zr = HD * 4 // nz

    def z_part(zz):
        return pl.ds(pl.multiple_of(lax.div(zz, 4) * zr, zr), zr), at(lax.rem(zz, 4), 128)

    def square_x():
        await_copy(r.ybin, r.syr.at[0])
        for p in range(3):
            r.gb[:, bp, p] = (r.gb[:, bp, p].astype(F32) + r.ybin[:, p].astype(F32)).astype(BF16)
            remote(r.gb.at[1 - w, bp, p], r.xbin.at[p], sends.sem(SUMS), r.sxr.at[0], x_dev).start()

    def over_pairs(which, p, total):
        if pairs == 1:
            return total
        mypair = lax.div(b, 2)
        r.sqpair[which, p, mypair] = total
        for k in range(1, pairs):
            dev = (lax.rem(b + 2 * k, nb), h, w)
            block = r.sqpair.at[which, p, mypair]
            remote(block, block, sends.sem(SUMS), r.sqpr.at[which, p, mypair], dev).start()
        for k in range(1, pairs):
            pp = lax.rem(mypair + k, pairs)
            await_copy(r.sqpair.at[which, p, pp], r.sqpr.at[which, p, pp])
        total = r.sqpair[which, p, 0].astype(F32)
        for k in range(1, pairs):
            total = total + r.sqpair[which, p, k].astype(F32)
        return total.astype(BF16)

    def scatter(which):
        for p in range(3):
            if which:
                await_copy(r.ycin.at[p], r.pyr.at[p])
                r.sq[1, p] = (r.gc[bp, p].astype(F32) + r.ycin[p].astype(F32)).astype(BF16)
            else:
                if p == 0:
                    await_copy(r.xbin, r.sxr.at[0])
                r.sq[0, p] = (r.gb[w, bp, p].astype(F32) + r.xbin[p].astype(F32)).astype(BF16)
            for k in range(nz - 1, 0, -1):
                zz, dev = z_dev(k)
                src, dst = r.sq.at[(which, p) + z_part(zz)], r.pzin.at[which, p, z]
                remote(src, dst, sends.sem(SUMS), r.pzr.at[which, p], dev).start()

    def gather(which):
        for p in range(3):
            total = r.sq[(which, p) + z_part(z)].astype(F32)
            await_copy(r.pzin.at[which, p, pl.ds(0, nz - 1)], r.pzr.at[which, p])
            for k in range(1, nz):
                zz, _ = z_dev(k)
                total = total + r.pzin[which, p, zz].astype(F32)
            block = (which, c, bp, p) + z_part(z)
            r.red_s[block] = over_pairs(which, p, total.astype(BF16))
            for k in range(nz - 1, 0, -1):
                _, dev = z_dev(k)
                ref = r.red_s.at[block]
                remote(ref, ref, sends.sem(SUMS), r.pgr.at[which, p], dev).start()

    def back(which):
        for p in range(3):
            await_copy(r.pzin.at[which, p, pl.ds(0, nz - 1)], r.pgr.at[which, p])
            block = r.red_s.at[which, c, bp, p]
            remote(block, block, sends.sem(SUMS), r.sbr.at[which, p], y_dev).start()

    def square_core(which):
        for p in range(3):
            await_copy(r.red_s.at[which, c, 1 - bp, p], r.sbr.at[which, p])
            block = r.red_s.at[which, c, :, p]
            remote(block, block, sends.sem(SUMS), r.scr.at[which], c_dev).start()

    def proj_y():
        for p in range(3):
            remote(r.gc.at[1 - bp, p], r.ycin.at[p], sends.sem(SUMS), r.pyr.at[p], y_dev).start()

    steps = dict(
        a1=ffn_first, a2=ffn_second, a3=ffn_third, a4=lambda: [ffn_hop(q) for q in range(1, hops)], a5=ffn_fourth,
        bx=square_x, bz=lambda: scatter(0), bg=lambda: gather(0), bb=lambda: back(0), bc=lambda: square_core(0),
        cy=proj_y, cz=lambda: scatter(1), cg=lambda: gather(1), cb=lambda: back(1), cc=lambda: square_core(1),
    )

    def take(point):
        for name in PLAN[point]:
            steps[name]()

    r.acc[...] = jnp.zeros_like(r.acc)

    def finish(s):
        @pl.when(lax.rem(s, dph) == sub)
        def _():
            total = r.acc[s]
            for k in range(1, dph):
                slot = r.pin_kv.at[lax.div(s, dph), k - 1]
                await_copy(slot, r.pkr.at[lax.div(s, dph), k - 1])
                total = total + r.pin_kv[lax.div(s, dph), k - 1]
            r.dkvsend[s, :HD] = (total[:HD] * SCALE).astype(BF16)
            r.dkvsend[s, HD:] = total[HD:].astype(BF16)
            dst = r.dqkv.at[group, pl.ds(HD, 2 * HD), :]

            @pl.when(s == h)
            def _():
                pltpu.make_async_copy(r.dkvsend.at[s], dst, r.dkr.at[group]).start()

            @pl.when(s != h)
            def _():
                remote(r.dkvsend.at[s], dst, sends.sem(BACK), r.dkr.at[group], (b, s, w)).start()

    def pairs_backward(where, full):
        spans = [slice(0, half if whole == "half" else rows) for whole in full]
        scores = [nn(r.kvn[j, span], r.qlow[i]) for (i, j), span in zip(where, spans)]
        gprobs = [nn(r.kvn[j, span], r.dhigh[i]) for (i, j), span in zip(where, spans)]
        for x, gp, (i, j), whole, span in zip(scores, gprobs, where, full, spans):
            x = masked(x, i, j) if whole else bias(x, j)
            probs = jnp.exp(x - r.lse[i])
            gscores = (probs * (gp - r.centre[i])).astype(BF16)
            r.acc[j, HD:, span] += nt(r.dhigh[i, HD:, :], probs.astype(BF16))
            r.acc[j, :HD, span] += nt(r.qt[i], gscores)
            r.dqa[i] += nn(r.kvt[j, :HD, span], gscores)

    def choose(kinds, where):
        taken = False
        for cond, full in kinds:

            @pl.when(jnp.logical_and(cond, jnp.logical_not(taken)))
            def _(full=full):
                pairs_backward(where, full)

            taken = jnp.logical_or(taken, cond)

    def pair_at(t, u):
        lo, hi = t, nh - 1 - t
        n = hi - lo + 1
        return jnp.where(u < n, hi, lo + u - n), jnp.where(u < n, lo + u, lo)

    def out_arrives(s):
        dout = r.dot[s]
        r.dhigh[s] = jnp.concatenate([jnp.zeros((HD, tq), BF16), dout], 0)
        r.centre[s] = jnp.sum(r.ot[s] * dout.astype(F32), 0, keepdims=True)

    def send_block(s):
        row = sub_row(s, sub, dph)
        r.dqsend[s] = (r.dqa[s] * SCALE).astype(BF16)
        dst = r.dqkv.at[group, pl.ds(0, HD), pl.ds(pl.multiple_of(row * tq, tq), tq)]

        @pl.when(s == h)
        def _():
            pltpu.make_async_copy(r.dqsend.at[s], dst, r.dkr.at[group]).start()

        @pl.when(s != h)
        def _():
            remote(r.dqsend.at[s], dst, sends.sem(BACK), r.dkr.at[group], (b, s, w)).start()

        owner = lax.rem(s, dph)

        @pl.when(owner != sub)
        def _():
            k = lax.rem(sub - owner + dph, dph)
            dev = (b, group * dph + owner, w)
            slot = lax.div(s, dph)
            remote(r.acc.at[s], r.pin_kv.at[slot, k - 1], sends.sem(BACK), r.pkr.at[slot, k - 1], dev).start()

    def round_backward(t, _):
        lo, hi = t, nh - 1 - t
        n = hi - lo + 1

        rowed = lax.div(n, 2)
        columned = rowed - 1

        def row_step(v, _):
            where = [pair_at(t, 2 * v), pair_at(t, 2 * v + 1)]
            kinds = [(t == 0, (True, True)), ((v == rowed - 1) & short(hi), (False, "half"))]
            choose(kinds + [(v == rowed - 1, (False, True)), (True, (False, False))], where)

            @pl.when((t > 0) & (v == jnp.minimum(1, rowed - 1)))
            def _():
                finish(lo - 1)

            return 0

        lax.fori_loop(0, rowed, row_step, 0)
        send_block(hi)

        @pl.when(t == 0)
        def _():
            await_copy(r.dot.at[pl.ds(0, nh - 1)], r.dr.at[0])
            lax.fori_loop(0, nh - 1, lambda s, z: (out_arrives(s), z)[1], 0)

        for at_round, point in ((0, "row0"), (nh // 8, "row1"), (nh // 4, "row2")):
            if PLAN[point]:

                @pl.when(t == at_round)
                def _(point=point):
                    take(point)

        def column_step(v, _):
            where = [pair_at(t, n + 2 * v), pair_at(t, n + 2 * v + 1)]
            kinds = [((v == 0) & short(lo), ("half", False)), (v == 0, (True, False))]
            choose(kinds + [(True, (False, False))], where)

            @pl.when(v == jnp.minimum(1, columned - 1))
            def _():
                finish(hi)

            return 0

        lax.fori_loop(0, columned, column_step, 0)
        pairs_backward([pair_at(t, 2 * n - 2)], (True,))
        send_block(lo)

        @pl.when(columned == 0)
        def _():
            finish(hi)

        for at_round, point in ((0, "col0"), (nh // 8, "col1"), (nh // 4, "col2")):
            if PLAN[point]:

                @pl.when(t == at_round)
                def _(point=point):
                    take(point)

        return 0

    r.dqa[...] = jnp.zeros_like(r.dqa)
    await_copy(r.dot.at[nh - 1], r.dr.at[1])
    out_arrives(nh - 1)
    take("begin")
    lax.fori_loop(0, nh // 2, round_backward, 0)
    finish(nh // 2 - 1)
    take("loop")

    def write(i, src, dst):
        pltpu.make_async_copy(src, dst, r.os.at[i]).start()

    ocopy.wait_recv()
    write(0, r.out_c, r.h_out_c)

    for t in range(heads):
        await_copy(r.dqkv.at[t], r.dkr.at[t])

        @pl.when(t % 2 != c)
        def _(t=t):
            remote(r.dqkv.at[t], r.dsib.at[t // 2], sends.sem(BACK), r.tr.at[0], c_dev).start()

    take("whole")
    wts = r.wt[...].reshape(heads * 3 * HD, wide)

    def grad_normed(span):
        return nn(flip(r.dqkv[:, :, span].reshape(heads * 3 * HD, half)), wts)

    r.psend[...] = grad_normed(theirs).astype(BF16)
    pcopy = sends.go(r.psend, r.precv, r.xr.at[8], x_dev)
    take("sent")
    await_copy(r.npair.at[1 - c], r.cr.at[0])
    await_copy(r.dsib, r.tr.at[0])
    for j in range(heads // 2):
        part = nn(r.dqkv[2 * j + c], r.npair[c]) + nn(r.dsib[j], r.npair[1 - c])
        for p in range(3):
            r.gc[j, p] = part[p * HD : (p + 1) * HD].astype(BF16)
    take("proj")
    gnorm = grad_normed(mine) + r.gterm[...]
    x = r.tokf[mine, :].astype(F32)
    centre = x - jnp.mean(x, -1, keepdims=True)
    rstd = lax.rsqrt(jnp.mean(centre * centre, -1, keepdims=True) + EPSILON)
    n = centre * rstd
    take("half")
    pcopy.wait_recv()
    gnorm = gnorm + r.precv[...].astype(F32)
    e = gnorm * r.vecf[0:1, :]
    result = r.ginp[...] + rstd * (
        e - jnp.mean(e, -1, keepdims=True) - n * jnp.mean(e * n, -1, keepdims=True)
    )
    r.tsend[...] = result.astype(BF16)
    tcopy = sends.go(r.tsend.at[:, other], r.trecv, r.xr.at[9], x_dev)
    r.vsum[0:1, :] = jnp.sum(gnorm * n, 0, keepdims=True)
    r.vsum[1:2, :] = jnp.sum(gnorm, 0, keepdims=True)
    me4 = 2 * c + w
    r.vin4[me4] = r.vsum[...]
    for dc in range(2):
        for dw in range(2):
            if dc or dw:
                cc, ww = lax.rem(c + dc, 2), lax.rem(w + dw, 2)
                dev = (b, 2 * z + cc, ww)
                sends.go(r.vin4.at[me4], r.vin4.at[me4], r.vr.at[0], dev)
    r.gtok[mine, :] = jnp.where(w == 0, result[:, :cw], result[:, cw:])
    write(1, r.gtok.at[mine], r.h_gtok.at[mine])
    take("norm")
    await_copy(r.vin4.at[pl.ds(0, 3)], r.vr.at[0])
    r.vinz[z] = r.vin4[0] + r.vin4[1] + r.vin4[2] + r.vin4[3]
    for k in range(1, nz):
        _, dev = z_dev(k)
        sends.go(r.vinz.at[z], r.vinz.at[z], r.vr.at[1], dev)
    take("vec")
    tcopy.wait_recv()
    r.gtok[theirs, :] = r.trecv[...].astype(F32)
    write(1, r.gtok.at[theirs], r.h_gtok.at[theirs])
    take("rows")
    await_copy(r.vinz.at[pl.ds(0, nz - 1)], r.vr.at[1])
    total = r.vinz[0]
    for k in range(1, nz):
        total = total + r.vinz[k]
    r.vinb[b] = total
    for k in range(1, nb):
        dev = (lax.rem(b + k, nb), h, w)
        sends.go(r.vinb.at[b], r.vinb.at[b], r.vr.at[2], dev)
    take("last")
    await_copy(r.vinb.at[pl.ds(0, nb - 1)], r.vr.at[2])
    total = r.vinb[0]
    for k in range(1, nb):
        total = total + r.vinb[k]
    r.red_v[...] = jnp.where(w == 0, total[:, :cw], total[:, cw:])
    write(2, r.red_v, r.h_red_v)
    write(3, r.red_s.at[0, c], r.h_red_s.at[0, c])
    take("end")
    write(3, r.red_s.at[1, c], r.h_red_s.at[1, c])
    await_copy(r.red_a.at[1 - bp], r.yr.at[3])
    write(4, r.red_a, r.h_red_a)
    for which in range(2):
        await_copy(r.red_s.at[which, 1 - c], r.scr.at[which])
        write(3, r.red_s.at[which, 1 - c], r.h_red_s.at[which, 1 - c])

    own_blocks = nh // dph
    loops = [(heads - 1) * nbytes(r.kvt.at[0]), (nh - 1) * nbytes(r.qt.at[0]), (dph - 1) * own_blocks * nbytes(r.kvt.at[0])]
    sends.count(LOOPS, *loops, nbytes(r.acts), nbytes(r.gpres))
    sends.count(BACK, (nh - 1) * nbytes(r.dqsend.at[0]), heads // 2 * nbytes(r.dqkv.at[0]))
    sends.count(BACK, (own_blocks - 1) * nbytes(r.dkvsend.at[0]), (nh - own_blocks) * nbytes(r.acc.at[0]))
    rowed = (nh + 2 * heads * per) * nbytes(r.osend.at[0])
    local_row = lax.div(sub_row(h, sub, dph) * tq, half) == w

    @pl.when(local_row)
    def _():
        sends.wait(ROWS, rowed - 2 * nbytes(r.osend.at[0]))

    @pl.when(jnp.logical_not(local_row))
    def _():
        sends.wait(ROWS, rowed)

    weights_sent()
    sums_sent()
    sends.finish()
    for i, ref in enumerate((r.out_c, r.gtok, r.red_v, r.red_s, r.red_a)):
        await_copy(ref, r.os.at[i])


def final_kernel(heads, *refs):
    (
        out_c, gtok, red_a, red_s, red_v,
        o_out, o_tok, o_g1, o_b1, o_wq, o_wk, o_wv, o_wo, o_gw1, o_gb1, o_g2, o_b2, o_gw2, o_gb2, o_up, o_dn,
    ) = refs
    o_out[...] = out_c[...]
    o_tok[...] = gtok[...]
    for i, ref in enumerate((o_g1, o_b1, o_gb1, o_g2, o_b2, o_gb2)):
        ref[...] = red_v[i : i + 1, :]
    _, quarter, units = red_a.shape[1:]
    o_up[:quarter, :] = red_a[0, 0].astype(F32)
    o_up[quarter:, :] = red_a[1, 0].astype(F32)
    o_dn[:, :quarter] = red_a[0, 1].astype(F32).T
    o_dn[:, quarter:] = red_a[1, 1].astype(F32).T
    eighth = quarter // 2
    for core in range(2):
        for y in range(2):
            base = (2 * core + y) * eighth
            o_wo[base : base + eighth, :] = red_s[0, core, y, 0].astype(F32)
    for m, ref in ((1, o_gw1), (2, o_gw2)):
        full = [red_s[0, core, y, m] for core in range(2) for y in range(2)]
        ref[...] = jnp.concatenate(full, 0).astype(F32).T
    for i, ref in enumerate((o_wq, o_wk, o_wv)):
        full = []
        for t in range(heads):
            full.append(red_s[1, t % 2, t // 2, i])
        ref[...] = jnp.concatenate(full, 0).astype(F32).T


def local(
    tokens, ln1_gain, ln1_bias, w_query, w_key, w_value, w_out, gate1_weight, gate1_bias,
    ln2_gain, ln2_bias, gate2_weight, gate2_bias, w_up, w_down, lengths, cotangent,
):
    nb, nh = lax.axis_size("batch"), lax.axis_size("hidden")
    rows, cw = tokens.shape
    units = w_up.shape[1]
    heads = cw // HD
    dph = nh // heads
    tq, half, wide, nz, pairs = rows // dph, rows // 2, 2 * cw, nh // 2, nb // 2
    quarter = half // 2
    zr = HD * 4 // nz
    per = half // tq
    sizes = (nb, nh, rows, cw, units, heads, dph, tq)

    ins = dict(
        lens=lengths, tok=tokens, cot=cotangent, v0=ln1_gain[None], v1=ln1_bias[None], v2=gate1_bias[None],
        v3=ln2_gain[None], v4=ln2_bias[None], v5=gate2_bias[None], wq=w_query, wk=w_key, wv=w_value,
        wo=w_out, wg1=gate1_weight, wg2=gate2_weight, wu=w_up, wd=w_down,
    )
    results = dict(
        out_c=((rows, cw), BF16),
        gtok=((rows, cw), F32),
        red_a=((2, 2, quarter, units), BF16),
        red_s=((2, 2, 2, 3, HD, wide), BF16),
        red_v=((8, cw), F32),
    )
    outs = {"h_" + name: spec for name, spec in results.items()}
    bufs = dict(
        **results, tally=((8192, 128), F32), wqkv=((3, wide, cw), BF16),
        vsrc=((8, cw), F32), vecf=((8, wide), F32), tokf=((rows, wide), BF16), cotr=((half, wide), BF16),
        g1f=((2, wide, cw), BF16), g2f=((2, wide, cw), BF16), wof=((2, cw, wide), BF16),
        wup=((nz, 2, 2, cw, units), BF16), wdn=((nz, 2, 2, units, cw), BF16),
        wt=((heads, 3 * HD, wide), BF16), npair=((2, rows, wide), BF16),
        qsrc=((heads, HD, rows), BF16), kvsrc=((heads, 2 * HD, rows), BF16),
        kvt=((nh, 2 * HD, rows), BF16), kvn=((nh, rows, 2 * HD), BF16), qt=((nh, HD, tq), BF16),
        qlow=((nh, 2 * HD, tq), BF16), dhigh=((nh, 2 * HD, tq), BF16), top=((nh, 1, tq), F32), total=((nh, 1, tq), F32),
        centre=((nh, 1, tq), F32), dqa=((nh, HD, tq), F32), ot=((nh, HD, tq), F32), lse=((nh, 1, tq), F32), osend=((nh, HD, tq), BF16),
        att=((2 * heads * HD, half), BF16),
        pre=((nz, 2, half, units), F32), actall=((half, nh * units), BF16), acts=((nz, half, units), BF16), actp=((nz, rows, units), BF16),
        gpres=((nz, half, units), BF16), gprep=((nz, rows, units), BF16),
        outr=((half, wide), BF16), gatt=((wide, half), BF16), dot=((nh, HD, tq), BF16),
        ginp=((half, wide), F32), gterm=((half, wide), F32), npt=((wide, rows), BF16), gbt=((wide, rows), BF16),
        lsrc=((3, wide, half), BF16), bpair=((3, rows, wide), BF16), apair=((3, 2, quarter, rows), BF16),
        vsum=((8, wide), F32),
        gb=((2, 2, 3, HD, wide), BF16), ybin=((2, 3, HD, wide), BF16), xbin=((3, HD, wide), BF16),
        ga=((2, nz, 2, 2, quarter, units), BF16), xin0=((nz, 2, quarter, units), BF16),
        yin1=((nz, 2, quarter, units), BF16), yin0=((nz, quarter, units), BF16), xin1=((nz, quarter, units), BF16),
        zs=((nz, 2, quarter, units), BF16), zin=((nz, 2, quarter, units), BF16),
        pin=((pairs, 2, quarter, units), BF16),
        gc=((2, 3, HD, wide), BF16), ycin=((3, HD, wide), BF16), sq=((2, 3, HD, wide), BF16),
        pzin=((2, 3, nz, zr, 128), BF16), sqpair=((2, 3, pairs, zr, 128), BF16),
        acc=((nh, 2 * HD, rows), F32), pin_kv=((nh // dph, max(dph - 1, 1), 2 * HD, rows), F32),
        dkvsend=((nh, 2 * HD, rows), BF16), dqsend=((nh, HD, tq), BF16),
        dqkv=((heads, 3 * HD, rows), BF16), dsib=((heads // 2, 3 * HD, rows), BF16),
        psend=((half, wide), BF16), precv=((half, wide), BF16),
        tsend=((half, wide), BF16), trecv=((half, cw), BF16),
        vin4=((4, 8, wide), F32), vinz=((nz, 8, wide), F32), vinb=((nb, 8, wide), F32),
    )
    sems = dict(
        ls=(6,), os=(5,), snd=(8,), xr=(10,), wzs=(2, nz), wzr=(nz,), gxr=(1,), gcr=(1,), kr=(nh,), qr=(nh,), cr=(3,),
        wxr=(nz,), wyr=(1,), wcr=(2,), fr=(nh,), orc=(1,), ar=(1,), pr=(1,), dr=(2,), yr=(4,), zsr=(nz,), par=(pairs,),
        sqpr=(2, 3, pairs) if pairs > 1 else (1,), pyr=(3,), pzr=(2, 3), pgr=(2, 3), sxr=(1,), syr=(1,), sbr=(2, 3),
        scr=(2,), pkr=(nh // dph, max(dph - 1, 1)), dkr=(heads,), tr=(1,), vr=(3,),
    )
    names = list(ins) + list(outs) + list(bufs) + list(sems)
    vmem = pl.BlockSpec(memory_space=pltpu.VMEM)
    any_space = pl.BlockSpec(memory_space=pl.ANY)
    in_specs = [vmem if name[0] == "v" else any_space for name in list(ins)[1:]]
    sums = pl.pallas_call(
        functools.partial(layer_kernel, names, sizes),
        out_shape=[jax.ShapeDtypeStruct(shape, kind) for shape, kind in outs.values()],
        in_specs=[pl.BlockSpec(memory_space=pltpu.SMEM)] + in_specs,
        out_specs=[any_space] * len(outs),
        scratch_shapes=[pltpu.VMEM(shape, kind) for shape, kind in bufs.values()]
        + [pltpu.SemaphoreType.DMA(shape) for shape in sems.values()],
        compiler_params=pltpu.CompilerParams(
            collective_id=1, has_side_effects=True, vmem_limit_bytes=VMEM_LIMIT
        ),
        cost_estimate=pl.CostEstimate(flops=10**10, bytes_accessed=10**7, transcendentals=10**7),
    )(*ins.values())
    grads = [
        ((rows, cw), BF16), ((rows, cw), F32), ((1, cw), F32), ((1, cw), F32),
        ((wide, cw), F32), ((wide, cw), F32), ((wide, cw), F32), ((cw, wide), F32),
        ((wide, cw), F32), ((1, cw), F32), ((1, cw), F32), ((1, cw), F32), ((wide, cw), F32), ((1, cw), F32),
        ((cw, units), F32), ((units, cw), F32),
    ]
    done = pl.pallas_call(
        functools.partial(final_kernel, heads),
        out_shape=[jax.ShapeDtypeStruct(shape, kind) for shape, kind in grads],
        in_specs=[vmem] * len(outs),
        out_specs=[vmem] * len(grads),
        compiler_params=pltpu.CompilerParams(vmem_limit_bytes=VMEM_LIMIT),
    )(*sums)
    return tuple(a[0] if a.shape[0] == 1 else a for a in done)


def solution(mesh):
    cols = P(None, "width")
    vec = P("width")
    in_specs = (
        P(("batch", "hidden"), "width"), vec, vec, cols, cols, cols, P("width", None), cols, vec, vec, vec,
        cols, vec, P("width", "hidden"), P("hidden", "width"), P("batch", None),
        P(("batch", "hidden"), "width"),
    )
    out_specs = (
        P(("batch", "hidden"), "width"), P(("batch", "hidden"), "width"), vec, vec, cols, cols, cols,
        P("width", None), cols, vec, vec, vec, cols, vec, P("width", "hidden"), P("hidden", "width"),
    )
    return jax.shard_map(local, mesh=mesh, in_specs=in_specs, out_specs=out_specs, check_vma=False)
```
